32 devices in a mesh: dp: 8 (over y, x, core), tensor: 4 (over z).
Axes of the slice: x: 2, y: 2, z: 4, core: 2. Of those that a mesh axis runs over, the one named last changes fastest.
Arguments:
- tokens: bfloat16 [4096, 2048], P('dp'), may hold values from -6 to 6
- cotangent: bfloat16 [4096, 2048], P('dp'), may hold values from -6 to 6
- parents: int32 [8, 4], P('dp'), may hold values from 0 to 2, as said below
- attention_routes: int32 [4096, 2], P('dp'), may hold values from 0 to 7, all different within a row; in each aligned block of 512 rows (0 to 511, 512 to 1023, ...) at most 160 rows name the same one
- expert_routes: int32 [4096, 2], P('dp'), may hold values from 0 to 7, all different within a row
- slot_order: int32 [8, 512], P('dp'), may hold values from 0 to 511, each once within a row
- gain_attention: bfloat16 [2048], P('dp'), may hold values from 0.5 to 1.5
- keyval_weight: bfloat16 [2, 2048, 2048], P(None, 'dp', 'tensor'), may hold values from -0.125 to 0.125
- query_weight: bfloat16 [8, 2048, 2048], P(None, 'dp', 'tensor'), may hold values from -0.125 to 0.125
- output_weight: bfloat16 [8, 2048, 2048], P(None, 'tensor', 'dp'), may hold values from -1.5 to 1.5
- attention_router: bfloat16 [2048, 8], P('dp'), may hold values from -0.0625 to 0.0625
- gain_feedforward: bfloat16 [2048], P('dp'), may hold values from 0.5 to 1.5
- expert_router: bfloat16 [2048, 8], P('dp'), may hold values from -0.0625 to 0.0625
- gate_up_weight: bfloat16 [8, 2, 2048, 5632], P(None, None, 'dp', 'tensor'), may hold values from -0.125 to 0.125
- down_weight: bfloat16 [8, 5632, 2048], P(None, 'tensor', 'dp'), may hold values from -0.15625 to 0.15625
Outputs:
- mixed: bfloat16 [4096, 2048], P('dp')
- grad_tokens: float32 [4096, 2048], P('dp')
- grad_gain_attention: float32 [2048], P('dp')
- grad_keyval: float32 [2, 2048, 2048], P(None, 'dp', 'tensor')
- grad_query: float32 [8, 2048, 2048], P(None, 'dp', 'tensor')
- grad_output: float32 [8, 2048, 2048], P(None, 'tensor', 'dp')
- grad_attention_router: float32 [2048, 8], P('dp')
- grad_gain_feedforward: float32 [2048], P('dp')
- grad_expert_router: float32 [2048, 8], P('dp')
- grad_gate_up: float32 [8, 2, 2048, 5632], P(None, None, 'dp', 'tensor')
- grad_down: float32 [8, 5632, 2048], P(None, 'tensor', 'dp')
The draws below stay inside these ranges and needn't reach their ends.
Inputs may be any that keep to these rules, and one draw needn't show every extreme that they name: `parents`: segment 0 of each tree is its root with parent 0; every other segment's parent is an earlier segment, and the last segment's parent is the one before it. `attention_routes`: each token names two different attention experts; among the pairs of one tree no attention expert is named more than 160 times, and in every draw some tree names some expert exactly 160 times. `expert_routes`: each token names two different feed-forward experts. `slot_order`: each tree's row holds every number of 0 to 511 once.
All inputs are finite; a program needn't handle non-finite values.
Results may differ from the reference program's by a relative error of at most 0.019.
Values may be sent and summed in bfloat16 or wider, within the bound.
A program may use at most 512 MiB of HBM per device.

```python
import math
import jax
import jax.numpy as jnp
import numpy as np
from jax import lax

D = 2048
H = 16
HD = 128
FF = 5632
EA = 8
EM = 8
TOPK = 2
SEG = 128
SEGS = 4
TOK_DEV = 512
TREES = 8
TOKENS = 4096
CAP_ATT = 160
CAP_MLP = 128


def draw_parents(key, part):
    key = jax.random.fold_in(key, 11)
    segment_index = jnp.arange(SEGS, dtype=jnp.int32)
    picks = jax.random.randint(key, (TREES, SEGS), 0, 1 << 20)
    parent = picks % jnp.maximum(segment_index, 1)[None, :]
    parent = jnp.where(segment_index[None, :] == SEGS - 1, max(SEGS - 2, 0), parent)
    return parent.astype(jnp.int32)


def levels(own_key, dims, pieces, least, largest):
    level = 1.0
    for axis_at, parts in pieces:
        steps = jax.random.uniform(jax.random.fold_in(jax.random.fold_in(own_key, 6), axis_at), (parts,), jnp.float32, least / len(pieces), largest / len(pieces))
        level = level * jnp.repeat(jnp.exp(steps), dims[axis_at] // parts).reshape((-1,) + (1,) * (len(dims) - 1 - axis_at))
    return level


def distinct(rng, rows, amount, top, lift):
    ranking = jax.random.permutation(jax.random.fold_in(rng, 1), amount)
    boost = ranking
    for power in range(3):
        boost = boost * boost // amount
    boost = boost * lift // amount
    chance = jax.random.randint(jax.random.fold_in(rng, 2), (rows, amount), 0, 4096) + boost
    holders = jax.random.permutation(jax.random.fold_in(rng, 3), rows)[jnp.arange(amount) % rows]
    chance = jnp.where(jnp.arange(rows)[:, None] == holders[None, :], 1 << 14, chance)
    score = chance * amount + jnp.arange(amount)
    return lax.top_k(score.astype(jnp.int32), top)[1].astype(jnp.int32)


def routed_block(rng, own, number, rows, count, top, bound, lean):
    sequence = jax.random.permutation(rng, count)
    crowded, ordinary = shares(count, rows * top, bound, lean, True), shares(count, rows * top, bound, lean, False)
    places = jnp.arange(count)

    def named(lengths, rotation):
        used = int((lengths > 0).sum())
        fixed = max(1, used // 4)
        shifted = fixed + (places - fixed + rotation * (used - fixed)) % max(1, count - fixed)
        return jnp.zeros((count,), jnp.int32).at[sequence[jnp.where(places < fixed, places, shifted)]].set(jnp.asarray(lengths, jnp.int32))

    lengths = jnp.where(number % 4 == 0, named(crowded, number // 4), named(ordinary, number - number // 4 - 1))
    mixed = jax.random.permutation(jax.random.fold_in(own, 3), count)
    giver, receiver = mixed[0:count // 2 * 2:2], mixed[1:count // 2 * 2:2]
    margin = jnp.minimum(lengths[giver] - 1, bound - lengths[receiver]) // 2
    margin = jnp.where((giver == sequence[0]) | (receiver == sequence[0]) | (lengths[receiver] == 0), 0, jnp.maximum(margin, 0))
    shifted = jax.random.randint(jax.random.fold_in(own, 4), (count // 2,), 0, 1 << 20) % (margin + 1)
    lengths = lengths.at[giver].add(-shifted).at[receiver].add(shifted)
    members = jnp.searchsorted(jnp.cumsum(lengths), jnp.arange(rows * top), side="right").astype(jnp.int32)
    listing = members.reshape(top, rows).T
    listing = listing[jax.random.permutation(jax.random.fold_in(own, 1), rows)]
    rotation = jax.random.randint(jax.random.fold_in(own, 2), (rows, 1), 0, top)
    return jnp.take_along_axis(listing, (jnp.arange(top)[None, :] + rotation) % top, axis=1)


def shares(number_of, total, limit, slope, full):
    weights = [(1 << 20) // math.isqrt(rank ** slope) + 1 for rank in range(1, number_of + 1)]
    largest = limit if full else min(limit, max(-(-total // number_of), total * weights[0] // sum(weights)))
    least = 1 if total - largest >= number_of - 1 else 0
    given, surplus = [largest] + [least] * (number_of - 1), total - largest - least * (number_of - 1)
    while surplus > 0:
        candidates = [i for i in range(1, number_of) if given[i] < largest] or [i for i in range(1, number_of) if given[i] < limit]
        pool, remaining = sum([weights[i] for i in candidates]), surplus
        for i in candidates:
            extra = min(limit - given[i], max(1, remaining * weights[i] // pool), surplus)
            given[i] = given[i] + extra
            surplus = surplus - extra
    return np.array(given)


def bell_draw(rng, extent, deviation, reach, cuts=(), kind=jnp.bfloat16):
    entries = jax.random.normal(rng, extent, jnp.float32) * deviation
    if len(cuts) > 0:
        entries = levels(rng, extent, cuts, -0.22, 0.18) * entries
    return jnp.clip(entries, min=-reach, max=reach).astype(kind)


def setup_inputs(seed: int = 0) -> dict:
    key_of = jax.random.split(jax.random.key(seed), 16)
    tokens = bell_draw(key_of[0], (TOKENS, D), 1.0, 6.0, ((0, 8),))
    cotangent = bell_draw(key_of[1], (TOKENS, D), 1.0, 6.0, ((0, 8),))
    parents = draw_parents(jax.random.fold_in(key_of[15], 71), 0)
    attention_routes_keys = jax.random.split(jax.random.fold_in(key_of[3], 1), TOKENS // TOK_DEV)
    attention_routes_turns = jax.random.permutation(jax.random.fold_in(key_of[3], 3), TOKENS // TOK_DEV)
    attention_routes = jax.vmap(lambda own, number: routed_block(jax.random.fold_in(key_of[3], 2), own, number, TOK_DEV, EA, TOPK, CAP_ATT, 0))(attention_routes_keys, attention_routes_turns).reshape((TOKENS, TOPK))
    expert_routes = distinct(key_of[4], TOKENS, EM, TOPK, 2048)
    slot_order = jax.vmap(lambda own: jax.random.permutation(own, TOK_DEV))(jax.random.split(key_of[5], TREES)).reshape((TREES, TOK_DEV)).astype(jnp.int32)
    gain_attention = jnp.clip(1.0 + 0.1 * jax.random.normal(key_of[6], (D,), jnp.float32), 0.5, 1.5).astype(jnp.bfloat16)
    keyval_weight = bell_draw(key_of[7], (2, D, H * HD), D ** -0.5, 0.125, ((1, 8), (2, 4)))
    query_weight = bell_draw(key_of[8], (EA, D, H * HD), D ** -0.5, 0.125, ((1, 8), (2, 4)))
    output_weight = bell_draw(key_of[9], (EA, H * HD, D), 16 ** -0.5, 1.5, ((1, 4), (2, 8)))
    attention_router = bell_draw(key_of[10], (D, EA), (4 * D) ** -0.5, 0.0625, ((0, 8),))
    gain_feedforward = jnp.clip(1.0 + 0.1 * jax.random.normal(key_of[11], (D,), jnp.float32), 0.5, 1.5).astype(jnp.bfloat16)
    expert_router = bell_draw(key_of[12], (D, EM), (4 * D) ** -0.5, 0.0625, ((0, 8),))
    gate_up_weight = bell_draw(key_of[13], (EM, 2, D, FF), D ** -0.5, 0.125, ((2, 8), (3, 4)))
    down_weight = bell_draw(key_of[14], (EM, FF, D), (FF // 4) ** -0.5, 0.15625, ((1, 4), (2, 8)))
    return {"tokens": tokens, "cotangent": cotangent, "parents": parents, "attention_routes": attention_routes, "expert_routes": expert_routes, "slot_order": slot_order, "gain_attention": gain_attention, "keyval_weight": keyval_weight, "query_weight": query_weight, "output_weight": output_weight, "attention_router": attention_router, "gain_feedforward": gain_feedforward, "expert_router": expert_router, "gate_up_weight": gate_up_weight, "down_weight": down_weight}


EPSILON = 1e-06
NEGATIVE = -1e+30
ROPE_BASE = 10000.0
PRECISE = lax.Precision.HIGHEST

@jax.custom_vjp
def low(v):
    return lax.optimization_barrier(v.astype(jnp.bfloat16)).astype(jnp.float32)

@jax.custom_vjp
def low_back(v):
    return v

def low_keep(v):
    return (low(v), None)

def low_pass(kept, grad):
    return (grad,)

def back_keep(v):
    return (v, None)

def back_low(kept, grad):
    return (low(grad),)
low.defvjp(low_keep, low_pass)
low_back.defvjp(back_keep, back_low)

def pad_rows(matrix):
    return jnp.concatenate([matrix, jnp.zeros((1,) + matrix.shape[1:], matrix.dtype)], axis=0)

def slot_maps(routes, priority, capacity, experts):
    pair_total = routes.shape[0] * routes.shape[1]
    flat_routes = routes.reshape(pair_total).astype(jnp.int32)
    flat_order = priority.reshape(pair_total).astype(jnp.int32)
    numbers = jnp.arange(pair_total, dtype=jnp.int32)
    inverse = jnp.zeros((pair_total,), jnp.int32).at[flat_order].set(numbers)
    ordered = flat_routes[inverse]
    one_hot = (ordered[:, None] == jnp.arange(experts, dtype=jnp.int32)[None, :]).astype(jnp.int32)
    before = jnp.cumsum(one_hot, axis=0) - one_hot
    slot_rank = lax.optimization_barrier(jnp.sum(before * one_hot, axis=1))[flat_order]
    slot_place = jnp.where(slot_rank < capacity, flat_routes * capacity + slot_rank, experts * capacity).astype(jnp.int32)
    slot_source = jnp.full((experts * capacity + 1,), pair_total, jnp.int32).at[slot_place].set(numbers)
    return (slot_place, slot_source[:experts * capacity])

def ancestry(parent_row):
    segment_count = parent_row.shape[0]
    indices = jnp.arange(segment_count, dtype=jnp.int32)
    walker = indices
    inside = indices[:, None] == indices[None, :]
    for travel in range(segment_count):
        walker = parent_row[walker]
        inside = inside | (walker[:, None] == indices[None, :])
    depth = lax.optimization_barrier(jnp.sum(inside.astype(jnp.int32), axis=1)) - 1
    return (inside, depth)

def rope_tables(position):
    half_width = HD // 2
    frequency = ROPE_BASE ** (-jnp.arange(half_width, dtype=jnp.float32) / half_width)
    angles = position.astype(jnp.float32)[:, None] * frequency[None, :]
    return (jnp.cos(angles)[:, None, :], jnp.sin(angles)[:, None, :])

def rotate(vector, cosine_table, sine_table):
    half_width = vector.shape[-1] // 2
    former, latter = (vector[..., :half_width], vector[..., half_width:])
    return jnp.concatenate([former * cosine_table - latter * sine_table, latter * cosine_table + former * sine_table], axis=-1)

def norm_of(values_in, gain):
    return values_in * lax.rsqrt(lax.optimization_barrier(jnp.mean(values_in * values_in, axis=-1, keepdims=True)) + EPSILON) * gain

def tree_forward(token_rows, parent_row, attention_pick, expert_pick, order_row, weights):
    gain_attention, keyval_weight, query_weight, output_weight, attention_router, gain_feedforward, expert_router, gate_up_weight, down_weight = weights
    tok_count = token_rows.shape[0]
    pair_count = TOPK * tok_count
    inside, depth = ancestry(parent_row)
    token_index = jnp.arange(tok_count, dtype=jnp.int32)
    segment = token_index // SEG
    position = depth[segment] * SEG + token_index % SEG
    cosine_table, sine_table = rope_tables(position)
    pair_token = jnp.arange(pair_count, dtype=jnp.int32) // TOPK
    normed = low(norm_of(token_rows, gain_attention))
    kv_raw = low_back(jnp.einsum('td,cdf->ctf', normed, keyval_weight, precision=PRECISE))
    key_rows = low(rotate(kv_raw[0].reshape(tok_count, H, HD), cosine_table, sine_table))
    values = low(kv_raw[1].reshape(tok_count, H, HD))
    att_logits = low_back(jnp.dot(normed, attention_router, precision=PRECISE))
    att_gates = jax.nn.softmax(jnp.take_along_axis(att_logits, attention_pick, axis=1), axis=-1)
    pair_order = jnp.arange(pair_count, dtype=jnp.int32).reshape(tok_count, TOPK)
    att_place, att_source = slot_maps(attention_pick, pair_order, CAP_ATT, EA)
    slot_token = jnp.where(att_source < pair_count, att_source // TOPK, tok_count)
    routed = pad_rows(normed)[slot_token].reshape(EA, CAP_ATT, D)
    query_slots = low_back(jnp.einsum('ecd,edf->ecf', routed, query_weight, precision=PRECISE))
    query_raw = query_slots.reshape(EA * CAP_ATT, H * HD)[att_place]
    queries = low(rotate(query_raw.reshape(pair_count, H, HD), cosine_table[pair_token], sine_table[pair_token]))
    allowed = inside[segment[pair_token]][:, segment] & (token_index[None, :] <= pair_token[:, None])
    scores = low_back(jnp.einsum('phd,jhd->hpj', queries, key_rows, precision=PRECISE) * HD ** (-0.5))
    scores = jnp.where(allowed[None], scores, NEGATIVE)
    probs = low(jax.nn.softmax(scores, axis=-1))
    attended = low_back(jnp.einsum('hpj,jhd->phd', probs, values, precision=PRECISE)).reshape(pair_count, H * HD)
    gated = low(attended * att_gates.reshape(pair_count, 1))
    gated_slots = pad_rows(gated)[att_source].reshape(EA, CAP_ATT, H * HD)
    att_slots = low_back(jnp.einsum('ecf,efd->ecd', gated_slots, output_weight, precision=PRECISE))
    att_out = att_slots.reshape(EA * CAP_ATT, D)[att_place].reshape(tok_count, TOPK, D).sum(axis=1)
    hidden_state = token_rows + att_out
    mlp_in = low(norm_of(hidden_state, gain_feedforward))
    mlp_logits = low_back(jnp.dot(mlp_in, expert_router, precision=PRECISE))
    mlp_gates = jax.nn.softmax(jnp.take_along_axis(mlp_logits, expert_pick, axis=1), axis=-1)
    priority = order_row[:, None] * TOPK + jnp.arange(TOPK, dtype=jnp.int32)[None, :]
    mlp_place, mlp_source = slot_maps(expert_pick, priority, CAP_MLP, EM)
    mlp_token = jnp.where(mlp_source < pair_count, mlp_source // TOPK, tok_count)
    expert_in = pad_rows(mlp_in)[mlp_token].reshape(EM, CAP_MLP, D)
    gate_up = low_back(jnp.einsum('ecd,egdf->egcf', expert_in, gate_up_weight, precision=PRECISE))
    activated = low(jax.nn.silu(gate_up[:, 0]) * gate_up[:, 1])
    expert_out = low_back(jnp.einsum('ecf,efd->ecd', activated, down_weight, precision=PRECISE))
    routed_out = pad_rows(expert_out.reshape(EM * CAP_MLP, D))[mlp_place]
    mlp_out = (routed_out * mlp_gates.reshape(pair_count, 1)).reshape(tok_count, TOPK, D).sum(axis=1)
    return hidden_state + mlp_out

def reference(tokens, cotangent, parents, attention_routes, expert_routes, slot_order, gain_attention, keyval_weight, query_weight, output_weight, attention_router, gain_feedforward, expert_router, gate_up_weight, down_weight):
    weights = tuple((weight_arg.astype(jnp.float32) for weight_arg in (gain_attention, keyval_weight, query_weight, output_weight, attention_router, gain_feedforward, expert_router, gate_up_weight, down_weight)))
    inputs = tokens.astype(jnp.float32).reshape(TREES, TOK_DEV, D)
    cotangents = cotangent.astype(jnp.float32).reshape(TREES, TOK_DEV, D)
    att_trees = attention_routes.reshape(TREES, TOK_DEV, TOPK)
    mlp_trees = expert_routes.reshape(TREES, TOK_DEV, TOPK)

    def forward(input_trees, weight_set):

        def one_tree(state_in, sliced):
            return (state_in, jax.checkpoint(tree_forward)(sliced[0], sliced[1], sliced[2], sliced[3], sliced[4], weight_set))
        state_out, outputs = lax.scan(one_tree, jnp.zeros((), jnp.float32), (input_trees, parents, att_trees, mlp_trees, slot_order))
        return outputs
    outputs, pullback = jax.vjp(forward, inputs, weights)
    grad_inputs, grad_weights = pullback(cotangents)
    mixed = outputs.reshape(TOKENS, D).astype(jnp.bfloat16)
    return (mixed, grad_inputs.reshape(TOKENS, D), grad_weights[0], grad_weights[1], grad_weights[2], grad_weights[3], grad_weights[4], grad_weights[5], grad_weights[6], grad_weights[7], grad_weights[8])
```

```python
import functools

import jax
import jax.numpy as jnp
from jax import lax
from jax.experimental import pallas as pl
from jax.experimental.pallas import tpu as pltpu
from jax.sharding import PartitionSpec as P

HD = 128
TOPK = 2
SEG = 128

EPSILON = 1e-06
NEGATIVE = -1e30
ROPE_BASE = 10000.0
F32 = jnp.float32
BF16 = jnp.bfloat16


def dot(a, b, out=F32):
    return jnp.dot(a, b, preferred_element_type=out)


def dot_tn(a, b, out=F32):
    return lax.dot_general(a, b, (((0,), (0,)), ((), ())), preferred_element_type=out)


def dot_nt(a, b, out=F32):
    return lax.dot_general(a, b, (((1,), (1,)), ((), ())), preferred_element_type=out)


def slot_places(routes, priority, capacity, experts):
    pair_total = routes.shape[0] * routes.shape[1]
    flat_routes = routes.reshape(pair_total)
    flat_order = priority.reshape(pair_total)
    same_expert = flat_routes[:, None] == flat_routes[None, :]
    earlier = flat_order[None, :] < flat_order[:, None]
    slot_rank = jnp.sum((same_expert & earlier).astype(jnp.int32), axis=1)
    slot_place = jnp.where(
        slot_rank < capacity, flat_routes * capacity + slot_rank, experts * capacity
    )
    return slot_place.reshape(routes.shape)


def slot_hits(place, slots):
    index = jnp.arange(slots, dtype=jnp.int32)[:, None]
    return [place[:, k][None, :] == index for k in range(place.shape[1])]


def ancestry(parent_row):
    segment_count = parent_row.shape[0]
    indices = jnp.arange(segment_count, dtype=jnp.int32)
    walker = indices
    inside = indices[:, None] == indices[None, :]
    for travel in range(segment_count):
        walker = parent_row[walker]
        inside = inside | (walker[:, None] == indices[None, :])
    depth = jnp.sum(inside.astype(jnp.int32), axis=1) - 1
    return (inside, depth)


def rope_tables(position):
    half_width = HD // 2
    frequency = ROPE_BASE ** (-jnp.arange(half_width, dtype=F32) / half_width)
    angles = position.astype(F32)[:, None] * frequency[None, :]
    cosine, sine = jnp.cos(angles), jnp.sin(angles)
    return (
        jnp.concatenate([cosine, cosine], axis=1),
        jnp.concatenate([-sine, sine], axis=1),
    )


def norm_forward(values_in):
    scale = lax.rsqrt(jnp.mean(values_in * values_in, axis=-1, keepdims=True) + EPSILON)
    return (values_in * scale, scale)


def norm_backward(grad_normed, normal, scale, gain):
    weighted = grad_normed * gain
    grad_in = scale * (weighted - normal * jnp.mean(weighted * normal, axis=-1, keepdims=True))
    return (grad_in, jnp.sum(grad_normed * normal, axis=0))


def router_backward(gates, grad_gates, picks, experts):
    grad_select = gates * (grad_gates - jnp.sum(gates * grad_gates, axis=1, keepdims=True))
    picked_hot = (picks[:, :, None] == jnp.arange(experts, dtype=jnp.int32)[None, None, :]).astype(
        F32
    )
    return jnp.sum(picked_hot * grad_select[:, :, None], axis=1).astype(BF16)


def picked_softmax(logits, picks):
    experts = logits.shape[1]
    hot = picks[:, :, None] == jnp.arange(experts, dtype=jnp.int32)[None, None, :]
    return jax.nn.softmax(jnp.sum(jnp.where(hot, logits[:, None, :], 0.0), axis=2), axis=-1)


def rope(v, cosine, sine):
    return v * cosine + pltpu.roll(v, HD // 2, axis=1) * sine


def rope_back(v, cosine, sine):
    return v * cosine - pltpu.roll(v, HD // 2, axis=1) * sine


def softmax_block(q, k, bias):
    scores = dot_nt(q, k) * HD ** (-0.5) + bias
    exp_scores = jnp.exp(scores - jnp.max(scores, axis=-1, keepdims=True))
    return exp_scores / jnp.sum(exp_scores, axis=-1, keepdims=True)


def attend_kernel(
    rows, q_raw, k_raw, v_raw, bias, gate, slot_cos, slot_sin, tok_cos, tok_sin,
    q_out, k_out, v_out, att_out, gated_out,
):
    k_out[...] = rope(k_raw[...], tok_cos[...], tok_sin[...]).astype(BF16)
    v_out[...] = v_raw[...].astype(BF16)

    @pl.loop(0, q_raw.shape[0] // rows)
    def _(i):
        at = pl.ds(pl.multiple_of(i * rows, rows), rows)
        q = rope(q_raw[at, :], slot_cos[at, :], slot_sin[at, :]).astype(BF16)
        q_out[at, :] = q
        probs = softmax_block(q, k_out[...], bias[at, :].astype(F32)).astype(BF16)
        attended = dot(probs, v_out[...])
        att_out[at, :] = attended
        gated_out[at, :] = (attended * gate[at, :]).astype(BF16)


def attend(q_raw, keyval, bias, gate, slot_tables, tok_tables):
    slots, width = q_raw.shape
    tok = keyval.shape[0]
    heads = width // HD
    head = lambda h: (0, h)
    whole = lambda h: (0, 0)
    rows = 256
    return pl.pallas_call(
        functools.partial(attend_kernel, rows),
        grid=(heads,),
        in_specs=[
            pl.BlockSpec((slots, HD), head),
            pl.BlockSpec((tok, HD), head),
            pl.BlockSpec((tok, HD), lambda h: (0, heads + h)),
            pl.BlockSpec((slots, tok), whole),
            pl.BlockSpec((slots, 1), whole),
            pl.BlockSpec((slots, HD), whole),
            pl.BlockSpec((slots, HD), whole),
            pl.BlockSpec((tok, HD), whole),
            pl.BlockSpec((tok, HD), whole),
        ],
        out_specs=[
            pl.BlockSpec((slots, HD), head),
            pl.BlockSpec((tok, HD), head),
            pl.BlockSpec((tok, HD), head),
            pl.BlockSpec((slots, HD), head),
            pl.BlockSpec((slots, HD), head),
        ],
        out_shape=[
            jax.ShapeDtypeStruct((slots, width), BF16),
            jax.ShapeDtypeStruct((tok, width), BF16),
            jax.ShapeDtypeStruct((tok, width), BF16),
            jax.ShapeDtypeStruct((slots, width), F32),
            jax.ShapeDtypeStruct((slots, width), BF16),
        ],
        compiler_params=pltpu.CompilerParams(vmem_limit_bytes=40 << 20),
        cost_estimate=pl.CostEstimate(
            flops=4 * slots * tok * width,
            bytes_accessed=slots * width * 12 + slots * tok * 2,
            transcendentals=slots * tok * heads,
        ),
    )(q_raw, keyval, keyval, bias, gate, *slot_tables, *tok_tables)


def attend_back_kernel(
    rows, q_ref, k_ref, v_ref, bias, gate, slot_cos, slot_sin, tok_cos, tok_sin, grad_gated,
    gq_out, gk_out, gv_out, gk_sum, gv_sum,
):
    gk_sum[...] = jnp.zeros_like(gk_sum)
    gv_sum[...] = jnp.zeros_like(gv_sum)

    @pl.loop(0, q_ref.shape[0] // rows)
    def _(i):
        at = pl.ds(pl.multiple_of(i * rows, rows), rows)
        q = q_ref[at, :]
        probs = softmax_block(q, k_ref[...], bias[at, :].astype(F32))
        grad_att = (grad_gated[at, :] * gate[at, :]).astype(BF16)
        grad_probs = dot_nt(grad_att, v_ref[...])
        centre = jnp.sum(probs * grad_probs, axis=-1, keepdims=True)
        grad_scores = (probs * (grad_probs - centre)).astype(BF16)
        grad_q = dot(grad_scores, k_ref[...]) * HD ** (-0.5)
        gq_out[at, :] = rope_back(grad_q, slot_cos[at, :], slot_sin[at, :]).astype(BF16)
        gk_sum[...] += dot_tn(grad_scores, q)
        gv_sum[...] += dot_tn(probs.astype(BF16), grad_att)

    grad_k = gk_sum[...] * HD ** (-0.5)
    gk_out[...] = rope_back(grad_k, tok_cos[...], tok_sin[...]).astype(BF16)
    gv_out[...] = gv_sum[...].astype(BF16)


def attend_back(q, k, v, bias, gate, slot_tables, tok_tables, grad_gated):
    slots, width = q.shape
    tok = k.shape[0]
    heads = width // HD
    head = lambda h: (0, h)
    whole = lambda h: (0, 0)
    rows = 256
    return pl.pallas_call(
        functools.partial(attend_back_kernel, rows),
        grid=(heads,),
        in_specs=[
            pl.BlockSpec((slots, HD), head),
            pl.BlockSpec((tok, HD), head),
            pl.BlockSpec((tok, HD), head),
            pl.BlockSpec((slots, tok), whole),
            pl.BlockSpec((slots, 1), whole),
            pl.BlockSpec((slots, HD), whole),
            pl.BlockSpec((slots, HD), whole),
            pl.BlockSpec((tok, HD), whole),
            pl.BlockSpec((tok, HD), whole),
            pl.BlockSpec((slots, HD), head),
        ],
        out_specs=[
            pl.BlockSpec((slots, HD), head),
            pl.BlockSpec((tok, HD), head),
            pl.BlockSpec((tok, HD), head),
        ],
        out_shape=[
            jax.ShapeDtypeStruct((slots, width), BF16),
            jax.ShapeDtypeStruct((tok, width), BF16),
            jax.ShapeDtypeStruct((tok, width), BF16),
        ],
        scratch_shapes=[pltpu.VMEM((tok, HD), F32), pltpu.VMEM((tok, HD), F32)],
        compiler_params=pltpu.CompilerParams(vmem_limit_bytes=40 << 20),
        cost_estimate=pl.CostEstimate(
            flops=10 * slots * tok * width,
            bytes_accessed=slots * width * 8 + slots * tok * 2,
            transcendentals=slots * tok * heads,
        ),
    )(q, k, v, bias, gate, *slot_tables, *tok_tables, grad_gated)


class Movers:
    def __init__(self, dp, experts):
        self.dp, self.experts, self.ratio = dp, experts, dp // experts
        self.groups = self.pairs = None
        if self.ratio > 1:
            self.groups = [[g * experts + e for e in range(experts)] for g in range(self.ratio)]
            self.pairs = [[g * experts + e for g in range(self.ratio)] for e in range(experts)]

    def swap(self, blocks):
        return lax.all_to_all(blocks, "dp", 0, 0, axis_index_groups=self.groups, tiled=True)

    def fetch(self, shards):
        mine = self.swap(shards)
        if self.ratio > 1:
            mine = lax.all_gather(mine, "dp", axis=0, axis_index_groups=self.pairs, tiled=True)
        return mine

    def give_back(self, slices):
        if self.ratio > 1:
            slices = lax.psum_scatter(
                slices, "dp", scatter_dimension=0, axis_index_groups=self.pairs, tiled=True
            )
        return self.swap(slices)


def reduce_rows(part):
    return lax.psum_scatter(part.astype(BF16), "tensor", scatter_dimension=0, tiled=True).astype(
        F32
    )


def gather_rows(rows):
    return lax.all_gather(rows.astype(BF16), "tensor", axis=0, tiled=True)


def on_device(
    dp_size,
    tensor_size,
    tokens,
    cotangent,
    parents,
    attention_routes,
    expert_routes,
    slot_order,
    gain_attention,
    keyval_weight,
    query_weight,
    output_weight,
    attention_router,
    gain_feedforward,
    expert_router,
    gate_up_weight,
    down_weight,
):
    tok_count, model_width = tokens.shape
    pair_count = TOPK * tok_count
    att_experts = query_weight.shape[0]
    mlp_experts = gate_up_weight.shape[0]
    att_cap = tok_count * 5 // 16
    mlp_cap = pair_count // mlp_experts
    att_slots = att_experts * att_cap
    mlp_slots = mlp_experts * mlp_cap
    width_here = query_weight.shape[2]
    rows_here = tok_count // tensor_size
    movers = Movers(dp_size, mlp_experts)

    small = jnp.concatenate(
        [gain_attention[:, None], gain_feedforward[:, None], attention_router, expert_router], axis=1
    )
    small_full = lax.all_gather(small, "dp", axis=0, tiled=True)
    keyval_full = lax.all_gather(keyval_weight, "dp", axis=1, tiled=True)
    query_full = lax.all_gather(query_weight, "dp", axis=1, tiled=True)
    output_full = lax.all_gather(output_weight, "dp", axis=2, tiled=True)
    gain_attn_full = small_full[:, 0].astype(F32)
    gain_mlp_full = small_full[:, 1].astype(F32)
    router_att = small_full[:, 2 : 2 + att_experts]
    router_mlp = small_full[:, 2 + att_experts :]

    gate_full = movers.fetch(gate_up_weight[:, 0]).reshape(model_width, -1)
    up_full = movers.fetch(gate_up_weight[:, 1]).reshape(model_width, -1)
    down_full = movers.fetch(down_weight)
    down_full = down_full.transpose(1, 0, 2).reshape(down_full.shape[1], model_width)

    inside, depth = ancestry(parents[0])
    token_index = jnp.arange(tok_count, dtype=jnp.int32)
    pair_order = jnp.arange(pair_count, dtype=jnp.int32).reshape(tok_count, TOPK)
    att_hits = slot_hits(
        slot_places(attention_routes, pair_order, att_cap, att_experts), att_slots
    )
    priority = slot_order[0][:, None] * TOPK + jnp.arange(TOPK, dtype=jnp.int32)[None, :]
    mlp_hits = slot_hits(slot_places(expert_routes, priority, mlp_cap, mlp_experts), mlp_slots)
    att_pick = (att_hits[0] | att_hits[1]).astype(BF16)
    mlp_pick = (mlp_hits[0] | mlp_hits[1]).astype(BF16)

    def to_slots(hits, pair_values):
        return jnp.sum(
            sum(jnp.where(hits[k], pair_values[:, k][None, :], 0) for k in range(TOPK)), axis=1
        )

    def to_pairs(hits, slot_values):
        return jnp.stack(
            [jnp.sum(jnp.where(hits[k], slot_values[:, None], 0.0), axis=0) for k in range(TOPK)],
            axis=1,
        )

    def position_of(token):
        segment = token // SEG
        level = jnp.sum(
            jnp.where(segment[:, None] == jnp.arange(depth.shape[0])[None, :], depth[None, :], 0),
            axis=1,
        )
        return level * SEG + token % SEG

    pair_token = jnp.broadcast_to(token_index[:, None], (tok_count, TOPK))
    slot_token = to_slots(att_hits, pair_token)
    slot_filled = jnp.any(att_hits[0] | att_hits[1], axis=1)
    slot_tables = rope_tables(position_of(slot_token))
    tok_tables = rope_tables(position_of(token_index))
    segment_hot = (
        (slot_token // SEG)[:, None] == jnp.arange(inside.shape[0], dtype=jnp.int32)[None, :]
    ).astype(F32)
    reach = dot(segment_hot, jnp.repeat(inside.astype(F32), SEG, axis=1)) > 0.5
    allowed = reach & (token_index[None, :] <= slot_token[:, None]) & slot_filled[:, None]
    bias = jnp.where(allowed, 0.0, NEGATIVE).astype(BF16)

    inputs = tokens.astype(F32)
    normal_attn, scale_attn = norm_forward(inputs)
    normed = (normal_attn * gain_attn_full).astype(BF16)
    att_gates = picked_softmax(dot(normed, router_att), attention_routes)
    att_gate_slots = to_slots(att_hits, att_gates)[:, None]
    keyval = jnp.concatenate([dot(normed, keyval_full[0]), dot(normed, keyval_full[1])], axis=1)
    routed = dot(att_pick, normed, BF16).reshape(att_experts, att_cap, model_width)
    query_raw = jnp.einsum(
        "ecd,edf->ecf", routed, query_full, preferred_element_type=F32
    ).reshape(att_slots, width_here)
    queries, key_rows, values, attended, gated = attend(
        query_raw, keyval, bias, att_gate_slots, slot_tables, tok_tables
    )
    gated_slots = gated.reshape(att_experts, att_cap, width_here)
    att_rows = jnp.einsum(
        "ecf,efd->ecd", gated_slots, output_full, preferred_element_type=F32
    ).reshape(att_slots, model_width)
    att_part = dot_tn(att_pick, att_rows.astype(BF16))

    z = lax.axis_index("tensor")

    def share(rows):
        return lax.dynamic_slice_in_dim(rows, z * rows_here, rows_here, axis=0)

    hidden = share(inputs) + reduce_rows(att_part)
    normal_mlp, scale_mlp = norm_forward(hidden)
    mlp_in_here = (normal_mlp * gain_mlp_full).astype(BF16)
    mlp_in = gather_rows(mlp_in_here)
    mlp_gates = picked_softmax(dot(mlp_in, router_mlp), expert_routes)
    mlp_gate_slots = to_slots(mlp_hits, mlp_gates)[:, None]
    expert_in = dot(mlp_pick, mlp_in, BF16)
    grad_rows = (dot(mlp_pick, cotangent) * mlp_gate_slots).astype(BF16)

    def send(rows):
        return movers.swap(rows.reshape(mlp_experts, mlp_cap, model_width)).reshape(
            mlp_slots, model_width
        )

    x_rows = send(expert_in)
    g_rows = send(grad_rows)
    gate = dot(x_rows, gate_full)
    up = dot(x_rows, up_full)
    sigmoid_gate = jax.nn.sigmoid(gate)
    silu_gate = gate * sigmoid_gate
    activated = (silu_gate * up).astype(BF16)
    expert_out = dot(activated, down_full, BF16)
    grad_act = dot_nt(g_rows, down_full)
    grad_gate = (grad_act * up * sigmoid_gate * (1.0 + gate * (1.0 - sigmoid_gate))).astype(BF16)
    grad_up = (grad_act * silu_gate).astype(BF16)
    grad_expert_in = (dot_nt(grad_gate, gate_full) + dot_nt(grad_up, up_full)).astype(BF16)
    out_slots = send(expert_out)
    grad_in_slots = send(grad_expert_in)
    per_dp = model_width // dp_size
    grad_gate_w = dot_tn(x_rows, grad_gate, BF16).reshape(dp_size, per_dp, -1)
    grad_up_w = dot_tn(x_rows, grad_up, BF16).reshape(dp_size, per_dp, -1)
    grad_down_w = (
        dot_tn(activated, g_rows, BF16).reshape(-1, dp_size, per_dp).transpose(1, 0, 2)
    )
    grad_gate_up_out = jnp.stack(
        [movers.give_back(grad_gate_w).astype(F32), movers.give_back(grad_up_w).astype(F32)], axis=1
    )
    grad_down_out = movers.give_back(grad_down_w).astype(F32)

    gate_matrix = sum(
        jnp.where(mlp_hits[k], mlp_gates[:, k][None, :], 0.0) for k in range(TOPK)
    )
    gate_high = gate_matrix.astype(BF16)
    gate_low = (gate_matrix - gate_high.astype(F32)).astype(BF16)
    mlp_part = dot_tn(gate_high, out_slots) + dot_tn(gate_low, out_slots)
    mixed = gather_rows(hidden + reduce_rows(mlp_part))
    alignment = dot_nt(out_slots, cotangent)
    grad_gates_part = jnp.stack(
        [jnp.sum(jnp.where(mlp_hits[k], alignment, 0.0), axis=0) for k in range(TOPK)], axis=1
    )
    grad_mlp_gates = lax.psum_scatter(grad_gates_part, "tensor", scatter_dimension=0, tiled=True)
    grad_mlp_in = reduce_rows(dot_tn(mlp_pick, grad_in_slots))
    grad_mlp_logits = router_backward(
        share(mlp_gates), grad_mlp_gates, share(expert_routes), mlp_experts
    )
    grad_router_mlp = dot_tn(mlp_in_here, grad_mlp_logits)
    grad_mlp_in = grad_mlp_in + dot_nt(grad_mlp_logits, router_mlp)
    grad_hidden_norm, grad_gain_mlp = norm_backward(
        grad_mlp_in, normal_mlp, scale_mlp, gain_mlp_full
    )
    grad_hidden = share(cotangent).astype(F32) + grad_hidden_norm
    grad_att_pair = gather_rows(grad_hidden)

    grad_att_rows = dot(att_pick, grad_att_pair, BF16).reshape(att_experts, att_cap, model_width)
    grad_gated = jnp.einsum(
        "ecd,efd->ecf", grad_att_rows, output_full, preferred_element_type=F32
    ).reshape(att_slots, width_here)
    grad_output_w = jnp.einsum(
        "ecf,ecd->efd", gated_slots, grad_att_rows, preferred_element_type=BF16
    )
    grad_output_out = lax.psum_scatter(grad_output_w, "dp", scatter_dimension=2, tiled=True)
    grad_att_gates = lax.psum_scatter(
        to_pairs(att_hits, jnp.sum(grad_gated * attended, axis=1)),
        "tensor",
        scatter_dimension=0,
        tiled=True,
    )
    grad_q, grad_k, grad_v = attend_back(
        queries, key_rows, values, bias, att_gate_slots, slot_tables, tok_tables, grad_gated
    )
    grad_query_slots = grad_q.reshape(att_experts, att_cap, width_here)
    grad_query_w = jnp.einsum(
        "ecd,ecf->edf", routed, grad_query_slots, preferred_element_type=BF16
    )
    grad_query_out = lax.psum_scatter(grad_query_w, "dp", scatter_dimension=1, tiled=True)
    grad_keyval_w = jnp.stack([dot_tn(normed, grad_k, BF16), dot_tn(normed, grad_v, BF16)])
    grad_keyval_out = lax.psum_scatter(grad_keyval_w, "dp", scatter_dimension=1, tiled=True)
    grad_routed = jnp.einsum(
        "ecf,edf->ecd", grad_query_slots, query_full, preferred_element_type=F32
    ).reshape(att_slots, model_width)
    grad_normed = reduce_rows(
        dot_tn(att_pick, grad_routed.astype(BF16))
        + dot_nt(grad_k, keyval_full[0])
        + dot_nt(grad_v, keyval_full[1])
    )
    grad_att_logits = router_backward(
        share(att_gates), grad_att_gates, share(attention_routes), att_experts
    )
    grad_router_att = dot_tn(share(normed), grad_att_logits)
    grad_normed = grad_normed + dot_nt(grad_att_logits, router_att)
    grad_input_norm, grad_gain_attn = norm_backward(
        grad_normed, share(normal_attn), share(scale_attn), gain_attn_full
    )
    grad_tokens = gather_rows(grad_hidden + grad_input_norm).astype(F32)
    small_grads = jnp.concatenate(
        [grad_gain_attn[:, None], grad_gain_mlp[:, None], grad_router_att, grad_router_mlp], axis=1
    )
    small_grads = lax.psum(
        lax.psum_scatter(small_grads, "dp", scatter_dimension=0, tiled=True), "tensor"
    )
    return (
        mixed,
        grad_tokens,
        small_grads[:, 0],
        grad_keyval_out.astype(F32),
        grad_query_out.astype(F32),
        grad_output_out.astype(F32),
        small_grads[:, 2 : 2 + att_experts],
        small_grads[:, 1],
        small_grads[:, 2 + att_experts :],
        grad_gate_up_out,
        grad_down_out,
    )


def solution(mesh):
    placed = (
        P("dp", None),
        P("dp", None),
        P("dp", None),
        P("dp", None),
        P("dp", None),
        P("dp", None),
        P("dp"),
        P(None, "dp", "tensor"),
        P(None, "dp", "tensor"),
        P(None, "tensor", "dp"),
        P("dp", None),
        P("dp"),
        P("dp", None),
        P(None, None, "dp", "tensor"),
        P(None, "tensor", "dp"),
    )
    return jax.shard_map(
        functools.partial(on_device, mesh.shape["dp"], mesh.shape["tensor"]),
        mesh=mesh,
        in_specs=placed,
        out_specs=(
            P("dp", None),
            P("dp", None),
            P("dp"),
            P(None, "dp", "tensor"),
            P(None, "dp", "tensor"),
            P(None, "tensor", "dp"),
            P("dp", None),
            P("dp"),
            P("dp", None),
            P(None, None, "dp", "tensor"),
            P(None, "tensor", "dp"),
        ),
        check_vma=False,
    )
```

```python
import functools

import jax
import jax.numpy as jnp
from jax import lax
from jax.experimental import pallas as pl
from jax.experimental.pallas import tpu as pltpu
from jax.sharding import PartitionSpec as P

HD = 128
TOPK = 2
SEG = 128

EPSILON = 1e-06
NEGATIVE = -1e30
ROPE_BASE = 10000.0
F32 = jnp.float32
BF16 = jnp.bfloat16


def dot(a, b, out=F32):
    return jnp.dot(a, b, preferred_element_type=out)


def dot_tn(a, b, out=F32):
    return lax.dot_general(a, b, (((0,), (0,)), ((), ())), preferred_element_type=out)


def dot_nt(a, b, out=F32):
    return lax.dot_general(a, b, (((1,), (1,)), ((), ())), preferred_element_type=out)


def slot_places(routes, priority, capacity, experts):
    pair_total = routes.shape[0] * routes.shape[1]
    flat_routes = routes.reshape(pair_total)
    flat_order = priority.reshape(pair_total)
    same_expert = flat_routes[:, None] == flat_routes[None, :]
    earlier = flat_order[None, :] < flat_order[:, None]
    slot_rank = jnp.sum((same_expert & earlier).astype(jnp.int32), axis=1)
    slot_place = jnp.where(
        slot_rank < capacity, flat_routes * capacity + slot_rank, experts * capacity
    )
    return slot_place.reshape(routes.shape)


def slot_hits(place, slots):
    index = jnp.arange(slots, dtype=jnp.int32)[:, None]
    return [place[:, k][None, :] == index for k in range(place.shape[1])]


def ancestry(parent_row):
    segment_count = parent_row.shape[0]
    indices = jnp.arange(segment_count, dtype=jnp.int32)
    walker = indices
    inside = indices[:, None] == indices[None, :]
    for travel in range(segment_count):
        walker = parent_row[walker]
        inside = inside | (walker[:, None] == indices[None, :])
    depth = jnp.sum(inside.astype(jnp.int32), axis=1) - 1
    return (inside, depth)


def rope_tables(position):
    half_width = HD // 2
    frequency = ROPE_BASE ** (-jnp.arange(half_width, dtype=F32) / half_width)
    angles = position.astype(F32)[:, None] * frequency[None, :]
    cosine, sine = jnp.cos(angles), jnp.sin(angles)
    return (
        jnp.concatenate([cosine, cosine], axis=1),
        jnp.concatenate([-sine, sine], axis=1),
    )


def norm_forward(values_in):
    scale = lax.rsqrt(jnp.mean(values_in * values_in, axis=-1, keepdims=True) + EPSILON)
    return (values_in * scale, scale)


def norm_backward(grad_normed, normal, scale, gain):
    weighted = grad_normed * gain
    grad_in = scale * (weighted - normal * jnp.mean(weighted * normal, axis=-1, keepdims=True))
    return (grad_in, jnp.sum(grad_normed * normal, axis=0))


def router_backward(gates, grad_gates, picks, experts):
    grad_select = gates * (grad_gates - jnp.sum(gates * grad_gates, axis=1, keepdims=True))
    picked_hot = (picks[:, :, None] == jnp.arange(experts, dtype=jnp.int32)[None, None, :]).astype(
        F32
    )
    return jnp.sum(picked_hot * grad_select[:, :, None], axis=1).astype(BF16)


def picked_softmax(logits, picks):
    experts = logits.shape[1]
    hot = picks[:, :, None] == jnp.arange(experts, dtype=jnp.int32)[None, None, :]
    return jax.nn.softmax(jnp.sum(jnp.where(hot, logits[:, None, :], 0.0), axis=2), axis=-1)


def rope(v, cosine, sine):
    return v * cosine + pltpu.roll(v, HD // 2, axis=1) * sine


def rope_back(v, cosine, sine):
    return v * cosine - pltpu.roll(v, HD // 2, axis=1) * sine


def softmax_block(q, k, bias):
    scores = dot_nt(q, k) * HD ** (-0.5) + bias
    exp_scores = jnp.exp(scores - jnp.max(scores, axis=-1, keepdims=True))
    return exp_scores / jnp.sum(exp_scores, axis=-1, keepdims=True)


def attend_kernel(
    rows, q_raw, k_raw, v_raw, bias, gate, slot_cos, slot_sin, tok_cos, tok_sin,
    q_out, k_out, v_out, att_out, gated_out,
):
    k_out[...] = rope(k_raw[...], tok_cos[...], tok_sin[...]).astype(BF16)
    v_out[...] = v_raw[...].astype(BF16)

    @pl.loop(0, q_raw.shape[0] // rows)
    def _(i):
        at = pl.ds(pl.multiple_of(i * rows, rows), rows)
        q = rope(q_raw[at, :], slot_cos[at, :], slot_sin[at, :]).astype(BF16)
        q_out[at, :] = q
        probs = softmax_block(q, k_out[...], bias[at, :].astype(F32)).astype(BF16)
        attended = dot(probs, v_out[...])
        att_out[at, :] = attended
        gated_out[at, :] = (attended * gate[at, :]).astype(BF16)


def attend(q_raw, keyval, bias, gate, slot_tables, tok_tables):
    slots, width = q_raw.shape
    tok = keyval.shape[0]
    heads = width // HD
    head = lambda h: (0, h)
    whole = lambda h: (0, 0)
    rows = 256
    return pl.pallas_call(
        functools.partial(attend_kernel, rows),
        grid=(heads,),
        in_specs=[
            pl.BlockSpec((slots, HD), head),
            pl.BlockSpec((tok, HD), head),
            pl.BlockSpec((tok, HD), lambda h: (0, heads + h)),
            pl.BlockSpec((slots, tok), whole),
            pl.BlockSpec((slots, 1), whole),
            pl.BlockSpec((slots, HD), whole),
            pl.BlockSpec((slots, HD), whole),
            pl.BlockSpec((tok, HD), whole),
            pl.BlockSpec((tok, HD), whole),
        ],
        out_specs=[
            pl.BlockSpec((slots, HD), head),
            pl.BlockSpec((tok, HD), head),
            pl.BlockSpec((tok, HD), head),
            pl.BlockSpec((slots, HD), head),
            pl.BlockSpec((slots, HD), head),
        ],
        out_shape=[
            jax.ShapeDtypeStruct((slots, width), BF16),
            jax.ShapeDtypeStruct((tok, width), BF16),
            jax.ShapeDtypeStruct((tok, width), BF16),
            jax.ShapeDtypeStruct((slots, width), F32),
            jax.ShapeDtypeStruct((slots, width), BF16),
        ],
        compiler_params=pltpu.CompilerParams(vmem_limit_bytes=40 << 20),
        cost_estimate=pl.CostEstimate(
            flops=4 * slots * tok * width,
            bytes_accessed=slots * width * 12 + slots * tok * 2,
            transcendentals=slots * tok * heads,
        ),
    )(q_raw, keyval, keyval, bias, gate, *slot_tables, *tok_tables)


def attend_back_kernel(
    rows, q_ref, k_ref, v_ref, bias, gate, slot_cos, slot_sin, tok_cos, tok_sin, grad_gated,
    gq_out, gk_out, gv_out, gk_sum, gv_sum,
):
    gk_sum[...] = jnp.zeros_like(gk_sum)
    gv_sum[...] = jnp.zeros_like(gv_sum)

    @pl.loop(0, q_ref.shape[0] // rows)
    def _(i):
        at = pl.ds(pl.multiple_of(i * rows, rows), rows)
        q = q_ref[at, :]
        probs = softmax_block(q, k_ref[...], bias[at, :].astype(F32))
        grad_att = (grad_gated[at, :] * gate[at, :]).astype(BF16)
        grad_probs = dot_nt(grad_att, v_ref[...])
        centre = jnp.sum(probs * grad_probs, axis=-1, keepdims=True)
        grad_scores = (probs * (grad_probs - centre)).astype(BF16)
        grad_q = dot(grad_scores, k_ref[...]) * HD ** (-0.5)
        gq_out[at, :] = rope_back(grad_q, slot_cos[at, :], slot_sin[at, :]).astype(BF16)
        gk_sum[...] += dot_tn(grad_scores, q)
        gv_sum[...] += dot_tn(probs.astype(BF16), grad_att)

    grad_k = gk_sum[...] * HD ** (-0.5)
    gk_out[...] = rope_back(grad_k, tok_cos[...], tok_sin[...]).astype(BF16)
    gv_out[...] = gv_sum[...].astype(BF16)


def attend_back(q, k, v, bias, gate, slot_tables, tok_tables, grad_gated):
    slots, width = q.shape
    tok = k.shape[0]
    heads = width // HD
    head = lambda h: (0, h)
    whole = lambda h: (0, 0)
    rows = 256
    return pl.pallas_call(
        functools.partial(attend_back_kernel, rows),
        grid=(heads,),
        in_specs=[
            pl.BlockSpec((slots, HD), head),
            pl.BlockSpec((tok, HD), head),
            pl.BlockSpec((tok, HD), head),
            pl.BlockSpec((slots, tok), whole),
            pl.BlockSpec((slots, 1), whole),
            pl.BlockSpec((slots, HD), whole),
            pl.BlockSpec((slots, HD), whole),
            pl.BlockSpec((tok, HD), whole),
            pl.BlockSpec((tok, HD), whole),
            pl.BlockSpec((slots, HD), head),
        ],
        out_specs=[
            pl.BlockSpec((slots, HD), head),
            pl.BlockSpec((tok, HD), head),
            pl.BlockSpec((tok, HD), head),
        ],
        out_shape=[
            jax.ShapeDtypeStruct((slots, width), BF16),
            jax.ShapeDtypeStruct((tok, width), BF16),
            jax.ShapeDtypeStruct((tok, width), BF16),
        ],
        scratch_shapes=[pltpu.VMEM((tok, HD), F32), pltpu.VMEM((tok, HD), F32)],
        compiler_params=pltpu.CompilerParams(vmem_limit_bytes=40 << 20),
        cost_estimate=pl.CostEstimate(
            flops=10 * slots * tok * width,
            bytes_accessed=slots * width * 8 + slots * tok * 2,
            transcendentals=slots * tok * heads,
        ),
    )(q, k, v, bias, gate, *slot_tables, *tok_tables, grad_gated)


class Square:
    def __init__(self):
        me = lax.axis_index("dp")
        self.core = lax.rem(me, 2)
        self.chip = me // 2
        x, y = lax.rem(self.chip, 2), self.chip // 2
        self.chip_x = self.chip + 1 - 2 * x
        self.chip_y = self.chip + 2 - 4 * y
        self.chip_far = 3 - self.chip
        self.twin = me + 1 - 2 * self.core
        self.near_x = 2 * self.chip_x + self.core
        self.near_y = 2 * self.chip_y + self.core


def send_to(source, target, send_sem, recv_sem, device):
    return pltpu.make_async_remote_copy(
        src_ref=source,
        dst_ref=target,
        send_sem=send_sem,
        recv_sem=recv_sem,
        device_id={"dp": device},
        device_id_type=pl.DeviceIdType.MESH,
    )


def map_grads_kernel(
    routed, grad_q, normed, grad_kv, out,
    give, keep, twin_in, far_in, near_in,
    twin_send, twin_recv, far_send, far_recv, near_send, near_recv,
):
    at = Square()
    experts = routed.shape[0]
    units, _, size, _ = keep.shape
    half = size // 2
    barrier = pltpu.get_barrier_semaphore()
    for device in (at.twin, at.near_x, at.near_y):
        pl.semaphore_signal(
            barrier, inc=1, device_id={"dp": device}, device_id_type=pl.DeviceIdType.MESH
        )
    pl.semaphore_wait(barrier, 3)

    def to_twin(u):
        return send_to(give.at[u], twin_in.at[u], twin_send.at[u], twin_recv.at[u], at.twin)

    def to_far(u):
        first = send_to(
            keep.at[u, at.chip_far, pl.ds(0, half)],
            far_in.at[u, 0], far_send.at[u, 0], far_recv.at[u, 0], at.near_x,
        )
        second = send_to(
            keep.at[u, at.chip_far, pl.ds(half, half)],
            far_in.at[u, 1], far_send.at[u, 1], far_recv.at[u, 1], at.near_y,
        )
        return first, second

    def to_near(u):
        first = send_to(
            keep.at[u, at.chip_x], near_in.at[u, 0], near_send.at[u, 0], near_recv.at[u, 0],
            at.near_x,
        )
        second = send_to(
            keep.at[u, at.chip_y], near_in.at[u, 1], near_send.at[u, 1], near_recv.at[u, 1],
            at.near_y,
        )
        return first, second

    def multiply(u, rows, grads):
        for target, core in ((give, 1 - at.core), (keep, at.core)):
            for chip in range(4):
                columns = pl.ds(pl.multiple_of((2 * chip + core) * size, size), size)
                target[u, chip] = dot_tn(rows[:, columns], grads[...]).astype(BF16)
            if target is give:
                to_twin(u).start()

    def join_twin(u):
        to_twin(u).wait_recv()

        def add(chip):
            keep[u, chip] = (keep[u, chip].astype(F32) + twin_in[u, chip].astype(F32)).astype(BF16)

        add(at.chip_far)
        for copy in to_far(u):
            copy.start()
        add(at.chip_x)
        add(at.chip_y)
        add(at.chip)

    @pl.loop(0, experts)
    def _(u):
        multiply(u, routed.at[u], grad_q.at[u])

        @pl.when(u > 0)
        def _():
            join_twin(u - 1)

    @pl.loop(experts, units)
    def _(u):
        multiply(u, normed, grad_kv.at[u - experts])
        join_twin(u - 1)

    join_twin(units - 1)

    @pl.loop(0, units)
    def _(u):
        for copy in to_far(u):
            copy.wait_recv()
        top, bottom = pl.ds(0, half), pl.ds(half, half)
        keep[u, at.chip_y, top, :] = (
            keep[u, at.chip_y, top, :].astype(F32) + far_in[u, 0].astype(F32)
        ).astype(BF16)
        keep[u, at.chip_x, bottom, :] = (
            keep[u, at.chip_x, bottom, :].astype(F32) + far_in[u, 1].astype(F32)
        ).astype(BF16)
        for copy in to_near(u):
            copy.start()

    @pl.loop(0, units)
    def _(u):
        for copy in to_near(u):
            copy.wait_recv()
        out[u] = (
            keep[u, at.chip].astype(F32) + near_in[u, 0].astype(F32) + near_in[u, 1].astype(F32)
        ).astype(BF16)

    @pl.loop(0, units)
    def _(u):
        to_twin(u).wait_send()
        for copy in (*to_far(u), *to_near(u)):
            copy.wait_send()


def map_grads(routed, grad_q, normed, grad_kv):
    experts, _, model_width = routed.shape
    width = grad_q.shape[2]
    units = experts + grad_kv.shape[0]
    size = model_width // 8
    vmem = pl.BlockSpec(memory_space=pltpu.VMEM)
    return pl.pallas_call(
        map_grads_kernel,
        in_specs=[vmem] * 4,
        out_specs=vmem,
        out_shape=jax.ShapeDtypeStruct((units, size, width), BF16),
        scratch_shapes=[
            pltpu.VMEM((units, 4, size, width), BF16),
            pltpu.VMEM((units, 4, size, width), BF16),
            pltpu.VMEM((units, 4, size, width), BF16),
            pltpu.VMEM((units, 2, size // 2, width), BF16),
            pltpu.VMEM((units, 2, size, width), BF16),
            pltpu.SemaphoreType.DMA((units,)),
            pltpu.SemaphoreType.DMA((units,)),
            pltpu.SemaphoreType.DMA((units, 2)),
            pltpu.SemaphoreType.DMA((units, 2)),
            pltpu.SemaphoreType.DMA((units, 2)),
            pltpu.SemaphoreType.DMA((units, 2)),
        ],
        compiler_params=pltpu.CompilerParams(
            collective_id=1, has_side_effects=True, vmem_limit_bytes=60 << 20
        ),
        cost_estimate=pl.CostEstimate(
            flops=2 * units * 160 * model_width * width,
            bytes_accessed=250 << 20,
            transcendentals=0,
        ),
    )(routed, grad_q, normed, grad_kv)


class Movers:
    def __init__(self, dp, experts, tensor):
        self.dp, self.experts, self.tensor = dp, experts, tensor
        self.ratio = dp // experts
        self.groups = self.pairs = None
        if self.ratio > 1:
            self.groups = [[g * experts + e for e in range(experts)] for g in range(self.ratio)]
            self.pairs = [[g * experts + e for g in range(self.ratio)] for e in range(experts)]

    def swap(self, blocks):
        return lax.all_to_all(blocks, "dp", 0, 0, axis_index_groups=self.groups, tiled=True)

    def fetch(self, shards):
        mine = self.swap(shards)
        if self.ratio > 1:
            mine = lax.all_gather(mine, "dp", axis=0, axis_index_groups=self.pairs, tiled=True)
        return mine

    def give_back(self, slices):
        if self.ratio > 1:
            slices = lax.psum_scatter(
                slices, "dp", scatter_dimension=0, axis_index_groups=self.pairs, tiled=True
            )
        return self.swap(slices)

    def exchange(self, rows):
        size = rows.shape[0] // self.experts
        blocks = [rows[:size]]
        for k in range(1, self.experts):
            pairs = [(i, i ^ k) for i in range(self.dp)]
            blocks.append(lax.ppermute(rows[k * size : (k + 1) * size], "dp", pairs))
        return jnp.concatenate(blocks, axis=0)

    def across(self, block, k):
        return lax.ppermute(block, "tensor", [(i, i ^ k) for i in range(self.tensor)])

    def reduce_rows(self, part, dtype=BF16):
        z = lax.axis_index("tensor")
        size = part.shape[0] // self.tensor
        total = lax.dynamic_slice_in_dim(part, z * size, size, axis=0)
        sent = part.astype(dtype)
        for k in range(1, self.tensor):
            block = lax.dynamic_slice_in_dim(sent, (z ^ k) * size, size, axis=0)
            total = total + self.across(block, k).astype(F32)
        return total

    def gather_rows(self, rows):
        z = lax.axis_index("tensor")
        size = rows.shape[0]
        rows = rows.astype(BF16)
        full = jnp.zeros((size * self.tensor,) + rows.shape[1:], BF16)
        for k in range(self.tensor):
            block = rows if k == 0 else self.across(rows, k)
            full = lax.dynamic_update_slice_in_dim(full, block, (z ^ k) * size, axis=0)
        return full


def map_sums(dp_size, routed, grad_q, normed, grad_k, grad_v):
    if dp_size == 8:
        both = map_grads(routed, grad_q, normed, jnp.stack([grad_k, grad_v]))
        return both[:-2], both[-2:]
    grad_query_w = jnp.einsum("ecd,ecf->edf", routed, grad_q, preferred_element_type=BF16)
    grad_keyval_w = jnp.stack([dot_tn(normed, grad_k, BF16), dot_tn(normed, grad_v, BF16)])
    return (
        lax.psum_scatter(grad_query_w, "dp", scatter_dimension=1, tiled=True),
        lax.psum_scatter(grad_keyval_w, "dp", scatter_dimension=1, tiled=True),
    )


def on_device(
    dp_size,
    tensor_size,
    tokens,
    cotangent,
    parents,
    attention_routes,
    expert_routes,
    slot_order,
    gain_attention,
    keyval_weight,
    query_weight,
    output_weight,
    attention_router,
    gain_feedforward,
    expert_router,
    gate_up_weight,
    down_weight,
):
    tok_count, model_width = tokens.shape
    pair_count = TOPK * tok_count
    att_experts = query_weight.shape[0]
    mlp_experts = gate_up_weight.shape[0]
    att_cap = tok_count * 5 // 16
    mlp_cap = pair_count // mlp_experts
    att_slots = att_experts * att_cap
    mlp_slots = mlp_experts * mlp_cap
    width_here = query_weight.shape[2]
    rows_here = tok_count // tensor_size
    movers = Movers(dp_size, mlp_experts, tensor_size)
    tie = lax.optimization_barrier

    small = jnp.concatenate(
        [gain_attention[:, None], gain_feedforward[:, None], attention_router, expert_router], axis=1
    )
    small_full = lax.all_gather(small, "dp", axis=0, tiled=True)
    small_full, keyval_weight, query_weight, output_weight, gate_up_weight, down_weight = tie(
        (small_full, keyval_weight, query_weight, output_weight, gate_up_weight, down_weight)
    )
    keyval_full = lax.all_gather(keyval_weight, "dp", axis=1, tiled=True)
    query_full = lax.all_gather(query_weight, "dp", axis=1, tiled=True)
    output_full = lax.all_gather(output_weight, "dp", axis=2, tiled=True)
    gain_attn_full = small_full[:, 0].astype(F32)
    gain_mlp_full = small_full[:, 1].astype(F32)
    router_att = small_full[:, 2 : 2 + att_experts]
    router_mlp = small_full[:, 2 + att_experts :]

    gate_full = movers.fetch(gate_up_weight[:, 0]).reshape(model_width, -1)
    up_full = movers.fetch(gate_up_weight[:, 1]).reshape(model_width, -1)
    down_full = movers.fetch(down_weight)
    down_full = down_full.transpose(1, 0, 2).reshape(down_full.shape[1], model_width)

    inside, depth = ancestry(parents[0])
    token_index = jnp.arange(tok_count, dtype=jnp.int32)
    pair_order = jnp.arange(pair_count, dtype=jnp.int32).reshape(tok_count, TOPK)
    att_hits = slot_hits(
        slot_places(attention_routes, pair_order, att_cap, att_experts), att_slots
    )
    priority = slot_order[0][:, None] * TOPK + jnp.arange(TOPK, dtype=jnp.int32)[None, :]
    home = lax.rem(lax.axis_index("dp"), mlp_experts)
    mlp_hits = slot_hits(
        slot_places(expert_routes ^ home, priority, mlp_cap, mlp_experts), mlp_slots
    )
    att_pick = (att_hits[0] | att_hits[1]).astype(BF16)
    mlp_pick = (mlp_hits[0] | mlp_hits[1]).astype(BF16)

    def to_slots(hits, pair_values):
        return jnp.sum(
            sum(jnp.where(hits[k], pair_values[:, k][None, :], 0) for k in range(TOPK)), axis=1
        )

    def to_pairs(hits, slot_values):
        return jnp.stack(
            [jnp.sum(jnp.where(hits[k], slot_values[:, None], 0.0), axis=0) for k in range(TOPK)],
            axis=1,
        )

    def position_of(token):
        segment = token // SEG
        level = jnp.sum(
            jnp.where(segment[:, None] == jnp.arange(depth.shape[0])[None, :], depth[None, :], 0),
            axis=1,
        )
        return level * SEG + token % SEG

    pair_token = jnp.broadcast_to(token_index[:, None], (tok_count, TOPK))
    slot_token = to_slots(att_hits, pair_token)
    slot_filled = jnp.any(att_hits[0] | att_hits[1], axis=1)
    slot_tables = rope_tables(position_of(slot_token))
    tok_tables = rope_tables(position_of(token_index))
    segment_hot = (
        (slot_token // SEG)[:, None] == jnp.arange(inside.shape[0], dtype=jnp.int32)[None, :]
    ).astype(F32)
    reach = dot(segment_hot, jnp.repeat(inside.astype(F32), SEG, axis=1)) > 0.5
    allowed = reach & (token_index[None, :] <= slot_token[:, None]) & slot_filled[:, None]
    bias = jnp.where(allowed, 0.0, NEGATIVE).astype(BF16)

    cot_rows = movers.exchange(dot(mlp_pick, cotangent, BF16))

    inputs = tokens.astype(F32)
    normal_attn, scale_attn = norm_forward(inputs)
    normed = (normal_attn * gain_attn_full).astype(BF16)
    att_gates = picked_softmax(dot(normed, router_att), attention_routes)
    att_gate_slots = to_slots(att_hits, att_gates)[:, None]
    keyval = jnp.concatenate([dot(normed, keyval_full[0]), dot(normed, keyval_full[1])], axis=1)
    routed = dot(att_pick, normed, BF16).reshape(att_experts, att_cap, model_width)
    query_raw = jnp.einsum(
        "ecd,edf->ecf", routed, query_full, preferred_element_type=F32
    ).reshape(att_slots, width_here)
    queries, key_rows, values, attended, gated = attend(
        query_raw, keyval, bias, att_gate_slots, slot_tables, tok_tables
    )
    gated_slots = gated.reshape(att_experts, att_cap, width_here)
    att_rows = jnp.einsum(
        "ecf,efd->ecd", gated_slots, output_full, preferred_element_type=F32
    ).reshape(att_slots, model_width)
    att_part = dot_tn(att_pick, att_rows.astype(BF16))

    z = lax.axis_index("tensor")

    def share(rows):
        return lax.dynamic_slice_in_dim(rows, z * rows_here, rows_here, axis=0)

    hidden = share(inputs) + movers.reduce_rows(att_part)
    normal_mlp, scale_mlp = norm_forward(hidden)
    mlp_in_here = (normal_mlp * gain_mlp_full).astype(BF16)
    mlp_in = movers.gather_rows(mlp_in_here)
    mlp_gates = picked_softmax(dot(mlp_in, router_mlp), expert_routes)
    mlp_gate_slots = to_slots(mlp_hits, mlp_gates)[:, None]
    gate_high = mlp_gate_slots.astype(BF16)
    gate_rest = mlp_gate_slots - gate_high.astype(F32)
    gate_mid = gate_rest.astype(BF16)
    gate_low = (gate_rest - gate_mid.astype(F32)).astype(BF16)
    expert_in = jnp.concatenate(
        [dot(mlp_pick, mlp_in, BF16), gate_high, gate_mid, gate_low]
        + [jnp.zeros((mlp_slots, HD - 3), BF16)],
        axis=1,
    )

    received = movers.exchange(expert_in)
    x_rows = received[:, :model_width]
    gate_columns = received[:, model_width : model_width + 3].astype(F32)
    gate_of_row = gate_columns[:, :1] + gate_columns[:, 1:2] + gate_columns[:, 2:]
    g_rows = (cot_rows.astype(F32) * gate_of_row).astype(BF16)
    gate = dot(x_rows, gate_full)
    up = dot(x_rows, up_full)
    sigmoid_gate = jax.nn.sigmoid(gate)
    silu_gate = gate * sigmoid_gate
    activated = (silu_gate * up).astype(BF16)
    expert_out = dot(activated, down_full, BF16)
    out_slots = movers.exchange(expert_out)
    grad_act = dot_nt(g_rows, down_full)
    grad_gate = (grad_act * up * sigmoid_gate * (1.0 + gate * (1.0 - sigmoid_gate))).astype(BF16)
    grad_up = (grad_act * silu_gate).astype(BF16)
    grad_expert_in = (dot_nt(grad_gate, gate_full) + dot_nt(grad_up, up_full)).astype(BF16)
    grad_in_slots = movers.exchange(grad_expert_in)
    grad_gate, grad_up, activated, _ = tie((grad_gate, grad_up, activated, grad_expert_in))
    per_dp = model_width // dp_size
    grad_gate_w = dot_tn(x_rows, grad_gate, BF16).reshape(dp_size, per_dp, -1)
    grad_up, activated, grad_gate_w, out_slots = tie((grad_up, activated, grad_gate_w, out_slots))
    grad_up_w = dot_tn(x_rows, grad_up, BF16).reshape(dp_size, per_dp, -1)
    grad_down_w = (
        dot_tn(activated, g_rows, BF16).reshape(-1, dp_size, per_dp).transpose(1, 0, 2)
    )
    grad_in_slots, out_slots, grad_gate_w, grad_up_w, grad_down_w = tie(
        (grad_in_slots, out_slots, grad_gate_w, grad_up_w, grad_down_w)
    )
    grad_gate_w = movers.give_back(grad_gate_w)
    grad_up_w = movers.give_back(grad_up_w)
    grad_down_w = movers.give_back(grad_down_w)

    alignment = dot_nt(out_slots, cotangent)
    grad_gates_part = jnp.stack(
        [jnp.sum(jnp.where(mlp_hits[k], alignment, 0.0), axis=0) for k in range(TOPK)], axis=1
    )
    grad_mlp_gates = movers.reduce_rows(grad_gates_part, F32)
    grad_mlp_in = movers.reduce_rows(dot_tn(mlp_pick, grad_in_slots))
    grad_mlp_logits = router_backward(
        share(mlp_gates), grad_mlp_gates, share(expert_routes), mlp_experts
    )
    grad_router_mlp = dot_tn(mlp_in_here, grad_mlp_logits)
    grad_mlp_in = grad_mlp_in + dot_nt(grad_mlp_logits, router_mlp)
    grad_hidden_norm, grad_gain_mlp = norm_backward(
        grad_mlp_in, normal_mlp, scale_mlp, gain_mlp_full
    )
    grad_hidden = share(cotangent).astype(F32) + grad_hidden_norm
    grad_hidden, grad_gate_w = tie((grad_hidden, grad_gate_w))
    grad_att_pair = movers.gather_rows(grad_hidden)

    gate_matrix = sum(
        jnp.where(mlp_hits[k], mlp_gates[:, k][None, :], 0.0) for k in range(TOPK)
    )
    matrix_high = gate_matrix.astype(BF16)
    matrix_low = (gate_matrix - matrix_high.astype(F32)).astype(BF16)
    mlp_part = dot_tn(matrix_high, out_slots) + dot_tn(matrix_low, out_slots)
    mlp_part, grad_att_pair = tie((mlp_part, grad_att_pair))
    mlp_sum = movers.reduce_rows(mlp_part)

    grad_att_rows = dot(att_pick, grad_att_pair, BF16).reshape(att_experts, att_cap, model_width)
    grad_output_w = jnp.einsum(
        "ecf,ecd->efd", gated_slots, grad_att_rows, preferred_element_type=BF16
    )
    grad_att_rows, grad_output_w = tie((grad_att_rows, grad_output_w))
    grad_gated = jnp.einsum(
        "ecd,efd->ecf", grad_att_rows, output_full, preferred_element_type=F32
    ).reshape(att_slots, width_here)
    grad_output_out = lax.psum_scatter(grad_output_w, "dp", scatter_dimension=2, tiled=True)
    grad_att_gates = movers.reduce_rows(
        to_pairs(att_hits, jnp.sum(grad_gated * attended, axis=1)), F32
    )
    grad_q, grad_k, grad_v = attend_back(
        queries, key_rows, values, bias, att_gate_slots, slot_tables, tok_tables, grad_gated
    )
    grad_query_slots = grad_q.reshape(att_experts, att_cap, width_here)
    grad_routed = jnp.einsum(
        "ecf,edf->ecd", grad_query_slots, query_full, preferred_element_type=F32
    ).reshape(att_slots, model_width)
    normed_part = (
        dot_tn(att_pick, grad_routed.astype(BF16))
        + dot_nt(grad_k, keyval_full[0])
        + dot_nt(grad_v, keyval_full[1])
    )
    grad_normed = movers.reduce_rows(normed_part)
    grad_query_slots, grad_k, grad_v, _, grad_up_w, mlp_sum = tie(
        (grad_query_slots, grad_k, grad_v, normed_part, grad_up_w, mlp_sum)
    )
    mixed = movers.gather_rows(hidden + mlp_sum)
    grad_query_out, grad_keyval_out = map_sums(
        dp_size, routed, grad_query_slots, normed, grad_k, grad_v
    )
    grad_normed, grad_down_w, grad_query_out, grad_output_out, mixed = tie(
        (grad_normed, grad_down_w, grad_query_out, grad_output_out, mixed)
    )
    grad_att_logits = router_backward(
        share(att_gates), grad_att_gates, share(attention_routes), att_experts
    )
    grad_router_att = dot_tn(share(normed), grad_att_logits)
    grad_normed = grad_normed + dot_nt(grad_att_logits, router_att)
    grad_input_norm, grad_gain_attn = norm_backward(
        grad_normed, share(normal_attn), share(scale_attn), gain_attn_full
    )
    grad_tokens = movers.gather_rows(grad_hidden + grad_input_norm).astype(F32)
    small_grads = jnp.concatenate(
        [grad_gain_attn[:, None], grad_gain_mlp[:, None], grad_router_att, grad_router_mlp], axis=1
    )
    small_grads = lax.psum(
        lax.psum_scatter(small_grads, "dp", scatter_dimension=0, tiled=True), "tensor"
    )
    return (
        mixed,
        grad_tokens,
        small_grads[:, 0],
        grad_keyval_out.astype(F32),
        grad_query_out.astype(F32),
        grad_output_out.astype(F32),
        small_grads[:, 2 : 2 + att_experts],
        small_grads[:, 1],
        small_grads[:, 2 + att_experts :],
        jnp.stack([grad_gate_w.astype(F32), grad_up_w.astype(F32)], axis=1),
        grad_down_w.astype(F32),
    )


def solution(mesh):
    placed = (
        P("dp", None),
        P("dp", None),
        P("dp", None),
        P("dp", None),
        P("dp", None),
        P("dp", None),
        P("dp"),
        P(None, "dp", "tensor"),
        P(None, "dp", "tensor"),
        P(None, "tensor", "dp"),
        P("dp", None),
        P("dp"),
        P("dp", None),
        P(None, None, "dp", "tensor"),
        P(None, "tensor", "dp"),
    )
    return jax.shard_map(
        functools.partial(on_device, mesh.shape["dp"], mesh.shape["tensor"]),
        mesh=mesh,
        in_specs=placed,
        out_specs=(
            P("dp", None),
            P("dp", None),
            P("dp"),
            P(None, "dp", "tensor"),
            P(None, "dp", "tensor"),
            P(None, "tensor", "dp"),
            P("dp", None),
            P("dp"),
            P("dp", None),
            P(None, None, "dp", "tensor"),
            P(None, "tensor", "dp"),
        ),
        check_vma=False,
    )
```

```python
import functools

import jax
import jax.numpy as jnp
from jax import lax
from jax.experimental import pallas as pl
from jax.experimental.pallas import tpu as pltpu
from jax.sharding import PartitionSpec as P

HD = 128
TOPK = 2
SEG = 128

EPSILON = 1e-06
NEGATIVE = -1e30
ROPE_BASE = 10000.0
F32 = jnp.float32
BF16 = jnp.bfloat16


def dot(a, b, out=F32):
    return jnp.dot(a, b, preferred_element_type=out)


def dot_tn(a, b, out=F32):
    return lax.dot_general(a, b, (((0,), (0,)), ((), ())), preferred_element_type=out)


def dot_nt(a, b, out=F32):
    return lax.dot_general(a, b, (((1,), (1,)), ((), ())), preferred_element_type=out)


def slot_places(routes, priority, capacity, experts):
    pair_total = routes.shape[0] * routes.shape[1]
    flat_routes = routes.reshape(pair_total)
    flat_order = priority.reshape(pair_total)
    same_expert = flat_routes[:, None] == flat_routes[None, :]
    earlier = flat_order[None, :] < flat_order[:, None]
    slot_rank = jnp.sum((same_expert & earlier).astype(jnp.int32), axis=1)
    slot_place = jnp.where(
        slot_rank < capacity, flat_routes * capacity + slot_rank, experts * capacity
    )
    return slot_place.reshape(routes.shape)


def slot_hits(place, slots):
    index = jnp.arange(slots, dtype=jnp.int32)[:, None]
    return [place[:, k][None, :] == index for k in range(place.shape[1])]


def ancestry(parent_row):
    segment_count = parent_row.shape[0]
    indices = jnp.arange(segment_count, dtype=jnp.int32)
    walker = indices
    inside = indices[:, None] == indices[None, :]
    for travel in range(segment_count):
        walker = parent_row[walker]
        inside = inside | (walker[:, None] == indices[None, :])
    depth = jnp.sum(inside.astype(jnp.int32), axis=1) - 1
    return (inside, depth)


def rope_tables(position):
    half_width = HD // 2
    frequency = ROPE_BASE ** (-jnp.arange(half_width, dtype=F32) / half_width)
    angles = position.astype(F32)[:, None] * frequency[None, :]
    cosine, sine = jnp.cos(angles), jnp.sin(angles)
    return (
        jnp.concatenate([cosine, cosine], axis=1),
        jnp.concatenate([-sine, sine], axis=1),
    )


def norm_forward(values_in):
    scale = lax.rsqrt(jnp.mean(values_in * values_in, axis=-1, keepdims=True) + EPSILON)
    return (values_in * scale, scale)


def norm_backward(grad_normed, normal, scale, gain):
    weighted = grad_normed * gain
    grad_in = scale * (weighted - normal * jnp.mean(weighted * normal, axis=-1, keepdims=True))
    return (grad_in, jnp.sum(grad_normed * normal, axis=0))


def router_backward(gates, products, picks, experts):
    grad_select = products - gates * jnp.sum(products, axis=1, keepdims=True)
    picked_hot = (picks[:, :, None] == jnp.arange(experts, dtype=jnp.int32)[None, None, :]).astype(
        F32
    )
    return jnp.sum(picked_hot * grad_select[:, :, None], axis=1).astype(BF16)


def with_column(rows, column):
    high = column.astype(BF16)
    rest = column - high.astype(F32)
    mid = rest.astype(BF16)
    low = (rest - mid.astype(F32)).astype(BF16)
    return jnp.concatenate(
        [rows, high, mid, low, jnp.zeros((rows.shape[0], HD - 3), BF16)], axis=1
    )


def without_column(both):
    width = both.shape[1] - HD
    parts = both[:, width : width + 3].astype(F32)
    return both[:, :width], parts[:, :1] + parts[:, 1:2] + parts[:, 2:]


def picked_softmax(logits, picks):
    experts = logits.shape[1]
    hot = picks[:, :, None] == jnp.arange(experts, dtype=jnp.int32)[None, None, :]
    return jax.nn.softmax(jnp.sum(jnp.where(hot, logits[:, None, :], 0.0), axis=2), axis=-1)


def rope(v, cosine, sine):
    return v * cosine + pltpu.roll(v, HD // 2, axis=1) * sine


def rope_back(v, cosine, sine):
    return v * cosine - pltpu.roll(v, HD // 2, axis=1) * sine


def softmax_block(q, k, bias):
    scores = dot_nt(q, k) * HD ** (-0.5) + bias
    exp_scores = jnp.exp(scores - jnp.max(scores, axis=-1, keepdims=True))
    return exp_scores / jnp.sum(exp_scores, axis=-1, keepdims=True)


def attend_kernel(
    rows, q_raw, k_raw, v_raw, bias, gate, slot_cos, slot_sin, tok_cos, tok_sin,
    q_out, k_out, v_out, att_out, gated_out,
):
    k_out[...] = rope(k_raw[...], tok_cos[...], tok_sin[...]).astype(BF16)
    v_out[...] = v_raw[...].astype(BF16)

    @pl.loop(0, q_raw.shape[0] // rows)
    def _(i):
        at = pl.ds(pl.multiple_of(i * rows, rows), rows)
        q = rope(q_raw[at, :], slot_cos[at, :], slot_sin[at, :]).astype(BF16)
        q_out[at, :] = q
        probs = softmax_block(q, k_out[...], bias[at, :].astype(F32)).astype(BF16)
        attended = dot(probs, v_out[...])
        att_out[at, :] = attended
        gated_out[at, :] = (attended * gate[at, :]).astype(BF16)


def attend(q_raw, keyval, bias, gate, slot_tables, tok_tables):
    slots, width = q_raw.shape
    tok = keyval.shape[0]
    heads = width // HD
    head = lambda h: (0, h)
    whole = lambda h: (0, 0)
    rows = 256
    return pl.pallas_call(
        functools.partial(attend_kernel, rows),
        grid=(heads,),
        in_specs=[
            pl.BlockSpec((slots, HD), head),
            pl.BlockSpec((tok, HD), head),
            pl.BlockSpec((tok, HD), lambda h: (0, heads + h)),
            pl.BlockSpec((slots, tok), whole),
            pl.BlockSpec((slots, 1), whole),
            pl.BlockSpec((slots, HD), whole),
            pl.BlockSpec((slots, HD), whole),
            pl.BlockSpec((tok, HD), whole),
            pl.BlockSpec((tok, HD), whole),
        ],
        out_specs=[
            pl.BlockSpec((slots, HD), head),
            pl.BlockSpec((tok, HD), head),
            pl.BlockSpec((tok, HD), head),
            pl.BlockSpec((slots, HD), head),
            pl.BlockSpec((slots, HD), head),
        ],
        out_shape=[
            jax.ShapeDtypeStruct((slots, width), BF16),
            jax.ShapeDtypeStruct((tok, width), BF16),
            jax.ShapeDtypeStruct((tok, width), BF16),
            jax.ShapeDtypeStruct((slots, width), F32),
            jax.ShapeDtypeStruct((slots, width), BF16),
        ],
        compiler_params=pltpu.CompilerParams(vmem_limit_bytes=40 << 20),
        cost_estimate=pl.CostEstimate(
            flops=4 * slots * tok * width,
            bytes_accessed=slots * width * 12 + slots * tok * 2,
            transcendentals=slots * tok * heads,
        ),
    )(q_raw, keyval, keyval, bias, gate, *slot_tables, *tok_tables)


def attend_back_kernel(
    rows, q_ref, k_ref, v_ref, bias, gate, slot_cos, slot_sin, tok_cos, tok_sin, grad_gated,
    gq_out, gk_out, gv_out, gk_sum, gv_sum,
):
    gk_sum[...] = jnp.zeros_like(gk_sum)
    gv_sum[...] = jnp.zeros_like(gv_sum)

    @pl.loop(0, q_ref.shape[0] // rows)
    def _(i):
        at = pl.ds(pl.multiple_of(i * rows, rows), rows)
        q = q_ref[at, :]
        probs = softmax_block(q, k_ref[...], bias[at, :].astype(F32))
        grad_att = (grad_gated[at, :] * gate[at, :]).astype(BF16)
        grad_probs = dot_nt(grad_att, v_ref[...])
        centre = jnp.sum(probs * grad_probs, axis=-1, keepdims=True)
        grad_scores = (probs * (grad_probs - centre)).astype(BF16)
        grad_q = dot(grad_scores, k_ref[...]) * HD ** (-0.5)
        gq_out[at, :] = rope_back(grad_q, slot_cos[at, :], slot_sin[at, :]).astype(BF16)
        gk_sum[...] += dot_tn(grad_scores, q)
        gv_sum[...] += dot_tn(probs.astype(BF16), grad_att)

    grad_k = gk_sum[...] * HD ** (-0.5)
    gk_out[...] = rope_back(grad_k, tok_cos[...], tok_sin[...]).astype(BF16)
    gv_out[...] = gv_sum[...].astype(BF16)


def attend_back(q, k, v, bias, gate, slot_tables, tok_tables, grad_gated):
    slots, width = q.shape
    tok = k.shape[0]
    heads = width // HD
    head = lambda h: (0, h)
    whole = lambda h: (0, 0)
    rows = 256
    return pl.pallas_call(
        functools.partial(attend_back_kernel, rows),
        grid=(heads,),
        in_specs=[
            pl.BlockSpec((slots, HD), head),
            pl.BlockSpec((tok, HD), head),
            pl.BlockSpec((tok, HD), head),
            pl.BlockSpec((slots, tok), whole),
            pl.BlockSpec((slots, 1), whole),
            pl.BlockSpec((slots, HD), whole),
            pl.BlockSpec((slots, HD), whole),
            pl.BlockSpec((tok, HD), whole),
            pl.BlockSpec((tok, HD), whole),
            pl.BlockSpec((slots, HD), head),
        ],
        out_specs=[
            pl.BlockSpec((slots, HD), head),
            pl.BlockSpec((tok, HD), head),
            pl.BlockSpec((tok, HD), head),
        ],
        out_shape=[
            jax.ShapeDtypeStruct((slots, width), BF16),
            jax.ShapeDtypeStruct((tok, width), BF16),
            jax.ShapeDtypeStruct((tok, width), BF16),
        ],
        scratch_shapes=[pltpu.VMEM((tok, HD), F32), pltpu.VMEM((tok, HD), F32)],
        compiler_params=pltpu.CompilerParams(vmem_limit_bytes=40 << 20),
        cost_estimate=pl.CostEstimate(
            flops=10 * slots * tok * width,
            bytes_accessed=slots * width * 8 + slots * tok * 2,
            transcendentals=slots * tok * heads,
        ),
    )(q, k, v, bias, gate, *slot_tables, *tok_tables, grad_gated)


class Square:
    def __init__(self):
        me = lax.axis_index("dp")
        self.core = lax.rem(me, 2)
        self.chip = me // 2
        x, y = lax.rem(self.chip, 2), self.chip // 2
        self.chip_x = self.chip + 1 - 2 * x
        self.chip_y = self.chip + 2 - 4 * y
        self.chip_far = 3 - self.chip
        self.twin = me + 1 - 2 * self.core
        self.near_x = 2 * self.chip_x + self.core
        self.near_y = 2 * self.chip_y + self.core


def send_to(source, target, send_sem, recv_sem, device):
    return pltpu.make_async_remote_copy(
        src_ref=source,
        dst_ref=target,
        send_sem=send_sem,
        recv_sem=recv_sem,
        device_id={"dp": device},
        device_id_type=pl.DeviceIdType.MESH,
    )


def greet(places):
    barrier = pltpu.get_barrier_semaphore()
    for place in places:
        pl.semaphore_signal(
            barrier, inc=1, device_id=place, device_id_type=pl.DeviceIdType.MESH
        )
    pl.semaphore_wait(barrier, len(places))


def send_across(source, target, send_sem, recv_sem, device):
    return pltpu.make_async_remote_copy(
        src_ref=source,
        dst_ref=target,
        send_sem=send_sem,
        recv_sem=recv_sem,
        device_id={"tensor": device},
        device_id_type=pl.DeviceIdType.MESH,
    )


def tensor_peers(count):
    z = lax.axis_index("tensor")
    return [lax.rem(z + k, count) for k in range(1, count)]


def share_rows(size):
    return pl.ds(pl.multiple_of(lax.axis_index("tensor") * size, size), size)


def rows_of(place, size):
    return pl.ds(pl.multiple_of(place * size, size), size)


def spread(count, source, target, sems):
    size = source.shape[0] // count
    copies = [
        send_to(
            source.at[pl.ds(k * size, size)], target.at[pl.ds(k * size, size)],
            sems[0].at[k], sems[1].at[k], partner(k),
        )
        for k in range(1, count)
    ]
    here = pltpu.make_async_copy(
        source.at[pl.ds(0, size)], target.at[pl.ds(0, size)], sems[0].at[0]
    )
    for copy in (*copies, here):
        copy.start()
    return (*copies, here)


def gather_kernel(axes, chunks, *refs):
    amount = len(axes)
    sources, targets = refs[:amount], refs[amount : 2 * amount]
    send_sem, recv_sem, own_sem = refs[2 * amount :]
    at = Square()
    me = 2 * at.chip + at.core
    far = 2 * at.chip_far + at.core
    greet([{"dp": p} for p in (at.twin, at.near_x, at.near_y)])

    def region(ref, axis, source, place, experts):
        size = source.shape[axis]
        at_place = pl.ds(pl.multiple_of(place * size, size), size)
        return ref.at[experts, at_place] if axis == 1 else ref.at[experts, :, at_place]

    first = 0
    plans = []
    for i in range(amount):
        count = sources[i].shape[0] // chunks[i]
        plans.append((i, first, count))
        first += count

    def copies(i, first, n):
        source, target, axis, size = sources[i], targets[i], axes[i], chunks[i]
        half = size // 2
        whole = pl.ds(n * size, size)
        top, bottom = pl.ds(n * size, half), pl.ds(n * size + half, half)
        unit = first + n

        def move(slot, place, experts, device, own=False):
            there = region(target, axis, source, place, experts)
            return send_to(
                source.at[experts] if own else there, there,
                send_sem.at[unit, slot], recv_sem.at[unit, slot], device,
            )

        return [
            functools.partial(move, 0, me, whole, at.near_x, True),
            functools.partial(move, 1, me, whole, at.near_y, True),
            functools.partial(move, 2, at.near_y, top, at.near_x),
            functools.partial(move, 3, at.near_x, bottom, at.near_y),
            functools.partial(move, 4, me, whole, at.twin, True),
            functools.partial(move, 5, at.near_x, whole, at.twin),
            functools.partial(move, 6, at.near_y, whole, at.twin),
            functools.partial(move, 7, far, top, at.twin),
            functools.partial(move, 8, far, bottom, at.twin),
        ]

    here = [
        pltpu.make_async_copy(
            sources[i], region(targets[i], axes[i], sources[i], me, pl.ds(0, sources[i].shape[0])),
            own_sem.at[i],
        )
        for i in range(amount)
    ]
    for i, first, count in plans:

        @pl.loop(0, count)
        def _(n):
            moves = copies(i, first, n)
            for slot in (0, 1, 4):
                moves[slot]().start()

    for copy in here:
        copy.start()
    for i, first, count in plans:

        @pl.loop(0, count)
        def _(n):
            moves = copies(i, first, n)
            moves[0]().wait_recv()
            moves[3]().start()
            moves[5]().start()
            moves[1]().wait_recv()
            moves[2]().start()
            moves[6]().start()

    for i, first, count in plans:

        @pl.loop(0, count)
        def _(n):
            moves = copies(i, first, n)
            moves[2]().wait_recv()
            moves[7]().start()
            moves[3]().wait_recv()
            moves[8]().start()

    for i, first, count in plans:

        @pl.loop(0, count)
        def _(n):
            moves = copies(i, first, n)
            for slot in (4, 5, 6, 7, 8):
                moves[slot]().wait_recv()
            for move in moves:
                move().wait_send()

    for copy in here:
        copy.wait()


def gather_maps(arrays, axes, chunks):
    units = sum(a.shape[0] // c for a, c in zip(arrays, chunks))
    shapes = [
        tuple(n * 8 if d == axis else n for d, n in enumerate(a.shape))
        for a, axis in zip(arrays, axes)
    ]
    return pl.pallas_call(
        functools.partial(gather_kernel, axes, chunks),
        in_specs=[HBM] * len(arrays),
        out_specs=[HBM] * len(arrays),
        out_shape=[jax.ShapeDtypeStruct(shape, BF16) for shape in shapes],
        scratch_shapes=[sems(units, 9), sems(units, 9), sems(len(arrays))],
        compiler_params=pltpu.CompilerParams(collective_id=5, has_side_effects=True),
        cost_estimate=pl.CostEstimate(flops=0, bytes_accessed=600 << 20, transcendentals=0),
    )(*arrays)


def deal(source, target, sems):
    me = lax.axis_index("dp")
    copies = [
        send_to(
            source.at[partner(k)], target.at[me], sems[0].at[k], sems[1].at[k], partner(k)
        )
        for k in range(1, source.shape[0])
    ]
    copies.append(pltpu.make_async_copy(source.at[me], target.at[me], sems[0].at[0]))
    for copy in copies:
        copy.start()
    return copies


def norm_back(total, products, hots, router, base, gain, hot_out, gain_out):
    first, second = products
    weights = hots[0] * first + hots[1] * second - hots[2] * (first + second)
    hot_out[...] = weights.astype(BF16)
    total = total + dot_nt(hot_out[...], router[...])
    scale = lax.rsqrt(jnp.mean(base * base, axis=-1, keepdims=True) + EPSILON)
    normal = base * scale
    gain_out[...] = jnp.sum(total * normal, axis=0, keepdims=True)
    weighted = total * gain
    return scale * (weighted - normal * jnp.mean(weighted * normal, axis=-1, keepdims=True))


def three_columns(block):
    return block[:, 0:1] + block[:, 1:2] + block[:, 2:3]


def hidden_kernel(
    pick, rows, x_here, gain, cot_hbm,
    hidden_out, mlp_in_out, cot_out,
    parts, sent, got, z_send, z_recv, g_send, g_recv, e_send, e_recv,
):
    count = z_send.shape[0] + 1
    width = rows.shape[1]
    tokens = pick.shape[1]
    size = tokens // count
    peers = tensor_peers(count)
    exchange_count = e_send.shape[0]
    greet(
        [{"dp": partner(k)} for k in range(1, exchange_count)] + [{"tensor": p} for p in peers]
    )
    moves = spread(exchange_count, cot_hbm, cot_out, (e_send, e_recv))

    @pl.loop(0, width // 512)
    def _(i):
        at = pl.ds(pl.multiple_of(i * 512, 512), 512)
        piece = dot_tn(pick[...], rows[:, at])
        parts[:, at] = piece
        sent[:, at] = piece.astype(BF16)

    copies = [
        send_across(sent.at[rows_of(p, size)], got.at[k], z_send.at[k], z_recv.at[k], p)
        for k, p in enumerate(peers)
    ]
    for copy in copies:
        copy.start()
    here = share_rows(size)
    hidden_out[...] = x_here[...].astype(F32) + parts[here, :]
    for k, copy in enumerate(copies):
        copy.wait_recv()
        hidden_out[...] += got[k].astype(F32)
    hidden = hidden_out[...]
    scale = lax.rsqrt(jnp.mean(hidden * hidden, axis=-1, keepdims=True) + EPSILON)
    mlp_in_out[here, :] = (hidden * scale * gain[...]).astype(BF16)
    more = [
        send_across(
            mlp_in_out.at[here], mlp_in_out.at[here], g_send.at[k], g_recv.at[k], p
        )
        for k, p in enumerate(peers)
    ]
    for copy in more:
        copy.start()
    for copy in copies:
        copy.wait_send()
    for copy in more:
        copy.wait()
    for copy in moves:
        copy.wait()


VMEM = pl.BlockSpec(memory_space=pltpu.VMEM)
HBM = pl.BlockSpec(memory_space=pl.ANY)


def sems(*shape):
    return pltpu.SemaphoreType.DMA(shape)


def hidden_step(tensor_size, peers, pick, rows, x_here, gain, cot_send):
    tokens, width = pick.shape[1], rows.shape[1]
    size = tokens // tensor_size
    around = tensor_size - 1
    return pl.pallas_call(
        hidden_kernel,
        in_specs=[VMEM, VMEM, VMEM, VMEM, HBM],
        out_specs=[VMEM, VMEM, HBM],
        out_shape=[
            jax.ShapeDtypeStruct((size, width), F32),
            jax.ShapeDtypeStruct((tokens, width), BF16),
            jax.ShapeDtypeStruct(cot_send.shape, BF16),
        ],
        scratch_shapes=[
            pltpu.VMEM((tokens, width), F32),
            pltpu.VMEM((tokens, width), BF16),
            pltpu.VMEM((around, size, width), BF16),
            sems(around), sems(around), sems(around), sems(around), sems(peers), sems(peers),
        ],
        compiler_params=pltpu.CompilerParams(
            collective_id=3, has_side_effects=True, vmem_limit_bytes=40 << 20
        ),
        cost_estimate=pl.CostEstimate(
            flops=2 * pick.shape[0] * tokens * width, bytes_accessed=300 << 20, transcendentals=0
        ),
    )(pick, rows, x_here, gain, cot_send)


def back_kernel(
    back, pick, hit_0, hit_1, hidden, cot_here, gain, router, hots, rows_hbm, maps_hbm,
    grad_out, pair_out, gain_out, hot_out, rows_out, maps_out,
    parts, sent, got, z_send, z_recv, g_send, g_recv, e_send, e_recv, w_send, w_recv,
):
    count = z_send.shape[0] + 1
    width = back.shape[1] - HD
    tokens = pick.shape[1]
    size = tokens // count
    peers = tensor_peers(count)
    exchange_count = e_send.shape[0]
    greet(
        [{"dp": partner(k)} for k in range(1, exchange_count)] + [{"tensor": p} for p in peers]
    )

    @pl.loop(0, width // 512)
    def _(i):
        at = pl.ds(pl.multiple_of(i * 512, 512), 512)
        piece = dot_tn(pick[...], back[:, at])
        parts[:, at] = piece
        sent[:, at] = piece.astype(BF16)

    for k, hit in enumerate((hit_0, hit_1)):
        at = pl.ds(width + k * HD, HD)
        piece = dot_tn(hit[...], back[:, width:])
        parts[:, at] = piece
        sent[:, at] = piece.astype(BF16)

    copies = [
        send_across(sent.at[rows_of(p, size)], got.at[k], z_send.at[k], z_recv.at[k], p)
        for k, p in enumerate(peers)
    ]
    for copy in copies:
        copy.start()
    moves = spread(exchange_count, rows_hbm, rows_out, (e_send, e_recv))
    dealt = deal(maps_hbm, maps_out, (w_send, w_recv))
    here = share_rows(size)
    total = parts[here, :]
    for k, copy in enumerate(copies):
        copy.wait_recv()
        total = total + got[k].astype(F32)
    products = (
        three_columns(total[:, width : width + HD]), three_columns(total[:, width + HD :])
    )
    grad_out[...] = cot_here[...].astype(F32) + norm_back(
        total[:, :width], products, hots, router, hidden[...], gain[...], hot_out, gain_out
    )
    pair_out[here, :] = grad_out[...].astype(BF16)
    more = [
        send_across(pair_out.at[here], pair_out.at[here], g_send.at[k], g_recv.at[k], p)
        for k, p in enumerate(peers)
    ]
    for copy in more:
        copy.start()
    for copy in copies:
        copy.wait_send()
    for copy in more:
        copy.wait()
    for copy in (*moves, *dealt):
        copy.wait()


def back_step(
    tensor_size, peers, back, pick, hits, hidden, cot_here, gain, router, hots, rows_send,
    maps,
):
    tokens, width = pick.shape[1], back.shape[1] - HD
    size = tokens // tensor_size
    around = tensor_size - 1
    wide = width + 2 * HD
    return pl.pallas_call(
        back_kernel,
        in_specs=[VMEM] * 9 + [HBM] * 2,
        out_specs=[VMEM] * 4 + [HBM] * 2,
        out_shape=[
            jax.ShapeDtypeStruct((size, width), F32),
            jax.ShapeDtypeStruct((tokens, width), BF16),
            jax.ShapeDtypeStruct((1, width), F32),
            jax.ShapeDtypeStruct((size, HD), BF16),
            jax.ShapeDtypeStruct(rows_send.shape, BF16),
            jax.ShapeDtypeStruct(maps.shape, BF16),
        ],
        scratch_shapes=[
            pltpu.VMEM((tokens, wide), F32),
            pltpu.VMEM((tokens, wide), BF16),
            pltpu.VMEM((around, size, wide), BF16),
            sems(around), sems(around), sems(around), sems(around), sems(peers), sems(peers),
            sems(peers), sems(peers),
        ],
        compiler_params=pltpu.CompilerParams(
            collective_id=4, has_side_effects=True, vmem_limit_bytes=40 << 20
        ),
        cost_estimate=pl.CostEstimate(
            flops=2 * pick.shape[0] * tokens * width, bytes_accessed=300 << 20, transcendentals=0
        ),
    )(back, pick, hits[0], hits[1], hidden, cot_here, gain, router, hots, rows_send, maps)


GIVE = 4
HALF_SMALL = 8


def final_kernel(
    routed_hbm, grad_q, normed, grad_kv, part_hbm, maps_hbm,
    grad_hidden, x_here, gain, router, hots, small,
    out, maps_out, tokens_out, small_out,
    give, keep, twin_in, far_in, near_in, routed, got_part, tokens_here,
    twin_send, twin_recv, far_send, far_recv, near_send, near_recv, load, own,
    p_send, p_recv, t_send, t_recv,
    hot_here, small_all, small_in, small_sum, small_got,
    s_send, s_recv, w_send, w_recv, d_send, d_recv,
):
    at = Square()
    experts = grad_q.shape[0]
    units, _, size, _ = keep.shape
    half = size // 2
    count = p_send.shape[0] + 1
    peers = tensor_peers(count)
    width = normed.shape[1]
    share = part_hbm.shape[0] // count

    def fetch(u):
        return pltpu.make_async_copy(
            routed_hbm.at[u], routed.at[lax.rem(u, 2)], load.at[lax.rem(u, 2)]
        )

    fetch(0).start()
    here = share_rows(share)
    mine = pltpu.make_async_copy(part_hbm.at[here], got_part.at[count - 1], own.at[0])
    mine.start()
    greet([{"dp": partner(k)} for k in range(1, 8)] + [{"tensor": p} for p in peers])
    part_copies = [
        send_across(part_hbm.at[rows_of(p, share)], got_part.at[k], p_send.at[k], p_recv.at[k], p)
        for k, p in enumerate(peers)
    ]
    for copy in part_copies:
        copy.start()
    dealt = deal(maps_hbm, maps_out, (d_send, d_recv))

    def to_twin(u):
        slot = lax.rem(u, GIVE)
        return send_to(give.at[slot], twin_in.at[u], twin_send.at[slot], twin_recv.at[u], at.twin)

    def to_far(u):
        first = send_to(
            keep.at[u, at.chip_far, pl.ds(0, half)],
            far_in.at[u, 0], far_send.at[u, 0], far_recv.at[u, 0], at.near_x,
        )
        second = send_to(
            keep.at[u, at.chip_far, pl.ds(half, half)],
            far_in.at[u, 1], far_send.at[u, 1], far_recv.at[u, 1], at.near_y,
        )
        return first, second

    def to_near(u):
        first = send_to(
            keep.at[u, at.chip_x], near_in.at[u, 0], near_send.at[u, 0], near_recv.at[u, 0],
            at.near_x,
        )
        second = send_to(
            keep.at[u, at.chip_y], near_in.at[u, 1], near_send.at[u, 1], near_recv.at[u, 1],
            at.near_y,
        )
        return first, second

    def multiply(u, rows, grads):
        slot = lax.rem(u, GIVE)

        @pl.when(u >= GIVE)
        def _():
            to_twin(u - GIVE).wait_send()

        for chip in range(4):
            columns = rows_of(2 * chip + 1 - at.core, size)
            give[slot, chip] = dot_tn(rows[:, columns], grads[...]).astype(BF16)
        to_twin(u).start()
        for chip in range(4):
            columns = rows_of(2 * chip + at.core, size)
            keep[u, chip] = dot_tn(rows[:, columns], grads[...]).astype(BF16)

    def join_twin(u):
        to_twin(u).wait_recv()

        def add(chip):
            keep[u, chip] = (keep[u, chip].astype(F32) + twin_in[u, chip].astype(F32)).astype(BF16)

        add(at.chip_far)
        for copy in to_far(u):
            copy.start()
        add(at.chip_x)
        add(at.chip_y)
        add(at.chip)

    @pl.loop(0, experts)
    def _(u):
        fetch(u).wait()

        @pl.when(u < experts - 1)
        def _():
            fetch(u + 1).start()

        multiply(u, routed.at[lax.rem(u, 2)], grad_q.at[u])

        @pl.when(u > 0)
        def _():
            join_twin(u - 1)

    @pl.loop(experts, units)
    def _(u):
        multiply(u, normed, grad_kv.at[u - experts])
        join_twin(u - 1)

    join_twin(units - 1)

    mine.wait()
    total = got_part[count - 1].astype(F32)
    for k, copy in enumerate(part_copies):
        copy.wait_recv()
        total = total + got_part[k].astype(F32)
    products = (
        three_columns(total[:, width : width + HD]), three_columns(total[:, width + HD :])
    )
    tokens_here[...] = (
        grad_hidden[...]
        + norm_back(
            total[:, :width], products, hots, router, x_here[...].astype(F32), gain[...],
            hot_here, small_all.at[pl.ds(0, 1)],
        )
    ).astype(BF16)
    token_copies = [
        send_across(tokens_here, tokens_out.at[here], t_send.at[k], t_recv.at[k], p)
        for k, p in enumerate(peers)
    ]
    for copy in token_copies:
        copy.start()
    kept = pltpu.make_async_copy(tokens_here, tokens_out.at[here], own.at[1])
    kept.start()

    small_all[1:HALF_SMALL, :] = small[1:HALF_SMALL, :]
    small_all[HALF_SMALL : 2 * HALF_SMALL, :] = dot_tn(hot_here[...], normed[here, :])[:HALF_SMALL]
    small_all[2 * HALF_SMALL :, :] = small[HALF_SMALL:, :]

    def small_block(place):
        return small_all.at[:, rows_of(place, size)]

    small_copies = [
        send_to(
            small_block(partner(k)), small_in.at[k], s_send.at[k], s_recv.at[k], partner(k)
        )
        for k in range(1, 8)
    ]
    for copy in small_copies:
        copy.start()

    @pl.loop(0, units)
    def _(u):
        for copy in to_far(u):
            copy.wait_recv()
        top, bottom = pl.ds(0, half), pl.ds(half, half)
        keep[u, at.chip_y, top, :] = (
            keep[u, at.chip_y, top, :].astype(F32) + far_in[u, 0].astype(F32)
        ).astype(BF16)
        keep[u, at.chip_x, bottom, :] = (
            keep[u, at.chip_x, bottom, :].astype(F32) + far_in[u, 1].astype(F32)
        ).astype(BF16)
        for copy in to_near(u):
            copy.start()

    @pl.loop(0, units)
    def _(u):
        for copy in to_near(u):
            copy.wait_recv()
        out[u] = (
            keep[u, at.chip].astype(F32) + near_in[u, 0].astype(F32) + near_in[u, 1].astype(F32)
        ).astype(BF16)

    block = small_all[:, rows_of(2 * at.chip + at.core, size)]
    for k, copy in enumerate(small_copies):
        copy.wait_recv()
        block = block + small_in[k + 1]
    small_sum[...] = block
    last_copies = [
        send_across(small_sum, small_got.at[k], w_send.at[k], w_recv.at[k], p)
        for k, p in enumerate(peers)
    ]
    for copy in last_copies:
        copy.start()

    @pl.loop(units - GIVE, units)
    def _(u):
        to_twin(u).wait_send()

    @pl.loop(0, units)
    def _(u):
        for copy in (*to_far(u), *to_near(u)):
            copy.wait_send()

    for k, copy in enumerate(last_copies):
        copy.wait_recv()
        block = block + small_got[k]
    small_out[...] = block
    for copy in (*part_copies, *small_copies, *last_copies):
        copy.wait_send()
    for copy in (*token_copies, *dealt, kept):
        copy.wait()


def final_step(
    tensor_size, routed, grad_q, normed, grad_kv, part, maps,
    grad_hidden, x_here, gain, router, hots, small,
):
    experts, rows, width = routed.shape
    columns = grad_q.shape[2]
    units = experts + grad_kv.shape[0]
    size = width // 8
    tokens, wide = part.shape
    share = tokens // tensor_size
    around = tensor_size - 1
    return pl.pallas_call(
        final_kernel,
        in_specs=[HBM, VMEM, VMEM, VMEM, HBM, HBM] + [VMEM] * 6,
        out_specs=[VMEM, HBM, HBM, VMEM],
        out_shape=[
            jax.ShapeDtypeStruct((units, size, columns), BF16),
            jax.ShapeDtypeStruct(maps.shape, BF16),
            jax.ShapeDtypeStruct((tokens, width), BF16),
            jax.ShapeDtypeStruct((3 * HALF_SMALL, size), F32),
        ],
        scratch_shapes=[
            pltpu.VMEM((GIVE, 4, size, columns), BF16),
            pltpu.VMEM((units, 4, size, columns), BF16),
            pltpu.VMEM((units, 4, size, columns), BF16),
            pltpu.VMEM((units, 2, size // 2, columns), BF16),
            pltpu.VMEM((units, 2, size, columns), BF16),
            pltpu.VMEM((2, rows, width), BF16),
            pltpu.VMEM((tensor_size, share, wide), BF16),
            pltpu.VMEM((share, width), BF16),
            sems(GIVE), sems(units), sems(units, 2), sems(units, 2), sems(units, 2),
            sems(units, 2), sems(2), sems(2),
            sems(around), sems(around), sems(around), sems(around),
            pltpu.VMEM((share, HD), BF16),
            pltpu.VMEM((3 * HALF_SMALL, width), F32),
            pltpu.VMEM((8, 3 * HALF_SMALL, size), F32),
            pltpu.VMEM((3 * HALF_SMALL, size), F32),
            pltpu.VMEM((around, 3 * HALF_SMALL, size), F32),
            sems(8), sems(8), sems(around), sems(around), sems(8), sems(8),
        ],
        compiler_params=pltpu.CompilerParams(
            collective_id=1, has_side_effects=True, vmem_limit_bytes=60 << 20
        ),
        cost_estimate=pl.CostEstimate(
            flops=2 * units * rows * width * columns,
            bytes_accessed=350 << 20,
            transcendentals=0,
        ),
    )(
        routed, grad_q, normed, grad_kv, part, maps,
        grad_hidden, x_here, gain, router, hots, small,
    )


def partner(k):
    me = lax.axis_index("dp")
    place = me
    for bit in (1, 2, 4):
        place = place + bit * lax.rem(k // bit, 2) * (1 - 2 * lax.rem(me // bit, 2))
    return place


def expert_kernel(
    x_ref, cot_hbm, gate_up_hbm, down_hbm,
    back_out, rows_out, grad_gate_hbm, grad_up_hbm, grad_down_hbm,
    x_all, g_all, w_gate, w_up, w_down, act, grads, back, product, stage_up, stage_down,
    x_send, x_recv, b_send, b_recv, load, up_sem, down_sem,
):
    peers = x_send.shape[0]
    slots, wide = x_all.shape
    width = wide - HD
    hidden = w_gate.shape[1]
    size = slots // peers
    pair = 2 * size
    step = 256
    whole_steps = hidden // step
    tail = hidden - whole_steps * step

    per = width // peers
    loads = [
        pltpu.make_async_copy(cot_hbm, g_all, load.at[0]),
        pltpu.make_async_copy(down_hbm, w_down, load.at[1]),
    ]
    for j in range(peers):
        for g, target in enumerate((w_gate, w_up)):
            loads.append(
                pltpu.make_async_copy(
                    gate_up_hbm.at[j, g], target.at[pl.ds(j * per, per)], load.at[2 + 2 * j + g]
                )
            )
    for copy in loads:
        copy.start()

    barrier = pltpu.get_barrier_semaphore()
    for k in range(1, peers):
        pl.semaphore_signal(
            barrier, inc=1, device_id={"dp": partner(k)}, device_id_type=pl.DeviceIdType.MESH
        )
    pl.semaphore_wait(barrier, peers - 1)

    def block(k):
        return pl.ds(pl.multiple_of(k * size, size), size)

    def send_x(k):
        return send_to(
            x_ref.at[block(k)], x_all.at[block(k)], x_send.at[k], x_recv.at[k], partner(k)
        )

    def send_back(k):
        return send_to(
            back.at[block(k)], back_out.at[block(k)], b_send.at[k], b_recv.at[k], partner(k)
        )

    for k in (1, 2, 4, 3, 5):
        send_x(k).start()
    x_all[0:size, :] = x_ref[0:size, :]
    for copy in loads:
        copy.wait()

    @pl.loop(0, peers // 2)
    def _(group):
        rows = pl.ds(pl.multiple_of(group * pair, pair), pair)

        @pl.when(group > 0)
        def _():
            send_x(2 * group).wait_recv()

        send_x(2 * group + 1).wait_recv()
        columns = x_all[rows, width:].astype(F32)
        gate_of_row = columns[:, 0:1] + columns[:, 1:2] + columns[:, 2:3]
        g_all[rows, :] = (g_all[rows, :].astype(F32) * gate_of_row).astype(BF16)
        product[...] = jnp.zeros_like(product)

        def chunk(start, amount):
            cols = pl.ds(start, amount)
            x = x_all[rows, 0:width]
            gate = dot(x, w_gate[:, cols])
            up = dot(x, w_up[:, cols])
            grad_act = jnp.zeros((pair, amount), F32)
            for j in range(peers):
                grad_act += dot_nt(g_all[rows, j * per : (j + 1) * per], w_down[j, cols, :])
            sigmoid = 1.0 / (1.0 + jnp.exp(-gate))
            silu = gate * sigmoid
            activated = (silu * up).astype(BF16)
            act[rows, cols] = activated
            both = activated.astype(F32) * grad_act
            for part in range(amount // HD):
                product[...] += both[:, part * HD : (part + 1) * HD]
            grads[rows, cols] = (
                grad_act * up * sigmoid * (1.0 + gate * (1.0 - sigmoid))
            ).astype(BF16)
            grads[rows, pl.ds(hidden + start, amount)] = (grad_act * silu).astype(BF16)

        @pl.loop(0, whole_steps)
        def _(i):
            chunk(pl.multiple_of(i * step, step), step)

        if tail:
            chunk(whole_steps * step, tail)

        @pl.loop(0, width // step)
        def _(i):
            at = pl.ds(pl.multiple_of(i * step, step), step)
            back[rows, at] = (
                dot_nt(grads[rows, 0:hidden], w_gate[at, :])
                + dot_nt(grads[rows, hidden:], w_up[at, :])
            ).astype(BF16)

        total = jnp.sum(product[...], axis=1, keepdims=True)
        high = total.astype(BF16).astype(F32)
        mid = (total - high).astype(BF16).astype(F32)
        lane = lax.broadcasted_iota(jnp.int32, (pair, HD), 1)
        back[rows, width:] = jnp.where(
            lane == 0, high, jnp.where(lane == 1, mid, jnp.where(lane == 2, total - high - mid, 0.0))
        ).astype(BF16)

        @pl.when(group == 0)
        def _():
            send_x(6).start()
            send_x(7).start()
            back_out[0:size, :] = back[0:size, :]

        @pl.when(group > 0)
        def _():
            send_back(2 * group).start()

        send_back(2 * group + 1).start()

    def store_up(j, slot):
        return (
            pltpu.make_async_copy(
                stage_up.at[slot, :, pl.ds(0, hidden)], grad_gate_hbm.at[j], up_sem.at[slot, 0]
            ),
            pltpu.make_async_copy(
                stage_up.at[slot, :, pl.ds(hidden, hidden)], grad_up_hbm.at[j], up_sem.at[slot, 1]
            ),
        )

    @pl.loop(0, peers)
    def _(j):
        slot = lax.rem(j, 2)

        @pl.when(j > 1)
        def _():
            for copy in store_up(j - 2, slot):
                copy.wait()

        at = pl.ds(pl.multiple_of(j * per, per), per)
        stage_up[slot] = dot_tn(x_all[:, at], grads[...]).astype(BF16)
        for copy in store_up(j, slot):
            copy.start()
        rows_out[:, at] = dot(act[...], w_down[j]).astype(BF16)

    def store_down(start, amount, slot):
        return pltpu.make_async_copy(
            stage_down.at[slot, :, pl.ds(0, amount)],
            grad_down_hbm.at[:, pl.ds(start, amount)],
            down_sem.at[slot],
        )

    def down_piece(start, amount, slot):
        piece = dot_tn(act[:, pl.ds(start, amount)], g_all[...]).astype(BF16)
        for j in range(peers):
            stage_down[slot, j, 0:amount, :] = piece[:, j * per : (j + 1) * per]
        store_down(start, amount, slot).start()

    @pl.loop(0, whole_steps)
    def _(i):
        slot = lax.rem(i, 2)

        @pl.when(i > 1)
        def _():
            store_down(pl.multiple_of((i - 2) * step, step), step, slot).wait()

        down_piece(pl.multiple_of(i * step, step), step, slot)

    last = whole_steps - 1
    store_down((last - 1) * step, step, (last - 1) % 2).wait()
    if tail:
        down_piece(whole_steps * step, tail, (last - 1) % 2)
        store_down(whole_steps * step, tail, (last - 1) % 2).wait()
    store_down(last * step, step, last % 2).wait()
    for j in (peers - 2, peers - 1):
        for copy in store_up(j, j % 2):
            copy.wait()
    for k in range(1, peers):
        send_x(k).wait_send()
        send_back(k).wait()


def expert_step(x_rows, cot_rows, up_slices, down_slices):
    slots, wide = x_rows.shape
    width = wide - HD
    peers, hidden, per = down_slices.shape
    vmem = pl.BlockSpec(memory_space=pltpu.VMEM)
    hbm = pl.BlockSpec(memory_space=pl.ANY)
    step = 256
    return pl.pallas_call(
        expert_kernel,
        in_specs=[vmem, hbm, hbm, hbm],
        out_specs=[vmem, vmem, hbm, hbm, hbm],
        out_shape=[
            jax.ShapeDtypeStruct((slots, wide), BF16),
            jax.ShapeDtypeStruct((slots, width), BF16),
            jax.ShapeDtypeStruct((peers, per, hidden), BF16),
            jax.ShapeDtypeStruct((peers, per, hidden), BF16),
            jax.ShapeDtypeStruct((peers, hidden, per), BF16),
        ],
        scratch_shapes=[
            pltpu.VMEM((slots, wide), BF16),
            pltpu.VMEM((slots, width), BF16),
            pltpu.VMEM((width, hidden), BF16),
            pltpu.VMEM((width, hidden), BF16),
            pltpu.VMEM((peers, hidden, per), BF16),
            pltpu.VMEM((slots, hidden), BF16),
            pltpu.VMEM((slots, 2 * hidden), BF16),
            pltpu.VMEM((slots, wide), BF16),
            pltpu.VMEM((2 * slots // peers, HD), F32),
            pltpu.VMEM((2, per, 2 * hidden), BF16),
            pltpu.VMEM((2, peers, step, per), BF16),
            pltpu.SemaphoreType.DMA((peers,)),
            pltpu.SemaphoreType.DMA((peers,)),
            pltpu.SemaphoreType.DMA((peers,)),
            pltpu.SemaphoreType.DMA((peers,)),
            pltpu.SemaphoreType.DMA((2 + 2 * peers,)),
            pltpu.SemaphoreType.DMA((2, 2)),
            pltpu.SemaphoreType.DMA((2,)),
        ],
        compiler_params=pltpu.CompilerParams(
            collective_id=2, has_side_effects=True, vmem_limit_bytes=60 << 20
        ),
        cost_estimate=pl.CostEstimate(
            flops=18 * slots * width * hidden, bytes_accessed=300 << 20, transcendentals=0
        ),
    )(x_rows, cot_rows, up_slices, down_slices)


class Movers:
    def __init__(self, dp, experts, tensor):
        self.dp, self.experts, self.tensor = dp, experts, tensor
        self.ratio = dp // experts
        self.groups = self.pairs = None
        if self.ratio > 1:
            self.groups = [[g * experts + e for e in range(experts)] for g in range(self.ratio)]
            self.pairs = [[g * experts + e for g in range(self.ratio)] for e in range(experts)]

    def swap(self, blocks):
        return lax.all_to_all(blocks, "dp", 0, 0, axis_index_groups=self.groups, tiled=True)

    def fetch(self, shards):
        mine = self.swap(shards)
        if self.ratio > 1:
            mine = lax.all_gather(mine, "dp", axis=0, axis_index_groups=self.pairs, tiled=True)
        return mine

    def give_back(self, slices):
        if self.ratio > 1:
            slices = lax.psum_scatter(
                slices, "dp", scatter_dimension=0, axis_index_groups=self.pairs, tiled=True
            )
        return self.swap(slices)

    def exchange(self, rows):
        size = rows.shape[0] // self.experts
        blocks = [rows[:size]]
        for k in range(1, self.experts):
            pairs = [(i, i ^ k) for i in range(self.dp)]
            blocks.append(lax.ppermute(rows[k * size : (k + 1) * size], "dp", pairs))
        return jnp.concatenate(blocks, axis=0)

    def across(self, block, k):
        return lax.ppermute(block, "tensor", [(i, i ^ k) for i in range(self.tensor)])

    def reduce_rows(self, part, dtype=BF16):
        z = lax.axis_index("tensor")
        size = part.shape[0] // self.tensor
        total = lax.dynamic_slice_in_dim(part, z * size, size, axis=0)
        sent = part.astype(dtype)
        for k in range(1, self.tensor):
            block = lax.dynamic_slice_in_dim(sent, (z ^ k) * size, size, axis=0)
            total = total + self.across(block, k).astype(F32)
        return total

    def gather_rows(self, rows):
        z = lax.axis_index("tensor")
        size = rows.shape[0]
        rows = rows.astype(BF16)
        full = jnp.zeros((size * self.tensor,) + rows.shape[1:], BF16)
        for k in range(self.tensor):
            block = rows if k == 0 else self.across(rows, k)
            full = lax.dynamic_update_slice_in_dim(full, block, (z ^ k) * size, axis=0)
        return full


def expert_plain(movers, expert_in, cot_rows, up_slices, down_slices):
    dp_size, hidden_here, per_dp = down_slices.shape
    model_width = dp_size * per_dp
    gate_full, up_full = (up_slices[:, g].reshape(model_width, hidden_here) for g in range(2))
    down_full = down_slices.transpose(1, 0, 2).reshape(hidden_here, model_width)
    x_rows, gate_of_row = without_column(movers.exchange(expert_in))
    g_rows = (cot_rows.astype(F32) * gate_of_row).astype(BF16)
    gate = dot(x_rows, gate_full)
    up = dot(x_rows, up_full)
    sigmoid_gate = jax.nn.sigmoid(gate)
    silu_gate = gate * sigmoid_gate
    activated = (silu_gate * up).astype(BF16)
    grad_act = dot_nt(g_rows, down_full)
    grad_gate = (grad_act * up * sigmoid_gate * (1.0 + gate * (1.0 - sigmoid_gate))).astype(BF16)
    grad_up = (grad_act * silu_gate).astype(BF16)
    gate_times_grad = jnp.sum(activated.astype(F32) * grad_act, axis=1, keepdims=True)
    grad_expert_in = with_column(
        (dot_nt(grad_gate, gate_full) + dot_nt(grad_up, up_full)).astype(BF16), gate_times_grad
    )
    return (
        movers.exchange(grad_expert_in),
        dot(activated, down_full, BF16),
        dot_tn(x_rows, grad_gate, BF16).reshape(dp_size, per_dp, -1),
        dot_tn(x_rows, grad_up, BF16).reshape(dp_size, per_dp, -1),
        dot_tn(activated, g_rows, BF16).reshape(-1, dp_size, per_dp).transpose(1, 0, 2),
    )


def on_device(
    dp_size,
    tensor_size,
    tokens,
    cotangent,
    parents,
    attention_routes,
    expert_routes,
    slot_order,
    gain_attention,
    keyval_weight,
    query_weight,
    output_weight,
    attention_router,
    gain_feedforward,
    expert_router,
    gate_up_weight,
    down_weight,
):
    tok_count, model_width = tokens.shape
    pair_count = TOPK * tok_count
    att_experts = query_weight.shape[0]
    mlp_experts = gate_up_weight.shape[0]
    att_cap = tok_count * 5 // 16
    mlp_cap = pair_count // mlp_experts
    att_slots = att_experts * att_cap
    mlp_slots = mlp_experts * mlp_cap
    width_here = query_weight.shape[2]
    rows_here = tok_count // tensor_size
    movers = Movers(dp_size, mlp_experts, tensor_size)
    fast = dp_size == 8 and mlp_experts == 8
    tie = lax.optimization_barrier

    small = jnp.concatenate(
        [gain_attention[:, None], gain_feedforward[:, None], attention_router, expert_router], axis=1
    )
    small_full = lax.all_gather(small, "dp", axis=0, tiled=True)
    small_full, down_weight = tie((small_full, down_weight))
    gain_attn_full = small_full[:, 0].astype(F32)
    gain_mlp_full = small_full[:, 1].astype(F32)
    router_att = small_full[:, 2 : 2 + att_experts]
    router_mlp = small_full[:, 2 + att_experts :]

    inside, depth = ancestry(parents[0])
    token_index = jnp.arange(tok_count, dtype=jnp.int32)
    pair_order = jnp.arange(pair_count, dtype=jnp.int32).reshape(tok_count, TOPK)
    att_hits = slot_hits(
        slot_places(attention_routes, pair_order, att_cap, att_experts), att_slots
    )
    priority = slot_order[0][:, None] * TOPK + jnp.arange(TOPK, dtype=jnp.int32)[None, :]
    home = lax.rem(lax.axis_index("dp"), mlp_experts)
    mlp_hits = slot_hits(
        slot_places(expert_routes ^ home, priority, mlp_cap, mlp_experts), mlp_slots
    )
    att_pick = (att_hits[0] | att_hits[1]).astype(BF16)
    mlp_pick = (mlp_hits[0] | mlp_hits[1]).astype(BF16)

    def to_slots(hits, pair_values):
        return jnp.sum(
            sum(jnp.where(hits[k], pair_values[:, k][None, :], 0) for k in range(TOPK)), axis=1
        )

    def to_pairs(hits, slot_values):
        return jnp.stack(
            [jnp.sum(jnp.where(hits[k], slot_values[:, None], 0.0), axis=0) for k in range(TOPK)],
            axis=1,
        )

    def position_of(token):
        segment = token // SEG
        level = jnp.sum(
            jnp.where(segment[:, None] == jnp.arange(depth.shape[0])[None, :], depth[None, :], 0),
            axis=1,
        )
        return level * SEG + token % SEG

    pair_token = jnp.broadcast_to(token_index[:, None], (tok_count, TOPK))
    slot_token = to_slots(att_hits, pair_token)
    slot_filled = jnp.any(att_hits[0] | att_hits[1], axis=1)
    slot_tables = rope_tables(position_of(slot_token))
    tok_tables = rope_tables(position_of(token_index))
    segment_hot = (
        (slot_token // SEG)[:, None] == jnp.arange(inside.shape[0], dtype=jnp.int32)[None, :]
    ).astype(F32)
    reach = dot(segment_hot, jnp.repeat(inside.astype(F32), SEG, axis=1)) > 0.5
    allowed = reach & (token_index[None, :] <= slot_token[:, None]) & slot_filled[:, None]
    bias = jnp.where(allowed, 0.0, NEGATIVE).astype(BF16)

    down_slices = movers.fetch(down_weight)
    cot_send = dot(mlp_pick, cotangent, BF16)

    inputs = tokens.astype(F32)
    normal_attn, scale_attn = norm_forward(inputs)
    normed = (normal_attn * gain_attn_full).astype(BF16)
    att_gates = picked_softmax(dot(normed, router_att), attention_routes)
    att_gate_slots = to_slots(att_hits, att_gates)[:, None]
    routed = dot(att_pick, normed, BF16).reshape(att_experts, att_cap, model_width)
    if fast:
        keyval_weight, query_weight, output_weight, *before = tie(
            (keyval_weight, query_weight, output_weight, routed, cot_send, bias, att_gate_slots)
            + slot_tables + tok_tables
        )
        routed, cot_send, bias, att_gate_slots = before[:4]
        slot_tables, tok_tables = before[4:6], before[6:8]
        keyval_full, query_full, output_full = gather_maps(
            (keyval_weight, query_weight, output_weight), (1, 1, 2), (2, 2, 2)
        )
    else:
        keyval_full = lax.all_gather(keyval_weight, "dp", axis=1, tiled=True)
        query_full = lax.all_gather(query_weight, "dp", axis=1, tiled=True)
        output_full = lax.all_gather(output_weight, "dp", axis=2, tiled=True)
    query_full, keyval_full, down_slices, gate_up_weight = tie(
        (query_full, keyval_full, down_slices, gate_up_weight)
    )
    up_slices = movers.fetch(gate_up_weight)
    keyval = jnp.concatenate([dot(normed, keyval_full[0]), dot(normed, keyval_full[1])], axis=1)
    query_raw = jnp.einsum(
        "ecd,edf->ecf", routed, query_full, preferred_element_type=F32
    ).reshape(att_slots, width_here)
    queries, key_rows, values, attended, gated = attend(
        query_raw, keyval, bias, att_gate_slots, slot_tables, tok_tables
    )
    gated_slots = gated.reshape(att_experts, att_cap, width_here)
    att_rows = jnp.einsum(
        "ecf,efd->ecd", gated_slots, output_full, preferred_element_type=F32
    ).reshape(att_slots, model_width)
    att_rows = att_rows.astype(BF16)

    z = lax.axis_index("tensor")

    def share(rows):
        return lax.dynamic_slice_in_dim(rows, z * rows_here, rows_here, axis=0)

    def hots(gates, picks, experts):
        lanes = jnp.arange(HD, dtype=jnp.int32)[None, :]
        hot = [(share(picks)[:, k : k + 1] == lanes).astype(F32) for k in range(TOPK)]
        return jnp.stack(hot + [sum(hot[k] * share(gates)[:, k : k + 1] for k in range(TOPK))])

    def padded(router):
        return jnp.pad(router, ((0, 0), (0, HD - router.shape[1])))

    if fast:
        hidden, mlp_in, cot_rows = hidden_step(
            tensor_size, mlp_experts, att_pick, att_rows, share(tokens), gain_mlp_full[None],
            cot_send,
        )
    else:
        hidden = share(inputs) + movers.reduce_rows(dot_tn(att_pick, att_rows))
        mlp_in = movers.gather_rows((norm_forward(hidden)[0] * gain_mlp_full).astype(BF16))
        cot_rows = movers.exchange(cot_send)
    mlp_in, up_slices, cot_rows = tie((mlp_in, up_slices, cot_rows))
    mlp_gates = picked_softmax(dot(mlp_in, router_mlp), expert_routes)
    mlp_gate_slots = to_slots(mlp_hits, mlp_gates)[:, None]
    expert_in = with_column(dot(mlp_pick, mlp_in, BF16), mlp_gate_slots)

    if fast:
        back = expert_step(expert_in, cot_rows, up_slices, down_slices)
    else:
        back = expert_plain(movers, expert_in, cot_rows, up_slices, down_slices)
    grad_in_slots, expert_out, grad_gate_w, grad_up_w, grad_down_w = back

    if fast:
        grad_hidden, grad_att_pair, grad_gain_mlp, grad_mlp_logits, out_slots, grad_gate_w = back_step(
            tensor_size, mlp_experts, grad_in_slots, mlp_pick,
            [hit.astype(BF16) for hit in mlp_hits], hidden, share(cotangent),
            gain_mlp_full[None], padded(router_mlp),
            hots(mlp_gates, expert_routes, mlp_experts), expert_out, grad_gate_w,
        )
        grad_gain_mlp = grad_gain_mlp[0]
        grad_mlp_logits = grad_mlp_logits[:, :mlp_experts]
    else:
        out_slots = movers.exchange(expert_out)
        grad_gate_w = movers.give_back(grad_gate_w)
        grad_in_slots, gate_times_grad = without_column(grad_in_slots)
        mlp_products = movers.reduce_rows(to_pairs(mlp_hits, gate_times_grad[:, 0]), F32)
        grad_mlp_in = movers.reduce_rows(dot_tn(mlp_pick, grad_in_slots))
        grad_mlp_logits = router_backward(
            share(mlp_gates), mlp_products, share(expert_routes), mlp_experts
        )
        grad_mlp_in = grad_mlp_in + dot_nt(grad_mlp_logits, router_mlp)
        normal_mlp, scale_mlp = norm_forward(hidden)
        grad_hidden_norm, grad_gain_mlp = norm_backward(
            grad_mlp_in, normal_mlp, scale_mlp, gain_mlp_full
        )
        grad_hidden = share(cotangent).astype(F32) + grad_hidden_norm
        grad_att_pair = movers.gather_rows(grad_hidden)
    grad_att_pair, grad_up_w = tie((grad_att_pair, grad_up_w))
    grad_up_w = movers.give_back(grad_up_w)
    grad_router_mlp = dot_tn(share(mlp_in), grad_mlp_logits)

    gate_matrix = sum(
        jnp.where(mlp_hits[k], mlp_gates[:, k][None, :], 0.0) for k in range(TOPK)
    )
    matrix_high = gate_matrix.astype(BF16)
    matrix_low = (gate_matrix - matrix_high.astype(F32)).astype(BF16)
    mlp_part = (dot_tn(matrix_high, out_slots) + dot_tn(matrix_low, out_slots)).astype(BF16)
    mlp_sum = movers.reduce_rows(mlp_part)

    grad_att_rows = dot(att_pick, grad_att_pair, BF16).reshape(att_experts, att_cap, model_width)
    grad_output_w = jnp.einsum(
        "ecf,ecd->efd", gated_slots, grad_att_rows, preferred_element_type=BF16
    )
    grad_att_rows, grad_output_w = tie((grad_att_rows, grad_output_w))
    grad_gated = jnp.einsum(
        "ecd,efd->ecf", grad_att_rows, output_full, preferred_element_type=F32
    ).reshape(att_slots, width_here)
    grad_output_out = lax.psum_scatter(grad_output_w, "dp", scatter_dimension=2, tiled=True)
    att_products = to_pairs(
        att_hits, jnp.sum(grad_gated * attended, axis=1) * att_gate_slots[:, 0]
    )
    grad_q, grad_k, grad_v = attend_back(
        queries, key_rows, values, bias, att_gate_slots, slot_tables, tok_tables, grad_gated
    )
    grad_query_slots = grad_q.reshape(att_experts, att_cap, width_here)
    grad_routed = jnp.einsum(
        "ecf,edf->ecd", grad_query_slots, query_full, preferred_element_type=F32
    ).reshape(att_slots, model_width)
    normed_part = (
        dot_tn(att_pick, grad_routed.astype(BF16))
        + dot_nt(grad_k, keyval_full[0])
        + dot_nt(grad_v, keyval_full[1])
    )
    normed_part = with_column(normed_part.astype(BF16), att_products[:, :1])
    normed_part = with_column(normed_part, att_products[:, 1:])
    grad_kv = jnp.stack([grad_k, grad_v])
    normed_part, grad_up_w, mlp_sum = tie((normed_part, grad_up_w, mlp_sum))
    mixed = movers.gather_rows(hidden + mlp_sum)
    if fast:
        small = jnp.concatenate(
            [
                jnp.zeros((1, model_width), F32),
                grad_gain_mlp[None],
                jnp.zeros((HALF_SMALL - 2, model_width), F32),
                grad_router_mlp.T,
            ],
            axis=0,
        )
        map_sums, grad_down_w, grad_tokens, small_grads = final_step(
            tensor_size, routed, grad_query_slots, normed, grad_kv, normed_part, grad_down_w,
            grad_hidden, share(tokens), gain_attn_full[None], padded(router_att),
            hots(att_gates, attention_routes, att_experts), small,
        )
        small_grads = jnp.concatenate([small_grads[:2], small_grads[HALF_SMALL:]], axis=0).T
        grad_query_out, grad_keyval_out = map_sums[:att_experts], map_sums[att_experts:]
    else:
        grad_query_w = jnp.einsum(
            "ecd,ecf->edf", routed, grad_query_slots, preferred_element_type=BF16
        )
        grad_keyval_w = jnp.stack([dot_tn(normed, grad, BF16) for grad in (grad_k, grad_v)])
        grad_query_out = lax.psum_scatter(grad_query_w, "dp", scatter_dimension=1, tiled=True)
        grad_keyval_out = lax.psum_scatter(grad_keyval_w, "dp", scatter_dimension=1, tiled=True)
        grad_down_w = movers.give_back(grad_down_w)
        grad_normed = movers.reduce_rows(normed_part[:, :model_width])
        grad_att_logits = router_backward(
            share(att_gates), movers.reduce_rows(att_products, F32), share(attention_routes),
            att_experts,
        )
        grad_normed = grad_normed + dot_nt(grad_att_logits, router_att)
        grad_input_norm, grad_gain_attn = norm_backward(
            grad_normed, share(normal_attn), share(scale_attn), gain_attn_full
        )
        grad_tokens = movers.gather_rows(grad_hidden + grad_input_norm)
        grad_router_att = dot_tn(share(normed), grad_att_logits)
        small_grads = jnp.concatenate(
            [grad_gain_attn[:, None], grad_gain_mlp[:, None], grad_router_att, grad_router_mlp],
            axis=1,
        )
        small_grads = lax.psum(
            lax.psum_scatter(small_grads, "dp", scatter_dimension=0, tiled=True), "tensor"
        )
    grad_tokens, grad_output_out = tie((grad_tokens, grad_output_out))
    grad_tokens = grad_tokens.astype(F32)
    return (
        mixed,
        grad_tokens,
        small_grads[:, 0],
        grad_keyval_out.astype(F32),
        grad_query_out.astype(F32),
        grad_output_out.astype(F32),
        small_grads[:, 2 : 2 + att_experts],
        small_grads[:, 1],
        small_grads[:, 2 + att_experts :],
        jnp.stack([grad_gate_w.astype(F32), grad_up_w.astype(F32)], axis=1),
        grad_down_w.astype(F32),
    )


def solution(mesh):
    placed = (
        P("dp", None),
        P("dp", None),
        P("dp", None),
        P("dp", None),
        P("dp", None),
        P("dp", None),
        P("dp"),
        P(None, "dp", "tensor"),
        P(None, "dp", "tensor"),
        P(None, "tensor", "dp"),
        P("dp", None),
        P("dp"),
        P("dp", None),
        P(None, None, "dp", "tensor"),
        P(None, "tensor", "dp"),
    )
    return jax.shard_map(
        functools.partial(on_device, mesh.shape["dp"], mesh.shape["tensor"]),
        mesh=mesh,
        in_specs=placed,
        out_specs=(
            P("dp", None),
            P("dp", None),
            P("dp"),
            P(None, "dp", "tensor"),
            P(None, "dp", "tensor"),
            P(None, "tensor", "dp"),
            P("dp", None),
            P("dp"),
            P("dp", None),
            P(None, None, "dp", "tensor"),
            P(None, "tensor", "dp"),
        ),
        check_vma=False,
    )
```

```python
import functools

import jax
import jax.numpy as jnp
from jax import lax
from jax.experimental import pallas as pl
from jax.experimental.pallas import tpu as pltpu
from jax.sharding import PartitionSpec as P

HD = 128
TOPK = 2
SEG = 128

EPSILON = 1e-06
NEGATIVE = -1e30
ROPE_BASE = 10000.0
F32 = jnp.float32
BF16 = jnp.bfloat16


def dot(a, b, out=F32):
    return jnp.dot(a, b, preferred_element_type=out)


def dot_tn(a, b, out=F32):
    return lax.dot_general(a, b, (((0,), (0,)), ((), ())), preferred_element_type=out)


def dot_nt(a, b, out=F32):
    return lax.dot_general(a, b, (((1,), (1,)), ((), ())), preferred_element_type=out)


def slot_places(routes, priority, capacity, experts):
    pair_total = routes.shape[0] * routes.shape[1]
    flat_routes = routes.reshape(pair_total)
    flat_order = priority.reshape(pair_total)
    same_expert = flat_routes[:, None] == flat_routes[None, :]
    earlier = flat_order[None, :] < flat_order[:, None]
    slot_rank = jnp.sum((same_expert & earlier).astype(jnp.int32), axis=1)
    slot_place = jnp.where(
        slot_rank < capacity, flat_routes * capacity + slot_rank, experts * capacity
    )
    return slot_place.reshape(routes.shape)


def slot_hits(place, slots):
    index = jnp.arange(slots, dtype=jnp.int32)[:, None]
    return [place[:, k][None, :] == index for k in range(place.shape[1])]


def ancestry(parent_row):
    segment_count = parent_row.shape[0]
    indices = jnp.arange(segment_count, dtype=jnp.int32)
    walker = indices
    inside = indices[:, None] == indices[None, :]
    for travel in range(segment_count):
        walker = parent_row[walker]
        inside = inside | (walker[:, None] == indices[None, :])
    depth = jnp.sum(inside.astype(jnp.int32), axis=1) - 1
    return (inside, depth)


def rope_tables(position):
    half_width = HD // 2
    frequency = ROPE_BASE ** (-jnp.arange(half_width, dtype=F32) / half_width)
    angles = position.astype(F32)[:, None] * frequency[None, :]
    cosine, sine = jnp.cos(angles), jnp.sin(angles)
    return (
        jnp.concatenate([cosine, cosine], axis=1),
        jnp.concatenate([-sine, sine], axis=1),
    )


def norm_forward(values_in):
    scale = lax.rsqrt(jnp.mean(values_in * values_in, axis=-1, keepdims=True) + EPSILON)
    return (values_in * scale, scale)


def norm_backward(grad_normed, normal, scale, gain):
    weighted = grad_normed * gain
    grad_in = scale * (weighted - normal * jnp.mean(weighted * normal, axis=-1, keepdims=True))
    return (grad_in, jnp.sum(grad_normed * normal, axis=0))


def router_backward(gates, products, picks, experts):
    grad_select = products - gates * jnp.sum(products, axis=1, keepdims=True)
    picked_hot = (picks[:, :, None] == jnp.arange(experts, dtype=jnp.int32)[None, None, :]).astype(
        F32
    )
    return jnp.sum(picked_hot * grad_select[:, :, None], axis=1).astype(BF16)


def with_column(rows, column):
    high = column.astype(BF16)
    rest = column - high.astype(F32)
    mid = rest.astype(BF16)
    low = (rest - mid.astype(F32)).astype(BF16)
    return jnp.concatenate(
        [rows, high, mid, low, jnp.zeros((rows.shape[0], HD - 3), BF16)], axis=1
    )


def without_column(both):
    width = both.shape[1] - HD
    parts = both[:, width : width + 3].astype(F32)
    return both[:, :width], parts[:, :1] + parts[:, 1:2] + parts[:, 2:]


def picked_softmax(logits, picks):
    experts = logits.shape[1]
    hot = picks[:, :, None] == jnp.arange(experts, dtype=jnp.int32)[None, None, :]
    return jax.nn.softmax(jnp.sum(jnp.where(hot, logits[:, None, :], 0.0), axis=2), axis=-1)


def rope(v, cosine, sine):
    return v * cosine + pltpu.roll(v, HD // 2, axis=1) * sine


def rope_back(v, cosine, sine):
    return v * cosine - pltpu.roll(v, HD // 2, axis=1) * sine


def softmax_block(q, k, bias):
    scores = dot_nt(q, k) * HD ** (-0.5) + bias
    exp_scores = jnp.exp(scores - jnp.max(scores, axis=-1, keepdims=True))
    return exp_scores / jnp.sum(exp_scores, axis=-1, keepdims=True)


def attend_kernel(
    rows, q_raw, k_raw, v_raw, bias, gate, slot_cos, slot_sin, tok_cos, tok_sin,
    q_out, k_out, v_out, att_out, gated_out,
):
    k_out[...] = rope(k_raw[...], tok_cos[...], tok_sin[...]).astype(BF16)
    v_out[...] = v_raw[...].astype(BF16)

    @pl.loop(0, q_raw.shape[0] // rows)
    def _(i):
        at = pl.ds(pl.multiple_of(i * rows, rows), rows)
        q = rope(q_raw[at, :], slot_cos[at, :], slot_sin[at, :]).astype(BF16)
        q_out[at, :] = q
        probs = softmax_block(q, k_out[...], bias[at, :].astype(F32)).astype(BF16)
        attended = dot(probs, v_out[...])
        att_out[at, :] = attended
        gated_out[at, :] = (attended * gate[at, :]).astype(BF16)


def attend(q_raw, keyval, bias, gate, slot_tables, tok_tables):
    slots, width = q_raw.shape
    tok = keyval.shape[0]
    heads = width // HD
    head = lambda h: (0, h)
    whole = lambda h: (0, 0)
    rows = 256
    return pl.pallas_call(
        functools.partial(attend_kernel, rows),
        grid=(heads,),
        in_specs=[
            pl.BlockSpec((slots, HD), head),
            pl.BlockSpec((tok, HD), head),
            pl.BlockSpec((tok, HD), lambda h: (0, heads + h)),
            pl.BlockSpec((slots, tok), whole),
            pl.BlockSpec((slots, 1), whole),
            pl.BlockSpec((slots, HD), whole),
            pl.BlockSpec((slots, HD), whole),
            pl.BlockSpec((tok, HD), whole),
            pl.BlockSpec((tok, HD), whole),
        ],
        out_specs=[
            pl.BlockSpec((slots, HD), head),
            pl.BlockSpec((tok, HD), head),
            pl.BlockSpec((tok, HD), head),
            pl.BlockSpec((slots, HD), head),
            pl.BlockSpec((slots, HD), head),
        ],
        out_shape=[
            jax.ShapeDtypeStruct((slots, width), BF16),
            jax.ShapeDtypeStruct((tok, width), BF16),
            jax.ShapeDtypeStruct((tok, width), BF16),
            jax.ShapeDtypeStruct((slots, width), F32),
            jax.ShapeDtypeStruct((slots, width), BF16),
        ],
        compiler_params=pltpu.CompilerParams(vmem_limit_bytes=40 << 20),
        cost_estimate=pl.CostEstimate(
            flops=4 * slots * tok * width,
            bytes_accessed=slots * width * 12 + slots * tok * 2,
            transcendentals=slots * tok * heads,
        ),
    )(q_raw, keyval, keyval, bias, gate, *slot_tables, *tok_tables)


def attend_back_kernel(
    rows, q_ref, k_ref, v_ref, bias, gate, slot_cos, slot_sin, tok_cos, tok_sin, grad_gated,
    gq_out, gk_out, gv_out, gk_sum, gv_sum,
):
    gk_sum[...] = jnp.zeros_like(gk_sum)
    gv_sum[...] = jnp.zeros_like(gv_sum)

    @pl.loop(0, q_ref.shape[0] // rows)
    def _(i):
        at = pl.ds(pl.multiple_of(i * rows, rows), rows)
        q = q_ref[at, :]
        probs = softmax_block(q, k_ref[...], bias[at, :].astype(F32))
        grad_att = (grad_gated[at, :] * gate[at, :]).astype(BF16)
        grad_probs = dot_nt(grad_att, v_ref[...])
        centre = jnp.sum(probs * grad_probs, axis=-1, keepdims=True)
        grad_scores = (probs * (grad_probs - centre)).astype(BF16)
        grad_q = dot(grad_scores, k_ref[...]) * HD ** (-0.5)
        gq_out[at, :] = rope_back(grad_q, slot_cos[at, :], slot_sin[at, :]).astype(BF16)
        gk_sum[...] += dot_tn(grad_scores, q)
        gv_sum[...] += dot_tn(probs.astype(BF16), grad_att)

    grad_k = gk_sum[...] * HD ** (-0.5)
    gk_out[...] = rope_back(grad_k, tok_cos[...], tok_sin[...]).astype(BF16)
    gv_out[...] = gv_sum[...].astype(BF16)


def attend_back(q, k, v, bias, gate, slot_tables, tok_tables, grad_gated):
    slots, width = q.shape
    tok = k.shape[0]
    heads = width // HD
    head = lambda h: (0, h)
    whole = lambda h: (0, 0)
    rows = 256
    return pl.pallas_call(
        functools.partial(attend_back_kernel, rows),
        grid=(heads,),
        in_specs=[
            pl.BlockSpec((slots, HD), head),
            pl.BlockSpec((tok, HD), head),
            pl.BlockSpec((tok, HD), head),
            pl.BlockSpec((slots, tok), whole),
            pl.BlockSpec((slots, 1), whole),
            pl.BlockSpec((slots, HD), whole),
            pl.BlockSpec((slots, HD), whole),
            pl.BlockSpec((tok, HD), whole),
            pl.BlockSpec((tok, HD), whole),
            pl.BlockSpec((slots, HD), head),
        ],
        out_specs=[
            pl.BlockSpec((slots, HD), head),
            pl.BlockSpec((tok, HD), head),
            pl.BlockSpec((tok, HD), head),
        ],
        out_shape=[
            jax.ShapeDtypeStruct((slots, width), BF16),
            jax.ShapeDtypeStruct((tok, width), BF16),
            jax.ShapeDtypeStruct((tok, width), BF16),
        ],
        scratch_shapes=[pltpu.VMEM((tok, HD), F32), pltpu.VMEM((tok, HD), F32)],
        compiler_params=pltpu.CompilerParams(vmem_limit_bytes=40 << 20),
        cost_estimate=pl.CostEstimate(
            flops=0, bytes_accessed=slots * width, transcendentals=0
        ),
    )(q, k, v, bias, gate, *slot_tables, *tok_tables, grad_gated)


class Square:
    def __init__(self):
        me = lax.axis_index("dp")
        self.core = lax.rem(me, 2)
        self.chip = me // 2
        x, y = lax.rem(self.chip, 2), self.chip // 2
        self.chip_x = self.chip + 1 - 2 * x
        self.chip_y = self.chip + 2 - 4 * y
        self.chip_far = 3 - self.chip
        self.twin = me + 1 - 2 * self.core
        self.near_x = 2 * self.chip_x + self.core
        self.near_y = 2 * self.chip_y + self.core


def send_to(source, target, send_sem, recv_sem, device):
    return pltpu.make_async_remote_copy(
        src_ref=source,
        dst_ref=target,
        send_sem=send_sem,
        recv_sem=recv_sem,
        device_id={"dp": device},
        device_id_type=pl.DeviceIdType.MESH,
    )


def greet(places):
    barrier = pltpu.get_barrier_semaphore()
    for place in places:
        pl.semaphore_signal(
            barrier, inc=1, device_id=place, device_id_type=pl.DeviceIdType.MESH
        )
    pl.semaphore_wait(barrier, len(places))


def send_across(source, target, send_sem, recv_sem, device):
    return pltpu.make_async_remote_copy(
        src_ref=source,
        dst_ref=target,
        send_sem=send_sem,
        recv_sem=recv_sem,
        device_id={"tensor": device},
        device_id_type=pl.DeviceIdType.MESH,
    )


def tensor_peers(count):
    z = lax.axis_index("tensor")
    return [lax.rem(z + k, count) for k in range(1, count)]


def share_rows(size):
    return pl.ds(pl.multiple_of(lax.axis_index("tensor") * size, size), size)


def rows_of(place, size):
    return pl.ds(pl.multiple_of(place * size, size), size)


def spread(count, source, target, sems):
    size = source.shape[0] // count
    copies = [
        send_to(
            source.at[pl.ds(k * size, size)], target.at[pl.ds(k * size, size)],
            sems[0].at[k], sems[1].at[k], partner(k),
        )
        for k in range(1, count)
    ]
    here = pltpu.make_async_copy(
        source.at[pl.ds(0, size)], target.at[pl.ds(0, size)], sems[0].at[0]
    )
    for copy in (*copies, here):
        copy.start()
    return (*copies, here)


def gather_kernel(axes, chunks, *refs):
    amount = len(axes)
    sources, rows = refs[:amount], refs[amount]
    targets, rows_out = refs[amount + 1 : 2 * amount + 1], refs[2 * amount + 1]
    send_sem, recv_sem, own_sem, e_send, e_recv, z_send, z_recv = refs[2 * amount + 2 :]
    count = z_send.shape[0] + 1
    exchange_count = e_send.shape[0]
    peers = tensor_peers(count)
    at = Square()
    me = 2 * at.chip + at.core
    far = 2 * at.chip_far + at.core
    greet(
        [{"dp": partner(k)} for k in range(1, exchange_count)] + [{"tensor": p} for p in peers]
    )
    columns = share_rows(rows.shape[1] // count)
    size = rows.shape[0] // exchange_count
    moved = [
        send_to(
            rows.at[pl.ds(k * size, size), columns], rows_out.at[pl.ds(k * size, size), columns],
            e_send.at[k], e_recv.at[k], partner(k),
        )
        for k in range(1, exchange_count)
    ]
    stay = pltpu.make_async_copy(
        rows.at[pl.ds(0, size), columns], rows_out.at[pl.ds(0, size), columns], e_send.at[0]
    )
    for copy in (*moved, stay):
        copy.start()

    def region(ref, axis, source, place, experts):
        size = source.shape[axis]
        at_place = pl.ds(pl.multiple_of(place * size, size), size)
        return ref.at[experts, at_place] if axis == 1 else ref.at[experts, :, at_place]

    first = 0
    plans = []
    for i in range(amount):
        count = sources[i].shape[0] // chunks[i]
        plans.append((i, first, count))
        first += count

    def copies(i, first, n):
        source, target, axis, size = sources[i], targets[i], axes[i], chunks[i]
        half = size // 2
        whole = pl.ds(n * size, size)
        top, bottom = pl.ds(n * size, half), pl.ds(n * size + half, half)
        unit = first + n

        def move(slot, place, experts, device, own=False):
            there = region(target, axis, source, place, experts)
            return send_to(
                source.at[experts] if own else there, there,
                send_sem.at[unit, slot], recv_sem.at[unit, slot], device,
            )

        return [
            functools.partial(move, 0, me, whole, at.near_x, True),
            functools.partial(move, 1, me, whole, at.near_y, True),
            functools.partial(move, 2, at.near_y, top, at.near_x),
            functools.partial(move, 3, at.near_x, bottom, at.near_y),
            functools.partial(move, 4, me, whole, at.twin, True),
            functools.partial(move, 5, at.near_x, whole, at.twin),
            functools.partial(move, 6, at.near_y, whole, at.twin),
            functools.partial(move, 7, far, top, at.twin),
            functools.partial(move, 8, far, bottom, at.twin),
        ]

    here = [
        pltpu.make_async_copy(
            sources[i], region(targets[i], axes[i], sources[i], me, pl.ds(0, sources[i].shape[0])),
            own_sem.at[i],
        )
        for i in range(amount)
    ]
    for i, first, count in plans:

        @pl.loop(0, count)
        def _(n):
            moves = copies(i, first, n)
            for slot in (0, 1, 4):
                moves[slot]().start()

    for copy in here:
        copy.start()
    for i, first, count in plans:

        @pl.loop(0, count)
        def _(n):
            moves = copies(i, first, n)
            moves[0]().wait_recv()
            moves[3]().start()
            moves[5]().start()
            moves[1]().wait_recv()
            moves[2]().start()
            moves[6]().start()

        if i == 0:
            stay.wait()
            for copy in moved:
                copy.wait_recv()
            across = [
                send_across(
                    rows_out.at[:, columns], rows_out.at[:, columns], z_send.at[k], z_recv.at[k], p
                )
                for k, p in enumerate(peers)
            ]
            for copy in across:
                copy.start()

    for i, first, count in plans:

        @pl.loop(0, count)
        def _(n):
            moves = copies(i, first, n)
            moves[2]().wait_recv()
            moves[7]().start()
            moves[3]().wait_recv()
            moves[8]().start()

    for i, first, count in plans:

        @pl.loop(0, count)
        def _(n):
            moves = copies(i, first, n)
            for slot in (4, 5, 6, 7, 8):
                moves[slot]().wait_recv()
            for move in moves:
                move().wait_send()

    for copy in (*here, *across):
        copy.wait()
    for copy in moved:
        copy.wait_send()


def gather_maps(tensor_size, peers, arrays, axes, chunks, rows):
    units = sum(a.shape[0] // c for a, c in zip(arrays, chunks))
    shapes = [
        tuple(n * 8 if d == axis else n for d, n in enumerate(a.shape))
        for a, axis in zip(arrays, axes)
    ]
    return pl.pallas_call(
        functools.partial(gather_kernel, axes, chunks),
        in_specs=[HBM] * (len(arrays) + 1),
        out_specs=[HBM] * (len(arrays) + 1),
        out_shape=[jax.ShapeDtypeStruct(shape, BF16) for shape in (*shapes, rows.shape)],
        scratch_shapes=[
            sems(units, 9), sems(units, 9), sems(len(arrays)), sems(peers), sems(peers),
            sems(tensor_size - 1), sems(tensor_size - 1),
        ],
        compiler_params=pltpu.CompilerParams(collective_id=5, has_side_effects=True),
        cost_estimate=pl.CostEstimate(flops=0, bytes_accessed=600 << 20, transcendentals=0),
    )(*arrays, rows)


def deal(source, target, sems):
    me = lax.axis_index("dp")
    copies = [
        send_to(
            source.at[partner(k)], target.at[me], sems[0].at[k], sems[1].at[k], partner(k)
        )
        for k in range(1, source.shape[0])
    ]
    copies.append(pltpu.make_async_copy(source.at[me], target.at[me], sems[0].at[0]))
    for copy in copies:
        copy.start()
    return copies


def norm_back(total, products, hots, router, base, gain, hot_out, gain_out):
    first, second = products
    weights = hots[0] * first + hots[1] * second - hots[2] * (first + second)
    hot_out[...] = weights.astype(BF16)
    total = total + dot_nt(hot_out[...], router[...])
    scale = lax.rsqrt(jnp.mean(base * base, axis=-1, keepdims=True) + EPSILON)
    normal = base * scale
    gain_out[...] = jnp.sum(total * normal, axis=0, keepdims=True)
    weighted = total * gain
    return scale * (weighted - normal * jnp.mean(weighted * normal, axis=-1, keepdims=True))


def three_columns(block):
    return block[:, 0:1] + block[:, 1:2] + block[:, 2:3]


def in_columns(column, lane):
    high = column.astype(BF16).astype(F32)
    mid = (column - high).astype(BF16).astype(F32)
    return jnp.where(
        lane == 0, high, jnp.where(lane == 1, mid, jnp.where(lane == 2, column - high - mid, 0.0))
    ).astype(BF16)


def hidden_kernel(
    pick, rows, x_here, gain, router, hot_0, hot_1, hit_0, hit_1, maps_hbm,
    hidden_out, mlp_in_out, gates_out, x_out, maps_out,
    parts, sent, got, z_send, z_recv, g_send, g_recv, d_send, d_recv,
):
    count = z_send.shape[0] + 1
    width = rows.shape[1]
    tokens = pick.shape[1]
    size = tokens // count
    peers = tensor_peers(count)
    greet(
        [{"dp": partner(k)} for k in range(1, d_send.shape[0])] + [{"tensor": p} for p in peers]
    )
    dealt = deal(maps_hbm, maps_out, (d_send, d_recv))

    @pl.loop(0, width // 512)
    def _(i):
        at = pl.ds(pl.multiple_of(i * 512, 512), 512)
        piece = dot_tn(pick[...], rows[:, at])
        parts[:, at] = piece
        sent[:, at] = piece.astype(BF16)

    copies = [
        send_across(sent.at[rows_of(p, size)], got.at[k], z_send.at[k], z_recv.at[k], p)
        for k, p in enumerate(peers)
    ]
    for copy in copies:
        copy.start()
    here = share_rows(size)
    hidden_out[...] = x_here[...].astype(F32) + parts[here, :]
    for k, copy in enumerate(copies):
        copy.wait_recv()
        hidden_out[...] += got[k].astype(F32)
    hidden = hidden_out[...]
    scale = lax.rsqrt(jnp.mean(hidden * hidden, axis=-1, keepdims=True) + EPSILON)
    mlp_in_out[here, :] = (hidden * scale * gain[...]).astype(BF16)
    more = [
        send_across(
            mlp_in_out.at[here], mlp_in_out.at[here], g_send.at[k], g_recv.at[k], p
        )
        for k, p in enumerate(peers)
    ]
    for copy in more:
        copy.start()
    for copy in copies:
        copy.wait_send()
    for copy in more:
        copy.wait()

    logits = dot(mlp_in_out[...], router[...])
    picked = [jnp.sum(logits * hot[...], axis=1, keepdims=True) for hot in (hot_0, hot_1)]
    highest = jnp.maximum(picked[0], picked[1])
    raised = [jnp.exp(value - highest) for value in picked]
    gates = [value / (raised[0] + raised[1]) for value in raised]
    lane = lax.broadcasted_iota(jnp.int32, (tokens, HD), 1)
    gates_out[...] = jnp.where(lane == 0, gates[0], jnp.where(lane == 1, gates[1], 0.0))
    columns = [in_columns(gate, lane) for gate in gates]
    x_out[:, width:] = (dot(hit_0[...], columns[0]) + dot(hit_1[...], columns[1])).astype(BF16)

    @pl.loop(0, width // 512)
    def _(i):
        at = pl.ds(pl.multiple_of(i * 512, 512), 512)
        x_out[:, at] = dot(hit_0[...] + hit_1[...], mlp_in_out[:, at]).astype(BF16)
    for copy in dealt:
        copy.wait()


VMEM = pl.BlockSpec(memory_space=pltpu.VMEM)
HBM = pl.BlockSpec(memory_space=pl.ANY)


def sems(*shape):
    return pltpu.SemaphoreType.DMA(shape)


def hidden_step(tensor_size, pick, rows, x_here, gain, router, hots, hits, maps):
    tokens, width = pick.shape[1], rows.shape[1]
    slots = hits[0].shape[0]
    size = tokens // tensor_size
    around = tensor_size - 1
    return pl.pallas_call(
        hidden_kernel,
        in_specs=[VMEM] * 9 + [HBM],
        out_specs=[VMEM] * 4 + [HBM],
        out_shape=[
            jax.ShapeDtypeStruct((size, width), F32),
            jax.ShapeDtypeStruct((tokens, width), BF16),
            jax.ShapeDtypeStruct((tokens, HD), F32),
            jax.ShapeDtypeStruct((slots, width + HD), BF16),
            jax.ShapeDtypeStruct(maps.shape, BF16),
        ],
        scratch_shapes=[
            pltpu.VMEM((tokens, width), F32),
            pltpu.VMEM((tokens, width), BF16),
            pltpu.VMEM((around, size, width), BF16),
            sems(around), sems(around), sems(around), sems(around),
            sems(maps.shape[0]), sems(maps.shape[0]),
        ],
        compiler_params=pltpu.CompilerParams(
            collective_id=3, has_side_effects=True, vmem_limit_bytes=48 << 20
        ),
        cost_estimate=pl.CostEstimate(
            flops=2 * pick.shape[0] * tokens * width, bytes_accessed=300 << 20, transcendentals=0
        ),
    )(pick, rows, x_here, gain, router, *hots, *hits, maps)


def back_kernel(
    back, pick, hit_0, hit_1, hidden, cot_here, gain, router, hots, gates, rows_hbm, gate_hbm, up_hbm,
    grad_out, pair_out, gain_out, hot_out, mixed_out, gate_maps, up_maps,
    parts, sent, got, z_send, z_recv, g_send, g_recv, e_send, e_recv, w_send, w_recv, u_send, u_recv,
    rows_in, columns_here, mlp_got, m_send, m_recv, own,
):
    count = z_send.shape[0] + 1
    width = back.shape[1] - HD
    tokens = pick.shape[1]
    size = tokens // count
    peers = tensor_peers(count)
    exchange_count = e_send.shape[0]
    greet(
        [{"dp": partner(k)} for k in range(1, exchange_count)] + [{"tensor": p} for p in peers]
    )
    moves = spread(exchange_count, rows_hbm, rows_in, (e_send, e_recv))
    dealt = deal(gate_hbm, gate_maps, (w_send, w_recv))
    dealt += deal(up_hbm, up_maps, (u_send, u_recv))

    @pl.loop(0, width // 512)
    def _(i):
        at = pl.ds(pl.multiple_of(i * 512, 512), 512)
        piece = dot_tn(pick[...], back[:, at])
        parts[:, at] = piece
        sent[:, at] = piece.astype(BF16)

    for k, hit in enumerate((hit_0, hit_1)):
        at = pl.ds(width + k * HD, HD)
        piece = dot_tn(hit[...], back[:, width:])
        parts[:, at] = piece
        sent[:, at] = piece.astype(BF16)

    copies = [
        send_across(sent.at[rows_of(p, size)], got.at[k], z_send.at[k], z_recv.at[k], p)
        for k, p in enumerate(peers)
    ]
    for copy in copies:
        copy.start()
    here = share_rows(size)
    total = parts[here, :]
    for k, copy in enumerate(copies):
        copy.wait_recv()
        total = total + got[k].astype(F32)
    products = (
        three_columns(total[:, width : width + HD]), three_columns(total[:, width + HD :])
    )
    grad_out[...] = cot_here[...].astype(F32) + norm_back(
        total[:, :width], products, hots, router, hidden[...], gain[...], hot_out, gain_out
    )
    pair_out[here, :] = grad_out[...].astype(BF16)
    more = [
        send_across(pair_out.at[here], pair_out.at[here], g_send.at[k], g_recv.at[k], p)
        for k, p in enumerate(peers)
    ]
    for copy in more:
        copy.start()
    for copy in moves:
        copy.wait()
    matrix = hit_0[...].astype(F32) * gates[0:1, :] + hit_1[...].astype(F32) * gates[1:2, :]
    high = matrix.astype(BF16)
    low = (matrix - high.astype(F32)).astype(BF16)
    columns_here[...] = (dot_tn(high, rows_in[...]) + dot_tn(low, rows_in[...])).astype(BF16)
    columns = share_rows(width // count)
    turned = [
        send_across(
            columns_here.at[rows_of(p, size)], mlp_got.at[:, columns], m_send.at[k], m_recv.at[k],
            p,
        )
        for k, p in enumerate(peers)
    ]
    turned.append(
        pltpu.make_async_copy(columns_here.at[here], mlp_got.at[:, columns], own.at[0])
    )
    for copy in turned:
        copy.start()
    for copy in turned:
        copy.wait()
    mixed_out[...] = (hidden[...] + mlp_got[...].astype(F32)).astype(BF16)
    for copy in copies:
        copy.wait_send()
    for copy in (*more, *dealt):
        copy.wait()


def back_step(
    tensor_size, peers, back, pick, hits, hidden, cot_here, gain, router, hots, gates,
    rows_send, gate_maps, up_maps,
):
    tokens, width = pick.shape[1], back.shape[1] - HD
    size = tokens // tensor_size
    around = tensor_size - 1
    wide = width + 2 * HD
    return pl.pallas_call(
        back_kernel,
        in_specs=[VMEM] * 10 + [HBM] * 3,
        out_specs=[VMEM] * 5 + [HBM] * 2,
        out_shape=[
            jax.ShapeDtypeStruct((size, width), F32),
            jax.ShapeDtypeStruct((tokens, width), BF16),
            jax.ShapeDtypeStruct((1, width), F32),
            jax.ShapeDtypeStruct((size, HD), BF16),
            jax.ShapeDtypeStruct((size, width), BF16),
            jax.ShapeDtypeStruct(gate_maps.shape, BF16),
            jax.ShapeDtypeStruct(up_maps.shape, BF16),
        ],
        scratch_shapes=[
            pltpu.VMEM((tokens, wide), F32),
            pltpu.VMEM((tokens, wide), BF16),
            pltpu.VMEM((around, size, wide), BF16),
            sems(around), sems(around), sems(around), sems(around), sems(peers), sems(peers),
            sems(peers), sems(peers), sems(peers), sems(peers),
            pltpu.VMEM(rows_send.shape, BF16),
            pltpu.VMEM((tokens, width // tensor_size), BF16),
            pltpu.VMEM((size, width), BF16),
            sems(around), sems(around), sems(1),
        ],
        compiler_params=pltpu.CompilerParams(
            collective_id=4, has_side_effects=True, vmem_limit_bytes=40 << 20
        ),
        cost_estimate=pl.CostEstimate(
            flops=2 * pick.shape[0] * tokens * width, bytes_accessed=300 << 20, transcendentals=0
        ),
    )(back, pick, hits[0], hits[1], hidden, cot_here, gain, router, hots, gates, rows_send, gate_maps, up_maps)


GIVE = 4
HALF_SMALL = 8


def final_kernel(
    routed_hbm, grad_q, normed, grad_kv, part_hbm,
    grad_hidden, x_here, gain, router, hots, small, mixed_here,
    out, tokens_out, small_out, mixed_out,
    give, keep, twin_in, far_in, near_in, routed, got_part, tokens_here,
    twin_send, twin_recv, far_send, far_recv, near_send, near_recv, load, own,
    p_send, p_recv, t_send, t_recv,
    hot_here, small_all, small_in, small_sum, small_got,
    s_send, s_recv, w_send, w_recv, a_send, a_recv,
):
    at = Square()
    experts = grad_q.shape[0]
    units, _, size, _ = keep.shape
    half = size // 2
    count = p_send.shape[0] + 1
    peers = tensor_peers(count)
    width = normed.shape[1]
    share = part_hbm.shape[0] // count

    def fetch(u):
        return pltpu.make_async_copy(
            routed_hbm.at[u], routed.at[lax.rem(u, 2)], load.at[lax.rem(u, 2)]
        )

    fetch(0).start()
    here = share_rows(share)
    mine = pltpu.make_async_copy(part_hbm.at[here], got_part.at[count - 1], own.at[0])
    mine.start()
    greet([{"dp": partner(k)} for k in range(1, 8)] + [{"tensor": p} for p in peers])
    part_copies = [
        send_across(part_hbm.at[rows_of(p, share)], got_part.at[k], p_send.at[k], p_recv.at[k], p)
        for k, p in enumerate(peers)
    ]
    mixed_copies = [
        send_across(mixed_here, mixed_out.at[here], a_send.at[k], a_recv.at[k], p)
        for k, p in enumerate(peers)
    ]
    mixed_copies.append(pltpu.make_async_copy(mixed_here, mixed_out.at[here], own.at[2]))
    for copy in (*part_copies, *mixed_copies):
        copy.start()

    def to_twin(u):
        slot = lax.rem(u, GIVE)
        return send_to(give.at[slot], twin_in.at[u], twin_send.at[slot], twin_recv.at[u], at.twin)

    def to_far(u):
        first = send_to(
            keep.at[u, at.chip_far, pl.ds(0, half)],
            far_in.at[u, 0], far_send.at[u, 0], far_recv.at[u, 0], at.near_x,
        )
        second = send_to(
            keep.at[u, at.chip_far, pl.ds(half, half)],
            far_in.at[u, 1], far_send.at[u, 1], far_recv.at[u, 1], at.near_y,
        )
        return first, second

    def to_near(u):
        first = send_to(
            keep.at[u, at.chip_x], near_in.at[u, 0], near_send.at[u, 0], near_recv.at[u, 0],
            at.near_x,
        )
        second = send_to(
            keep.at[u, at.chip_y], near_in.at[u, 1], near_send.at[u, 1], near_recv.at[u, 1],
            at.near_y,
        )
        return first, second

    def multiply(u, rows, grads):
        slot = lax.rem(u, GIVE)

        @pl.when(u >= GIVE)
        def _():
            to_twin(u - GIVE).wait_send()

        for chip in range(4):
            columns = rows_of(2 * chip + 1 - at.core, size)
            give[slot, chip] = dot_tn(rows[:, columns], grads[...]).astype(BF16)
        to_twin(u).start()
        for chip in range(4):
            columns = rows_of(2 * chip + at.core, size)
            keep[u, chip] = dot_tn(rows[:, columns], grads[...]).astype(BF16)

    def join_twin(u):
        to_twin(u).wait_recv()

        def add(chip):
            keep[u, chip] = (keep[u, chip].astype(F32) + twin_in[u, chip].astype(F32)).astype(BF16)

        add(at.chip_far)
        for copy in to_far(u):
            copy.start()
        add(at.chip_x)
        add(at.chip_y)
        add(at.chip)

    @pl.loop(0, experts)
    def _(u):
        fetch(u).wait()

        @pl.when(u < experts - 1)
        def _():
            fetch(u + 1).start()

        multiply(u, routed.at[lax.rem(u, 2)], grad_q.at[u])

        @pl.when(u > 0)
        def _():
            join_twin(u - 1)

    @pl.loop(experts, units)
    def _(u):
        multiply(u, normed, grad_kv.at[u - experts])
        join_twin(u - 1)

    join_twin(units - 1)

    mine.wait()
    total = got_part[count - 1].astype(F32)
    for k, copy in enumerate(part_copies):
        copy.wait_recv()
        total = total + got_part[k].astype(F32)
    products = (
        three_columns(total[:, width : width + HD]), three_columns(total[:, width + HD :])
    )
    tokens_here[...] = (
        grad_hidden[...]
        + norm_back(
            total[:, :width], products, hots, router, x_here[...].astype(F32), gain[...],
            hot_here, small_all.at[pl.ds(0, 1)],
        )
    ).astype(BF16)
    token_copies = [
        send_across(tokens_here, tokens_out.at[here], t_send.at[k], t_recv.at[k], p)
        for k, p in enumerate(peers)
    ]
    for copy in token_copies:
        copy.start()
    kept = pltpu.make_async_copy(tokens_here, tokens_out.at[here], own.at[1])
    kept.start()

    small_all[1:HALF_SMALL, :] = small[1:HALF_SMALL, :]
    small_all[HALF_SMALL : 2 * HALF_SMALL, :] = dot_tn(hot_here[...], normed[here, :])[:HALF_SMALL]
    small_all[2 * HALF_SMALL :, :] = small[HALF_SMALL:, :]

    def small_block(place):
        return small_all.at[:, rows_of(place, size)]

    small_copies = [
        send_to(
            small_block(partner(k)), small_in.at[k], s_send.at[k], s_recv.at[k], partner(k)
        )
        for k in range(1, 8)
    ]
    for copy in small_copies:
        copy.start()

    @pl.loop(0, units)
    def _(u):
        for copy in to_far(u):
            copy.wait_recv()
        top, bottom = pl.ds(0, half), pl.ds(half, half)
        keep[u, at.chip_y, top, :] = (
            keep[u, at.chip_y, top, :].astype(F32) + far_in[u, 0].astype(F32)
        ).astype(BF16)
        keep[u, at.chip_x, bottom, :] = (
            keep[u, at.chip_x, bottom, :].astype(F32) + far_in[u, 1].astype(F32)
        ).astype(BF16)
        for copy in to_near(u):
            copy.start()

    @pl.loop(0, units)
    def _(u):
        for copy in to_near(u):
            copy.wait_recv()
        out[u] = (
            keep[u, at.chip].astype(F32) + near_in[u, 0].astype(F32) + near_in[u, 1].astype(F32)
        ).astype(BF16)

    block = small_all[:, rows_of(2 * at.chip + at.core, size)]
    for k, copy in enumerate(small_copies):
        copy.wait_recv()
        block = block + small_in[k + 1]
    small_sum[...] = block
    last_copies = [
        send_across(small_sum, small_got.at[k], w_send.at[k], w_recv.at[k], p)
        for k, p in enumerate(peers)
    ]
    for copy in last_copies:
        copy.start()

    @pl.loop(units - GIVE, units)
    def _(u):
        to_twin(u).wait_send()

    @pl.loop(0, units)
    def _(u):
        for copy in (*to_far(u), *to_near(u)):
            copy.wait_send()

    for k, copy in enumerate(last_copies):
        copy.wait_recv()
        block = block + small_got[k]
    small_out[...] = block
    for copy in (*part_copies, *small_copies, *last_copies):
        copy.wait_send()
    for copy in (*token_copies, *mixed_copies, kept):
        copy.wait()


def final_step(
    tensor_size, routed, grad_q, normed, grad_kv, part, grad_hidden, x_here, gain,
    router, hots, small, mixed_here,
):
    experts, rows, width = routed.shape
    columns = grad_q.shape[2]
    units = experts + grad_kv.shape[0]
    size = width // 8
    tokens, wide = part.shape
    share = tokens // tensor_size
    around = tensor_size - 1
    return pl.pallas_call(
        final_kernel,
        in_specs=[HBM, VMEM, VMEM, VMEM, HBM] + [VMEM] * 7,
        out_specs=[VMEM, HBM, VMEM, HBM],
        out_shape=[
            jax.ShapeDtypeStruct((units, size, columns), BF16),
            jax.ShapeDtypeStruct((tokens, width), BF16),
            jax.ShapeDtypeStruct((3 * HALF_SMALL, size), F32),
            jax.ShapeDtypeStruct((tokens, width), BF16),
        ],
        scratch_shapes=[
            pltpu.VMEM((GIVE, 4, size, columns), BF16),
            pltpu.VMEM((units, 4, size, columns), BF16),
            pltpu.VMEM((units, 4, size, columns), BF16),
            pltpu.VMEM((units, 2, size // 2, columns), BF16),
            pltpu.VMEM((units, 2, size, columns), BF16),
            pltpu.VMEM((2, rows, width), BF16),
            pltpu.VMEM((tensor_size, share, wide), BF16),
            pltpu.VMEM((share, width), BF16),
            sems(GIVE), sems(units), sems(units, 2), sems(units, 2), sems(units, 2),
            sems(units, 2), sems(2), sems(3),
            sems(around), sems(around), sems(around), sems(around),
            pltpu.VMEM((share, HD), BF16),
            pltpu.VMEM((3 * HALF_SMALL, width), F32),
            pltpu.VMEM((8, 3 * HALF_SMALL, size), F32),
            pltpu.VMEM((3 * HALF_SMALL, size), F32),
            pltpu.VMEM((around, 3 * HALF_SMALL, size), F32),
            sems(8), sems(8), sems(around), sems(around), sems(around), sems(around),
        ],
        compiler_params=pltpu.CompilerParams(
            collective_id=1, has_side_effects=True, vmem_limit_bytes=60 << 20
        ),
        cost_estimate=pl.CostEstimate(flops=0, bytes_accessed=1 << 20, transcendentals=0),
    )(
        routed, grad_q, normed, grad_kv, part, grad_hidden, x_here, gain, router, hots, small,
        mixed_here,
    )


def widen_kernel(first, second, third, both_out, third_out):
    both_out[:, 0] = first[...].astype(F32)
    both_out[:, 1] = second[...].astype(F32)
    third_out[...] = third[...].astype(F32)


def widen(first, second, third):
    experts, rows, columns = first.shape
    narrow = pl.BlockSpec((1, rows, columns), lambda e: (e, 0, 0))
    turned = pl.BlockSpec((1,) + third.shape[1:], lambda e: (e, 0, 0))
    return pl.pallas_call(
        widen_kernel,
        grid=(experts,),
        in_specs=[narrow, narrow, turned],
        out_specs=[pl.BlockSpec((1, 2, rows, columns), lambda e: (e, 0, 0, 0)), turned],
        out_shape=[
            jax.ShapeDtypeStruct((experts, 2, rows, columns), F32),
            jax.ShapeDtypeStruct(third.shape, F32),
        ],
        compiler_params=pltpu.CompilerParams(vmem_limit_bytes=32 << 20),
        cost_estimate=pl.CostEstimate(
            flops=0, bytes_accessed=6 * (2 * first.size + third.size), transcendentals=0
        ),
    )(first, second, third)


def partner(k):
    me = lax.axis_index("dp")
    place = me
    for bit in (1, 2, 4):
        place = place + bit * lax.rem(k // bit, 2) * (1 - 2 * lax.rem(me // bit, 2))
    return place


def expert_kernel(
    x_hbm, cot_hbm, gate_up_hbm, down_hbm, rest_hbm,
    back_out, rows_out, grad_gate_hbm, grad_up_hbm, grad_down_hbm,
    x_all, g_all, w_gate, w_up, w_down, act, grads, back, product, stage_up, stage_down,
    rows_here, rows_got, x_send, x_recv, b_send, b_recv, load, up_sem, down_sem, r_send, r_recv,
):
    peers = x_send.shape[0]
    slots, wide = x_all.shape
    width = wide - HD
    hidden = w_gate.shape[1]
    size = slots // peers
    pair = 2 * size
    step = 256
    whole_steps = hidden // step
    tail = hidden - whole_steps * step

    per = width // peers
    first = down_hbm.shape[1]
    loads = [
        pltpu.make_async_copy(cot_hbm, g_all, load.at[0]),
        pltpu.make_async_copy(down_hbm, w_down.at[:, pl.ds(0, first)], load.at[1]),
        pltpu.make_async_copy(
            rest_hbm, w_down.at[:, pl.ds(first, hidden - first)], load.at[3 + 2 * peers]
        ),
        pltpu.make_async_copy(
            x_hbm.at[pl.ds(0, size)], x_all.at[pl.ds(0, size)], load.at[2 + 2 * peers]
        ),
    ]
    for j in range(peers):
        for g, target in enumerate((w_gate, w_up)):
            loads.append(
                pltpu.make_async_copy(
                    gate_up_hbm.at[j, g], target.at[pl.ds(j * per, per)], load.at[2 + 2 * j + g]
                )
            )
    for copy in loads:
        copy.start()

    around = tensor_peers(r_send.shape[0] + 1)
    share = width // (len(around) + 1)
    greet([{"dp": partner(k)} for k in range(1, peers)] + [{"tensor": p} for p in around])

    def block(k):
        return pl.ds(pl.multiple_of(k * size, size), size)

    def send_x(k):
        return send_to(
            x_hbm.at[block(k)], x_all.at[block(k)], x_send.at[k], x_recv.at[k], partner(k)
        )

    def send_back(k):
        return send_to(
            back.at[block(k)], back_out.at[block(k)], b_send.at[k], b_recv.at[k], partner(k)
        )

    for k in (1, 2, 4, 3, 5):
        send_x(k).start()
    for copy in loads:
        copy.wait()

    def send_rows(k, group):
        rows = rows_of(group, pair)
        return send_across(
            rows_here.at[rows, rows_of(around[k], share)], rows_got.at[k, rows],
            r_send.at[k, group], r_recv.at[k, group], around[k],
        )

    @pl.loop(0, peers // 2)
    def _(group):
        rows = pl.ds(pl.multiple_of(group * pair, pair), pair)

        @pl.when(group > 0)
        def _():
            send_x(2 * group).wait_recv()

        send_x(2 * group + 1).wait_recv()
        columns = x_all[rows, width:].astype(F32)
        gate_of_row = columns[:, 0:1] + columns[:, 1:2] + columns[:, 2:3]
        g_all[rows, :] = (g_all[rows, :].astype(F32) * gate_of_row).astype(BF16)
        product[...] = jnp.zeros_like(product)

        def chunk(start, amount):
            cols = pl.ds(start, amount)
            x = x_all[rows, 0:width]
            gate = dot(x, w_gate[:, cols])
            up = dot(x, w_up[:, cols])
            grad_act = jnp.zeros((pair, amount), F32)
            for j in range(peers):
                grad_act += dot_nt(g_all[rows, j * per : (j + 1) * per], w_down[j, cols, :])
            sigmoid = 1.0 / (1.0 + jnp.exp(-gate))
            silu = gate * sigmoid
            activated = (silu * up).astype(BF16)
            act[rows, cols] = activated
            both = activated.astype(F32) * grad_act
            for part in range(amount // HD):
                product[...] += both[:, part * HD : (part + 1) * HD]
            grads[rows, cols] = (
                grad_act * up * sigmoid * (1.0 + gate * (1.0 - sigmoid))
            ).astype(BF16)
            grads[rows, pl.ds(hidden + start, amount)] = (grad_act * silu).astype(BF16)

        @pl.loop(0, whole_steps)
        def _(i):
            chunk(pl.multiple_of(i * step, step), step)

        if tail:
            chunk(whole_steps * step, tail)

        @pl.loop(0, width // step)
        def _(i):
            at = pl.ds(pl.multiple_of(i * step, step), step)
            back[rows, at] = (
                dot_nt(grads[rows, 0:hidden], w_gate[at, :])
                + dot_nt(grads[rows, hidden:], w_up[at, :])
            ).astype(BF16)

        total = jnp.sum(product[...], axis=1, keepdims=True)
        back[rows, width:] = in_columns(
            total, lax.broadcasted_iota(jnp.int32, (pair, HD), 1)
        )

        @pl.when(group == 0)
        def _():
            send_x(6).start()
            send_x(7).start()
            back_out[0:size, :] = back[0:size, :]

        @pl.when(group > 0)
        def _():
            send_back(2 * group).start()

        send_back(2 * group + 1).start()
        for j in range(peers):
            rows_here[rows, j * per : (j + 1) * per] = dot(act[rows, :], w_down[j]).astype(BF16)
        for k in range(len(around)):
            send_rows(k, group).start()

    def store_up(j, slot):
        return (
            pltpu.make_async_copy(
                stage_up.at[slot, :, pl.ds(0, hidden)], grad_gate_hbm.at[j], up_sem.at[slot, 0]
            ),
            pltpu.make_async_copy(
                stage_up.at[slot, :, pl.ds(hidden, hidden)], grad_up_hbm.at[j], up_sem.at[slot, 1]
            ),
        )

    @pl.loop(0, peers)
    def _(j):
        slot = lax.rem(j, 2)

        @pl.when(j > 1)
        def _():
            for copy in store_up(j - 2, slot):
                copy.wait()

        at = pl.ds(pl.multiple_of(j * per, per), per)
        stage_up[slot] = dot_tn(x_all[:, at], grads[...]).astype(BF16)
        for copy in store_up(j, slot):
            copy.start()

    def store_down(start, amount, slot):
        return pltpu.make_async_copy(
            stage_down.at[slot, :, pl.ds(0, amount)],
            grad_down_hbm.at[:, pl.ds(start, amount)],
            down_sem.at[slot],
        )

    def down_piece(start, amount, slot):
        piece = dot_tn(act[:, pl.ds(start, amount)], g_all[...]).astype(BF16)
        for j in range(peers):
            stage_down[slot, j, 0:amount, :] = piece[:, j * per : (j + 1) * per]
        store_down(start, amount, slot).start()

    @pl.loop(0, whole_steps)
    def _(i):
        slot = lax.rem(i, 2)

        @pl.when(i > 1)
        def _():
            store_down(pl.multiple_of((i - 2) * step, step), step, slot).wait()

        down_piece(pl.multiple_of(i * step, step), step, slot)

    last = whole_steps - 1
    store_down((last - 1) * step, step, (last - 1) % 2).wait()
    if tail:
        down_piece(whole_steps * step, tail, (last - 1) % 2)
        store_down(whole_steps * step, tail, (last - 1) % 2).wait()
    store_down(last * step, step, last % 2).wait()
    for j in (peers - 2, peers - 1):
        for copy in store_up(j, j % 2):
            copy.wait()

    @pl.loop(0, peers // 2)
    def _(group):
        rows = rows_of(group, pair)
        total = rows_here[rows, share_rows(share)].astype(F32)
        for k in range(len(around)):
            send_rows(k, group).wait()
            total = total + rows_got[k, rows, :].astype(F32)
        rows_out[rows, :] = total.astype(BF16)

    for k in range(1, peers):
        send_x(k).wait_send()
        send_back(k).wait()


def expert_step(tensor_size, x_rows, cot_rows, up_slices, down_slices, down_rest):
    slots, wide = x_rows.shape
    width = wide - HD
    peers, hidden, per = down_slices.shape
    hidden += down_rest.shape[1]
    vmem = pl.BlockSpec(memory_space=pltpu.VMEM)
    hbm = pl.BlockSpec(memory_space=pl.ANY)
    step = 256
    return pl.pallas_call(
        expert_kernel,
        in_specs=[hbm] * 5,
        out_specs=[vmem, vmem, hbm, hbm, hbm],
        out_shape=[
            jax.ShapeDtypeStruct((slots, wide), BF16),
            jax.ShapeDtypeStruct((slots, width // tensor_size), BF16),
            jax.ShapeDtypeStruct((peers, per, hidden), BF16),
            jax.ShapeDtypeStruct((peers, per, hidden), BF16),
            jax.ShapeDtypeStruct((peers, hidden, per), BF16),
        ],
        scratch_shapes=[
            pltpu.VMEM((slots, wide), BF16),
            pltpu.VMEM((slots, width), BF16),
            pltpu.VMEM((width, hidden), BF16),
            pltpu.VMEM((width, hidden), BF16),
            pltpu.VMEM((peers, hidden, per), BF16),
            pltpu.VMEM((slots, hidden), BF16),
            pltpu.VMEM((slots, 2 * hidden), BF16),
            pltpu.VMEM((slots, wide), BF16),
            pltpu.VMEM((2 * slots // peers, HD), F32),
            pltpu.VMEM((2, per, 2 * hidden), BF16),
            pltpu.VMEM((2, peers, step, per), BF16),
            pltpu.VMEM((slots, width), BF16),
            pltpu.VMEM((tensor_size - 1, slots, width // tensor_size), BF16),
            pltpu.SemaphoreType.DMA((peers,)),
            pltpu.SemaphoreType.DMA((peers,)),
            pltpu.SemaphoreType.DMA((peers,)),
            pltpu.SemaphoreType.DMA((peers,)),
            sems(4 + 2 * peers), sems(2, 2), sems(2),
            sems(tensor_size - 1, peers // 2), sems(tensor_size - 1, peers // 2),
        ],
        compiler_params=pltpu.CompilerParams(
            collective_id=2, has_side_effects=True, vmem_limit_bytes=60 << 20
        ),
        cost_estimate=pl.CostEstimate(
            flops=18 * slots * width * hidden, bytes_accessed=300 << 20, transcendentals=0
        ),
    )(x_rows, cot_rows, up_slices, down_slices, down_rest)


class Movers:
    def __init__(self, dp, experts, tensor):
        self.dp, self.experts, self.tensor = dp, experts, tensor
        self.ratio = dp // experts
        self.groups = self.pairs = None
        if self.ratio > 1:
            self.groups = [[g * experts + e for e in range(experts)] for g in range(self.ratio)]
            self.pairs = [[g * experts + e for g in range(self.ratio)] for e in range(experts)]

    def swap(self, blocks):
        return lax.all_to_all(blocks, "dp", 0, 0, axis_index_groups=self.groups, tiled=True)

    def fetch(self, shards):
        mine = self.swap(shards)
        if self.ratio > 1:
            mine = lax.all_gather(mine, "dp", axis=0, axis_index_groups=self.pairs, tiled=True)
        return mine

    def give_back(self, slices):
        if self.ratio > 1:
            slices = lax.psum_scatter(
                slices, "dp", scatter_dimension=0, axis_index_groups=self.pairs, tiled=True
            )
        return self.swap(slices)

    def exchange(self, rows):
        size = rows.shape[0] // self.experts
        blocks = [rows[:size]]
        for k in range(1, self.experts):
            pairs = [(i, i ^ k) for i in range(self.dp)]
            blocks.append(lax.ppermute(rows[k * size : (k + 1) * size], "dp", pairs))
        return jnp.concatenate(blocks, axis=0)

    def across(self, block, k):
        return lax.ppermute(block, "tensor", [(i, i ^ k) for i in range(self.tensor)])

    def reduce_rows(self, part, dtype=BF16):
        z = lax.axis_index("tensor")
        size = part.shape[0] // self.tensor
        total = lax.dynamic_slice_in_dim(part, z * size, size, axis=0)
        sent = part.astype(dtype)
        for k in range(1, self.tensor):
            block = lax.dynamic_slice_in_dim(sent, (z ^ k) * size, size, axis=0)
            total = total + self.across(block, k).astype(F32)
        return total

    def gather_rows(self, rows):
        z = lax.axis_index("tensor")
        size = rows.shape[0]
        rows = rows.astype(BF16)
        full = jnp.zeros((size * self.tensor,) + rows.shape[1:], BF16)
        for k in range(self.tensor):
            block = rows if k == 0 else self.across(rows, k)
            full = lax.dynamic_update_slice_in_dim(full, block, (z ^ k) * size, axis=0)
        return full


def expert_plain(movers, expert_in, cot_rows, up_slices, down_slices):
    dp_size, hidden_here, per_dp = down_slices.shape
    model_width = dp_size * per_dp
    gate_full, up_full = (up_slices[:, g].reshape(model_width, hidden_here) for g in range(2))
    down_full = down_slices.transpose(1, 0, 2).reshape(hidden_here, model_width)
    x_rows, gate_of_row = without_column(movers.exchange(expert_in))
    g_rows = (cot_rows.astype(F32) * gate_of_row).astype(BF16)
    gate = dot(x_rows, gate_full)
    up = dot(x_rows, up_full)
    sigmoid_gate = jax.nn.sigmoid(gate)
    silu_gate = gate * sigmoid_gate
    activated = (silu_gate * up).astype(BF16)
    grad_act = dot_nt(g_rows, down_full)
    grad_gate = (grad_act * up * sigmoid_gate * (1.0 + gate * (1.0 - sigmoid_gate))).astype(BF16)
    grad_up = (grad_act * silu_gate).astype(BF16)
    gate_times_grad = jnp.sum(activated.astype(F32) * grad_act, axis=1, keepdims=True)
    grad_expert_in = with_column(
        (dot_nt(grad_gate, gate_full) + dot_nt(grad_up, up_full)).astype(BF16), gate_times_grad
    )
    return (
        movers.exchange(grad_expert_in),
        dot(activated, down_full, BF16),
        dot_tn(x_rows, grad_gate, BF16).reshape(dp_size, per_dp, -1),
        dot_tn(x_rows, grad_up, BF16).reshape(dp_size, per_dp, -1),
        dot_tn(activated, g_rows, BF16).reshape(-1, dp_size, per_dp).transpose(1, 0, 2),
    )


def on_device(
    dp_size,
    tensor_size,
    tokens,
    cotangent,
    parents,
    attention_routes,
    expert_routes,
    slot_order,
    gain_attention,
    keyval_weight,
    query_weight,
    output_weight,
    attention_router,
    gain_feedforward,
    expert_router,
    gate_up_weight,
    down_weight,
):
    tok_count, model_width = tokens.shape
    pair_count = TOPK * tok_count
    att_experts = query_weight.shape[0]
    mlp_experts = gate_up_weight.shape[0]
    att_cap = tok_count * 5 // 16
    mlp_cap = pair_count // mlp_experts
    att_slots = att_experts * att_cap
    mlp_slots = mlp_experts * mlp_cap
    width_here = query_weight.shape[2]
    rows_here = tok_count // tensor_size
    movers = Movers(dp_size, mlp_experts, tensor_size)
    fast = dp_size == 8 and mlp_experts == 8
    tie = lax.optimization_barrier

    small = jnp.concatenate(
        [gain_attention[:, None], gain_feedforward[:, None], attention_router, expert_router], axis=1
    )
    small_full = lax.all_gather(small, "dp", axis=0, tiled=True)
    small_full, down_weight = tie((small_full, down_weight))
    gain_attn_full = small_full[:, 0].astype(F32)
    gain_mlp_full = small_full[:, 1].astype(F32)
    router_att = small_full[:, 2 : 2 + att_experts]
    router_mlp = small_full[:, 2 + att_experts :]

    inside, depth = ancestry(parents[0])
    token_index = jnp.arange(tok_count, dtype=jnp.int32)
    pair_order = jnp.arange(pair_count, dtype=jnp.int32).reshape(tok_count, TOPK)
    att_hits = slot_hits(
        slot_places(attention_routes, pair_order, att_cap, att_experts), att_slots
    )
    priority = slot_order[0][:, None] * TOPK + jnp.arange(TOPK, dtype=jnp.int32)[None, :]
    home = lax.rem(lax.axis_index("dp"), mlp_experts)
    mlp_hits = slot_hits(
        slot_places(expert_routes ^ home, priority, mlp_cap, mlp_experts), mlp_slots
    )
    att_pick = (att_hits[0] | att_hits[1]).astype(BF16)
    mlp_pick = (mlp_hits[0] | mlp_hits[1]).astype(BF16)

    def to_slots(hits, pair_values):
        return jnp.sum(
            sum(jnp.where(hits[k], pair_values[:, k][None, :], 0) for k in range(TOPK)), axis=1
        )

    def to_pairs(hits, slot_values):
        return jnp.stack(
            [jnp.sum(jnp.where(hits[k], slot_values[:, None], 0.0), axis=0) for k in range(TOPK)],
            axis=1,
        )

    def position_of(token):
        segment = token // SEG
        level = jnp.sum(
            jnp.where(segment[:, None] == jnp.arange(depth.shape[0])[None, :], depth[None, :], 0),
            axis=1,
        )
        return level * SEG + token % SEG

    pair_token = jnp.broadcast_to(token_index[:, None], (tok_count, TOPK))
    slot_token = to_slots(att_hits, pair_token)
    slot_filled = jnp.any(att_hits[0] | att_hits[1], axis=1)
    slot_tables = rope_tables(position_of(slot_token))
    tok_tables = rope_tables(position_of(token_index))
    segment_hot = (
        (slot_token // SEG)[:, None] == jnp.arange(inside.shape[0], dtype=jnp.int32)[None, :]
    ).astype(F32)
    reach = dot(segment_hot, jnp.repeat(inside.astype(F32), SEG, axis=1)) > 0.5
    allowed = reach & (token_index[None, :] <= slot_token[:, None]) & slot_filled[:, None]
    bias = jnp.where(allowed, 0.0, NEGATIVE).astype(BF16)

    early = down_weight.shape[1] // 2 if fast else down_weight.shape[1]
    down_slices = movers.fetch(down_weight[:, :early])
    cot_send = dot(mlp_pick, cotangent, BF16)

    inputs = tokens.astype(F32)
    normal_attn, scale_attn = norm_forward(inputs)
    normed = (normal_attn * gain_attn_full).astype(BF16)
    att_gates = picked_softmax(dot(normed, router_att), attention_routes)
    att_gate_slots = to_slots(att_hits, att_gates)[:, None]
    routed = dot(att_pick, normed, BF16).reshape(att_experts, att_cap, model_width)
    if fast:
        mlp_bits = tuple(hit.astype(BF16) for hit in mlp_hits)
        expert_lanes = [
            (expert_routes[:, k : k + 1] == jnp.arange(HD, dtype=jnp.int32)[None, :]).astype(F32)
            for k in range(TOPK)
        ]
        keyval_weight, query_weight, output_weight, *before = tie(
            (keyval_weight, query_weight, output_weight, routed, cot_send, bias, att_gate_slots)
            + slot_tables + tok_tables + mlp_bits + tuple(expert_lanes)
        )
        routed, cot_send, bias, att_gate_slots = before[:4]
        slot_tables, tok_tables = before[4:6], before[6:8]
        mlp_bits, expert_lanes = before[8:10], before[10:12]
        keyval_full, query_full, output_full, cot_rows = gather_maps(
            tensor_size, mlp_experts,
            (keyval_weight, query_weight, output_weight), (1, 1, 2), (2, 2, 2), cot_send,
        )
    else:
        keyval_full = lax.all_gather(keyval_weight, "dp", axis=1, tiled=True)
        query_full = lax.all_gather(query_weight, "dp", axis=1, tiled=True)
        output_full = lax.all_gather(output_weight, "dp", axis=2, tiled=True)
    query_full, keyval_full, down_slices, gate_up_weight = tie(
        (query_full, keyval_full, down_slices, gate_up_weight)
    )
    up_slices = movers.fetch(gate_up_weight)
    keyval = jnp.concatenate([dot(normed, keyval_full[0]), dot(normed, keyval_full[1])], axis=1)
    query_raw = jnp.einsum(
        "ecd,edf->ecf", routed, query_full, preferred_element_type=F32
    ).reshape(att_slots, width_here)
    queries, key_rows, values, attended, gated = attend(
        query_raw, keyval, bias, att_gate_slots, slot_tables, tok_tables
    )
    gated_slots = gated.reshape(att_experts, att_cap, width_here)
    att_rows = jnp.einsum(
        "ecf,efd->ecd", gated_slots, output_full, preferred_element_type=F32
    ).reshape(att_slots, model_width)
    att_rows = att_rows.astype(BF16)

    z = lax.axis_index("tensor")

    def share(rows):
        return lax.dynamic_slice_in_dim(rows, z * rows_here, rows_here, axis=0)

    def hots(gates, picks, experts):
        lanes = jnp.arange(HD, dtype=jnp.int32)[None, :]
        hot = [(share(picks)[:, k : k + 1] == lanes).astype(F32) for k in range(TOPK)]
        return jnp.stack(hot + [sum(hot[k] * share(gates)[:, k : k + 1] for k in range(TOPK))])

    def padded(router):
        return jnp.pad(router, ((0, 0), (0, HD - router.shape[1])))

    if fast:
        hidden, mlp_in, mlp_gates, expert_in, down_rest = hidden_step(
            tensor_size, att_pick, att_rows, share(tokens), gain_mlp_full[None],
            padded(router_mlp), expert_lanes, mlp_bits, down_weight[:, early:],
        )
        mlp_gates = mlp_gates[:, :TOPK]
    else:
        hidden = share(inputs) + movers.reduce_rows(dot_tn(att_pick, att_rows))
        mlp_in = movers.gather_rows((norm_forward(hidden)[0] * gain_mlp_full).astype(BF16))
        cot_rows = movers.exchange(cot_send)
        mlp_gates = picked_softmax(dot(mlp_in, router_mlp), expert_routes)
        expert_in = with_column(
            dot(mlp_pick, mlp_in, BF16), to_slots(mlp_hits, mlp_gates)[:, None]
        )
    expert_in, up_slices = tie((expert_in, up_slices))

    if fast:
        back = expert_step(
            tensor_size, expert_in, cot_rows, up_slices, down_slices, down_rest
        )
    else:
        back = expert_plain(movers, expert_in, cot_rows, up_slices, down_slices)
    grad_in_slots, expert_out, grad_gate_w, grad_up_w, grad_down_w = back

    if fast:
        (
            grad_hidden, grad_att_pair, grad_gain_mlp, grad_mlp_logits, mixed, grad_gate_w,
            grad_up_w,
        ) = back_step(
            tensor_size, mlp_experts, grad_in_slots, mlp_pick,
            mlp_bits, hidden, share(cotangent),
            gain_mlp_full[None], padded(router_mlp),
            hots(mlp_gates, expert_routes, mlp_experts), mlp_gates.T, expert_out, grad_gate_w, grad_up_w,
        )
        grad_gain_mlp = grad_gain_mlp[0]
        grad_mlp_logits = grad_mlp_logits[:, :mlp_experts]
    else:
        out_slots = movers.exchange(expert_out)
        grad_gate_w = movers.give_back(grad_gate_w)
        grad_up_w = movers.give_back(grad_up_w)
        grad_in_slots, gate_times_grad = without_column(grad_in_slots)
        mlp_products = movers.reduce_rows(to_pairs(mlp_hits, gate_times_grad[:, 0]), F32)
        grad_mlp_in = movers.reduce_rows(dot_tn(mlp_pick, grad_in_slots))
        grad_mlp_logits = router_backward(
            share(mlp_gates), mlp_products, share(expert_routes), mlp_experts
        )
        grad_mlp_in = grad_mlp_in + dot_nt(grad_mlp_logits, router_mlp)
        normal_mlp, scale_mlp = norm_forward(hidden)
        grad_hidden_norm, grad_gain_mlp = norm_backward(
            grad_mlp_in, normal_mlp, scale_mlp, gain_mlp_full
        )
        grad_hidden = share(cotangent).astype(F32) + grad_hidden_norm
        grad_att_pair = movers.gather_rows(grad_hidden)
        gate_matrix = sum(
            jnp.where(mlp_hits[k], mlp_gates[:, k][None, :], 0.0) for k in range(TOPK)
        )
        matrix_high = gate_matrix.astype(BF16)
        matrix_low = (gate_matrix - matrix_high.astype(F32)).astype(BF16)
        mlp_part = (dot_tn(matrix_high, out_slots) + dot_tn(matrix_low, out_slots)).astype(BF16)
        mixed = movers.gather_rows(hidden + movers.reduce_rows(mlp_part))
    grad_router_mlp = dot_tn(share(mlp_in), grad_mlp_logits)

    grad_att_pair, grad_down_w = tie((grad_att_pair, grad_down_w))
    grad_down_w = movers.give_back(grad_down_w)

    grad_att_rows = dot(att_pick, grad_att_pair, BF16).reshape(att_experts, att_cap, model_width)
    grad_output_w = jnp.einsum(
        "ecf,ecd->efd", gated_slots, grad_att_rows, preferred_element_type=BF16
    )
    grad_att_rows, grad_output_w = tie((grad_att_rows, grad_output_w))
    grad_gated = jnp.einsum(
        "ecd,efd->ecf", grad_att_rows, output_full, preferred_element_type=F32
    ).reshape(att_slots, width_here)
    grad_output_out = lax.psum_scatter(grad_output_w, "dp", scatter_dimension=2, tiled=True)
    att_products = to_pairs(
        att_hits, jnp.sum(grad_gated * attended, axis=1) * att_gate_slots[:, 0]
    )
    grad_q, grad_k, grad_v = attend_back(
        queries, key_rows, values, bias, att_gate_slots, slot_tables, tok_tables, grad_gated
    )
    grad_query_slots = grad_q.reshape(att_experts, att_cap, width_here)
    grad_routed = jnp.einsum(
        "ecf,edf->ecd", grad_query_slots, query_full, preferred_element_type=F32
    ).reshape(att_slots, model_width)
    normed_part = (
        dot_tn(att_pick, grad_routed.astype(BF16))
        + dot_nt(grad_k, keyval_full[0])
        + dot_nt(grad_v, keyval_full[1])
    )
    normed_part = with_column(normed_part.astype(BF16), att_products[:, :1])
    normed_part = with_column(normed_part, att_products[:, 1:])
    grad_kv = jnp.stack([grad_k, grad_v])
    if fast:
        small = jnp.concatenate(
            [
                jnp.zeros((1, model_width), F32),
                grad_gain_mlp[None],
                jnp.zeros((HALF_SMALL - 2, model_width), F32),
                grad_router_mlp.T,
            ],
            axis=0,
        )
        map_sums, grad_tokens, small_grads, mixed = final_step(
            tensor_size, routed, grad_query_slots, normed, grad_kv, normed_part,
            grad_hidden, share(tokens), gain_attn_full[None], padded(router_att),
            hots(att_gates, attention_routes, att_experts), small, mixed,
        )
        small_grads = jnp.concatenate([small_grads[:2], small_grads[HALF_SMALL:]], axis=0).T
        grad_query_out, grad_keyval_out = map_sums[:att_experts], map_sums[att_experts:]
    else:
        grad_query_w = jnp.einsum(
            "ecd,ecf->edf", routed, grad_query_slots, preferred_element_type=BF16
        )
        grad_keyval_w = jnp.stack([dot_tn(normed, grad, BF16) for grad in (grad_k, grad_v)])
        grad_query_out = lax.psum_scatter(grad_query_w, "dp", scatter_dimension=1, tiled=True)
        grad_keyval_out = lax.psum_scatter(grad_keyval_w, "dp", scatter_dimension=1, tiled=True)
        grad_normed = movers.reduce_rows(normed_part[:, :model_width])
        grad_att_logits = router_backward(
            share(att_gates), movers.reduce_rows(att_products, F32), share(attention_routes),
            att_experts,
        )
        grad_normed = grad_normed + dot_nt(grad_att_logits, router_att)
        grad_input_norm, grad_gain_attn = norm_backward(
            grad_normed, share(normal_attn), share(scale_attn), gain_attn_full
        )
        grad_tokens = movers.gather_rows(grad_hidden + grad_input_norm)
        grad_router_att = dot_tn(share(normed), grad_att_logits)
        small_grads = jnp.concatenate(
            [grad_gain_attn[:, None], grad_gain_mlp[:, None], grad_router_att, grad_router_mlp],
            axis=1,
        )
        small_grads = lax.psum(
            lax.psum_scatter(small_grads, "dp", scatter_dimension=0, tiled=True), "tensor"
        )
    grad_tokens, grad_output_out, grad_down_w = tie((grad_tokens, grad_output_out, grad_down_w))
    grad_tokens = grad_tokens.astype(F32)
    grad_up_w, grad_down_w = widen(grad_gate_w, grad_up_w, grad_down_w)
    return (
        mixed,
        grad_tokens,
        small_grads[:, 0],
        grad_keyval_out.astype(F32),
        grad_query_out.astype(F32),
        grad_output_out.astype(F32),
        small_grads[:, 2 : 2 + att_experts],
        small_grads[:, 1],
        small_grads[:, 2 + att_experts :],
        grad_up_w,
        grad_down_w,
    )


def solution(mesh):
    placed = (
        P("dp", None),
        P("dp", None),
        P("dp", None),
        P("dp", None),
        P("dp", None),
        P("dp", None),
        P("dp"),
        P(None, "dp", "tensor"),
        P(None, "dp", "tensor"),
        P(None, "tensor", "dp"),
        P("dp", None),
        P("dp"),
        P("dp", None),
        P(None, None, "dp", "tensor"),
        P(None, "tensor", "dp"),
    )
    return jax.shard_map(
        functools.partial(on_device, mesh.shape["dp"], mesh.shape["tensor"]),
        mesh=mesh,
        in_specs=placed,
        out_specs=(
            P("dp", None),
            P("dp", None),
            P("dp"),
            P(None, "dp", "tensor"),
            P(None, "dp", "tensor"),
            P(None, "tensor", "dp"),
            P("dp", None),
            P("dp"),
            P("dp", None),
            P(None, None, "dp", "tensor"),
            P(None, "tensor", "dp"),
        ),
        check_vma=False,
    )
```

```python
import functools

import jax
import jax.numpy as jnp
from jax import lax
from jax.experimental import pallas as pl
from jax.experimental.pallas import tpu as pltpu
from jax.sharding import PartitionSpec as P

HD = 128
TOPK = 2
SEG = 128

EPSILON = 1e-06
NEGATIVE = -1e30
ROPE_BASE = 10000.0
F32 = jnp.float32
BF16 = jnp.bfloat16


def dot(a, b, out=F32):
    return jnp.dot(a, b, preferred_element_type=out)


def dot_tn(a, b, out=F32):
    return lax.dot_general(a, b, (((0,), (0,)), ((), ())), preferred_element_type=out)


def dot_nt(a, b, out=F32):
    return lax.dot_general(a, b, (((1,), (1,)), ((), ())), preferred_element_type=out)


def slot_places(routes, priority, capacity, experts):
    pair_total = routes.shape[0] * routes.shape[1]
    flat_routes = routes.reshape(pair_total)
    flat_order = priority.reshape(pair_total)
    same_expert = flat_routes[:, None] == flat_routes[None, :]
    earlier = flat_order[None, :] < flat_order[:, None]
    slot_rank = jnp.sum((same_expert & earlier).astype(jnp.int32), axis=1)
    slot_place = jnp.where(
        slot_rank < capacity, flat_routes * capacity + slot_rank, experts * capacity
    )
    return slot_place.reshape(routes.shape)


def slot_hits(place, slots):
    index = jnp.arange(slots, dtype=jnp.int32)[:, None]
    return [place[:, k][None, :] == index for k in range(place.shape[1])]


def ancestry(parent_row):
    segment_count = parent_row.shape[0]
    indices = jnp.arange(segment_count, dtype=jnp.int32)
    walker = indices
    inside = indices[:, None] == indices[None, :]
    for travel in range(segment_count):
        walker = parent_row[walker]
        inside = inside | (walker[:, None] == indices[None, :])
    depth = jnp.sum(inside.astype(jnp.int32), axis=1) - 1
    return (inside, depth)


def rope_tables(position):
    half_width = HD // 2
    frequency = ROPE_BASE ** (-jnp.arange(half_width, dtype=F32) / half_width)
    angles = position.astype(F32)[:, None] * frequency[None, :]
    cosine, sine = jnp.cos(angles), jnp.sin(angles)
    return (
        jnp.concatenate([cosine, cosine], axis=1),
        jnp.concatenate([-sine, sine], axis=1),
    )


def norm_forward(values_in):
    scale = lax.rsqrt(jnp.mean(values_in * values_in, axis=-1, keepdims=True) + EPSILON)
    return (values_in * scale, scale)


def norm_backward(grad_normed, normal, scale, gain):
    weighted = grad_normed * gain
    grad_in = scale * (weighted - normal * jnp.mean(weighted * normal, axis=-1, keepdims=True))
    return (grad_in, jnp.sum(grad_normed * normal, axis=0))


def router_backward(gates, products, picks, experts):
    grad_select = products - gates * jnp.sum(products, axis=1, keepdims=True)
    picked_hot = (picks[:, :, None] == jnp.arange(experts, dtype=jnp.int32)[None, None, :]).astype(
        F32
    )
    return jnp.sum(picked_hot * grad_select[:, :, None], axis=1).astype(BF16)


def with_column(rows, column):
    high = column.astype(BF16)
    rest = column - high.astype(F32)
    mid = rest.astype(BF16)
    low = (rest - mid.astype(F32)).astype(BF16)
    return jnp.concatenate(
        [rows, high, mid, low, jnp.zeros((rows.shape[0], HD - 3), BF16)], axis=1
    )


def without_column(both):
    width = both.shape[1] - HD
    parts = both[:, width : width + 3].astype(F32)
    return both[:, :width], parts[:, :1] + parts[:, 1:2] + parts[:, 2:]


def picked_softmax(logits, picks):
    experts = logits.shape[1]
    hot = picks[:, :, None] == jnp.arange(experts, dtype=jnp.int32)[None, None, :]
    return jax.nn.softmax(jnp.sum(jnp.where(hot, logits[:, None, :], 0.0), axis=2), axis=-1)


def rope(v, cosine, sine):
    return v * cosine + pltpu.roll(v, HD // 2, axis=1) * sine


def rope_back(v, cosine, sine):
    return v * cosine - pltpu.roll(v, HD // 2, axis=1) * sine


def softmax_block(q, k, bias):
    scores = dot_nt(q, k) * HD ** (-0.5) + bias
    exp_scores = jnp.exp(scores - jnp.max(scores, axis=-1, keepdims=True))
    return exp_scores / jnp.sum(exp_scores, axis=-1, keepdims=True)


def attend_kernel(
    rows, q_raw, k_raw, v_raw, bias, gate, slot_cos, slot_sin, tok_cos, tok_sin,
    q_out, k_out, v_out, att_out, gated_out,
):
    k_out[...] = rope(k_raw[...], tok_cos[...], tok_sin[...]).astype(BF16)
    v_out[...] = v_raw[...].astype(BF16)

    @pl.loop(0, q_raw.shape[0] // rows)
    def _(i):
        at = pl.ds(pl.multiple_of(i * rows, rows), rows)
        q = rope(q_raw[at, :], slot_cos[at, :], slot_sin[at, :]).astype(BF16)
        q_out[at, :] = q
        probs = softmax_block(q, k_out[...], bias[at, :].astype(F32)).astype(BF16)
        attended = dot(probs, v_out[...])
        att_out[at, :] = attended
        gated_out[at, :] = (attended * gate[at, :]).astype(BF16)


def attend(q_raw, keyval, bias, gate, slot_tables, tok_tables):
    slots, width = q_raw.shape
    tok = keyval.shape[0]
    heads = width // HD
    head = lambda h: (0, h)
    whole = lambda h: (0, 0)
    rows = 256
    return pl.pallas_call(
        functools.partial(attend_kernel, rows),
        grid=(heads,),
        in_specs=[
            pl.BlockSpec((slots, HD), head),
            pl.BlockSpec((tok, HD), head),
            pl.BlockSpec((tok, HD), lambda h: (0, heads + h)),
            pl.BlockSpec((slots, tok), whole),
            pl.BlockSpec((slots, 1), whole),
            pl.BlockSpec((slots, HD), whole),
            pl.BlockSpec((slots, HD), whole),
            pl.BlockSpec((tok, HD), whole),
            pl.BlockSpec((tok, HD), whole),
        ],
        out_specs=[
            pl.BlockSpec((slots, HD), head),
            pl.BlockSpec((tok, HD), head),
            pl.BlockSpec((tok, HD), head),
            pl.BlockSpec((slots, HD), head),
            pl.BlockSpec((slots, HD), head),
        ],
        out_shape=[
            jax.ShapeDtypeStruct((slots, width), BF16),
            jax.ShapeDtypeStruct((tok, width), BF16),
            jax.ShapeDtypeStruct((tok, width), BF16),
            jax.ShapeDtypeStruct((slots, width), F32),
            jax.ShapeDtypeStruct((slots, width), BF16),
        ],
        compiler_params=pltpu.CompilerParams(vmem_limit_bytes=40 << 20),
        cost_estimate=pl.CostEstimate(
            flops=4 * slots * tok * width,
            bytes_accessed=slots * width * 12 + slots * tok * 2,
            transcendentals=slots * tok * heads,
        ),
    )(q_raw, keyval, keyval, bias, gate, *slot_tables, *tok_tables)


def attend_back_kernel(
    rows, q_ref, k_ref, v_ref, bias, gate, slot_cos, slot_sin, tok_cos, tok_sin, grad_gated,
    gq_out, gk_out, gv_out, gk_sum, gv_sum,
):
    gk_sum[...] = jnp.zeros_like(gk_sum)
    gv_sum[...] = jnp.zeros_like(gv_sum)

    @pl.loop(0, q_ref.shape[0] // rows)
    def _(i):
        at = pl.ds(pl.multiple_of(i * rows, rows), rows)
        q = q_ref[at, :]
        probs = softmax_block(q, k_ref[...], bias[at, :].astype(F32))
        grad_att = (grad_gated[at, :] * gate[at, :]).astype(BF16)
        grad_probs = dot_nt(grad_att, v_ref[...])
        centre = jnp.sum(probs * grad_probs, axis=-1, keepdims=True)
        grad_scores = (probs * (grad_probs - centre)).astype(BF16)
        grad_q = dot(grad_scores, k_ref[...]) * HD ** (-0.5)
        gq_out[at, :] = rope_back(grad_q, slot_cos[at, :], slot_sin[at, :]).astype(BF16)
        gk_sum[...] += dot_tn(grad_scores, q)
        gv_sum[...] += dot_tn(probs.astype(BF16), grad_att)

    grad_k = gk_sum[...] * HD ** (-0.5)
    gk_out[...] = rope_back(grad_k, tok_cos[...], tok_sin[...]).astype(BF16)
    gv_out[...] = gv_sum[...].astype(BF16)


def attend_back(q, k, v, bias, gate, slot_tables, tok_tables, grad_gated):
    slots, width = q.shape
    tok = k.shape[0]
    heads = width // HD
    head = lambda h: (0, h)
    whole = lambda h: (0, 0)
    rows = 256
    return pl.pallas_call(
        functools.partial(attend_back_kernel, rows),
        grid=(heads,),
        in_specs=[
            pl.BlockSpec((slots, HD), head),
            pl.BlockSpec((tok, HD), head),
            pl.BlockSpec((tok, HD), head),
            pl.BlockSpec((slots, tok), whole),
            pl.BlockSpec((slots, 1), whole),
            pl.BlockSpec((slots, HD), whole),
            pl.BlockSpec((slots, HD), whole),
            pl.BlockSpec((tok, HD), whole),
            pl.BlockSpec((tok, HD), whole),
            pl.BlockSpec((slots, HD), head),
        ],
        out_specs=[
            pl.BlockSpec((slots, HD), head),
            pl.BlockSpec((tok, HD), head),
            pl.BlockSpec((tok, HD), head),
        ],
        out_shape=[
            jax.ShapeDtypeStruct((slots, width), BF16),
            jax.ShapeDtypeStruct((tok, width), BF16),
            jax.ShapeDtypeStruct((tok, width), BF16),
        ],
        scratch_shapes=[pltpu.VMEM((tok, HD), F32), pltpu.VMEM((tok, HD), F32)],
        compiler_params=pltpu.CompilerParams(vmem_limit_bytes=40 << 20),
        cost_estimate=pl.CostEstimate(
            flops=0, bytes_accessed=slots * width, transcendentals=0
        ),
    )(q, k, v, bias, gate, *slot_tables, *tok_tables, grad_gated)


class Square:
    def __init__(self):
        me = lax.axis_index("dp")
        self.core = lax.rem(me, 2)
        self.chip = me // 2
        x, y = lax.rem(self.chip, 2), self.chip // 2
        self.chip_x = self.chip + 1 - 2 * x
        self.chip_y = self.chip + 2 - 4 * y
        self.chip_far = 3 - self.chip
        self.twin = me + 1 - 2 * self.core
        self.near_x = 2 * self.chip_x + self.core
        self.near_y = 2 * self.chip_y + self.core


def send_to(source, target, send_sem, recv_sem, device):
    return pltpu.make_async_remote_copy(
        src_ref=source,
        dst_ref=target,
        send_sem=send_sem,
        recv_sem=recv_sem,
        device_id={"dp": device},
        device_id_type=pl.DeviceIdType.MESH,
    )


def greet(places):
    barrier = pltpu.get_barrier_semaphore()
    for place in places:
        pl.semaphore_signal(
            barrier, inc=1, device_id=place, device_id_type=pl.DeviceIdType.MESH
        )
    pl.semaphore_wait(barrier, len(places))


def send_across(source, target, send_sem, recv_sem, device):
    return pltpu.make_async_remote_copy(
        src_ref=source,
        dst_ref=target,
        send_sem=send_sem,
        recv_sem=recv_sem,
        device_id={"tensor": device},
        device_id_type=pl.DeviceIdType.MESH,
    )


def tensor_peers(count):
    z = lax.axis_index("tensor")
    return [lax.rem(z + k, count) for k in range(1, count)]


def share_rows(size):
    return pl.ds(pl.multiple_of(lax.axis_index("tensor") * size, size), size)


def rows_of(place, size):
    return pl.ds(pl.multiple_of(place * size, size), size)


def spread(count, source, target, sems):
    size = source.shape[0] // count
    copies = [
        send_to(
            source.at[pl.ds(k * size, size)], target.at[pl.ds(k * size, size)],
            sems[0].at[k], sems[1].at[k], partner(k),
        )
        for k in range(1, count)
    ]
    here = pltpu.make_async_copy(
        source.at[pl.ds(0, size)], target.at[pl.ds(0, size)], sems[0].at[0]
    )
    for copy in (*copies, here):
        copy.start()
    return (*copies, here)


def gather_kernel(axes, chunks, *refs):
    amount = len(axes)
    sources, rows = refs[:amount], refs[amount]
    targets, rows_out = refs[amount + 1 : 2 * amount + 1], refs[2 * amount + 1]
    send_sem, recv_sem, own_sem, e_send, e_recv, z_send, z_recv = refs[2 * amount + 2 :]
    count = z_send.shape[0] + 1
    exchange_count = e_send.shape[0]
    peers = tensor_peers(count)
    at = Square()
    me = 2 * at.chip + at.core
    far = 2 * at.chip_far + at.core
    greet(
        [{"dp": partner(k)} for k in range(1, exchange_count)] + [{"tensor": p} for p in peers]
    )
    columns = share_rows(rows.shape[1] // count)
    size = rows.shape[0] // exchange_count
    moved = [
        send_to(
            rows.at[pl.ds(k * size, size), columns], rows_out.at[pl.ds(k * size, size), columns],
            e_send.at[k], e_recv.at[k], partner(k),
        )
        for k in range(1, exchange_count)
    ]
    stay = pltpu.make_async_copy(
        rows.at[pl.ds(0, size), columns], rows_out.at[pl.ds(0, size), columns], e_send.at[0]
    )
    for copy in (*moved, stay):
        copy.start()

    def region(ref, axis, source, place, experts):
        size = source.shape[axis]
        at_place = pl.ds(pl.multiple_of(place * size, size), size)
        return ref.at[experts, at_place] if axis == 1 else ref.at[experts, :, at_place]

    first = 0
    plans = []
    for i in range(amount):
        count = sources[i].shape[0] // chunks[i]
        plans.append((i, first, count))
        first += count

    def copies(i, first, n):
        source, target, axis, size = sources[i], targets[i], axes[i], chunks[i]
        half = size // 2
        whole = pl.ds(n * size, size)
        top, bottom = pl.ds(n * size, half), pl.ds(n * size + half, half)
        unit = first + n

        def move(slot, place, experts, device, own=False):
            there = region(target, axis, source, place, experts)
            return send_to(
                source.at[experts] if own else there, there,
                send_sem.at[unit, slot], recv_sem.at[unit, slot], device,
            )

        return [
            functools.partial(move, 0, me, whole, at.near_x, True),
            functools.partial(move, 1, me, whole, at.near_y, True),
            functools.partial(move, 2, at.near_y, top, at.near_x),
            functools.partial(move, 3, at.near_x, bottom, at.near_y),
            functools.partial(move, 4, me, whole, at.twin, True),
            functools.partial(move, 5, at.near_x, whole, at.twin),
            functools.partial(move, 6, at.near_y, whole, at.twin),
            functools.partial(move, 7, far, top, at.twin),
            functools.partial(move, 8, far, bottom, at.twin),
        ]

    here = [
        pltpu.make_async_copy(
            sources[i], region(targets[i], axes[i], sources[i], me, pl.ds(0, sources[i].shape[0])),
            own_sem.at[i],
        )
        for i in range(amount)
    ]
    for i, first, count in plans:

        @pl.loop(0, count)
        def _(n):
            moves = copies(i, first, n)
            for slot in (0, 1, 4):
                moves[slot]().start()

    for copy in here:
        copy.start()
    for i, first, count in plans:

        @pl.loop(0, count)
        def _(n):
            moves = copies(i, first, n)
            moves[0]().wait_recv()
            moves[3]().start()
            moves[5]().start()
            moves[1]().wait_recv()
            moves[2]().start()
            moves[6]().start()

        if i == 0:
            stay.wait()
            for copy in moved:
                copy.wait_recv()
            across = [
                send_across(
                    rows_out.at[:, columns], rows_out.at[:, columns], z_send.at[k], z_recv.at[k], p
                )
                for k, p in enumerate(peers)
            ]
            for copy in across:
                copy.start()

    for i, first, count in plans:

        @pl.loop(0, count)
        def _(n):
            moves = copies(i, first, n)
            moves[2]().wait_recv()
            moves[7]().start()
            moves[3]().wait_recv()
            moves[8]().start()

    for i, first, count in plans:

        @pl.loop(0, count)
        def _(n):
            moves = copies(i, first, n)
            for slot in (4, 5, 6, 7, 8):
                moves[slot]().wait_recv()
            for move in moves:
                move().wait_send()

    for copy in (*here, *across):
        copy.wait()
    for copy in moved:
        copy.wait_send()


def gather_maps(tensor_size, peers, arrays, axes, chunks, rows):
    units = sum(a.shape[0] // c for a, c in zip(arrays, chunks))
    shapes = [
        tuple(n * 8 if d == axis else n for d, n in enumerate(a.shape))
        for a, axis in zip(arrays, axes)
    ]
    return pl.pallas_call(
        functools.partial(gather_kernel, axes, chunks),
        in_specs=[HBM] * (len(arrays) + 1),
        out_specs=[HBM] * (len(arrays) + 1),
        out_shape=[jax.ShapeDtypeStruct(shape, BF16) for shape in (*shapes, rows.shape)],
        scratch_shapes=[
            sems(units, 9), sems(units, 9), sems(len(arrays)), sems(peers), sems(peers),
            sems(tensor_size - 1), sems(tensor_size - 1),
        ],
        compiler_params=pltpu.CompilerParams(collective_id=5, has_side_effects=True),
        cost_estimate=pl.CostEstimate(flops=0, bytes_accessed=600 << 20, transcendentals=0),
    )(*arrays, rows)


def deal(source, target, sems, rows=None):
    me = lax.axis_index("dp")

    def block(place):
        return source.at[place] if rows is None else source.at[place, rows]

    copies = [
        send_to(block(partner(k)), target.at[me], sems[0].at[k], sems[1].at[k], partner(k))
        for k in range(1, source.shape[0])
    ]
    copies.append(pltpu.make_async_copy(block(me), target.at[me], sems[0].at[0]))
    for copy in copies:
        copy.start()
    return copies


def norm_back(total, products, hots, router, base, gain, hot_out, gain_out):
    first, second = products
    weights = hots[0] * first + hots[1] * second - hots[2] * (first + second)
    hot_out[...] = weights.astype(BF16)
    total = total + dot_nt(hot_out[...], router[...])
    scale = lax.rsqrt(jnp.mean(base * base, axis=-1, keepdims=True) + EPSILON)
    normal = base * scale
    gain_out[...] = jnp.sum(total * normal, axis=0, keepdims=True)
    weighted = total * gain
    return scale * (weighted - normal * jnp.mean(weighted * normal, axis=-1, keepdims=True))


def three_columns(block):
    return block[:, 0:1] + block[:, 1:2] + block[:, 2:3]


def in_columns(column, lane):
    high = column.astype(BF16).astype(F32)
    mid = (column - high).astype(BF16).astype(F32)
    return jnp.where(
        lane == 0, high, jnp.where(lane == 1, mid, jnp.where(lane == 2, column - high - mid, 0.0))
    ).astype(BF16)


def hidden_kernel(
    pick, rows, x_here, gain, router, hot_0, hot_1, hit_0, hit_1, maps_hbm,
    hidden_out, mlp_in_out, gates_out, x_out, maps_out,
    parts, sent, got, z_send, z_recv, g_send, g_recv, d_send, d_recv,
):
    count = z_send.shape[0] + 1
    width = rows.shape[1]
    tokens = pick.shape[1]
    size = tokens // count
    peers = tensor_peers(count)
    greet(
        [{"dp": partner(k)} for k in range(1, d_send.shape[0])] + [{"tensor": p} for p in peers]
    )
    dealt = deal(maps_hbm, maps_out, (d_send, d_recv))

    @pl.loop(0, width // 512)
    def _(i):
        at = pl.ds(pl.multiple_of(i * 512, 512), 512)
        piece = dot_tn(pick[...], rows[:, at])
        parts[:, at] = piece
        sent[:, at] = piece.astype(BF16)

    copies = [
        send_across(sent.at[rows_of(p, size)], got.at[k], z_send.at[k], z_recv.at[k], p)
        for k, p in enumerate(peers)
    ]
    for copy in copies:
        copy.start()
    here = share_rows(size)
    hidden_out[...] = x_here[...].astype(F32) + parts[here, :]
    for k, copy in enumerate(copies):
        copy.wait_recv()
        hidden_out[...] += got[k].astype(F32)
    hidden = hidden_out[...]
    scale = lax.rsqrt(jnp.mean(hidden * hidden, axis=-1, keepdims=True) + EPSILON)
    mlp_in_out[here, :] = (hidden * scale * gain[...]).astype(BF16)
    more = [
        send_across(
            mlp_in_out.at[here], mlp_in_out.at[here], g_send.at[k], g_recv.at[k], p
        )
        for k, p in enumerate(peers)
    ]
    for copy in more:
        copy.start()
    for copy in copies:
        copy.wait_send()
    for copy in more:
        copy.wait()

    logits = dot(mlp_in_out[...], router[...])
    picked = [jnp.sum(logits * hot[...], axis=1, keepdims=True) for hot in (hot_0, hot_1)]
    highest = jnp.maximum(picked[0], picked[1])
    raised = [jnp.exp(value - highest) for value in picked]
    gates = [value / (raised[0] + raised[1]) for value in raised]
    lane = lax.broadcasted_iota(jnp.int32, (tokens, HD), 1)
    gates_out[...] = jnp.where(lane == 0, gates[0], jnp.where(lane == 1, gates[1], 0.0))
    columns = [in_columns(gate, lane) for gate in gates]
    x_out[:, width:] = (dot(hit_0[...], columns[0]) + dot(hit_1[...], columns[1])).astype(BF16)

    @pl.loop(0, width // 512)
    def _(i):
        at = pl.ds(pl.multiple_of(i * 512, 512), 512)
        x_out[:, at] = dot(hit_0[...] + hit_1[...], mlp_in_out[:, at]).astype(BF16)
    for copy in dealt:
        copy.wait()


VMEM = pl.BlockSpec(memory_space=pltpu.VMEM)
HBM = pl.BlockSpec(memory_space=pl.ANY)


def sems(*shape):
    return pltpu.SemaphoreType.DMA(shape)


def hidden_step(tensor_size, pick, rows, x_here, gain, router, hots, hits, maps):
    tokens, width = pick.shape[1], rows.shape[1]
    slots = hits[0].shape[0]
    size = tokens // tensor_size
    around = tensor_size - 1
    return pl.pallas_call(
        hidden_kernel,
        in_specs=[VMEM] * 9 + [HBM],
        out_specs=[VMEM] * 4 + [HBM],
        out_shape=[
            jax.ShapeDtypeStruct((size, width), F32),
            jax.ShapeDtypeStruct((tokens, width), BF16),
            jax.ShapeDtypeStruct((tokens, HD), F32),
            jax.ShapeDtypeStruct((slots, width + HD), BF16),
            jax.ShapeDtypeStruct(maps.shape, BF16),
        ],
        scratch_shapes=[
            pltpu.VMEM((tokens, width), F32),
            pltpu.VMEM((tokens, width), BF16),
            pltpu.VMEM((around, size, width), BF16),
            sems(around), sems(around), sems(around), sems(around),
            sems(maps.shape[0]), sems(maps.shape[0]),
        ],
        compiler_params=pltpu.CompilerParams(
            collective_id=3, has_side_effects=True, vmem_limit_bytes=48 << 20
        ),
        cost_estimate=pl.CostEstimate(
            flops=2 * pick.shape[0] * tokens * width, bytes_accessed=300 << 20, transcendentals=0
        ),
    )(pick, rows, x_here, gain, router, *hots, *hits, maps)


def back_kernel(
    back, pick, hit_0, hit_1, hidden, cot_here, gain, router, hots, gates, att_pick, gated,
    rows_hbm, gate_hbm, up_hbm,
    grad_out, pair_out, gain_out, hot_out, mixed_out, att_rows, gate_maps, up_maps, grad_output,
    parts, sent, got, z_send, z_recv, g_send, g_recv, e_send, e_recv, w_send, w_recv, u_send, u_recv,
    rows_in, columns_here, mlp_got, m_send, m_recv, own, stage, stage_sem,
):
    count = z_send.shape[0] + 1
    width = back.shape[1] - HD
    tokens = pick.shape[1]
    size = tokens // count
    peers = tensor_peers(count)
    exchange_count = e_send.shape[0]
    greet(
        [{"dp": partner(k)} for k in range(1, exchange_count)] + [{"tensor": p} for p in peers]
    )
    moves = spread(exchange_count, rows_hbm, rows_in, (e_send, e_recv))
    dealt = deal(gate_hbm, gate_maps, (w_send, w_recv))
    dealt += deal(up_hbm, up_maps, (u_send, u_recv))

    @pl.loop(0, width // 512)
    def _(i):
        at = pl.ds(pl.multiple_of(i * 512, 512), 512)
        piece = dot_tn(pick[...], back[:, at])
        parts[:, at] = piece
        sent[:, at] = piece.astype(BF16)

    for k, hit in enumerate((hit_0, hit_1)):
        at = pl.ds(width + k * HD, HD)
        piece = dot_tn(hit[...], back[:, width:])
        parts[:, at] = piece
        sent[:, at] = piece.astype(BF16)

    copies = [
        send_across(sent.at[rows_of(p, size)], got.at[k], z_send.at[k], z_recv.at[k], p)
        for k, p in enumerate(peers)
    ]
    for copy in copies:
        copy.start()
    here = share_rows(size)
    total = parts[here, :]
    for k, copy in enumerate(copies):
        copy.wait_recv()
        total = total + got[k].astype(F32)
    products = (
        three_columns(total[:, width : width + HD]), three_columns(total[:, width + HD :])
    )
    grad_out[...] = cot_here[...].astype(F32) + norm_back(
        total[:, :width], products, hots, router, hidden[...], gain[...], hot_out, gain_out
    )
    pair_out[here, :] = grad_out[...].astype(BF16)
    more = [
        send_across(pair_out.at[here], pair_out.at[here], g_send.at[k], g_recv.at[k], p)
        for k, p in enumerate(peers)
    ]
    for copy in more:
        copy.start()
    for copy in moves:
        copy.wait()
    matrix = hit_0[...].astype(F32) * gates[0:1, :] + hit_1[...].astype(F32) * gates[1:2, :]
    high = matrix.astype(BF16)
    low = (matrix - high.astype(F32)).astype(BF16)
    columns_here[...] = (dot_tn(high, rows_in[...]) + dot_tn(low, rows_in[...])).astype(BF16)
    columns = share_rows(width // count)
    turned = [
        send_across(
            columns_here.at[rows_of(p, size)], mlp_got.at[:, columns], m_send.at[k], m_recv.at[k],
            p,
        )
        for k, p in enumerate(peers)
    ]
    turned.append(
        pltpu.make_async_copy(columns_here.at[here], mlp_got.at[:, columns], own.at[0])
    )
    for copy in turned:
        copy.start()
    for copy in turned:
        copy.wait()
    mixed_out[...] = (hidden[...] + mlp_got[...].astype(F32)).astype(BF16)
    for copy in copies:
        copy.wait_send()
    for copy in more:
        copy.wait()

    @pl.loop(0, width // 512)
    def _(i):
        at = rows_of(i, 512)
        att_rows[:, at] = dot(att_pick[...], pair_out[:, at]).astype(BF16)

    experts, cap = grad_output.shape[0], gated.shape[0] // grad_output.shape[0]

    def store(e):
        slot = lax.rem(e, 2)
        return pltpu.make_async_copy(stage.at[slot], grad_output.at[e], stage_sem.at[slot])

    @pl.loop(0, experts)
    def _(e):
        @pl.when(e > 1)
        def _():
            store(e - 2).wait()

        at = rows_of(e, cap)
        stage[lax.rem(e, 2)] = dot_tn(gated[at, :], att_rows[at, :]).astype(BF16)
        store(e).start()

    for e in (experts - 2, experts - 1):
        store(e).wait()
    for copy in dealt:
        copy.wait()


def back_step(
    tensor_size, peers, back, pick, hits, hidden, cot_here, gain, router, hots, gates,
    att_pick, gated, experts, rows_send, gate_maps, up_maps,
):
    tokens, width = pick.shape[1], back.shape[1] - HD
    size = tokens // tensor_size
    around = tensor_size - 1
    wide = width + 2 * HD
    return pl.pallas_call(
        back_kernel,
        in_specs=[VMEM] * 12 + [HBM] * 3,
        out_specs=[VMEM] * 6 + [HBM] * 3,
        out_shape=[
            jax.ShapeDtypeStruct((size, width), F32),
            jax.ShapeDtypeStruct((tokens, width), BF16),
            jax.ShapeDtypeStruct((1, width), F32),
            jax.ShapeDtypeStruct((size, HD), BF16),
            jax.ShapeDtypeStruct((size, width), BF16),
            jax.ShapeDtypeStruct((att_pick.shape[0], width), BF16),
            jax.ShapeDtypeStruct(gate_maps.shape, BF16),
            jax.ShapeDtypeStruct(up_maps.shape, BF16),
            jax.ShapeDtypeStruct((experts, gated.shape[1], width), BF16),
        ],
        scratch_shapes=[
            pltpu.VMEM((tokens, wide), F32),
            pltpu.VMEM((tokens, wide), BF16),
            pltpu.VMEM((around, size, wide), BF16),
            sems(around), sems(around), sems(around), sems(around), sems(peers), sems(peers),
            sems(peers), sems(peers), sems(peers), sems(peers),
            pltpu.VMEM(rows_send.shape, BF16),
            pltpu.VMEM((tokens, width // tensor_size), BF16),
            pltpu.VMEM((size, width), BF16),
            sems(around), sems(around), sems(1),
            pltpu.VMEM((2, gated.shape[1], width), BF16),
            sems(2),
        ],
        compiler_params=pltpu.CompilerParams(
            collective_id=4, has_side_effects=True, vmem_limit_bytes=56 << 20
        ),
        cost_estimate=pl.CostEstimate(
            flops=2 * pick.shape[0] * tokens * width, bytes_accessed=300 << 20, transcendentals=0
        ),
    )(back, pick, hits[0], hits[1], hidden, cot_here, gain, router, hots, gates, att_pick, gated, rows_send, gate_maps, up_maps)


GIVE = 4
HALF_SMALL = 8


def final_kernel(
    routed_hbm, grad_q, normed, grad_kv, part_hbm,
    grad_hidden, x_here, gain, router, hots, small, maps_hbm,
    out, tokens_out, small_out, maps_out,
    give, keep, twin_in, far_in, near_in, routed, got_part, tokens_here,
    twin_send, twin_recv, far_send, far_recv, near_send, near_recv, load, own,
    p_send, p_recv, t_send, t_recv,
    hot_here, small_all, small_in, small_sum, small_got,
    s_send, s_recv, w_send, w_recv, d_send, d_recv,
):
    at = Square()
    experts = grad_q.shape[0]
    units, _, size, _ = keep.shape
    half = size // 2
    count = p_send.shape[0] + 1
    peers = tensor_peers(count)
    width = normed.shape[1]
    share = part_hbm.shape[0] // count

    def fetch(u):
        return pltpu.make_async_copy(
            routed_hbm.at[u], routed.at[lax.rem(u, 2)], load.at[lax.rem(u, 2)]
        )

    fetch(0).start()
    here = share_rows(share)
    mine = pltpu.make_async_copy(part_hbm.at[here], got_part.at[count - 1], own.at[0])
    mine.start()
    greet([{"dp": partner(k)} for k in range(1, 8)] + [{"tensor": p} for p in peers])
    part_copies = [
        send_across(part_hbm.at[rows_of(p, share)], got_part.at[k], p_send.at[k], p_recv.at[k], p)
        for k, p in enumerate(peers)
    ]
    for copy in part_copies:
        copy.start()
    late = maps_out.shape[1]
    dealt = deal(maps_hbm, maps_out, (d_send, d_recv), pl.ds(maps_hbm.shape[1] - late, late))

    def to_twin(u):
        slot = lax.rem(u, GIVE)
        return send_to(give.at[slot], twin_in.at[u], twin_send.at[slot], twin_recv.at[u], at.twin)

    def to_far(u):
        first = send_to(
            keep.at[u, at.chip_far, pl.ds(0, half)],
            far_in.at[u, 0], far_send.at[u, 0], far_recv.at[u, 0], at.near_x,
        )
        second = send_to(
            keep.at[u, at.chip_far, pl.ds(half, half)],
            far_in.at[u, 1], far_send.at[u, 1], far_recv.at[u, 1], at.near_y,
        )
        return first, second

    def to_near(u):
        first = send_to(
            keep.at[u, at.chip_x], near_in.at[u, 0], near_send.at[u, 0], near_recv.at[u, 0],
            at.near_x,
        )
        second = send_to(
            keep.at[u, at.chip_y], near_in.at[u, 1], near_send.at[u, 1], near_recv.at[u, 1],
            at.near_y,
        )
        return first, second

    def multiply(u, rows, grads):
        slot = lax.rem(u, GIVE)

        @pl.when(u >= GIVE)
        def _():
            to_twin(u - GIVE).wait_send()

        for chip in range(4):
            columns = rows_of(2 * chip + 1 - at.core, size)
            give[slot, chip] = dot_tn(rows[:, columns], grads[...]).astype(BF16)
        to_twin(u).start()
        for chip in range(4):
            columns = rows_of(2 * chip + at.core, size)
            keep[u, chip] = dot_tn(rows[:, columns], grads[...]).astype(BF16)

    def join_twin(u):
        to_twin(u).wait_recv()

        def add(chip):
            keep[u, chip] = (keep[u, chip].astype(F32) + twin_in[u, chip].astype(F32)).astype(BF16)

        add(at.chip_far)
        for copy in to_far(u):
            copy.start()
        add(at.chip_x)
        add(at.chip_y)
        add(at.chip)

    @pl.loop(0, experts)
    def _(u):
        fetch(u).wait()

        @pl.when(u < experts - 1)
        def _():
            fetch(u + 1).start()

        multiply(u, routed.at[lax.rem(u, 2)], grad_q.at[u])

        @pl.when(u > 0)
        def _():
            join_twin(u - 1)

    @pl.loop(experts, units)
    def _(u):
        multiply(u, normed, grad_kv.at[u - experts])
        join_twin(u - 1)

    join_twin(units - 1)

    mine.wait()
    total = got_part[count - 1].astype(F32)
    for k, copy in enumerate(part_copies):
        copy.wait_recv()
        total = total + got_part[k].astype(F32)
    products = (
        three_columns(total[:, width : width + HD]), three_columns(total[:, width + HD :])
    )
    tokens_here[...] = (
        grad_hidden[...]
        + norm_back(
            total[:, :width], products, hots, router, x_here[...].astype(F32), gain[...],
            hot_here, small_all.at[pl.ds(0, 1)],
        )
    ).astype(BF16)
    token_copies = [
        send_across(tokens_here, tokens_out.at[here], t_send.at[k], t_recv.at[k], p)
        for k, p in enumerate(peers)
    ]
    for copy in token_copies:
        copy.start()
    kept = pltpu.make_async_copy(tokens_here, tokens_out.at[here], own.at[1])
    kept.start()

    small_all[1:HALF_SMALL, :] = small[1:HALF_SMALL, :]
    small_all[HALF_SMALL : 2 * HALF_SMALL, :] = dot_tn(hot_here[...], normed[here, :])[:HALF_SMALL]
    small_all[2 * HALF_SMALL :, :] = small[HALF_SMALL:, :]

    def small_block(place):
        return small_all.at[:, rows_of(place, size)]

    small_copies = [
        send_to(
            small_block(partner(k)), small_in.at[k], s_send.at[k], s_recv.at[k], partner(k)
        )
        for k in range(1, 8)
    ]
    for copy in small_copies:
        copy.start()

    @pl.loop(0, units)
    def _(u):
        for copy in to_far(u):
            copy.wait_recv()
        top, bottom = pl.ds(0, half), pl.ds(half, half)
        keep[u, at.chip_y, top, :] = (
            keep[u, at.chip_y, top, :].astype(F32) + far_in[u, 0].astype(F32)
        ).astype(BF16)
        keep[u, at.chip_x, bottom, :] = (
            keep[u, at.chip_x, bottom, :].astype(F32) + far_in[u, 1].astype(F32)
        ).astype(BF16)
        for copy in to_near(u):
            copy.start()

    @pl.loop(0, units)
    def _(u):
        for copy in to_near(u):
            copy.wait_recv()
        out[u] = (
            keep[u, at.chip].astype(F32) + near_in[u, 0].astype(F32) + near_in[u, 1].astype(F32)
        ).astype(BF16)

    block = small_all[:, rows_of(2 * at.chip + at.core, size)]
    for k, copy in enumerate(small_copies):
        copy.wait_recv()
        block = block + small_in[k + 1]
    small_sum[...] = block
    last_copies = [
        send_across(small_sum, small_got.at[k], w_send.at[k], w_recv.at[k], p)
        for k, p in enumerate(peers)
    ]
    for copy in last_copies:
        copy.start()

    @pl.loop(units - GIVE, units)
    def _(u):
        to_twin(u).wait_send()

    @pl.loop(0, units)
    def _(u):
        for copy in (*to_far(u), *to_near(u)):
            copy.wait_send()

    for k, copy in enumerate(last_copies):
        copy.wait_recv()
        block = block + small_got[k]
    small_out[...] = block
    for copy in (*part_copies, *small_copies, *last_copies):
        copy.wait_send()
    for copy in (*token_copies, *dealt, kept):
        copy.wait()


def final_step(
    tensor_size, routed, grad_q, normed, grad_kv, part, grad_hidden, x_here, gain,
    router, hots, small, maps, late,
):
    experts, rows, width = routed.shape
    columns = grad_q.shape[2]
    units = experts + grad_kv.shape[0]
    size = width // 8
    tokens, wide = part.shape
    share = tokens // tensor_size
    around = tensor_size - 1
    return pl.pallas_call(
        final_kernel,
        in_specs=[HBM, VMEM, VMEM, VMEM, HBM] + [VMEM] * 6 + [HBM],
        out_specs=[VMEM, HBM, VMEM, HBM],
        out_shape=[
            jax.ShapeDtypeStruct((units, size, columns), BF16),
            jax.ShapeDtypeStruct((tokens, width), BF16),
            jax.ShapeDtypeStruct((3 * HALF_SMALL, size), F32),
            jax.ShapeDtypeStruct((maps.shape[0], late) + maps.shape[2:], BF16),
        ],
        scratch_shapes=[
            pltpu.VMEM((GIVE, 4, size, columns), BF16),
            pltpu.VMEM((units, 4, size, columns), BF16),
            pltpu.VMEM((units, 4, size, columns), BF16),
            pltpu.VMEM((units, 2, size // 2, columns), BF16),
            pltpu.VMEM((units, 2, size, columns), BF16),
            pltpu.VMEM((2, rows, width), BF16),
            pltpu.VMEM((tensor_size, share, wide), BF16),
            pltpu.VMEM((share, width), BF16),
            sems(GIVE), sems(units), sems(units, 2), sems(units, 2), sems(units, 2),
            sems(units, 2), sems(2), sems(3),
            sems(around), sems(around), sems(around), sems(around),
            pltpu.VMEM((share, HD), BF16),
            pltpu.VMEM((3 * HALF_SMALL, width), F32),
            pltpu.VMEM((8, 3 * HALF_SMALL, size), F32),
            pltpu.VMEM((3 * HALF_SMALL, size), F32),
            pltpu.VMEM((around, 3 * HALF_SMALL, size), F32),
            sems(8), sems(8), sems(around), sems(around), sems(8), sems(8),
        ],
        compiler_params=pltpu.CompilerParams(
            collective_id=1, has_side_effects=True, vmem_limit_bytes=60 << 20
        ),
        cost_estimate=pl.CostEstimate(flops=0, bytes_accessed=1 << 20, transcendentals=0),
    )(
        routed, grad_q, normed, grad_kv, part, grad_hidden, x_here, gain, router, hots, small,
        maps,
    )


def widen_kernel(first, second, third, fourth, both_out, third_out):
    both_out[:, 0] = first[...].astype(F32)
    both_out[:, 1] = second[...].astype(F32)
    early = third.shape[1]
    third_out[:, 0:early] = third[...].astype(F32)
    third_out[:, early:] = fourth[...].astype(F32)


def widen(first, second, third, fourth):
    experts, rows, columns = first.shape
    narrow = pl.BlockSpec((1, rows, columns), lambda e: (e, 0, 0))
    whole = (experts, third.shape[1] + fourth.shape[1], third.shape[2])

    def block(shape):
        return pl.BlockSpec((1,) + shape[1:], lambda e: (e, 0, 0))

    return pl.pallas_call(
        widen_kernel,
        grid=(experts,),
        in_specs=[narrow, narrow, block(third.shape), block(fourth.shape)],
        out_specs=[pl.BlockSpec((1, 2, rows, columns), lambda e: (e, 0, 0, 0)), block(whole)],
        out_shape=[
            jax.ShapeDtypeStruct((experts, 2, rows, columns), F32),
            jax.ShapeDtypeStruct(whole, F32),
        ],
        compiler_params=pltpu.CompilerParams(vmem_limit_bytes=32 << 20),
        cost_estimate=pl.CostEstimate(
            flops=0, bytes_accessed=6 * (2 * first.size + third.size + fourth.size), transcendentals=0
        ),
    )(first, second, third, fourth)


def turn_kernel(
    rows, q_ref, k_ref, v_ref, bias, gate, slot_cos, slot_sin, tok_cos, tok_sin, attended,
    hit_0, hit_1, mixed_here, output_hbm, query_hbm, keyval_hbm, maps_hbm,
    gq_out, gkv_out, part_out, maps_out, mixed_out,
    grad_gated, grad_routed, weight, product, gk_sum, gv_sum,
    load, d_send, d_recv, a_send, a_recv, own,
):
    count = a_send.shape[0] + 1
    peers = tensor_peers(count)
    experts, cap, width = rows.shape
    slots, here_width = q_ref.shape
    heads = here_width // HD
    step = 256
    greet(
        [{"dp": partner(k)} for k in range(1, d_send.shape[0])] + [{"tensor": p} for p in peers]
    )
    dealt = deal(maps_hbm, maps_out, (d_send, d_recv), pl.ds(0, maps_out.shape[1]))
    here = share_rows(mixed_here.shape[0])
    mixed_copies = [
        send_across(mixed_here, mixed_out.at[here], a_send.at[k], a_recv.at[k], p)
        for k, p in enumerate(peers)
    ]
    mixed_copies.append(pltpu.make_async_copy(mixed_here, mixed_out.at[here], own.at[0]))
    for copy in mixed_copies:
        copy.start()

    def fetch_output(e):
        slot = lax.rem(e, 2)
        return pltpu.make_async_copy(output_hbm.at[e], weight.at[slot], load.at[slot])

    def fetch_query(e, half):
        size = width // 2
        return pltpu.make_async_copy(
            query_hbm.at[e, pl.ds(half * size, size)], weight_rows(half), load.at[2 + half]
        )

    def weight_rows(half):
        return turned.at[half]

    turned = grad_routed[1]
    routed_out = grad_routed[0]

    fetch_output(0).start()

    @pl.loop(0, experts)
    def _(e):
        fetch_output(e).wait()

        @pl.when(e < experts - 1)
        def _():
            fetch_output(e + 1).start()

        at = pl.ds(pl.multiple_of(e * cap, cap), cap)
        grad_gated[at, :] = dot_nt(rows[e], weight[lax.rem(e, 2)])

    fetch_query(0, 0).start()
    fetch_query(0, 1).start()

    @pl.loop(0, heads)
    def _(h):
        lanes = rows_of(h, HD)
        gk_sum[...] = jnp.zeros_like(gk_sum)
        gv_sum[...] = jnp.zeros_like(gv_sum)

        @pl.loop(0, slots // step)
        def _(i):
            at = pl.ds(pl.multiple_of(i * step, step), step)
            q = q_ref[at, lanes]
            keys, values = k_ref[:, lanes], v_ref[:, lanes]
            probs = softmax_block(q, keys, bias[at, :].astype(F32))
            scaled = grad_gated[at, lanes] * gate[at, :]
            joined = scaled * attended[at, lanes]

            @pl.when(h == 0)
            def _():
                product[at, :] = joined

            @pl.when(h > 0)
            def _():
                product[at, :] += joined

            grad_att = scaled.astype(BF16)
            grad_probs = dot_nt(grad_att, values)
            centre = jnp.sum(probs * grad_probs, axis=-1, keepdims=True)
            grad_scores = (probs * (grad_probs - centre)).astype(BF16)
            grad_q = dot(grad_scores, keys) * HD ** (-0.5)
            gq_out[at, lanes] = rope_back(grad_q, slot_cos[at, :], slot_sin[at, :]).astype(BF16)
            gk_sum[...] += dot_tn(grad_scores, q)
            gv_sum[...] += dot_tn(probs.astype(BF16), grad_att)

        grad_k = gk_sum[...] * HD ** (-0.5)
        gkv_out[0, :, lanes] = rope_back(grad_k, tok_cos[...], tok_sin[...]).astype(BF16)
        gkv_out[1, :, lanes] = gv_sum[...].astype(BF16)

    @pl.loop(0, experts)
    def _(e):
        at = pl.ds(pl.multiple_of(e * cap, cap), cap)
        for half in range(2):
            fetch_query(e, half).wait()
            routed_out[at, pl.ds(half * (width // 2), width // 2)] = dot_nt(
                gq_out[at, :], turned[half]
            ).astype(BF16)

            @pl.when(e < experts - 1)
            def _():
                fetch_query(e + 1, half).start()

    def fetch_keyval(i):
        slot = lax.rem(i, 2)
        block = pl.ds(pl.multiple_of(i * 512, 512), 512)
        return [
            pltpu.make_async_copy(
                keyval_hbm.at[c, block], turned.at[slot, pl.ds(c * 512, 512)],
                load.at[4 + 2 * slot + c],
            )
            for c in range(2)
        ]

    for copy in fetch_keyval(0):
        copy.start()

    @pl.loop(0, width // 512)
    def _(i):
        for copy in fetch_keyval(i):
            copy.wait()

        @pl.when(i < width // 512 - 1)
        def _():
            for copy in fetch_keyval(i + 1):
                copy.start()

        at = rows_of(i, 512)
        maps = turned.at[lax.rem(i, 2)]
        part_out[:, at] = (
            dot_tn(hit_0[...] + hit_1[...], routed_out[:, at])
            + dot_nt(gkv_out[0], maps[0:512, :])
            + dot_nt(gkv_out[1], maps[512:1024, :])
        ).astype(BF16)

    columns = in_columns(
        jnp.sum(product[...], axis=1, keepdims=True),
        lax.broadcasted_iota(jnp.int32, (slots, HD), 1),
    )
    part_out[:, width : width + HD] = dot_tn(hit_0[...], columns).astype(BF16)
    part_out[:, width + HD :] = dot_tn(hit_1[...], columns).astype(BF16)
    for copy in (*mixed_copies, *dealt):
        copy.wait()


def turn_step(
    tensor_size, rows, q, k, v, bias, gate, slot_tables, tok_tables, attended, hits, mixed_here,
    output_full, query_full, keyval_full, maps, early,
):
    experts, cap, width = rows.shape
    slots, here_width = q.shape
    tok = k.shape[0]
    around = tensor_size - 1
    return pl.pallas_call(
        lambda *refs: turn_kernel(*refs[:24], (refs[24], refs[25]), *refs[26:]),
        in_specs=[VMEM] * 14 + [HBM] * 4,
        out_specs=[VMEM, VMEM, VMEM, HBM, HBM],
        out_shape=[
            jax.ShapeDtypeStruct((slots, here_width), BF16),
            jax.ShapeDtypeStruct((2, tok, here_width), BF16),
            jax.ShapeDtypeStruct((tok, width + 2 * HD), BF16),
            jax.ShapeDtypeStruct((maps.shape[0], early) + maps.shape[2:], BF16),
            jax.ShapeDtypeStruct((tok, width), BF16),
        ],
        scratch_shapes=[
            pltpu.VMEM((slots, here_width), F32),
            pltpu.VMEM((slots, width), BF16),
            pltpu.VMEM((2, width // 2, here_width), BF16),
            pltpu.VMEM((2, here_width, width), BF16),
            pltpu.VMEM((slots, HD), F32),
            pltpu.VMEM((tok, HD), F32),
            pltpu.VMEM((tok, HD), F32),
            sems(8), sems(8), sems(8), sems(around), sems(around), sems(1),
        ],
        compiler_params=pltpu.CompilerParams(
            collective_id=6, has_side_effects=True, vmem_limit_bytes=58 << 20
        ),
        cost_estimate=pl.CostEstimate(
            flops=10 * slots * tok * here_width, bytes_accessed=300 << 20, transcendentals=0
        ),
    )(
        rows, q, k, v, bias, gate, *slot_tables, *tok_tables, attended, *hits, mixed_here,
        output_full, query_full, keyval_full, maps,
    )


def partner(k):
    me = lax.axis_index("dp")
    place = me
    for bit in (1, 2, 4):
        place = place + bit * lax.rem(k // bit, 2) * (1 - 2 * lax.rem(me // bit, 2))
    return place


def expert_kernel(
    x_hbm, cot_hbm, gate_up_hbm, down_hbm, rest_hbm,
    back_out, rows_out, grad_gate_hbm, grad_up_hbm, grad_down_hbm,
    x_all, g_all, w_gate, w_up, w_down, act, grads, back, product, stage_up, stage_down,
    rows_here, rows_got, x_send, x_recv, b_send, b_recv, load, up_sem, down_sem, r_send, r_recv,
):
    peers = x_send.shape[0]
    slots, wide = x_all.shape
    width = wide - HD
    hidden = w_gate.shape[1]
    size = slots // peers
    pair = 2 * size
    step = 256
    whole_steps = hidden // step
    tail = hidden - whole_steps * step

    per = width // peers
    first = down_hbm.shape[1]
    loads = [
        pltpu.make_async_copy(cot_hbm, g_all, load.at[0]),
        pltpu.make_async_copy(down_hbm, w_down.at[:, pl.ds(0, first)], load.at[1]),
        pltpu.make_async_copy(
            rest_hbm, w_down.at[:, pl.ds(first, hidden - first)], load.at[3 + 2 * peers]
        ),
        pltpu.make_async_copy(
            x_hbm.at[pl.ds(0, size)], x_all.at[pl.ds(0, size)], load.at[2 + 2 * peers]
        ),
    ]
    for j in range(peers):
        for g, target in enumerate((w_gate, w_up)):
            loads.append(
                pltpu.make_async_copy(
                    gate_up_hbm.at[j, g], target.at[pl.ds(j * per, per)], load.at[2 + 2 * j + g]
                )
            )
    for copy in loads:
        copy.start()

    around = tensor_peers(r_send.shape[0] + 1)
    share = width // (len(around) + 1)
    greet([{"dp": partner(k)} for k in range(1, peers)] + [{"tensor": p} for p in around])

    def block(k):
        return pl.ds(pl.multiple_of(k * size, size), size)

    def send_x(k):
        return send_to(
            x_hbm.at[block(k)], x_all.at[block(k)], x_send.at[k], x_recv.at[k], partner(k)
        )

    def send_back(k):
        return send_to(
            back.at[block(k)], back_out.at[block(k)], b_send.at[k], b_recv.at[k], partner(k)
        )

    for k in (1, 2, 4, 3, 5):
        send_x(k).start()
    for copy in loads:
        copy.wait()

    def send_rows(k, group):
        rows = rows_of(group, pair)
        return send_across(
            rows_here.at[rows, rows_of(around[k], share)], rows_got.at[k, rows],
            r_send.at[k, group], r_recv.at[k, group], around[k],
        )

    @pl.loop(0, peers // 2)
    def _(group):
        rows = pl.ds(pl.multiple_of(group * pair, pair), pair)

        @pl.when(group > 0)
        def _():
            send_x(2 * group).wait_recv()

        send_x(2 * group + 1).wait_recv()
        columns = x_all[rows, width:].astype(F32)
        gate_of_row = columns[:, 0:1] + columns[:, 1:2] + columns[:, 2:3]
        g_all[rows, :] = (g_all[rows, :].astype(F32) * gate_of_row).astype(BF16)
        product[...] = jnp.zeros_like(product)

        def chunk(start, amount):
            cols = pl.ds(start, amount)
            x = x_all[rows, 0:width]
            gate = dot(x, w_gate[:, cols])
            up = dot(x, w_up[:, cols])
            grad_act = jnp.zeros((pair, amount), F32)
            for j in range(peers):
                grad_act += dot_nt(g_all[rows, j * per : (j + 1) * per], w_down[j, cols, :])
            sigmoid = 1.0 / (1.0 + jnp.exp(-gate))
            silu = gate * sigmoid
            activated = (silu * up).astype(BF16)
            act[rows, cols] = activated
            both = activated.astype(F32) * grad_act
            for part in range(amount // HD):
                product[...] += both[:, part * HD : (part + 1) * HD]
            grads[rows, cols] = (
                grad_act * up * sigmoid * (1.0 + gate * (1.0 - sigmoid))
            ).astype(BF16)
            grads[rows, pl.ds(hidden + start, amount)] = (grad_act * silu).astype(BF16)

        @pl.loop(0, whole_steps)
        def _(i):
            chunk(pl.multiple_of(i * step, step), step)

        if tail:
            chunk(whole_steps * step, tail)

        @pl.loop(0, width // step)
        def _(i):
            at = pl.ds(pl.multiple_of(i * step, step), step)
            back[rows, at] = (
                dot_nt(grads[rows, 0:hidden], w_gate[at, :])
                + dot_nt(grads[rows, hidden:], w_up[at, :])
            ).astype(BF16)

        total = jnp.sum(product[...], axis=1, keepdims=True)
        back[rows, width:] = in_columns(
            total, lax.broadcasted_iota(jnp.int32, (pair, HD), 1)
        )

        @pl.when(group == 0)
        def _():
            send_x(6).start()
            send_x(7).start()
            back_out[0:size, :] = back[0:size, :]

        @pl.when(group > 0)
        def _():
            send_back(2 * group).start()

        send_back(2 * group + 1).start()
        for j in range(peers):
            rows_here[rows, j * per : (j + 1) * per] = dot(act[rows, :], w_down[j]).astype(BF16)
        for k in range(len(around)):
            send_rows(k, group).start()

    def store_up(j, slot):
        return (
            pltpu.make_async_copy(
                stage_up.at[slot, :, pl.ds(0, hidden)], grad_gate_hbm.at[j], up_sem.at[slot, 0]
            ),
            pltpu.make_async_copy(
                stage_up.at[slot, :, pl.ds(hidden, hidden)], grad_up_hbm.at[j], up_sem.at[slot, 1]
            ),
        )

    @pl.loop(0, peers)
    def _(j):
        slot = lax.rem(j, 2)

        @pl.when(j > 1)
        def _():
            for copy in store_up(j - 2, slot):
                copy.wait()

        at = pl.ds(pl.multiple_of(j * per, per), per)
        stage_up[slot] = dot_tn(x_all[:, at], grads[...]).astype(BF16)
        for copy in store_up(j, slot):
            copy.start()

    def store_down(start, amount, slot):
        return pltpu.make_async_copy(
            stage_down.at[slot, :, pl.ds(0, amount)],
            grad_down_hbm.at[:, pl.ds(start, amount)],
            down_sem.at[slot],
        )

    def down_piece(start, amount, slot):
        piece = dot_tn(act[:, pl.ds(start, amount)], g_all[...]).astype(BF16)
        for j in range(peers):
            stage_down[slot, j, 0:amount, :] = piece[:, j * per : (j + 1) * per]
        store_down(start, amount, slot).start()

    @pl.loop(0, whole_steps)
    def _(i):
        slot = lax.rem(i, 2)

        @pl.when(i > 1)
        def _():
            store_down(pl.multiple_of((i - 2) * step, step), step, slot).wait()

        down_piece(pl.multiple_of(i * step, step), step, slot)

    last = whole_steps - 1
    store_down((last - 1) * step, step, (last - 1) % 2).wait()
    if tail:
        down_piece(whole_steps * step, tail, (last - 1) % 2)
        store_down(whole_steps * step, tail, (last - 1) % 2).wait()
    store_down(last * step, step, last % 2).wait()
    for j in (peers - 2, peers - 1):
        for copy in store_up(j, j % 2):
            copy.wait()

    @pl.loop(0, peers // 2)
    def _(group):
        rows = rows_of(group, pair)
        total = rows_here[rows, share_rows(share)].astype(F32)
        for k in range(len(around)):
            send_rows(k, group).wait()
            total = total + rows_got[k, rows, :].astype(F32)
        rows_out[rows, :] = total.astype(BF16)

    for k in range(1, peers):
        send_x(k).wait_send()
        send_back(k).wait()


def expert_step(tensor_size, x_rows, cot_rows, up_slices, down_slices, down_rest):
    slots, wide = x_rows.shape
    width = wide - HD
    peers, hidden, per = down_slices.shape
    hidden += down_rest.shape[1]
    vmem = pl.BlockSpec(memory_space=pltpu.VMEM)
    hbm = pl.BlockSpec(memory_space=pl.ANY)
    step = 256
    return pl.pallas_call(
        expert_kernel,
        in_specs=[hbm] * 5,
        out_specs=[vmem, vmem, hbm, hbm, hbm],
        out_shape=[
            jax.ShapeDtypeStruct((slots, wide), BF16),
            jax.ShapeDtypeStruct((slots, width // tensor_size), BF16),
            jax.ShapeDtypeStruct((peers, per, hidden), BF16),
            jax.ShapeDtypeStruct((peers, per, hidden), BF16),
            jax.ShapeDtypeStruct((peers, hidden, per), BF16),
        ],
        scratch_shapes=[
            pltpu.VMEM((slots, wide), BF16),
            pltpu.VMEM((slots, width), BF16),
            pltpu.VMEM((width, hidden), BF16),
            pltpu.VMEM((width, hidden), BF16),
            pltpu.VMEM((peers, hidden, per), BF16),
            pltpu.VMEM((slots, hidden), BF16),
            pltpu.VMEM((slots, 2 * hidden), BF16),
            pltpu.VMEM((slots, wide), BF16),
            pltpu.VMEM((2 * slots // peers, HD), F32),
            pltpu.VMEM((2, per, 2 * hidden), BF16),
            pltpu.VMEM((2, peers, step, per), BF16),
            pltpu.VMEM((slots, width), BF16),
            pltpu.VMEM((tensor_size - 1, slots, width // tensor_size), BF16),
            pltpu.SemaphoreType.DMA((peers,)),
            pltpu.SemaphoreType.DMA((peers,)),
            pltpu.SemaphoreType.DMA((peers,)),
            pltpu.SemaphoreType.DMA((peers,)),
            sems(4 + 2 * peers), sems(2, 2), sems(2),
            sems(tensor_size - 1, peers // 2), sems(tensor_size - 1, peers // 2),
        ],
        compiler_params=pltpu.CompilerParams(
            collective_id=2, has_side_effects=True, vmem_limit_bytes=60 << 20
        ),
        cost_estimate=pl.CostEstimate(
            flops=18 * slots * width * hidden, bytes_accessed=300 << 20, transcendentals=0
        ),
    )(x_rows, cot_rows, up_slices, down_slices, down_rest)


class Movers:
    def __init__(self, dp, experts, tensor):
        self.dp, self.experts, self.tensor = dp, experts, tensor
        self.ratio = dp // experts
        self.groups = self.pairs = None
        if self.ratio > 1:
            self.groups = [[g * experts + e for e in range(experts)] for g in range(self.ratio)]
            self.pairs = [[g * experts + e for g in range(self.ratio)] for e in range(experts)]

    def swap(self, blocks):
        return lax.all_to_all(blocks, "dp", 0, 0, axis_index_groups=self.groups, tiled=True)

    def fetch(self, shards):
        mine = self.swap(shards)
        if self.ratio > 1:
            mine = lax.all_gather(mine, "dp", axis=0, axis_index_groups=self.pairs, tiled=True)
        return mine

    def give_back(self, slices):
        if self.ratio > 1:
            slices = lax.psum_scatter(
                slices, "dp", scatter_dimension=0, axis_index_groups=self.pairs, tiled=True
            )
        return self.swap(slices)

    def exchange(self, rows):
        size = rows.shape[0] // self.experts
        blocks = [rows[:size]]
        for k in range(1, self.experts):
            pairs = [(i, i ^ k) for i in range(self.dp)]
            blocks.append(lax.ppermute(rows[k * size : (k + 1) * size], "dp", pairs))
        return jnp.concatenate(blocks, axis=0)

    def across(self, block, k):
        return lax.ppermute(block, "tensor", [(i, i ^ k) for i in range(self.tensor)])

    def reduce_rows(self, part, dtype=BF16):
        z = lax.axis_index("tensor")
        size = part.shape[0] // self.tensor
        total = lax.dynamic_slice_in_dim(part, z * size, size, axis=0)
        sent = part.astype(dtype)
        for k in range(1, self.tensor):
            block = lax.dynamic_slice_in_dim(sent, (z ^ k) * size, size, axis=0)
            total = total + self.across(block, k).astype(F32)
        return total

    def gather_rows(self, rows):
        z = lax.axis_index("tensor")
        size = rows.shape[0]
        rows = rows.astype(BF16)
        full = jnp.zeros((size * self.tensor,) + rows.shape[1:], BF16)
        for k in range(self.tensor):
            block = rows if k == 0 else self.across(rows, k)
            full = lax.dynamic_update_slice_in_dim(full, block, (z ^ k) * size, axis=0)
        return full


def expert_plain(movers, expert_in, cot_rows, up_slices, down_slices):
    dp_size, hidden_here, per_dp = down_slices.shape
    model_width = dp_size * per_dp
    gate_full, up_full = (up_slices[:, g].reshape(model_width, hidden_here) for g in range(2))
    down_full = down_slices.transpose(1, 0, 2).reshape(hidden_here, model_width)
    x_rows, gate_of_row = without_column(movers.exchange(expert_in))
    g_rows = (cot_rows.astype(F32) * gate_of_row).astype(BF16)
    gate = dot(x_rows, gate_full)
    up = dot(x_rows, up_full)
    sigmoid_gate = jax.nn.sigmoid(gate)
    silu_gate = gate * sigmoid_gate
    activated = (silu_gate * up).astype(BF16)
    grad_act = dot_nt(g_rows, down_full)
    grad_gate = (grad_act * up * sigmoid_gate * (1.0 + gate * (1.0 - sigmoid_gate))).astype(BF16)
    grad_up = (grad_act * silu_gate).astype(BF16)
    gate_times_grad = jnp.sum(activated.astype(F32) * grad_act, axis=1, keepdims=True)
    grad_expert_in = with_column(
        (dot_nt(grad_gate, gate_full) + dot_nt(grad_up, up_full)).astype(BF16), gate_times_grad
    )
    return (
        movers.exchange(grad_expert_in),
        dot(activated, down_full, BF16),
        dot_tn(x_rows, grad_gate, BF16).reshape(dp_size, per_dp, -1),
        dot_tn(x_rows, grad_up, BF16).reshape(dp_size, per_dp, -1),
        dot_tn(activated, g_rows, BF16).reshape(-1, dp_size, per_dp).transpose(1, 0, 2),
    )


def on_device(
    dp_size,
    tensor_size,
    tokens,
    cotangent,
    parents,
    attention_routes,
    expert_routes,
    slot_order,
    gain_attention,
    keyval_weight,
    query_weight,
    output_weight,
    attention_router,
    gain_feedforward,
    expert_router,
    gate_up_weight,
    down_weight,
):
    tok_count, model_width = tokens.shape
    pair_count = TOPK * tok_count
    att_experts = query_weight.shape[0]
    mlp_experts = gate_up_weight.shape[0]
    att_cap = tok_count * 5 // 16
    mlp_cap = pair_count // mlp_experts
    att_slots = att_experts * att_cap
    mlp_slots = mlp_experts * mlp_cap
    width_here = query_weight.shape[2]
    rows_here = tok_count // tensor_size
    movers = Movers(dp_size, mlp_experts, tensor_size)
    fast = dp_size == 8 and mlp_experts == 8
    tie = lax.optimization_barrier

    small = jnp.concatenate(
        [gain_attention[:, None], gain_feedforward[:, None], attention_router, expert_router], axis=1
    )
    small_full = lax.all_gather(small, "dp", axis=0, tiled=True)
    small_full, down_weight = tie((small_full, down_weight))
    gain_attn_full = small_full[:, 0].astype(F32)
    gain_mlp_full = small_full[:, 1].astype(F32)
    router_att = small_full[:, 2 : 2 + att_experts]
    router_mlp = small_full[:, 2 + att_experts :]

    inside, depth = ancestry(parents[0])
    token_index = jnp.arange(tok_count, dtype=jnp.int32)
    pair_order = jnp.arange(pair_count, dtype=jnp.int32).reshape(tok_count, TOPK)
    att_hits = slot_hits(
        slot_places(attention_routes, pair_order, att_cap, att_experts), att_slots
    )
    priority = slot_order[0][:, None] * TOPK + jnp.arange(TOPK, dtype=jnp.int32)[None, :]
    home = lax.rem(lax.axis_index("dp"), mlp_experts)
    mlp_hits = slot_hits(
        slot_places(expert_routes ^ home, priority, mlp_cap, mlp_experts), mlp_slots
    )
    att_pick = (att_hits[0] | att_hits[1]).astype(BF16)
    mlp_pick = (mlp_hits[0] | mlp_hits[1]).astype(BF16)

    def to_slots(hits, pair_values):
        return jnp.sum(
            sum(jnp.where(hits[k], pair_values[:, k][None, :], 0) for k in range(TOPK)), axis=1
        )

    def to_pairs(hits, slot_values):
        return jnp.stack(
            [jnp.sum(jnp.where(hits[k], slot_values[:, None], 0.0), axis=0) for k in range(TOPK)],
            axis=1,
        )

    def position_of(token):
        segment = token // SEG
        level = jnp.sum(
            jnp.where(segment[:, None] == jnp.arange(depth.shape[0])[None, :], depth[None, :], 0),
            axis=1,
        )
        return level * SEG + token % SEG

    pair_token = jnp.broadcast_to(token_index[:, None], (tok_count, TOPK))
    slot_token = to_slots(att_hits, pair_token)
    slot_filled = jnp.any(att_hits[0] | att_hits[1], axis=1)
    slot_tables = rope_tables(position_of(slot_token))
    tok_tables = rope_tables(position_of(token_index))
    segment_hot = (
        (slot_token // SEG)[:, None] == jnp.arange(inside.shape[0], dtype=jnp.int32)[None, :]
    ).astype(F32)
    reach = dot(segment_hot, jnp.repeat(inside.astype(F32), SEG, axis=1)) > 0.5
    allowed = reach & (token_index[None, :] <= slot_token[:, None]) & slot_filled[:, None]
    bias = jnp.where(allowed, 0.0, NEGATIVE).astype(BF16)

    early = down_weight.shape[1] // 2 if fast else down_weight.shape[1]
    down_slices = movers.fetch(down_weight[:, :early])
    cot_send = dot(mlp_pick, cotangent, BF16)

    inputs = tokens.astype(F32)
    normal_attn, scale_attn = norm_forward(inputs)
    normed = (normal_attn * gain_attn_full).astype(BF16)
    att_gates = picked_softmax(dot(normed, router_att), attention_routes)
    att_gate_slots = to_slots(att_hits, att_gates)[:, None]
    routed = dot(att_pick, normed, BF16).reshape(att_experts, att_cap, model_width)
    if fast:
        mlp_bits = tuple(hit.astype(BF16) for hit in mlp_hits)
        expert_lanes = [
            (expert_routes[:, k : k + 1] == jnp.arange(HD, dtype=jnp.int32)[None, :]).astype(F32)
            for k in range(TOPK)
        ]
        keyval_weight, query_weight, output_weight, *before = tie(
            (keyval_weight, query_weight, output_weight, routed, cot_send, bias, att_gate_slots)
            + slot_tables + tok_tables + mlp_bits + tuple(expert_lanes)
        )
        routed, cot_send, bias, att_gate_slots = before[:4]
        slot_tables, tok_tables = before[4:6], before[6:8]
        mlp_bits, expert_lanes = before[8:10], before[10:12]
        keyval_full, query_full, output_full, cot_rows = gather_maps(
            tensor_size, mlp_experts,
            (keyval_weight, query_weight, output_weight), (1, 1, 2), (2, 2, 2), cot_send,
        )
    else:
        keyval_full = lax.all_gather(keyval_weight, "dp", axis=1, tiled=True)
        query_full = lax.all_gather(query_weight, "dp", axis=1, tiled=True)
        output_full = lax.all_gather(output_weight, "dp", axis=2, tiled=True)
    query_full, keyval_full, down_slices, gate_up_weight = tie(
        (query_full, keyval_full, down_slices, gate_up_weight)
    )
    up_slices = movers.fetch(gate_up_weight)
    keyval = jnp.concatenate([dot(normed, keyval_full[0]), dot(normed, keyval_full[1])], axis=1)
    query_raw = jnp.einsum(
        "ecd,edf->ecf", routed, query_full, preferred_element_type=F32
    ).reshape(att_slots, width_here)
    queries, key_rows, values, attended, gated = attend(
        query_raw, keyval, bias, att_gate_slots, slot_tables, tok_tables
    )
    gated_slots = gated.reshape(att_experts, att_cap, width_here)
    att_rows = jnp.einsum(
        "ecf,efd->ecd", gated_slots, output_full, preferred_element_type=F32
    ).reshape(att_slots, model_width)
    att_rows = att_rows.astype(BF16)

    z = lax.axis_index("tensor")

    def share(rows):
        return lax.dynamic_slice_in_dim(rows, z * rows_here, rows_here, axis=0)

    def hots(gates, picks, experts):
        lanes = jnp.arange(HD, dtype=jnp.int32)[None, :]
        hot = [(share(picks)[:, k : k + 1] == lanes).astype(F32) for k in range(TOPK)]
        return jnp.stack(hot + [sum(hot[k] * share(gates)[:, k : k + 1] for k in range(TOPK))])

    def padded(router):
        return jnp.pad(router, ((0, 0), (0, HD - router.shape[1])))

    if fast:
        hidden, mlp_in, mlp_gates, expert_in, down_rest = hidden_step(
            tensor_size, att_pick, att_rows, share(tokens), gain_mlp_full[None],
            padded(router_mlp), expert_lanes, mlp_bits, down_weight[:, early:],
        )
        mlp_gates = mlp_gates[:, :TOPK]
    else:
        hidden = share(inputs) + movers.reduce_rows(dot_tn(att_pick, att_rows))
        mlp_in = movers.gather_rows((norm_forward(hidden)[0] * gain_mlp_full).astype(BF16))
        cot_rows = movers.exchange(cot_send)
        mlp_gates = picked_softmax(dot(mlp_in, router_mlp), expert_routes)
        expert_in = with_column(
            dot(mlp_pick, mlp_in, BF16), to_slots(mlp_hits, mlp_gates)[:, None]
        )
    expert_in, up_slices = tie((expert_in, up_slices))

    if fast:
        back = expert_step(
            tensor_size, expert_in, cot_rows, up_slices, down_slices, down_rest
        )
    else:
        back = expert_plain(movers, expert_in, cot_rows, up_slices, down_slices)
    grad_in_slots, expert_out, grad_gate_w, grad_up_w, grad_down_w = back

    if fast:
        (
            grad_hidden, _, grad_gain_mlp, grad_mlp_logits, mixed, grad_att_rows, grad_gate_w,
            grad_up_w, grad_output_w,
        ) = back_step(
            tensor_size, mlp_experts, grad_in_slots, mlp_pick,
            mlp_bits, hidden, share(cotangent),
            gain_mlp_full[None], padded(router_mlp),
            hots(mlp_gates, expert_routes, mlp_experts), mlp_gates.T, att_pick, gated, att_experts,
            expert_out, grad_gate_w, grad_up_w,
        )
        grad_gain_mlp = grad_gain_mlp[0]
        grad_mlp_logits = grad_mlp_logits[:, :mlp_experts]
    else:
        out_slots = movers.exchange(expert_out)
        grad_gate_w = movers.give_back(grad_gate_w)
        grad_up_w = movers.give_back(grad_up_w)
        grad_in_slots, gate_times_grad = without_column(grad_in_slots)
        mlp_products = movers.reduce_rows(to_pairs(mlp_hits, gate_times_grad[:, 0]), F32)
        grad_mlp_in = movers.reduce_rows(dot_tn(mlp_pick, grad_in_slots))
        grad_mlp_logits = router_backward(
            share(mlp_gates), mlp_products, share(expert_routes), mlp_experts
        )
        grad_mlp_in = grad_mlp_in + dot_nt(grad_mlp_logits, router_mlp)
        normal_mlp, scale_mlp = norm_forward(hidden)
        grad_hidden_norm, grad_gain_mlp = norm_backward(
            grad_mlp_in, normal_mlp, scale_mlp, gain_mlp_full
        )
        grad_hidden = share(cotangent).astype(F32) + grad_hidden_norm
        grad_att_pair = movers.gather_rows(grad_hidden)
        grad_att_rows = dot(att_pick, grad_att_pair, BF16)
        grad_output_w = jnp.einsum(
            "ecf,ecd->efd",
            gated_slots,
            grad_att_rows.reshape(att_experts, att_cap, model_width),
            preferred_element_type=BF16,
        )
        gate_matrix = sum(
            jnp.where(mlp_hits[k], mlp_gates[:, k][None, :], 0.0) for k in range(TOPK)
        )
        matrix_high = gate_matrix.astype(BF16)
        matrix_low = (gate_matrix - matrix_high.astype(F32)).astype(BF16)
        mlp_part = (dot_tn(matrix_high, out_slots) + dot_tn(matrix_low, out_slots)).astype(BF16)
        mixed = movers.gather_rows(hidden + movers.reduce_rows(mlp_part))
    grad_router_mlp = dot_tn(share(mlp_in), grad_mlp_logits)

    grad_att_rows = grad_att_rows.reshape(att_experts, att_cap, model_width)
    grad_output_out = lax.psum_scatter(grad_output_w, "dp", scatter_dimension=2, tiled=True)
    if fast:
        half = grad_down_w.shape[1] // 2
        grad_q, grad_kv, normed_part, grad_down_early, mixed = turn_step(
            tensor_size, grad_att_rows, queries, key_rows, values, bias, att_gate_slots,
            slot_tables, tok_tables, attended, [hit.astype(BF16) for hit in att_hits], mixed,
            output_full, query_full, keyval_full, grad_down_w, half,
        )
    else:
        grad_down_early, grad_down_late = jnp.split(movers.give_back(grad_down_w), 2, axis=1)
        grad_gated = jnp.einsum(
            "ecd,efd->ecf", grad_att_rows, output_full, preferred_element_type=F32
        ).reshape(att_slots, width_here)
        att_products = to_pairs(
            att_hits, jnp.sum(grad_gated * attended, axis=1) * att_gate_slots[:, 0]
        )
        grad_q, grad_k, grad_v = attend_back(
            queries, key_rows, values, bias, att_gate_slots, slot_tables, tok_tables, grad_gated
        )
        grad_routed = jnp.einsum(
            "ecf,edf->ecd",
            grad_q.reshape(att_experts, att_cap, width_here),
            query_full,
            preferred_element_type=F32,
        ).reshape(att_slots, model_width)
        normed_part = (
            dot_tn(att_pick, grad_routed.astype(BF16))
            + dot_nt(grad_k, keyval_full[0])
            + dot_nt(grad_v, keyval_full[1])
        )
        grad_kv = jnp.stack([grad_k, grad_v])
    grad_query_slots = grad_q.reshape(att_experts, att_cap, width_here)
    if fast:
        small = jnp.concatenate(
            [
                jnp.zeros((1, model_width), F32),
                grad_gain_mlp[None],
                jnp.zeros((HALF_SMALL - 2, model_width), F32),
                grad_router_mlp.T,
            ],
            axis=0,
        )
        map_sums, grad_tokens, small_grads, grad_down_late = final_step(
            tensor_size, routed, grad_query_slots, normed, grad_kv, normed_part,
            grad_hidden, share(tokens), gain_attn_full[None], padded(router_att),
            hots(att_gates, attention_routes, att_experts), small, grad_down_w,
            grad_down_w.shape[1] - half,
        )
        small_grads = jnp.concatenate([small_grads[:2], small_grads[HALF_SMALL:]], axis=0).T
        grad_query_out, grad_keyval_out = map_sums[:att_experts], map_sums[att_experts:]
    else:
        grad_query_w = jnp.einsum(
            "ecd,ecf->edf", routed, grad_query_slots, preferred_element_type=BF16
        )
        grad_keyval_w = jnp.stack([dot_tn(normed, grad, BF16) for grad in grad_kv])
        grad_query_out = lax.psum_scatter(grad_query_w, "dp", scatter_dimension=1, tiled=True)
        grad_keyval_out = lax.psum_scatter(grad_keyval_w, "dp", scatter_dimension=1, tiled=True)
        grad_normed = movers.reduce_rows(normed_part)
        grad_att_logits = router_backward(
            share(att_gates), movers.reduce_rows(att_products, F32), share(attention_routes),
            att_experts,
        )
        grad_normed = grad_normed + dot_nt(grad_att_logits, router_att)
        grad_input_norm, grad_gain_attn = norm_backward(
            grad_normed, share(normal_attn), share(scale_attn), gain_attn_full
        )
        grad_tokens = movers.gather_rows(grad_hidden + grad_input_norm)
        grad_router_att = dot_tn(share(normed), grad_att_logits)
        small_grads = jnp.concatenate(
            [grad_gain_attn[:, None], grad_gain_mlp[:, None], grad_router_att, grad_router_mlp],
            axis=1,
        )
        small_grads = lax.psum(
            lax.psum_scatter(small_grads, "dp", scatter_dimension=0, tiled=True), "tensor"
        )
    grad_tokens, grad_output_out = tie((grad_tokens, grad_output_out))
    grad_tokens = grad_tokens.astype(F32)
    grad_up_w, grad_down_w = widen(
        grad_gate_w, grad_up_w, grad_down_early, grad_down_late
    )
    return (
        mixed,
        grad_tokens,
        small_grads[:, 0],
        grad_keyval_out.astype(F32),
        grad_query_out.astype(F32),
        grad_output_out.astype(F32),
        small_grads[:, 2 : 2 + att_experts],
        small_grads[:, 1],
        small_grads[:, 2 + att_experts :],
        grad_up_w,
        grad_down_w,
    )


def solution(mesh):
    placed = (
        P("dp", None),
        P("dp", None),
        P("dp", None),
        P("dp", None),
        P("dp", None),
        P("dp", None),
        P("dp"),
        P(None, "dp", "tensor"),
        P(None, "dp", "tensor"),
        P(None, "tensor", "dp"),
        P("dp", None),
        P("dp"),
        P("dp", None),
        P(None, None, "dp", "tensor"),
        P(None, "tensor", "dp"),
    )
    return jax.shard_map(
        functools.partial(on_device, mesh.shape["dp"], mesh.shape["tensor"]),
        mesh=mesh,
        in_specs=placed,
        out_specs=(
            P("dp", None),
            P("dp", None),
            P("dp"),
            P(None, "dp", "tensor"),
            P(None, "dp", "tensor"),
            P(None, "tensor", "dp"),
            P("dp", None),
            P("dp"),
            P("dp", None),
            P(None, None, "dp", "tensor"),
            P(None, "tensor", "dp"),
        ),
        check_vma=False,
    )
```

```python
import functools

import jax
import jax.numpy as jnp
from jax import lax
from jax.experimental import pallas as pl
from jax.experimental.pallas import tpu as pltpu
from jax.sharding import PartitionSpec as P

HD = 128
TOPK = 2
SEG = 128

EPSILON = 1e-06
NEGATIVE = -1e30
ROPE_BASE = 10000.0
F32 = jnp.float32
BF16 = jnp.bfloat16


def dot(a, b, out=F32):
    return jnp.dot(a, b, preferred_element_type=out)


def dot_tn(a, b, out=F32):
    return lax.dot_general(a, b, (((0,), (0,)), ((), ())), preferred_element_type=out)


def dot_nt(a, b, out=F32):
    return lax.dot_general(a, b, (((1,), (1,)), ((), ())), preferred_element_type=out)


def slot_places(routes, priority, capacity, experts):
    pair_total = routes.shape[0] * routes.shape[1]
    flat_routes = routes.reshape(pair_total)
    flat_order = priority.reshape(pair_total)
    same_expert = flat_routes[:, None] == flat_routes[None, :]
    earlier = flat_order[None, :] < flat_order[:, None]
    slot_rank = jnp.sum((same_expert & earlier).astype(jnp.int32), axis=1)
    slot_place = jnp.where(
        slot_rank < capacity, flat_routes * capacity + slot_rank, experts * capacity
    )
    return slot_place.reshape(routes.shape)


def slot_hits(place, slots):
    index = jnp.arange(slots, dtype=jnp.int32)[:, None]
    return [place[:, k][None, :] == index for k in range(place.shape[1])]


def ancestry(parent_row):
    segment_count = parent_row.shape[0]
    indices = jnp.arange(segment_count, dtype=jnp.int32)
    walker = indices
    inside = indices[:, None] == indices[None, :]
    for travel in range(segment_count):
        walker = parent_row[walker]
        inside = inside | (walker[:, None] == indices[None, :])
    depth = jnp.sum(inside.astype(jnp.int32), axis=1) - 1
    return (inside, depth)


def rope_tables(position):
    half_width = HD // 2
    frequency = ROPE_BASE ** (-jnp.arange(half_width, dtype=F32) / half_width)
    angles = position.astype(F32)[:, None] * frequency[None, :]
    cosine, sine = jnp.cos(angles), jnp.sin(angles)
    return (
        jnp.concatenate([cosine, cosine], axis=1),
        jnp.concatenate([-sine, sine], axis=1),
    )


def norm_forward(values_in):
    scale = lax.rsqrt(jnp.mean(values_in * values_in, axis=-1, keepdims=True) + EPSILON)
    return (values_in * scale, scale)


def norm_backward(grad_normed, normal, scale, gain):
    weighted = grad_normed * gain
    grad_in = scale * (weighted - normal * jnp.mean(weighted * normal, axis=-1, keepdims=True))
    return (grad_in, jnp.sum(grad_normed * normal, axis=0))


def router_backward(gates, products, picks, experts):
    grad_select = products - gates * jnp.sum(products, axis=1, keepdims=True)
    picked_hot = (picks[:, :, None] == jnp.arange(experts, dtype=jnp.int32)[None, None, :]).astype(
        F32
    )
    return jnp.sum(picked_hot * grad_select[:, :, None], axis=1).astype(BF16)


def with_column(rows, column):
    high = column.astype(BF16)
    rest = column - high.astype(F32)
    mid = rest.astype(BF16)
    low = (rest - mid.astype(F32)).astype(BF16)
    return jnp.concatenate(
        [rows, high, mid, low, jnp.zeros((rows.shape[0], HD - 3), BF16)], axis=1
    )


def without_column(both):
    width = both.shape[1] - HD
    parts = both[:, width : width + 3].astype(F32)
    return both[:, :width], parts[:, :1] + parts[:, 1:2] + parts[:, 2:]


def picked_softmax(logits, picks):
    experts = logits.shape[1]
    hot = picks[:, :, None] == jnp.arange(experts, dtype=jnp.int32)[None, None, :]
    return jax.nn.softmax(jnp.sum(jnp.where(hot, logits[:, None, :], 0.0), axis=2), axis=-1)


def rope(v, cosine, sine):
    return v * cosine + pltpu.roll(v, HD // 2, axis=1) * sine


def rope_back(v, cosine, sine):
    return v * cosine - pltpu.roll(v, HD // 2, axis=1) * sine


def softmax_block(q, k, bias):
    scores = dot_nt(q, k) * HD ** (-0.5) + bias
    exp_scores = jnp.exp(scores - jnp.max(scores, axis=-1, keepdims=True))
    return exp_scores / jnp.sum(exp_scores, axis=-1, keepdims=True)


def attend_kernel(
    rows, q_raw, k_raw, v_raw, bias, gate, slot_cos, slot_sin, tok_cos, tok_sin,
    q_out, k_out, v_out, att_out, gated_out,
):
    k_out[...] = rope(k_raw[...], tok_cos[...], tok_sin[...]).astype(BF16)
    v_out[...] = v_raw[...].astype(BF16)

    @pl.loop(0, q_raw.shape[0] // rows)
    def _(i):
        at = pl.ds(pl.multiple_of(i * rows, rows), rows)
        q = rope(q_raw[at, :], slot_cos[at, :], slot_sin[at, :]).astype(BF16)
        q_out[at, :] = q
        probs = softmax_block(q, k_out[...], bias[at, :].astype(F32)).astype(BF16)
        attended = dot(probs, v_out[...])
        att_out[at, :] = attended
        gated_out[at, :] = (attended * gate[at, :]).astype(BF16)


def attend(q_raw, keyval, bias, gate, slot_tables, tok_tables):
    slots, width = q_raw.shape
    tok = keyval.shape[0]
    heads = width // HD
    head = lambda h: (0, h)
    whole = lambda h: (0, 0)
    rows = 256
    return pl.pallas_call(
        functools.partial(attend_kernel, rows),
        grid=(heads,),
        in_specs=[
            pl.BlockSpec((slots, HD), head),
            pl.BlockSpec((tok, HD), head),
            pl.BlockSpec((tok, HD), lambda h: (0, heads + h)),
            pl.BlockSpec((slots, tok), whole),
            pl.BlockSpec((slots, 1), whole),
            pl.BlockSpec((slots, HD), whole),
            pl.BlockSpec((slots, HD), whole),
            pl.BlockSpec((tok, HD), whole),
            pl.BlockSpec((tok, HD), whole),
        ],
        out_specs=[
            pl.BlockSpec((slots, HD), head),
            pl.BlockSpec((tok, HD), head),
            pl.BlockSpec((tok, HD), head),
            pl.BlockSpec((slots, HD), head),
            pl.BlockSpec((slots, HD), head),
        ],
        out_shape=[
            jax.ShapeDtypeStruct((slots, width), BF16),
            jax.ShapeDtypeStruct((tok, width), BF16),
            jax.ShapeDtypeStruct((tok, width), BF16),
            jax.ShapeDtypeStruct((slots, width), F32),
            jax.ShapeDtypeStruct((slots, width), BF16),
        ],
        compiler_params=pltpu.CompilerParams(vmem_limit_bytes=40 << 20),
        cost_estimate=pl.CostEstimate(
            flops=4 * slots * tok * width,
            bytes_accessed=slots * width * 12 + slots * tok * 2,
            transcendentals=slots * tok * heads,
        ),
    )(q_raw, keyval, keyval, bias, gate, *slot_tables, *tok_tables)


def attend_back_kernel(
    rows, q_ref, k_ref, v_ref, bias, gate, slot_cos, slot_sin, tok_cos, tok_sin, grad_gated,
    gq_out, gk_out, gv_out, gk_sum, gv_sum,
):
    gk_sum[...] = jnp.zeros_like(gk_sum)
    gv_sum[...] = jnp.zeros_like(gv_sum)

    @pl.loop(0, q_ref.shape[0] // rows)
    def _(i):
        at = pl.ds(pl.multiple_of(i * rows, rows), rows)
        q = q_ref[at, :]
        probs = softmax_block(q, k_ref[...], bias[at, :].astype(F32))
        grad_att = (grad_gated[at, :] * gate[at, :]).astype(BF16)
        grad_probs = dot_nt(grad_att, v_ref[...])
        centre = jnp.sum(probs * grad_probs, axis=-1, keepdims=True)
        grad_scores = (probs * (grad_probs - centre)).astype(BF16)
        grad_q = dot(grad_scores, k_ref[...]) * HD ** (-0.5)
        gq_out[at, :] = rope_back(grad_q, slot_cos[at, :], slot_sin[at, :]).astype(BF16)
        gk_sum[...] += dot_tn(grad_scores, q)
        gv_sum[...] += dot_tn(probs.astype(BF16), grad_att)

    grad_k = gk_sum[...] * HD ** (-0.5)
    gk_out[...] = rope_back(grad_k, tok_cos[...], tok_sin[...]).astype(BF16)
    gv_out[...] = gv_sum[...].astype(BF16)


def attend_back(q, k, v, bias, gate, slot_tables, tok_tables, grad_gated):
    slots, width = q.shape
    tok = k.shape[0]
    heads = width // HD
    head = lambda h: (0, h)
    whole = lambda h: (0, 0)
    rows = 256
    return pl.pallas_call(
        functools.partial(attend_back_kernel, rows),
        grid=(heads,),
        in_specs=[
            pl.BlockSpec((slots, HD), head),
            pl.BlockSpec((tok, HD), head),
            pl.BlockSpec((tok, HD), head),
            pl.BlockSpec((slots, tok), whole),
            pl.BlockSpec((slots, 1), whole),
            pl.BlockSpec((slots, HD), whole),
            pl.BlockSpec((slots, HD), whole),
            pl.BlockSpec((tok, HD), whole),
            pl.BlockSpec((tok, HD), whole),
            pl.BlockSpec((slots, HD), head),
        ],
        out_specs=[
            pl.BlockSpec((slots, HD), head),
            pl.BlockSpec((tok, HD), head),
            pl.BlockSpec((tok, HD), head),
        ],
        out_shape=[
            jax.ShapeDtypeStruct((slots, width), BF16),
            jax.ShapeDtypeStruct((tok, width), BF16),
            jax.ShapeDtypeStruct((tok, width), BF16),
        ],
        scratch_shapes=[pltpu.VMEM((tok, HD), F32), pltpu.VMEM((tok, HD), F32)],
        compiler_params=pltpu.CompilerParams(vmem_limit_bytes=40 << 20),
        cost_estimate=pl.CostEstimate(
            flops=0, bytes_accessed=slots * width, transcendentals=0
        ),
    )(q, k, v, bias, gate, *slot_tables, *tok_tables, grad_gated)


class Square:
    def __init__(self):
        me = lax.axis_index("dp")
        self.core = lax.rem(me, 2)
        self.chip = me // 2
        x, y = lax.rem(self.chip, 2), self.chip // 2
        self.chip_x = self.chip + 1 - 2 * x
        self.chip_y = self.chip + 2 - 4 * y
        self.chip_far = 3 - self.chip
        self.twin = me + 1 - 2 * self.core
        self.near_x = 2 * self.chip_x + self.core
        self.near_y = 2 * self.chip_y + self.core


def send_to(source, target, send_sem, recv_sem, device):
    return pltpu.make_async_remote_copy(
        src_ref=source,
        dst_ref=target,
        send_sem=send_sem,
        recv_sem=recv_sem,
        device_id={"dp": device},
        device_id_type=pl.DeviceIdType.MESH,
    )


def greet(places):
    barrier = pltpu.get_barrier_semaphore()
    for place in places:
        pl.semaphore_signal(
            barrier, inc=1, device_id=place, device_id_type=pl.DeviceIdType.MESH
        )
    pl.semaphore_wait(barrier, len(places))


def send_across(source, target, send_sem, recv_sem, device):
    return pltpu.make_async_remote_copy(
        src_ref=source,
        dst_ref=target,
        send_sem=send_sem,
        recv_sem=recv_sem,
        device_id={"tensor": device},
        device_id_type=pl.DeviceIdType.MESH,
    )


def tensor_peers(count):
    z = lax.axis_index("tensor")
    return [lax.rem(z + k, count) for k in range(1, count)]


def share_rows(size):
    return pl.ds(pl.multiple_of(lax.axis_index("tensor") * size, size), size)


def rows_of(place, size):
    return pl.ds(pl.multiple_of(place * size, size), size)


def spread(count, source, target, sems):
    size = source.shape[0] // count
    copies = [
        send_to(
            source.at[pl.ds(k * size, size)], target.at[pl.ds(k * size, size)],
            sems[0].at[k], sems[1].at[k], partner(k),
        )
        for k in range(1, count)
    ]
    here = pltpu.make_async_copy(
        source.at[pl.ds(0, size)], target.at[pl.ds(0, size)], sems[0].at[0]
    )
    for copy in (*copies, here):
        copy.start()
    return (*copies, here)


def gather_kernel(axes, chunks, *refs):
    amount = len(axes)
    sources, rows = refs[:amount], refs[amount]
    targets, rows_out = refs[amount + 1 : 2 * amount + 1], refs[2 * amount + 1]
    send_sem, recv_sem, own_sem, e_send, e_recv, z_send, z_recv = refs[2 * amount + 2 :]
    count = z_send.shape[0] + 1
    exchange_count = e_send.shape[0]
    peers = tensor_peers(count)
    at = Square()
    me = 2 * at.chip + at.core
    far = 2 * at.chip_far + at.core
    greet(
        [{"dp": partner(k)} for k in range(1, exchange_count)] + [{"tensor": p} for p in peers]
    )
    columns = share_rows(rows.shape[1] // count)
    size = rows.shape[0] // exchange_count
    moved = [
        send_to(
            rows.at[pl.ds(k * size, size), columns], rows_out.at[pl.ds(k * size, size), columns],
            e_send.at[k], e_recv.at[k], partner(k),
        )
        for k in range(1, exchange_count)
    ]
    stay = pltpu.make_async_copy(
        rows.at[pl.ds(0, size), columns], rows_out.at[pl.ds(0, size), columns], e_send.at[0]
    )
    for copy in (*moved, stay):
        copy.start()

    def region(ref, axis, source, place, experts):
        size = source.shape[axis]
        at_place = pl.ds(pl.multiple_of(place * size, size), size)
        return ref.at[experts, at_place] if axis == 1 else ref.at[experts, :, at_place]

    first = 0
    plans = []
    for i in range(amount):
        count = sources[i].shape[0] // chunks[i]
        plans.append((i, first, count))
        first += count

    def copies(i, first, n):
        source, target, axis, size = sources[i], targets[i], axes[i], chunks[i]
        half = size // 2
        whole = pl.ds(n * size, size)
        top, bottom = pl.ds(n * size, half), pl.ds(n * size + half, half)
        unit = first + n

        def move(slot, place, experts, device, own=False):
            there = region(target, axis, source, place, experts)
            return send_to(
                source.at[experts] if own else there, there,
                send_sem.at[unit, slot], recv_sem.at[unit, slot], device,
            )

        return [
            functools.partial(move, 0, me, whole, at.near_x, True),
            functools.partial(move, 1, me, whole, at.near_y, True),
            functools.partial(move, 2, at.near_y, top, at.near_x),
            functools.partial(move, 3, at.near_x, bottom, at.near_y),
            functools.partial(move, 4, me, whole, at.twin, True),
            functools.partial(move, 5, at.near_x, whole, at.twin),
            functools.partial(move, 6, at.near_y, whole, at.twin),
            functools.partial(move, 7, far, top, at.twin),
            functools.partial(move, 8, far, bottom, at.twin),
        ]

    here = [
        pltpu.make_async_copy(
            sources[i], region(targets[i], axes[i], sources[i], me, pl.ds(0, sources[i].shape[0])),
            own_sem.at[i],
        )
        for i in range(amount)
    ]
    for i, first, count in plans:

        @pl.loop(0, count)
        def _(n):
            moves = copies(i, first, n)
            for slot in (0, 1, 4):
                moves[slot]().start()

    for copy in here:
        copy.start()
    for i, first, count in plans:

        @pl.loop(0, count)
        def _(n):
            moves = copies(i, first, n)
            moves[0]().wait_recv()
            moves[3]().start()
            moves[5]().start()
            moves[1]().wait_recv()
            moves[2]().start()
            moves[6]().start()

        if i == 0:
            stay.wait()
            for copy in moved:
                copy.wait_recv()
            across = [
                send_across(
                    rows_out.at[:, columns], rows_out.at[:, columns], z_send.at[k], z_recv.at[k], p
                )
                for k, p in enumerate(peers)
            ]
            for copy in across:
                copy.start()

    for i, first, count in plans:

        @pl.loop(0, count)
        def _(n):
            moves = copies(i, first, n)
            moves[2]().wait_recv()
            moves[7]().start()
            moves[3]().wait_recv()
            moves[8]().start()

    for i, first, count in plans:

        @pl.loop(0, count)
        def _(n):
            moves = copies(i, first, n)
            for slot in (4, 5, 6, 7, 8):
                moves[slot]().wait_recv()
            for move in moves:
                move().wait_send()

    for copy in (*here, *across):
        copy.wait()
    for copy in moved:
        copy.wait_send()


def gather_maps(tensor_size, peers, arrays, axes, chunks, rows):
    units = sum(a.shape[0] // c for a, c in zip(arrays, chunks))
    shapes = [
        tuple(n * 8 if d == axis else n for d, n in enumerate(a.shape))
        for a, axis in zip(arrays, axes)
    ]
    return pl.pallas_call(
        functools.partial(gather_kernel, axes, chunks),
        in_specs=[HBM] * (len(arrays) + 1),
        out_specs=[HBM] * (len(arrays) + 1),
        out_shape=[jax.ShapeDtypeStruct(shape, BF16) for shape in (*shapes, rows.shape)],
        scratch_shapes=[
            sems(units, 9), sems(units, 9), sems(len(arrays)), sems(peers), sems(peers),
            sems(tensor_size - 1), sems(tensor_size - 1),
        ],
        compiler_params=pltpu.CompilerParams(collective_id=5, has_side_effects=True),
        cost_estimate=pl.CostEstimate(flops=0, bytes_accessed=600 << 20, transcendentals=0),
    )(*arrays, rows)


def deal(source, target, sems, rows=None):
    me = lax.axis_index("dp")

    def block(place):
        return source.at[place] if rows is None else source.at[place, rows]

    copies = [
        send_to(block(partner(k)), target.at[me], sems[0].at[k], sems[1].at[k], partner(k))
        for k in range(1, source.shape[0])
    ]
    copies.append(pltpu.make_async_copy(block(me), target.at[me], sems[0].at[0]))
    for copy in copies:
        copy.start()
    return copies


def norm_back(total, products, hots, router, base, gain, hot_out, gain_out):
    first, second = products
    weights = hots[0] * first + hots[1] * second - hots[2] * (first + second)
    hot_out[...] = weights.astype(BF16)
    total = total + dot_nt(hot_out[...], router[...])
    scale = lax.rsqrt(jnp.mean(base * base, axis=-1, keepdims=True) + EPSILON)
    normal = base * scale
    gain_out[...] = jnp.sum(total * normal, axis=0, keepdims=True)
    weighted = total * gain
    return scale * (weighted - normal * jnp.mean(weighted * normal, axis=-1, keepdims=True))


def three_columns(block):
    return block[:, 0:1] + block[:, 1:2] + block[:, 2:3]


def in_columns(column, lane):
    high = column.astype(BF16).astype(F32)
    mid = (column - high).astype(BF16).astype(F32)
    return jnp.where(
        lane == 0, high, jnp.where(lane == 1, mid, jnp.where(lane == 2, column - high - mid, 0.0))
    ).astype(BF16)


def hidden_kernel(
    pick, rows, x_here, gain, router, hot_0, hot_1, hit_0, hit_1, maps_hbm,
    hidden_out, mlp_in_out, gates_out, x_out, maps_out,
    parts, sent, got, z_send, z_recv, g_send, g_recv, d_send, d_recv,
):
    count = z_send.shape[0] + 1
    width = rows.shape[1]
    tokens = pick.shape[1]
    size = tokens // count
    peers = tensor_peers(count)
    greet(
        [{"dp": partner(k)} for k in range(1, d_send.shape[0])] + [{"tensor": p} for p in peers]
    )
    dealt = deal(maps_hbm, maps_out, (d_send, d_recv))

    @pl.loop(0, width // 512)
    def _(i):
        at = pl.ds(pl.multiple_of(i * 512, 512), 512)
        piece = dot_tn(pick[...], rows[:, at])
        parts[:, at] = piece
        sent[:, at] = piece.astype(BF16)

    copies = [
        send_across(sent.at[rows_of(p, size)], got.at[k], z_send.at[k], z_recv.at[k], p)
        for k, p in enumerate(peers)
    ]
    for copy in copies:
        copy.start()
    here = share_rows(size)
    hidden_out[...] = x_here[...].astype(F32) + parts[here, :]
    for k, copy in enumerate(copies):
        copy.wait_recv()
        hidden_out[...] += got[k].astype(F32)
    hidden = hidden_out[...]
    scale = lax.rsqrt(jnp.mean(hidden * hidden, axis=-1, keepdims=True) + EPSILON)
    mlp_in_out[here, :] = (hidden * scale * gain[...]).astype(BF16)
    more = [
        send_across(
            mlp_in_out.at[here], mlp_in_out.at[here], g_send.at[k], g_recv.at[k], p
        )
        for k, p in enumerate(peers)
    ]
    for copy in more:
        copy.start()
    for copy in copies:
        copy.wait_send()
    for copy in more:
        copy.wait()

    logits = dot(mlp_in_out[...], router[...])
    picked = [jnp.sum(logits * hot[...], axis=1, keepdims=True) for hot in (hot_0, hot_1)]
    highest = jnp.maximum(picked[0], picked[1])
    raised = [jnp.exp(value - highest) for value in picked]
    gates = [value / (raised[0] + raised[1]) for value in raised]
    lane = lax.broadcasted_iota(jnp.int32, (tokens, HD), 1)
    gates_out[...] = jnp.where(lane == 0, gates[0], jnp.where(lane == 1, gates[1], 0.0))
    columns = [in_columns(gate, lane) for gate in gates]
    x_out[:, width:] = (dot(hit_0[...], columns[0]) + dot(hit_1[...], columns[1])).astype(BF16)

    @pl.loop(0, width // 512)
    def _(i):
        at = pl.ds(pl.multiple_of(i * 512, 512), 512)
        x_out[:, at] = dot(hit_0[...] + hit_1[...], mlp_in_out[:, at]).astype(BF16)
    for copy in dealt:
        copy.wait()


VMEM = pl.BlockSpec(memory_space=pltpu.VMEM)
HBM = pl.BlockSpec(memory_space=pl.ANY)


def sems(*shape):
    return pltpu.SemaphoreType.DMA(shape)


def hidden_step(tensor_size, pick, rows, x_here, gain, router, hots, hits, maps):
    tokens, width = pick.shape[1], rows.shape[1]
    slots = hits[0].shape[0]
    size = tokens // tensor_size
    around = tensor_size - 1
    return pl.pallas_call(
        hidden_kernel,
        in_specs=[VMEM] * 9 + [HBM],
        out_specs=[VMEM] * 4 + [HBM],
        out_shape=[
            jax.ShapeDtypeStruct((size, width), F32),
            jax.ShapeDtypeStruct((tokens, width), BF16),
            jax.ShapeDtypeStruct((tokens, HD), F32),
            jax.ShapeDtypeStruct((slots, width + HD), BF16),
            jax.ShapeDtypeStruct(maps.shape, BF16),
        ],
        scratch_shapes=[
            pltpu.VMEM((tokens, width), F32),
            pltpu.VMEM((tokens, width), BF16),
            pltpu.VMEM((around, size, width), BF16),
            sems(around), sems(around), sems(around), sems(around),
            sems(maps.shape[0]), sems(maps.shape[0]),
        ],
        compiler_params=pltpu.CompilerParams(
            collective_id=3, has_side_effects=True, vmem_limit_bytes=48 << 20
        ),
        cost_estimate=pl.CostEstimate(
            flops=2 * pick.shape[0] * tokens * width, bytes_accessed=300 << 20, transcendentals=0
        ),
    )(pick, rows, x_here, gain, router, *hots, *hits, maps)


def back_kernel(
    back, pick, hit_0, hit_1, hidden, cot_here, gain, router, hots, gates, att_pick, gated,
    rows_hbm, gate_hbm, up_hbm,
    grad_out, pair_out, gain_out, hot_out, mixed_out, att_rows, gate_maps, up_maps, grad_output,
    parts, sent, got, z_send, z_recv, g_send, g_recv, e_send, e_recv, w_send, w_recv, u_send, u_recv,
    rows_in, columns_here, mlp_got, m_send, m_recv, own, stage, stage_sem,
):
    count = z_send.shape[0] + 1
    width = back.shape[1] - HD
    tokens = pick.shape[1]
    size = tokens // count
    peers = tensor_peers(count)
    exchange_count = e_send.shape[0]
    greet(
        [{"dp": partner(k)} for k in range(1, exchange_count)] + [{"tensor": p} for p in peers]
    )
    moves = spread(exchange_count, rows_hbm, rows_in, (e_send, e_recv))
    dealt = deal(gate_hbm, gate_maps, (w_send, w_recv))
    dealt += deal(up_hbm, up_maps, (u_send, u_recv))

    @pl.loop(0, width // 512)
    def _(i):
        at = pl.ds(pl.multiple_of(i * 512, 512), 512)
        piece = dot_tn(pick[...], back[:, at])
        parts[:, at] = piece
        sent[:, at] = piece.astype(BF16)

    for k, hit in enumerate((hit_0, hit_1)):
        at = pl.ds(width + k * HD, HD)
        piece = dot_tn(hit[...], back[:, width:])
        parts[:, at] = piece
        sent[:, at] = piece.astype(BF16)

    copies = [
        send_across(sent.at[rows_of(p, size)], got.at[k], z_send.at[k], z_recv.at[k], p)
        for k, p in enumerate(peers)
    ]
    for copy in copies:
        copy.start()
    here = share_rows(size)
    total = parts[here, :]
    for k, copy in enumerate(copies):
        copy.wait_recv()
        total = total + got[k].astype(F32)
    products = (
        three_columns(total[:, width : width + HD]), three_columns(total[:, width + HD :])
    )
    grad_out[...] = cot_here[...].astype(F32) + norm_back(
        total[:, :width], products, hots, router, hidden[...], gain[...], hot_out, gain_out
    )
    pair_out[here, :] = grad_out[...].astype(BF16)
    more = [
        send_across(pair_out.at[here], pair_out.at[here], g_send.at[k], g_recv.at[k], p)
        for k, p in enumerate(peers)
    ]
    for copy in more:
        copy.start()
    for copy in moves:
        copy.wait()
    matrix = hit_0[...].astype(F32) * gates[0:1, :] + hit_1[...].astype(F32) * gates[1:2, :]
    high = matrix.astype(BF16)
    low = (matrix - high.astype(F32)).astype(BF16)
    columns_here[...] = (dot_tn(high, rows_in[...]) + dot_tn(low, rows_in[...])).astype(BF16)
    columns = share_rows(width // count)
    turned = [
        send_across(
            columns_here.at[rows_of(p, size)], mlp_got.at[:, columns], m_send.at[k], m_recv.at[k],
            p,
        )
        for k, p in enumerate(peers)
    ]
    turned.append(
        pltpu.make_async_copy(columns_here.at[here], mlp_got.at[:, columns], own.at[0])
    )
    for copy in turned:
        copy.start()
    for copy in turned:
        copy.wait()
    mixed_out[...] = (hidden[...] + mlp_got[...].astype(F32)).astype(BF16)
    for copy in copies:
        copy.wait_send()
    for copy in more:
        copy.wait()

    @pl.loop(0, width // 512)
    def _(i):
        at = rows_of(i, 512)
        att_rows[:, at] = dot(att_pick[...], pair_out[:, at]).astype(BF16)

    experts, cap = grad_output.shape[0], gated.shape[0] // grad_output.shape[0]

    def store(e):
        slot = lax.rem(e, 2)
        return pltpu.make_async_copy(stage.at[slot], grad_output.at[e], stage_sem.at[slot])

    @pl.loop(0, experts)
    def _(e):
        @pl.when(e > 1)
        def _():
            store(e - 2).wait()

        at = rows_of(e, cap)
        stage[lax.rem(e, 2)] = dot_tn(gated[at, :], att_rows[at, :]).astype(BF16)
        store(e).start()

    for e in (experts - 2, experts - 1):
        store(e).wait()
    for copy in dealt:
        copy.wait()


def back_step(
    tensor_size, peers, back, pick, hits, hidden, cot_here, gain, router, hots, gates,
    att_pick, gated, experts, rows_send, gate_maps, up_maps,
):
    tokens, width = pick.shape[1], back.shape[1] - HD
    size = tokens // tensor_size
    around = tensor_size - 1
    wide = width + 2 * HD
    return pl.pallas_call(
        back_kernel,
        in_specs=[VMEM] * 12 + [HBM] * 3,
        out_specs=[VMEM] * 6 + [HBM] * 3,
        out_shape=[
            jax.ShapeDtypeStruct((size, width), F32),
            jax.ShapeDtypeStruct((tokens, width), BF16),
            jax.ShapeDtypeStruct((1, width), F32),
            jax.ShapeDtypeStruct((size, HD), BF16),
            jax.ShapeDtypeStruct((size, width), BF16),
            jax.ShapeDtypeStruct((att_pick.shape[0], width), BF16),
            jax.ShapeDtypeStruct(gate_maps.shape, BF16),
            jax.ShapeDtypeStruct(up_maps.shape, BF16),
            jax.ShapeDtypeStruct((experts, gated.shape[1], width), BF16),
        ],
        scratch_shapes=[
            pltpu.VMEM((tokens, wide), F32),
            pltpu.VMEM((tokens, wide), BF16),
            pltpu.VMEM((around, size, wide), BF16),
            sems(around), sems(around), sems(around), sems(around), sems(peers), sems(peers),
            sems(peers), sems(peers), sems(peers), sems(peers),
            pltpu.VMEM(rows_send.shape, BF16),
            pltpu.VMEM((tokens, width // tensor_size), BF16),
            pltpu.VMEM((size, width), BF16),
            sems(around), sems(around), sems(1),
            pltpu.VMEM((2, gated.shape[1], width), BF16),
            sems(2),
        ],
        compiler_params=pltpu.CompilerParams(
            collective_id=4, has_side_effects=True, vmem_limit_bytes=56 << 20
        ),
        cost_estimate=pl.CostEstimate(
            flops=2 * pick.shape[0] * tokens * width, bytes_accessed=300 << 20, transcendentals=0
        ),
    )(back, pick, hits[0], hits[1], hidden, cot_here, gain, router, hots, gates, att_pick, gated, rows_send, gate_maps, up_maps)


GIVE = 4
HALF_SMALL = 8


def final_kernel(
    routed_hbm, grad_q, normed, grad_kv, part_hbm,
    grad_hidden, x_here, gain, router, hots, small, maps_hbm,
    out, tokens_out, small_out, maps_out,
    give, keep, twin_in, far_in, near_in, routed, got_part, tokens_here,
    twin_send, twin_recv, far_send, far_recv, near_send, near_recv, load, own,
    p_send, p_recv, t_send, t_recv,
    hot_here, small_all, small_in, small_sum, small_got,
    s_send, s_recv, w_send, w_recv, d_send, d_recv,
):
    at = Square()
    experts = grad_q.shape[0]
    units, _, size, _ = keep.shape
    half = size // 2
    count = p_send.shape[0] + 1
    peers = tensor_peers(count)
    width = normed.shape[1]
    share = part_hbm.shape[0] // count

    def fetch(u):
        return pltpu.make_async_copy(
            routed_hbm.at[u], routed.at[lax.rem(u, 2)], load.at[lax.rem(u, 2)]
        )

    fetch(0).start()
    here = share_rows(share)
    mine = pltpu.make_async_copy(part_hbm.at[here], got_part.at[count - 1], own.at[0])
    mine.start()
    greet([{"dp": partner(k)} for k in range(1, 8)] + [{"tensor": p} for p in peers])
    part_copies = [
        send_across(part_hbm.at[rows_of(p, share)], got_part.at[k], p_send.at[k], p_recv.at[k], p)
        for k, p in enumerate(peers)
    ]
    for copy in part_copies:
        copy.start()

    def to_twin(u):
        slot = lax.rem(u, GIVE)
        return send_to(give.at[slot], twin_in.at[u], twin_send.at[slot], twin_recv.at[u], at.twin)

    def to_far(u):
        first = send_to(
            keep.at[u, at.chip_far, pl.ds(0, half)],
            far_in.at[u, 0], far_send.at[u, 0], far_recv.at[u, 0], at.near_x,
        )
        second = send_to(
            keep.at[u, at.chip_far, pl.ds(half, half)],
            far_in.at[u, 1], far_send.at[u, 1], far_recv.at[u, 1], at.near_y,
        )
        return first, second

    def to_near(u):
        first = send_to(
            keep.at[u, at.chip_x], near_in.at[u, 0], near_send.at[u, 0], near_recv.at[u, 0],
            at.near_x,
        )
        second = send_to(
            keep.at[u, at.chip_y], near_in.at[u, 1], near_send.at[u, 1], near_recv.at[u, 1],
            at.near_y,
        )
        return first, second

    def multiply(u, rows, grads):
        slot = lax.rem(u, GIVE)

        @pl.when(u >= GIVE)
        def _():
            to_twin(u - GIVE).wait_send()

        for chip in range(4):
            columns = rows_of(2 * chip + 1 - at.core, size)
            give[slot, chip] = dot_tn(rows[:, columns], grads[...]).astype(BF16)
        to_twin(u).start()
        for chip in range(4):
            columns = rows_of(2 * chip + at.core, size)
            keep[u, chip] = dot_tn(rows[:, columns], grads[...]).astype(BF16)

    def join_twin(u):
        to_twin(u).wait_recv()

        def add(chip):
            keep[u, chip] = (keep[u, chip].astype(F32) + twin_in[u, chip].astype(F32)).astype(BF16)

        add(at.chip_far)
        for copy in to_far(u):
            copy.start()
        add(at.chip_x)
        add(at.chip_y)
        add(at.chip)

    @pl.loop(0, experts)
    def _(u):
        fetch(u).wait()

        @pl.when(u < experts - 1)
        def _():
            fetch(u + 1).start()

        multiply(u, routed.at[lax.rem(u, 2)], grad_q.at[u])

        @pl.when(u > 0)
        def _():
            join_twin(u - 1)

    @pl.loop(experts, units)
    def _(u):
        multiply(u, normed, grad_kv.at[u - experts])
        join_twin(u - 1)

    join_twin(units - 1)

    mine.wait()
    total = got_part[count - 1].astype(F32)
    for k, copy in enumerate(part_copies):
        copy.wait_recv()
        total = total + got_part[k].astype(F32)
    products = (
        three_columns(total[:, width : width + HD]), three_columns(total[:, width + HD :])
    )
    tokens_here[...] = (
        grad_hidden[...]
        + norm_back(
            total[:, :width], products, hots, router, x_here[...].astype(F32), gain[...],
            hot_here, small_all.at[pl.ds(0, 1)],
        )
    ).astype(BF16)
    token_copies = [
        send_across(tokens_here, tokens_out.at[here], t_send.at[k], t_recv.at[k], p)
        for k, p in enumerate(peers)
    ]
    for copy in token_copies:
        copy.start()
    kept = pltpu.make_async_copy(tokens_here, tokens_out.at[here], own.at[1])
    kept.start()

    small_all[1:HALF_SMALL, :] = small[1:HALF_SMALL, :]
    small_all[HALF_SMALL : 2 * HALF_SMALL, :] = dot_tn(hot_here[...], normed[here, :])[:HALF_SMALL]
    small_all[2 * HALF_SMALL :, :] = small[HALF_SMALL:, :]

    def small_block(place):
        return small_all.at[:, rows_of(place, size)]

    small_copies = [
        send_to(
            small_block(partner(k)), small_in.at[k], s_send.at[k], s_recv.at[k], partner(k)
        )
        for k in range(1, 8)
    ]
    for copy in small_copies:
        copy.start()

    @pl.loop(0, units)
    def _(u):
        for copy in to_far(u):
            copy.wait_recv()
        top, bottom = pl.ds(0, half), pl.ds(half, half)
        keep[u, at.chip_y, top, :] = (
            keep[u, at.chip_y, top, :].astype(F32) + far_in[u, 0].astype(F32)
        ).astype(BF16)
        keep[u, at.chip_x, bottom, :] = (
            keep[u, at.chip_x, bottom, :].astype(F32) + far_in[u, 1].astype(F32)
        ).astype(BF16)
        for copy in to_near(u):
            copy.start()

    late = maps_out.shape[1]
    dealt = deal(maps_hbm, maps_out, (d_send, d_recv), pl.ds(maps_hbm.shape[1] - late, late))

    @pl.loop(0, units)
    def _(u):
        for copy in to_near(u):
            copy.wait_recv()
        out[u] = (
            keep[u, at.chip].astype(F32) + near_in[u, 0].astype(F32) + near_in[u, 1].astype(F32)
        ).astype(BF16)

    block = small_all[:, rows_of(2 * at.chip + at.core, size)]
    for k, copy in enumerate(small_copies):
        copy.wait_recv()
        block = block + small_in[k + 1]
    small_sum[...] = block
    last_copies = [
        send_across(small_sum, small_got.at[k], w_send.at[k], w_recv.at[k], p)
        for k, p in enumerate(peers)
    ]
    for copy in last_copies:
        copy.start()

    @pl.loop(units - GIVE, units)
    def _(u):
        to_twin(u).wait_send()

    @pl.loop(0, units)
    def _(u):
        for copy in (*to_far(u), *to_near(u)):
            copy.wait_send()

    for k, copy in enumerate(last_copies):
        copy.wait_recv()
        block = block + small_got[k]
    small_out[...] = block
    for copy in (*part_copies, *small_copies, *last_copies):
        copy.wait_send()
    for copy in (*token_copies, *dealt, kept):
        copy.wait()


def final_step(
    tensor_size, routed, grad_q, normed, grad_kv, part, grad_hidden, x_here, gain,
    router, hots, small, maps, late,
):
    experts, rows, width = routed.shape
    columns = grad_q.shape[2]
    units = experts + grad_kv.shape[0]
    size = width // 8
    tokens, wide = part.shape
    share = tokens // tensor_size
    around = tensor_size - 1
    return pl.pallas_call(
        final_kernel,
        in_specs=[HBM, VMEM, VMEM, VMEM, HBM] + [VMEM] * 6 + [HBM],
        out_specs=[VMEM, HBM, VMEM, HBM],
        out_shape=[
            jax.ShapeDtypeStruct((units, size, columns), BF16),
            jax.ShapeDtypeStruct((tokens, width), BF16),
            jax.ShapeDtypeStruct((3 * HALF_SMALL, size), F32),
            jax.ShapeDtypeStruct((maps.shape[0], late) + maps.shape[2:], BF16),
        ],
        scratch_shapes=[
            pltpu.VMEM((GIVE, 4, size, columns), BF16),
            pltpu.VMEM((units, 4, size, columns), BF16),
            pltpu.VMEM((units, 4, size, columns), BF16),
            pltpu.VMEM((units, 2, size // 2, columns), BF16),
            pltpu.VMEM((units, 2, size, columns), BF16),
            pltpu.VMEM((2, rows, width), BF16),
            pltpu.VMEM((tensor_size, share, wide), BF16),
            pltpu.VMEM((share, width), BF16),
            sems(GIVE), sems(units), sems(units, 2), sems(units, 2), sems(units, 2),
            sems(units, 2), sems(2), sems(3),
            sems(around), sems(around), sems(around), sems(around),
            pltpu.VMEM((share, HD), BF16),
            pltpu.VMEM((3 * HALF_SMALL, width), F32),
            pltpu.VMEM((8, 3 * HALF_SMALL, size), F32),
            pltpu.VMEM((3 * HALF_SMALL, size), F32),
            pltpu.VMEM((around, 3 * HALF_SMALL, size), F32),
            sems(8), sems(8), sems(around), sems(around), sems(8), sems(8),
        ],
        compiler_params=pltpu.CompilerParams(
            collective_id=1, has_side_effects=True, vmem_limit_bytes=60 << 20
        ),
        cost_estimate=pl.CostEstimate(flops=0, bytes_accessed=1 << 20, transcendentals=0),
    )(
        routed, grad_q, normed, grad_kv, part, grad_hidden, x_here, gain, router, hots, small,
        maps,
    )


def widen_kernel(first, second, third, fourth, both_out, third_out):
    both_out[:, 0] = first[...].astype(F32)
    both_out[:, 1] = second[...].astype(F32)
    early = third.shape[1]
    third_out[:, 0:early] = third[...].astype(F32)
    third_out[:, early:] = fourth[...].astype(F32)


def widen(first, second, third, fourth):
    experts, rows, columns = first.shape
    narrow = pl.BlockSpec((1, rows, columns), lambda e: (e, 0, 0))
    whole = (experts, third.shape[1] + fourth.shape[1], third.shape[2])

    def block(shape):
        return pl.BlockSpec((1,) + shape[1:], lambda e: (e, 0, 0))

    return pl.pallas_call(
        widen_kernel,
        grid=(experts,),
        in_specs=[narrow, narrow, block(third.shape), block(fourth.shape)],
        out_specs=[pl.BlockSpec((1, 2, rows, columns), lambda e: (e, 0, 0, 0)), block(whole)],
        out_shape=[
            jax.ShapeDtypeStruct((experts, 2, rows, columns), F32),
            jax.ShapeDtypeStruct(whole, F32),
        ],
        compiler_params=pltpu.CompilerParams(vmem_limit_bytes=32 << 20),
        cost_estimate=pl.CostEstimate(
            flops=0, bytes_accessed=6 * (2 * first.size + third.size + fourth.size), transcendentals=0
        ),
    )(first, second, third, fourth)


def turn_kernel(
    rows, q_ref, k_ref, v_ref, bias, gate, slot_cos, slot_sin, tok_cos, tok_sin, attended,
    hit_0, hit_1, mixed_here, output_hbm, query_hbm, keyval_hbm, maps_hbm,
    gq_out, gkv_out, part_out, maps_out, mixed_out,
    grad_gated, grad_routed, weight, product, gk_sum, gv_sum,
    load, d_send, d_recv, a_send, a_recv, own,
):
    count = a_send.shape[0] + 1
    peers = tensor_peers(count)
    experts, cap, width = rows.shape
    slots, here_width = q_ref.shape
    heads = here_width // HD
    step = 256
    greet(
        [{"dp": partner(k)} for k in range(1, d_send.shape[0])] + [{"tensor": p} for p in peers]
    )
    dealt = deal(maps_hbm, maps_out, (d_send, d_recv), pl.ds(0, maps_out.shape[1]))
    here = share_rows(mixed_here.shape[0])
    mixed_copies = [
        send_across(mixed_here, mixed_out.at[here], a_send.at[k], a_recv.at[k], p)
        for k, p in enumerate(peers)
    ]
    mixed_copies.append(pltpu.make_async_copy(mixed_here, mixed_out.at[here], own.at[0]))
    for copy in mixed_copies:
        copy.start()

    def fetch_output(e):
        slot = lax.rem(e, 2)
        return pltpu.make_async_copy(output_hbm.at[e], weight.at[slot], load.at[slot])

    def fetch_query(e, half):
        size = width // 2
        return pltpu.make_async_copy(
            query_hbm.at[e, pl.ds(half * size, size)], weight_rows(half), load.at[2 + half]
        )

    def weight_rows(half):
        return turned.at[half]

    turned = grad_routed[1]
    routed_out = grad_routed[0]

    fetch_output(0).start()

    @pl.loop(0, experts)
    def _(e):
        fetch_output(e).wait()

        @pl.when(e < experts - 1)
        def _():
            fetch_output(e + 1).start()

        at = pl.ds(pl.multiple_of(e * cap, cap), cap)
        grad_gated[at, :] = dot_nt(rows[e], weight[lax.rem(e, 2)])

    fetch_query(0, 0).start()
    fetch_query(0, 1).start()

    @pl.loop(0, heads)
    def _(h):
        lanes = rows_of(h, HD)
        gk_sum[...] = jnp.zeros_like(gk_sum)
        gv_sum[...] = jnp.zeros_like(gv_sum)

        @pl.loop(0, slots // step)
        def _(i):
            at = pl.ds(pl.multiple_of(i * step, step), step)
            q = q_ref[at, lanes]
            keys, values = k_ref[:, lanes], v_ref[:, lanes]
            probs = softmax_block(q, keys, bias[at, :].astype(F32))
            scaled = grad_gated[at, lanes] * gate[at, :]
            joined = scaled * attended[at, lanes]

            @pl.when(h == 0)
            def _():
                product[at, :] = joined

            @pl.when(h > 0)
            def _():
                product[at, :] += joined

            grad_att = scaled.astype(BF16)
            grad_probs = dot_nt(grad_att, values)
            centre = jnp.sum(probs * grad_probs, axis=-1, keepdims=True)
            grad_scores = (probs * (grad_probs - centre)).astype(BF16)
            grad_q = dot(grad_scores, keys) * HD ** (-0.5)
            gq_out[at, lanes] = rope_back(grad_q, slot_cos[at, :], slot_sin[at, :]).astype(BF16)
            gk_sum[...] += dot_tn(grad_scores, q)
            gv_sum[...] += dot_tn(probs.astype(BF16), grad_att)

        grad_k = gk_sum[...] * HD ** (-0.5)
        gkv_out[0, :, lanes] = rope_back(grad_k, tok_cos[...], tok_sin[...]).astype(BF16)
        gkv_out[1, :, lanes] = gv_sum[...].astype(BF16)

    @pl.loop(0, experts)
    def _(e):
        at = pl.ds(pl.multiple_of(e * cap, cap), cap)
        for half in range(2):
            fetch_query(e, half).wait()
            routed_out[at, pl.ds(half * (width // 2), width // 2)] = dot_nt(
                gq_out[at, :], turned[half]
            ).astype(BF16)

            @pl.when(e < experts - 1)
            def _():
                fetch_query(e + 1, half).start()

    def fetch_keyval(i):
        slot = lax.rem(i, 2)
        block = pl.ds(pl.multiple_of(i * 512, 512), 512)
        return [
            pltpu.make_async_copy(
                keyval_hbm.at[c, block], turned.at[slot, pl.ds(c * 512, 512)],
                load.at[4 + 2 * slot + c],
            )
            for c in range(2)
        ]

    for copy in fetch_keyval(0):
        copy.start()

    @pl.loop(0, width // 512)
    def _(i):
        for copy in fetch_keyval(i):
            copy.wait()

        @pl.when(i < width // 512 - 1)
        def _():
            for copy in fetch_keyval(i + 1):
                copy.start()

        at = rows_of(i, 512)
        maps = turned.at[lax.rem(i, 2)]
        part_out[:, at] = (
            dot_tn(hit_0[...] + hit_1[...], routed_out[:, at])
            + dot_nt(gkv_out[0], maps[0:512, :])
            + dot_nt(gkv_out[1], maps[512:1024, :])
        ).astype(BF16)

    columns = in_columns(
        jnp.sum(product[...], axis=1, keepdims=True),
        lax.broadcasted_iota(jnp.int32, (slots, HD), 1),
    )
    part_out[:, width : width + HD] = dot_tn(hit_0[...], columns).astype(BF16)
    part_out[:, width + HD :] = dot_tn(hit_1[...], columns).astype(BF16)
    for copy in (*mixed_copies, *dealt):
        copy.wait()


def turn_step(
    tensor_size, rows, q, k, v, bias, gate, slot_tables, tok_tables, attended, hits, mixed_here,
    output_full, query_full, keyval_full, maps, early,
):
    experts, cap, width = rows.shape
    slots, here_width = q.shape
    tok = k.shape[0]
    around = tensor_size - 1
    return pl.pallas_call(
        lambda *refs: turn_kernel(*refs[:24], (refs[24], refs[25]), *refs[26:]),
        in_specs=[VMEM] * 14 + [HBM] * 4,
        out_specs=[VMEM, VMEM, VMEM, HBM, HBM],
        out_shape=[
            jax.ShapeDtypeStruct((slots, here_width), BF16),
            jax.ShapeDtypeStruct((2, tok, here_width), BF16),
            jax.ShapeDtypeStruct((tok, width + 2 * HD), BF16),
            jax.ShapeDtypeStruct((maps.shape[0], early) + maps.shape[2:], BF16),
            jax.ShapeDtypeStruct((tok, width), BF16),
        ],
        scratch_shapes=[
            pltpu.VMEM((slots, here_width), F32),
            pltpu.VMEM((slots, width), BF16),
            pltpu.VMEM((2, width // 2, here_width), BF16),
            pltpu.VMEM((2, here_width, width), BF16),
            pltpu.VMEM((slots, HD), F32),
            pltpu.VMEM((tok, HD), F32),
            pltpu.VMEM((tok, HD), F32),
            sems(8), sems(8), sems(8), sems(around), sems(around), sems(1),
        ],
        compiler_params=pltpu.CompilerParams(
            collective_id=6, has_side_effects=True, vmem_limit_bytes=58 << 20
        ),
        cost_estimate=pl.CostEstimate(
            flops=10 * slots * tok * here_width, bytes_accessed=300 << 20, transcendentals=0
        ),
    )(
        rows, q, k, v, bias, gate, *slot_tables, *tok_tables, attended, *hits, mixed_here,
        output_full, query_full, keyval_full, maps,
    )


def partner(k):
    me = lax.axis_index("dp")
    place = me
    for bit in (1, 2, 4):
        place = place + bit * lax.rem(k // bit, 2) * (1 - 2 * lax.rem(me // bit, 2))
    return place


def expert_kernel(
    x_hbm, cot_hbm, gate_up_hbm, down_hbm, rest_hbm,
    back_out, rows_out, grad_gate_hbm, grad_up_hbm, grad_down_hbm,
    x_all, g_all, w_gate, w_up, w_down, act, grads, back, product, stage_up, stage_down,
    rows_here, rows_got, x_send, x_recv, b_send, b_recv, load, up_sem, down_sem, r_send, r_recv,
):
    peers = x_send.shape[0]
    slots, wide = x_all.shape
    width = wide - HD
    hidden = w_gate.shape[1]
    size = slots // peers
    pair = 2 * size
    step = 256
    whole_steps = hidden // step
    tail = hidden - whole_steps * step

    per = width // peers
    first = down_hbm.shape[1]
    loads = [
        pltpu.make_async_copy(cot_hbm, g_all, load.at[0]),
        pltpu.make_async_copy(down_hbm, w_down.at[:, pl.ds(0, first)], load.at[1]),
        pltpu.make_async_copy(
            rest_hbm, w_down.at[:, pl.ds(first, hidden - first)], load.at[3 + 2 * peers]
        ),
        pltpu.make_async_copy(
            x_hbm.at[pl.ds(0, size)], x_all.at[pl.ds(0, size)], load.at[2 + 2 * peers]
        ),
    ]
    for j in range(peers):
        for g, target in enumerate((w_gate, w_up)):
            loads.append(
                pltpu.make_async_copy(
                    gate_up_hbm.at[j, g], target.at[pl.ds(j * per, per)], load.at[2 + 2 * j + g]
                )
            )
    for copy in loads:
        copy.start()

    around = tensor_peers(r_send.shape[0] + 1)
    share = width // (len(around) + 1)
    greet([{"dp": partner(k)} for k in range(1, peers)] + [{"tensor": p} for p in around])

    def block(k):
        return pl.ds(pl.multiple_of(k * size, size), size)

    def send_x(k):
        return send_to(
            x_hbm.at[block(k)], x_all.at[block(k)], x_send.at[k], x_recv.at[k], partner(k)
        )

    def send_back(k):
        return send_to(
            back.at[block(k)], back_out.at[block(k)], b_send.at[k], b_recv.at[k], partner(k)
        )

    for k in (1, 2, 4, 3, 5):
        send_x(k).start()
    for copy in loads:
        copy.wait()

    def send_rows(k, group):
        rows = rows_of(group, pair)
        return send_across(
            rows_here.at[rows, rows_of(around[k], share)], rows_got.at[k, rows],
            r_send.at[k, group], r_recv.at[k, group], around[k],
        )

    @pl.loop(0, peers // 2)
    def _(group):
        rows = pl.ds(pl.multiple_of(group * pair, pair), pair)

        @pl.when(group > 0)
        def _():
            send_x(2 * group).wait_recv()

        send_x(2 * group + 1).wait_recv()
        columns = x_all[rows, width:].astype(F32)
        gate_of_row = columns[:, 0:1] + columns[:, 1:2] + columns[:, 2:3]
        g_all[rows, :] = (g_all[rows, :].astype(F32) * gate_of_row).astype(BF16)
        product[...] = jnp.zeros_like(product)

        def chunk(start, amount):
            cols = pl.ds(start, amount)
            x = x_all[rows, 0:width]
            gate = dot(x, w_gate[:, cols])
            up = dot(x, w_up[:, cols])
            grad_act = jnp.zeros((pair, amount), F32)
            for j in range(peers):
                grad_act += dot_nt(g_all[rows, j * per : (j + 1) * per], w_down[j, cols, :])
            sigmoid = 1.0 / (1.0 + jnp.exp(-gate))
            silu = gate * sigmoid
            activated = (silu * up).astype(BF16)
            act[rows, cols] = activated
            both = activated.astype(F32) * grad_act
            for part in range(amount // HD):
                product[...] += both[:, part * HD : (part + 1) * HD]
            grads[rows, cols] = (
                grad_act * up * sigmoid * (1.0 + gate * (1.0 - sigmoid))
            ).astype(BF16)
            grads[rows, pl.ds(hidden + start, amount)] = (grad_act * silu).astype(BF16)

        @pl.loop(0, whole_steps)
        def _(i):
            chunk(pl.multiple_of(i * step, step), step)

        if tail:
            chunk(whole_steps * step, tail)

        @pl.loop(0, width // step)
        def _(i):
            at = pl.ds(pl.multiple_of(i * step, step), step)
            back[rows, at] = (
                dot_nt(grads[rows, 0:hidden], w_gate[at, :])
                + dot_nt(grads[rows, hidden:], w_up[at, :])
            ).astype(BF16)

        total = jnp.sum(product[...], axis=1, keepdims=True)
        back[rows, width:] = in_columns(
            total, lax.broadcasted_iota(jnp.int32, (pair, HD), 1)
        )

        @pl.when(group == 0)
        def _():
            send_x(6).start()
            send_x(7).start()
            back_out[0:size, :] = back[0:size, :]

        @pl.when(group > 0)
        def _():
            send_back(2 * group).start()

        send_back(2 * group + 1).start()
        for j in range(peers):
            rows_here[rows, j * per : (j + 1) * per] = dot(act[rows, :], w_down[j]).astype(BF16)
        for k in range(len(around)):
            send_rows(k, group).start()

    def store_up(j, slot):
        return (
            pltpu.make_async_copy(
                stage_up.at[slot, :, pl.ds(0, hidden)], grad_gate_hbm.at[j], up_sem.at[slot, 0]
            ),
            pltpu.make_async_copy(
                stage_up.at[slot, :, pl.ds(hidden, hidden)], grad_up_hbm.at[j], up_sem.at[slot, 1]
            ),
        )

    @pl.loop(0, peers)
    def _(j):
        slot = lax.rem(j, 2)

        @pl.when(j > 1)
        def _():
            for copy in store_up(j - 2, slot):
                copy.wait()

        at = pl.ds(pl.multiple_of(j * per, per), per)
        stage_up[slot] = dot_tn(x_all[:, at], grads[...]).astype(BF16)
        for copy in store_up(j, slot):
            copy.start()

    def store_down(start, amount, slot):
        return pltpu.make_async_copy(
            stage_down.at[slot, :, pl.ds(0, amount)],
            grad_down_hbm.at[:, pl.ds(start, amount)],
            down_sem.at[slot],
        )

    def down_piece(start, amount, slot):
        piece = dot_tn(act[:, pl.ds(start, amount)], g_all[...]).astype(BF16)
        for j in range(peers):
            stage_down[slot, j, 0:amount, :] = piece[:, j * per : (j + 1) * per]
        store_down(start, amount, slot).start()

    @pl.loop(0, whole_steps)
    def _(i):
        slot = lax.rem(i, 2)

        @pl.when(i > 1)
        def _():
            store_down(pl.multiple_of((i - 2) * step, step), step, slot).wait()

        down_piece(pl.multiple_of(i * step, step), step, slot)

    last = whole_steps - 1
    store_down((last - 1) * step, step, (last - 1) % 2).wait()
    if tail:
        down_piece(whole_steps * step, tail, (last - 1) % 2)
        store_down(whole_steps * step, tail, (last - 1) % 2).wait()
    store_down(last * step, step, last % 2).wait()
    for j in (peers - 2, peers - 1):
        for copy in store_up(j, j % 2):
            copy.wait()

    @pl.loop(0, peers // 2)
    def _(group):
        rows = rows_of(group, pair)
        total = rows_here[rows, share_rows(share)].astype(F32)
        for k in range(len(around)):
            send_rows(k, group).wait()
            total = total + rows_got[k, rows, :].astype(F32)
        rows_out[rows, :] = total.astype(BF16)

    for k in range(1, peers):
        send_x(k).wait_send()
        send_back(k).wait()


def expert_step(tensor_size, x_rows, cot_rows, up_slices, down_slices, down_rest):
    slots, wide = x_rows.shape
    width = wide - HD
    peers, hidden, per = down_slices.shape
    hidden += down_rest.shape[1]
    vmem = pl.BlockSpec(memory_space=pltpu.VMEM)
    hbm = pl.BlockSpec(memory_space=pl.ANY)
    step = 256
    return pl.pallas_call(
        expert_kernel,
        in_specs=[hbm] * 5,
        out_specs=[vmem, vmem, hbm, hbm, hbm],
        out_shape=[
            jax.ShapeDtypeStruct((slots, wide), BF16),
            jax.ShapeDtypeStruct((slots, width // tensor_size), BF16),
            jax.ShapeDtypeStruct((peers, per, hidden), BF16),
            jax.ShapeDtypeStruct((peers, per, hidden), BF16),
            jax.ShapeDtypeStruct((peers, hidden, per), BF16),
        ],
        scratch_shapes=[
            pltpu.VMEM((slots, wide), BF16),
            pltpu.VMEM((slots, width), BF16),
            pltpu.VMEM((width, hidden), BF16),
            pltpu.VMEM((width, hidden), BF16),
            pltpu.VMEM((peers, hidden, per), BF16),
            pltpu.VMEM((slots, hidden), BF16),
            pltpu.VMEM((slots, 2 * hidden), BF16),
            pltpu.VMEM((slots, wide), BF16),
            pltpu.VMEM((2 * slots // peers, HD), F32),
            pltpu.VMEM((2, per, 2 * hidden), BF16),
            pltpu.VMEM((2, peers, step, per), BF16),
            pltpu.VMEM((slots, width), BF16),
            pltpu.VMEM((tensor_size - 1, slots, width // tensor_size), BF16),
            pltpu.SemaphoreType.DMA((peers,)),
            pltpu.SemaphoreType.DMA((peers,)),
            pltpu.SemaphoreType.DMA((peers,)),
            pltpu.SemaphoreType.DMA((peers,)),
            sems(4 + 2 * peers), sems(2, 2), sems(2),
            sems(tensor_size - 1, peers // 2), sems(tensor_size - 1, peers // 2),
        ],
        compiler_params=pltpu.CompilerParams(
            collective_id=2, has_side_effects=True, vmem_limit_bytes=60 << 20
        ),
        cost_estimate=pl.CostEstimate(
            flops=18 * slots * width * hidden, bytes_accessed=300 << 20, transcendentals=0
        ),
    )(x_rows, cot_rows, up_slices, down_slices, down_rest)


class Movers:
    def __init__(self, dp, experts, tensor):
        self.dp, self.experts, self.tensor = dp, experts, tensor
        self.ratio = dp // experts
        self.groups = self.pairs = None
        if self.ratio > 1:
            self.groups = [[g * experts + e for e in range(experts)] for g in range(self.ratio)]
            self.pairs = [[g * experts + e for g in range(self.ratio)] for e in range(experts)]

    def swap(self, blocks):
        return lax.all_to_all(blocks, "dp", 0, 0, axis_index_groups=self.groups, tiled=True)

    def fetch(self, shards):
        mine = self.swap(shards)
        if self.ratio > 1:
            mine = lax.all_gather(mine, "dp", axis=0, axis_index_groups=self.pairs, tiled=True)
        return mine

    def give_back(self, slices):
        if self.ratio > 1:
            slices = lax.psum_scatter(
                slices, "dp", scatter_dimension=0, axis_index_groups=self.pairs, tiled=True
            )
        return self.swap(slices)

    def exchange(self, rows):
        size = rows.shape[0] // self.experts
        blocks = [rows[:size]]
        for k in range(1, self.experts):
            pairs = [(i, i ^ k) for i in range(self.dp)]
            blocks.append(lax.ppermute(rows[k * size : (k + 1) * size], "dp", pairs))
        return jnp.concatenate(blocks, axis=0)

    def across(self, block, k):
        return lax.ppermute(block, "tensor", [(i, i ^ k) for i in range(self.tensor)])

    def reduce_rows(self, part, dtype=BF16):
        z = lax.axis_index("tensor")
        size = part.shape[0] // self.tensor
        total = lax.dynamic_slice_in_dim(part, z * size, size, axis=0)
        sent = part.astype(dtype)
        for k in range(1, self.tensor):
            block = lax.dynamic_slice_in_dim(sent, (z ^ k) * size, size, axis=0)
            total = total + self.across(block, k).astype(F32)
        return total

    def gather_rows(self, rows):
        z = lax.axis_index("tensor")
        size = rows.shape[0]
        rows = rows.astype(BF16)
        full = jnp.zeros((size * self.tensor,) + rows.shape[1:], BF16)
        for k in range(self.tensor):
            block = rows if k == 0 else self.across(rows, k)
            full = lax.dynamic_update_slice_in_dim(full, block, (z ^ k) * size, axis=0)
        return full


def expert_plain(movers, expert_in, cot_rows, up_slices, down_slices):
    dp_size, hidden_here, per_dp = down_slices.shape
    model_width = dp_size * per_dp
    gate_full, up_full = (up_slices[:, g].reshape(model_width, hidden_here) for g in range(2))
    down_full = down_slices.transpose(1, 0, 2).reshape(hidden_here, model_width)
    x_rows, gate_of_row = without_column(movers.exchange(expert_in))
    g_rows = (cot_rows.astype(F32) * gate_of_row).astype(BF16)
    gate = dot(x_rows, gate_full)
    up = dot(x_rows, up_full)
    sigmoid_gate = jax.nn.sigmoid(gate)
    silu_gate = gate * sigmoid_gate
    activated = (silu_gate * up).astype(BF16)
    grad_act = dot_nt(g_rows, down_full)
    grad_gate = (grad_act * up * sigmoid_gate * (1.0 + gate * (1.0 - sigmoid_gate))).astype(BF16)
    grad_up = (grad_act * silu_gate).astype(BF16)
    gate_times_grad = jnp.sum(activated.astype(F32) * grad_act, axis=1, keepdims=True)
    grad_expert_in = with_column(
        (dot_nt(grad_gate, gate_full) + dot_nt(grad_up, up_full)).astype(BF16), gate_times_grad
    )
    return (
        movers.exchange(grad_expert_in),
        dot(activated, down_full, BF16),
        dot_tn(x_rows, grad_gate, BF16).reshape(dp_size, per_dp, -1),
        dot_tn(x_rows, grad_up, BF16).reshape(dp_size, per_dp, -1),
        dot_tn(activated, g_rows, BF16).reshape(-1, dp_size, per_dp).transpose(1, 0, 2),
    )


def on_device(
    dp_size,
    tensor_size,
    tokens,
    cotangent,
    parents,
    attention_routes,
    expert_routes,
    slot_order,
    gain_attention,
    keyval_weight,
    query_weight,
    output_weight,
    attention_router,
    gain_feedforward,
    expert_router,
    gate_up_weight,
    down_weight,
):
    tok_count, model_width = tokens.shape
    pair_count = TOPK * tok_count
    att_experts = query_weight.shape[0]
    mlp_experts = gate_up_weight.shape[0]
    att_cap = tok_count * 5 // 16
    mlp_cap = pair_count // mlp_experts
    att_slots = att_experts * att_cap
    mlp_slots = mlp_experts * mlp_cap
    width_here = query_weight.shape[2]
    rows_here = tok_count // tensor_size
    movers = Movers(dp_size, mlp_experts, tensor_size)
    fast = dp_size == 8 and mlp_experts == 8
    tie = lax.optimization_barrier

    small = jnp.concatenate(
        [gain_attention[:, None], gain_feedforward[:, None], attention_router, expert_router], axis=1
    )
    small_full = lax.all_gather(small, "dp", axis=0, tiled=True)
    small_full, down_weight = tie((small_full, down_weight))
    gain_attn_full = small_full[:, 0].astype(F32)
    gain_mlp_full = small_full[:, 1].astype(F32)
    router_att = small_full[:, 2 : 2 + att_experts]
    router_mlp = small_full[:, 2 + att_experts :]

    inside, depth = ancestry(parents[0])
    token_index = jnp.arange(tok_count, dtype=jnp.int32)
    pair_order = jnp.arange(pair_count, dtype=jnp.int32).reshape(tok_count, TOPK)
    att_hits = slot_hits(
        slot_places(attention_routes, pair_order, att_cap, att_experts), att_slots
    )
    priority = slot_order[0][:, None] * TOPK + jnp.arange(TOPK, dtype=jnp.int32)[None, :]
    home = lax.rem(lax.axis_index("dp"), mlp_experts)
    mlp_hits = slot_hits(
        slot_places(expert_routes ^ home, priority, mlp_cap, mlp_experts), mlp_slots
    )
    att_pick = (att_hits[0] | att_hits[1]).astype(BF16)
    mlp_pick = (mlp_hits[0] | mlp_hits[1]).astype(BF16)

    def to_slots(hits, pair_values):
        return jnp.sum(
            sum(jnp.where(hits[k], pair_values[:, k][None, :], 0) for k in range(TOPK)), axis=1
        )

    def to_pairs(hits, slot_values):
        return jnp.stack(
            [jnp.sum(jnp.where(hits[k], slot_values[:, None], 0.0), axis=0) for k in range(TOPK)],
            axis=1,
        )

    def position_of(token):
        segment = token // SEG
        level = jnp.sum(
            jnp.where(segment[:, None] == jnp.arange(depth.shape[0])[None, :], depth[None, :], 0),
            axis=1,
        )
        return level * SEG + token % SEG

    pair_token = jnp.broadcast_to(token_index[:, None], (tok_count, TOPK))
    slot_token = to_slots(att_hits, pair_token)
    slot_filled = jnp.any(att_hits[0] | att_hits[1], axis=1)
    slot_tables = rope_tables(position_of(slot_token))
    tok_tables = rope_tables(position_of(token_index))
    segment_hot = (
        (slot_token // SEG)[:, None] == jnp.arange(inside.shape[0], dtype=jnp.int32)[None, :]
    ).astype(F32)
    reach = dot(segment_hot, jnp.repeat(inside.astype(F32), SEG, axis=1)) > 0.5
    allowed = reach & (token_index[None, :] <= slot_token[:, None]) & slot_filled[:, None]
    bias = jnp.where(allowed, 0.0, NEGATIVE).astype(BF16)

    early = down_weight.shape[1] // 2 if fast else down_weight.shape[1]
    down_slices = movers.fetch(down_weight[:, :early])
    cot_send = dot(mlp_pick, cotangent, BF16)

    inputs = tokens.astype(F32)
    normal_attn, scale_attn = norm_forward(inputs)
    normed = (normal_attn * gain_attn_full).astype(BF16)
    att_gates = picked_softmax(dot(normed, router_att), attention_routes)
    att_gate_slots = to_slots(att_hits, att_gates)[:, None]
    routed = dot(att_pick, normed, BF16).reshape(att_experts, att_cap, model_width)
    if fast:
        mlp_bits = tuple(hit.astype(BF16) for hit in mlp_hits)
        expert_lanes = [
            (expert_routes[:, k : k + 1] == jnp.arange(HD, dtype=jnp.int32)[None, :]).astype(F32)
            for k in range(TOPK)
        ]
        keyval_weight, query_weight, output_weight, *before = tie(
            (keyval_weight, query_weight, output_weight, routed, cot_send, bias, att_gate_slots)
            + slot_tables + tok_tables + mlp_bits + tuple(expert_lanes)
        )
        routed, cot_send, bias, att_gate_slots = before[:4]
        slot_tables, tok_tables = before[4:6], before[6:8]
        mlp_bits, expert_lanes = before[8:10], before[10:12]
        keyval_full, query_full, output_full, cot_rows = gather_maps(
            tensor_size, mlp_experts,
            (keyval_weight, query_weight, output_weight), (1, 1, 2), (2, 2, 2), cot_send,
        )
    else:
        keyval_full = lax.all_gather(keyval_weight, "dp", axis=1, tiled=True)
        query_full = lax.all_gather(query_weight, "dp", axis=1, tiled=True)
        output_full = lax.all_gather(output_weight, "dp", axis=2, tiled=True)
    query_full, keyval_full, down_slices, gate_up_weight = tie(
        (query_full, keyval_full, down_slices, gate_up_weight)
    )
    up_slices = movers.fetch(gate_up_weight)
    keyval = jnp.concatenate([dot(normed, keyval_full[0]), dot(normed, keyval_full[1])], axis=1)
    query_raw = jnp.einsum(
        "ecd,edf->ecf", routed, query_full, preferred_element_type=F32
    ).reshape(att_slots, width_here)
    queries, key_rows, values, attended, gated = attend(
        query_raw, keyval, bias, att_gate_slots, slot_tables, tok_tables
    )
    gated_slots = gated.reshape(att_experts, att_cap, width_here)
    att_rows = jnp.einsum(
        "ecf,efd->ecd", gated_slots, output_full, preferred_element_type=F32
    ).reshape(att_slots, model_width)
    att_rows = att_rows.astype(BF16)

    z = lax.axis_index("tensor")

    def share(rows):
        return lax.dynamic_slice_in_dim(rows, z * rows_here, rows_here, axis=0)

    def hots(gates, picks, experts):
        lanes = jnp.arange(HD, dtype=jnp.int32)[None, :]
        hot = [(share(picks)[:, k : k + 1] == lanes).astype(F32) for k in range(TOPK)]
        return jnp.stack(hot + [sum(hot[k] * share(gates)[:, k : k + 1] for k in range(TOPK))])

    def padded(router):
        return jnp.pad(router, ((0, 0), (0, HD - router.shape[1])))

    if fast:
        hidden, mlp_in, mlp_gates, expert_in, down_rest = hidden_step(
            tensor_size, att_pick, att_rows, share(tokens), gain_mlp_full[None],
            padded(router_mlp), expert_lanes, mlp_bits, down_weight[:, early:],
        )
        mlp_gates = mlp_gates[:, :TOPK]
    else:
        hidden = share(inputs) + movers.reduce_rows(dot_tn(att_pick, att_rows))
        mlp_in = movers.gather_rows((norm_forward(hidden)[0] * gain_mlp_full).astype(BF16))
        cot_rows = movers.exchange(cot_send)
        mlp_gates = picked_softmax(dot(mlp_in, router_mlp), expert_routes)
        expert_in = with_column(
            dot(mlp_pick, mlp_in, BF16), to_slots(mlp_hits, mlp_gates)[:, None]
        )
    expert_in, up_slices = tie((expert_in, up_slices))

    if fast:
        back = expert_step(
            tensor_size, expert_in, cot_rows, up_slices, down_slices, down_rest
        )
    else:
        back = expert_plain(movers, expert_in, cot_rows, up_slices, down_slices)
    grad_in_slots, expert_out, grad_gate_w, grad_up_w, grad_down_w = back

    if fast:
        (
            grad_hidden, _, grad_gain_mlp, grad_mlp_logits, mixed, grad_att_rows, grad_gate_w,
            grad_up_w, grad_output_w,
        ) = back_step(
            tensor_size, mlp_experts, grad_in_slots, mlp_pick,
            mlp_bits, hidden, share(cotangent),
            gain_mlp_full[None], padded(router_mlp),
            hots(mlp_gates, expert_routes, mlp_experts), mlp_gates.T, att_pick, gated, att_experts,
            expert_out, grad_gate_w, grad_up_w,
        )
        grad_gain_mlp = grad_gain_mlp[0]
        grad_mlp_logits = grad_mlp_logits[:, :mlp_experts]
    else:
        out_slots = movers.exchange(expert_out)
        grad_gate_w = movers.give_back(grad_gate_w)
        grad_up_w = movers.give_back(grad_up_w)
        grad_in_slots, gate_times_grad = without_column(grad_in_slots)
        mlp_products = movers.reduce_rows(to_pairs(mlp_hits, gate_times_grad[:, 0]), F32)
        grad_mlp_in = movers.reduce_rows(dot_tn(mlp_pick, grad_in_slots))
        grad_mlp_logits = router_backward(
            share(mlp_gates), mlp_products, share(expert_routes), mlp_experts
        )
        grad_mlp_in = grad_mlp_in + dot_nt(grad_mlp_logits, router_mlp)
        normal_mlp, scale_mlp = norm_forward(hidden)
        grad_hidden_norm, grad_gain_mlp = norm_backward(
            grad_mlp_in, normal_mlp, scale_mlp, gain_mlp_full
        )
        grad_hidden = share(cotangent).astype(F32) + grad_hidden_norm
        grad_att_pair = movers.gather_rows(grad_hidden)
        grad_att_rows = dot(att_pick, grad_att_pair, BF16)
        grad_output_w = jnp.einsum(
            "ecf,ecd->efd",
            gated_slots,
            grad_att_rows.reshape(att_experts, att_cap, model_width),
            preferred_element_type=BF16,
        )
        gate_matrix = sum(
            jnp.where(mlp_hits[k], mlp_gates[:, k][None, :], 0.0) for k in range(TOPK)
        )
        matrix_high = gate_matrix.astype(BF16)
        matrix_low = (gate_matrix - matrix_high.astype(F32)).astype(BF16)
        mlp_part = (dot_tn(matrix_high, out_slots) + dot_tn(matrix_low, out_slots)).astype(BF16)
        mixed = movers.gather_rows(hidden + movers.reduce_rows(mlp_part))
    grad_router_mlp = dot_tn(share(mlp_in), grad_mlp_logits)

    grad_att_rows = grad_att_rows.reshape(att_experts, att_cap, model_width)
    grad_output_out = lax.psum_scatter(grad_output_w, "dp", scatter_dimension=2, tiled=True)
    if fast:
        half = grad_down_w.shape[1] * 5 // 128 * 16
        grad_q, grad_kv, normed_part, grad_down_early, mixed = turn_step(
            tensor_size, grad_att_rows, queries, key_rows, values, bias, att_gate_slots,
            slot_tables, tok_tables, attended, [hit.astype(BF16) for hit in att_hits], mixed,
            output_full, query_full, keyval_full, grad_down_w, half,
        )
    else:
        grad_down_early, grad_down_late = jnp.split(movers.give_back(grad_down_w), 2, axis=1)
        grad_gated = jnp.einsum(
            "ecd,efd->ecf", grad_att_rows, output_full, preferred_element_type=F32
        ).reshape(att_slots, width_here)
        att_products = to_pairs(
            att_hits, jnp.sum(grad_gated * attended, axis=1) * att_gate_slots[:, 0]
        )
        grad_q, grad_k, grad_v = attend_back(
            queries, key_rows, values, bias, att_gate_slots, slot_tables, tok_tables, grad_gated
        )
        grad_routed = jnp.einsum(
            "ecf,edf->ecd",
            grad_q.reshape(att_experts, att_cap, width_here),
            query_full,
            preferred_element_type=F32,
        ).reshape(att_slots, model_width)
        normed_part = (
            dot_tn(att_pick, grad_routed.astype(BF16))
            + dot_nt(grad_k, keyval_full[0])
            + dot_nt(grad_v, keyval_full[1])
        )
        grad_kv = jnp.stack([grad_k, grad_v])
    grad_query_slots = grad_q.reshape(att_experts, att_cap, width_here)
    if fast:
        small = jnp.concatenate(
            [
                jnp.zeros((1, model_width), F32),
                grad_gain_mlp[None],
                jnp.zeros((HALF_SMALL - 2, model_width), F32),
                grad_router_mlp.T,
            ],
            axis=0,
        )
        map_sums, grad_tokens, small_grads, grad_down_late = final_step(
            tensor_size, routed, grad_query_slots, normed, grad_kv, normed_part,
            grad_hidden, share(tokens), gain_attn_full[None], padded(router_att),
            hots(att_gates, attention_routes, att_experts), small, grad_down_w,
            grad_down_w.shape[1] - half,
        )
        small_grads = jnp.concatenate([small_grads[:2], small_grads[HALF_SMALL:]], axis=0).T
        grad_query_out, grad_keyval_out = map_sums[:att_experts], map_sums[att_experts:]
    else:
        grad_query_w = jnp.einsum(
            "ecd,ecf->edf", routed, grad_query_slots, preferred_element_type=BF16
        )
        grad_keyval_w = jnp.stack([dot_tn(normed, grad, BF16) for grad in grad_kv])
        grad_query_out = lax.psum_scatter(grad_query_w, "dp", scatter_dimension=1, tiled=True)
        grad_keyval_out = lax.psum_scatter(grad_keyval_w, "dp", scatter_dimension=1, tiled=True)
        grad_normed = movers.reduce_rows(normed_part)
        grad_att_logits = router_backward(
            share(att_gates), movers.reduce_rows(att_products, F32), share(attention_routes),
            att_experts,
        )
        grad_normed = grad_normed + dot_nt(grad_att_logits, router_att)
        grad_input_norm, grad_gain_attn = norm_backward(
            grad_normed, share(normal_attn), share(scale_attn), gain_attn_full
        )
        grad_tokens = movers.gather_rows(grad_hidden + grad_input_norm)
        grad_router_att = dot_tn(share(normed), grad_att_logits)
        small_grads = jnp.concatenate(
            [grad_gain_attn[:, None], grad_gain_mlp[:, None], grad_router_att, grad_router_mlp],
            axis=1,
        )
        small_grads = lax.psum(
            lax.psum_scatter(small_grads, "dp", scatter_dimension=0, tiled=True), "tensor"
        )
    grad_tokens, grad_output_out = tie((grad_tokens, grad_output_out))
    grad_tokens = grad_tokens.astype(F32)
    grad_up_w, grad_down_w = widen(
        grad_gate_w, grad_up_w, grad_down_early, grad_down_late
    )
    return (
        mixed,
        grad_tokens,
        small_grads[:, 0],
        grad_keyval_out.astype(F32),
        grad_query_out.astype(F32),
        grad_output_out.astype(F32),
        small_grads[:, 2 : 2 + att_experts],
        small_grads[:, 1],
        small_grads[:, 2 + att_experts :],
        grad_up_w,
        grad_down_w,
    )


def solution(mesh):
    placed = (
        P("dp", None),
        P("dp", None),
        P("dp", None),
        P("dp", None),
        P("dp", None),
        P("dp", None),
        P("dp"),
        P(None, "dp", "tensor"),
        P(None, "dp", "tensor"),
        P(None, "tensor", "dp"),
        P("dp", None),
        P("dp"),
        P("dp", None),
        P(None, None, "dp", "tensor"),
        P(None, "tensor", "dp"),
    )
    return jax.shard_map(
        functools.partial(on_device, mesh.shape["dp"], mesh.shape["tensor"]),
        mesh=mesh,
        in_specs=placed,
        out_specs=(
            P("dp", None),
            P("dp", None),
            P("dp"),
            P(None, "dp", "tensor"),
            P(None, "dp", "tensor"),
            P(None, "tensor", "dp"),
            P("dp", None),
            P("dp"),
            P("dp", None),
            P(None, None, "dp", "tensor"),
            P(None, "tensor", "dp"),
        ),
        check_vma=False,
    )
```

```python
import functools

import jax
import jax.numpy as jnp
from jax import lax
from jax.experimental import pallas as pl
from jax.experimental.pallas import tpu as pltpu
from jax.sharding import PartitionSpec as P

HD = 128
TOPK = 2
SEG = 128

EPSILON = 1e-06
NEGATIVE = -1e30
ROPE_BASE = 10000.0
F32 = jnp.float32
BF16 = jnp.bfloat16


def dot(a, b, out=F32):
    return jnp.dot(a, b, preferred_element_type=out)


def dot_tn(a, b, out=F32):
    return lax.dot_general(a, b, (((0,), (0,)), ((), ())), preferred_element_type=out)


def dot_nt(a, b, out=F32):
    return lax.dot_general(a, b, (((1,), (1,)), ((), ())), preferred_element_type=out)


def slot_places(routes, priority, capacity, experts):
    pair_total = routes.shape[0] * routes.shape[1]
    flat_routes = routes.reshape(pair_total)
    flat_order = priority.reshape(pair_total)
    same_expert = flat_routes[:, None] == flat_routes[None, :]
    earlier = flat_order[None, :] < flat_order[:, None]
    slot_rank = jnp.sum((same_expert & earlier).astype(jnp.int32), axis=1)
    slot_place = jnp.where(
        slot_rank < capacity, flat_routes * capacity + slot_rank, experts * capacity
    )
    return slot_place.reshape(routes.shape)


def slot_hits(place, slots):
    index = jnp.arange(slots, dtype=jnp.int32)[:, None]
    return [place[:, k][None, :] == index for k in range(place.shape[1])]


def ancestry(parent_row):
    segment_count = parent_row.shape[0]
    indices = jnp.arange(segment_count, dtype=jnp.int32)
    walker = indices
    inside = indices[:, None] == indices[None, :]
    for travel in range(segment_count):
        walker = parent_row[walker]
        inside = inside | (walker[:, None] == indices[None, :])
    depth = jnp.sum(inside.astype(jnp.int32), axis=1) - 1
    return (inside, depth)


def rope_tables(position):
    half_width = HD // 2
    frequency = ROPE_BASE ** (-jnp.arange(half_width, dtype=F32) / half_width)
    angles = position.astype(F32)[:, None] * frequency[None, :]
    cosine, sine = jnp.cos(angles), jnp.sin(angles)
    return (
        jnp.concatenate([cosine, cosine], axis=1),
        jnp.concatenate([-sine, sine], axis=1),
    )


def norm_forward(values_in):
    scale = lax.rsqrt(jnp.mean(values_in * values_in, axis=-1, keepdims=True) + EPSILON)
    return (values_in * scale, scale)


def norm_backward(grad_normed, normal, scale, gain):
    weighted = grad_normed * gain
    grad_in = scale * (weighted - normal * jnp.mean(weighted * normal, axis=-1, keepdims=True))
    return (grad_in, jnp.sum(grad_normed * normal, axis=0))


def router_backward(gates, products, picks, experts):
    grad_select = products - gates * jnp.sum(products, axis=1, keepdims=True)
    picked_hot = (picks[:, :, None] == jnp.arange(experts, dtype=jnp.int32)[None, None, :]).astype(
        F32
    )
    return jnp.sum(picked_hot * grad_select[:, :, None], axis=1).astype(BF16)


def with_column(rows, column):
    high = column.astype(BF16)
    rest = column - high.astype(F32)
    mid = rest.astype(BF16)
    low = (rest - mid.astype(F32)).astype(BF16)
    return jnp.concatenate(
        [rows, high, mid, low, jnp.zeros((rows.shape[0], HD - 3), BF16)], axis=1
    )


def without_column(both):
    width = both.shape[1] - HD
    parts = both[:, width : width + 3].astype(F32)
    return both[:, :width], parts[:, :1] + parts[:, 1:2] + parts[:, 2:]


def picked_softmax(logits, picks):
    experts = logits.shape[1]
    hot = picks[:, :, None] == jnp.arange(experts, dtype=jnp.int32)[None, None, :]
    return jax.nn.softmax(jnp.sum(jnp.where(hot, logits[:, None, :], 0.0), axis=2), axis=-1)


def rope(v, cosine, sine):
    return v * cosine + pltpu.roll(v, HD // 2, axis=1) * sine


def rope_back(v, cosine, sine):
    return v * cosine - pltpu.roll(v, HD // 2, axis=1) * sine


def softmax_block(q, k, bias):
    scores = dot_nt(q, k) * HD ** (-0.5) + bias
    exp_scores = jnp.exp(scores - jnp.max(scores, axis=-1, keepdims=True))
    return exp_scores / jnp.sum(exp_scores, axis=-1, keepdims=True)


def attend_kernel(
    rows, q_raw, k_raw, v_raw, bias, gate, slot_cos, slot_sin, tok_cos, tok_sin,
    q_out, k_out, v_out, att_out, gated_out,
):
    k_out[...] = rope(k_raw[...], tok_cos[...], tok_sin[...]).astype(BF16)
    v_out[...] = v_raw[...].astype(BF16)

    @pl.loop(0, q_raw.shape[0] // rows)
    def _(i):
        at = pl.ds(pl.multiple_of(i * rows, rows), rows)
        q = rope(q_raw[at, :], slot_cos[at, :], slot_sin[at, :]).astype(BF16)
        q_out[at, :] = q
        probs = softmax_block(q, k_out[...], bias[at, :].astype(F32)).astype(BF16)
        attended = dot(probs, v_out[...])
        att_out[at, :] = attended
        gated_out[at, :] = (attended * gate[at, :]).astype(BF16)


def attend(q_raw, keyval, bias, gate, slot_tables, tok_tables):
    slots, width = q_raw.shape
    tok = keyval.shape[0]
    heads = width // HD
    head = lambda h: (0, h)
    whole = lambda h: (0, 0)
    rows = 256
    return pl.pallas_call(
        functools.partial(attend_kernel, rows),
        grid=(heads,),
        in_specs=[
            pl.BlockSpec((slots, HD), head),
            pl.BlockSpec((tok, HD), head),
            pl.BlockSpec((tok, HD), lambda h: (0, heads + h)),
            pl.BlockSpec((slots, tok), whole),
            pl.BlockSpec((slots, 1), whole),
            pl.BlockSpec((slots, HD), whole),
            pl.BlockSpec((slots, HD), whole),
            pl.BlockSpec((tok, HD), whole),
            pl.BlockSpec((tok, HD), whole),
        ],
        out_specs=[
            pl.BlockSpec((slots, HD), head),
            pl.BlockSpec((tok, HD), head),
            pl.BlockSpec((tok, HD), head),
            pl.BlockSpec((slots, HD), head),
            pl.BlockSpec((slots, HD), head),
        ],
        out_shape=[
            jax.ShapeDtypeStruct((slots, width), BF16),
            jax.ShapeDtypeStruct((tok, width), BF16),
            jax.ShapeDtypeStruct((tok, width), BF16),
            jax.ShapeDtypeStruct((slots, width), F32),
            jax.ShapeDtypeStruct((slots, width), BF16),
        ],
        compiler_params=pltpu.CompilerParams(vmem_limit_bytes=40 << 20),
        cost_estimate=pl.CostEstimate(
            flops=4 * slots * tok * width,
            bytes_accessed=slots * width * 12 + slots * tok * 2,
            transcendentals=slots * tok * heads,
        ),
    )(q_raw, keyval, keyval, bias, gate, *slot_tables, *tok_tables)


def attend_back_kernel(
    rows, q_ref, k_ref, v_ref, bias, gate, slot_cos, slot_sin, tok_cos, tok_sin, grad_gated,
    gq_out, gk_out, gv_out, gk_sum, gv_sum,
):
    gk_sum[...] = jnp.zeros_like(gk_sum)
    gv_sum[...] = jnp.zeros_like(gv_sum)

    @pl.loop(0, q_ref.shape[0] // rows)
    def _(i):
        at = pl.ds(pl.multiple_of(i * rows, rows), rows)
        q = q_ref[at, :]
        probs = softmax_block(q, k_ref[...], bias[at, :].astype(F32))
        grad_att = (grad_gated[at, :] * gate[at, :]).astype(BF16)
        grad_probs = dot_nt(grad_att, v_ref[...])
        centre = jnp.sum(probs * grad_probs, axis=-1, keepdims=True)
        grad_scores = (probs * (grad_probs - centre)).astype(BF16)
        grad_q = dot(grad_scores, k_ref[...]) * HD ** (-0.5)
        gq_out[at, :] = rope_back(grad_q, slot_cos[at, :], slot_sin[at, :]).astype(BF16)
        gk_sum[...] += dot_tn(grad_scores, q)
        gv_sum[...] += dot_tn(probs.astype(BF16), grad_att)

    grad_k = gk_sum[...] * HD ** (-0.5)
    gk_out[...] = rope_back(grad_k, tok_cos[...], tok_sin[...]).astype(BF16)
    gv_out[...] = gv_sum[...].astype(BF16)


def attend_back(q, k, v, bias, gate, slot_tables, tok_tables, grad_gated):
    slots, width = q.shape
    tok = k.shape[0]
    heads = width // HD
    head = lambda h: (0, h)
    whole = lambda h: (0, 0)
    rows = 256
    return pl.pallas_call(
        functools.partial(attend_back_kernel, rows),
        grid=(heads,),
        in_specs=[
            pl.BlockSpec((slots, HD), head),
            pl.BlockSpec((tok, HD), head),
            pl.BlockSpec((tok, HD), head),
            pl.BlockSpec((slots, tok), whole),
            pl.BlockSpec((slots, 1), whole),
            pl.BlockSpec((slots, HD), whole),
            pl.BlockSpec((slots, HD), whole),
            pl.BlockSpec((tok, HD), whole),
            pl.BlockSpec((tok, HD), whole),
            pl.BlockSpec((slots, HD), head),
        ],
        out_specs=[
            pl.BlockSpec((slots, HD), head),
            pl.BlockSpec((tok, HD), head),
            pl.BlockSpec((tok, HD), head),
        ],
        out_shape=[
            jax.ShapeDtypeStruct((slots, width), BF16),
            jax.ShapeDtypeStruct((tok, width), BF16),
            jax.ShapeDtypeStruct((tok, width), BF16),
        ],
        scratch_shapes=[pltpu.VMEM((tok, HD), F32), pltpu.VMEM((tok, HD), F32)],
        compiler_params=pltpu.CompilerParams(vmem_limit_bytes=40 << 20),
        cost_estimate=pl.CostEstimate(
            flops=0, bytes_accessed=slots * width, transcendentals=0
        ),
    )(q, k, v, bias, gate, *slot_tables, *tok_tables, grad_gated)


class Square:
    def __init__(self):
        me = lax.axis_index("dp")
        self.core = lax.rem(me, 2)
        self.chip = me // 2
        x, y = lax.rem(self.chip, 2), self.chip // 2
        self.chip_x = self.chip + 1 - 2 * x
        self.chip_y = self.chip + 2 - 4 * y
        self.chip_far = 3 - self.chip
        self.twin = me + 1 - 2 * self.core
        self.near_x = 2 * self.chip_x + self.core
        self.near_y = 2 * self.chip_y + self.core


def send_to(source, target, send_sem, recv_sem, device):
    return pltpu.make_async_remote_copy(
        src_ref=source,
        dst_ref=target,
        send_sem=send_sem,
        recv_sem=recv_sem,
        device_id={"dp": device},
        device_id_type=pl.DeviceIdType.MESH,
    )


def greet(places):
    barrier = pltpu.get_barrier_semaphore()
    for place in places:
        pl.semaphore_signal(
            barrier, inc=1, device_id=place, device_id_type=pl.DeviceIdType.MESH
        )
    pl.semaphore_wait(barrier, len(places))


def send_across(source, target, send_sem, recv_sem, device):
    return pltpu.make_async_remote_copy(
        src_ref=source,
        dst_ref=target,
        send_sem=send_sem,
        recv_sem=recv_sem,
        device_id={"tensor": device},
        device_id_type=pl.DeviceIdType.MESH,
    )


def tensor_peers(count):
    z = lax.axis_index("tensor")
    return [lax.rem(z + k, count) for k in range(1, count)]


def share_rows(size):
    return pl.ds(pl.multiple_of(lax.axis_index("tensor") * size, size), size)


def rows_of(place, size):
    return pl.ds(pl.multiple_of(place * size, size), size)


def spread(count, source, target, sems):
    size = source.shape[0] // count
    copies = [
        send_to(
            source.at[pl.ds(k * size, size)], target.at[pl.ds(k * size, size)],
            sems[0].at[k], sems[1].at[k], partner(k),
        )
        for k in range(1, count)
    ]
    here = pltpu.make_async_copy(
        source.at[pl.ds(0, size)], target.at[pl.ds(0, size)], sems[0].at[0]
    )
    for copy in (*copies, here):
        copy.start()
    return (*copies, here)


def gather_kernel(axes, chunks, *refs):
    amount = len(axes)
    sources, rows = refs[:amount], refs[amount]
    targets, rows_out = refs[amount + 1 : 2 * amount + 1], refs[2 * amount + 1]
    send_sem, recv_sem, own_sem, e_send, e_recv, z_send, z_recv = refs[2 * amount + 2 :]
    count = z_send.shape[0] + 1
    exchange_count = e_send.shape[0]
    peers = tensor_peers(count)
    at = Square()
    me = 2 * at.chip + at.core
    far = 2 * at.chip_far + at.core
    greet(
        [{"dp": partner(k)} for k in range(1, exchange_count)] + [{"tensor": p} for p in peers]
    )
    columns = share_rows(rows.shape[1] // count)
    size = rows.shape[0] // exchange_count
    moved = [
        send_to(
            rows.at[pl.ds(k * size, size), columns], rows_out.at[pl.ds(k * size, size), columns],
            e_send.at[k], e_recv.at[k], partner(k),
        )
        for k in range(1, exchange_count)
    ]
    stay = pltpu.make_async_copy(
        rows.at[pl.ds(0, size), columns], rows_out.at[pl.ds(0, size), columns], e_send.at[0]
    )
    for copy in (*moved, stay):
        copy.start()

    def region(ref, axis, source, place, experts):
        size = source.shape[axis]
        at_place = pl.ds(pl.multiple_of(place * size, size), size)
        return ref.at[experts, at_place] if axis == 1 else ref.at[experts, :, at_place]

    first = 0
    plans = []
    for i in range(amount):
        count = sources[i].shape[0] // chunks[i]
        plans.append((i, first, count))
        first += count

    def copies(i, first, n):
        source, target, axis, size = sources[i], targets[i], axes[i], chunks[i]
        half = size // 2
        whole = pl.ds(n * size, size)
        top, bottom = pl.ds(n * size, half), pl.ds(n * size + half, half)
        unit = first + n

        def move(slot, place, experts, device, own=False):
            there = region(target, axis, source, place, experts)
            return send_to(
                source.at[experts] if own else there, there,
                send_sem.at[unit, slot], recv_sem.at[unit, slot], device,
            )

        return [
            functools.partial(move, 0, me, whole, at.near_x, True),
            functools.partial(move, 1, me, whole, at.near_y, True),
            functools.partial(move, 2, at.near_y, top, at.near_x),
            functools.partial(move, 3, at.near_x, bottom, at.near_y),
            functools.partial(move, 4, me, whole, at.twin, True),
            functools.partial(move, 5, at.near_x, whole, at.twin),
            functools.partial(move, 6, at.near_y, whole, at.twin),
            functools.partial(move, 7, far, top, at.twin),
            functools.partial(move, 8, far, bottom, at.twin),
        ]

    here = [
        pltpu.make_async_copy(
            sources[i], region(targets[i], axes[i], sources[i], me, pl.ds(0, sources[i].shape[0])),
            own_sem.at[i],
        )
        for i in range(amount)
    ]
    for i, first, count in plans:

        @pl.loop(0, count)
        def _(n):
            moves = copies(i, first, n)
            for slot in (0, 1, 4):
                moves[slot]().start()

    for copy in here:
        copy.start()
    for i, first, count in plans:

        @pl.loop(0, count)
        def _(n):
            moves = copies(i, first, n)
            moves[0]().wait_recv()
            moves[3]().start()
            moves[5]().start()
            moves[1]().wait_recv()
            moves[2]().start()
            moves[6]().start()

        if i == 0:
            stay.wait()
            for copy in moved:
                copy.wait_recv()
            across = [
                send_across(
                    rows_out.at[:, columns], rows_out.at[:, columns], z_send.at[k], z_recv.at[k], p
                )
                for k, p in enumerate(peers)
            ]
            for copy in across:
                copy.start()

    for i, first, count in plans:

        @pl.loop(0, count)
        def _(n):
            moves = copies(i, first, n)
            moves[2]().wait_recv()
            moves[7]().start()
            moves[3]().wait_recv()
            moves[8]().start()

    for i, first, count in plans:

        @pl.loop(0, count)
        def _(n):
            moves = copies(i, first, n)
            for slot in (4, 5, 6, 7, 8):
                moves[slot]().wait_recv()
            for move in moves:
                move().wait_send()

    for copy in (*here, *across):
        copy.wait()
    for copy in moved:
        copy.wait_send()


def gather_maps(tensor_size, peers, arrays, axes, chunks, rows):
    units = sum(a.shape[0] // c for a, c in zip(arrays, chunks))
    shapes = [
        tuple(n * 8 if d == axis else n for d, n in enumerate(a.shape))
        for a, axis in zip(arrays, axes)
    ]
    return pl.pallas_call(
        functools.partial(gather_kernel, axes, chunks),
        in_specs=[HBM] * (len(arrays) + 1),
        out_specs=[HBM] * (len(arrays) + 1),
        out_shape=[jax.ShapeDtypeStruct(shape, BF16) for shape in (*shapes, rows.shape)],
        scratch_shapes=[
            sems(units, 9), sems(units, 9), sems(len(arrays)), sems(peers), sems(peers),
            sems(tensor_size - 1), sems(tensor_size - 1),
        ],
        compiler_params=pltpu.CompilerParams(collective_id=5, has_side_effects=True),
        cost_estimate=pl.CostEstimate(flops=0, bytes_accessed=600 << 20, transcendentals=0),
    )(*arrays, rows)


def deal(source, target, sems, rows=None):
    me = lax.axis_index("dp")

    def block(place):
        return source.at[place] if rows is None else source.at[place, rows]

    copies = [
        send_to(block(partner(k)), target.at[me], sems[0].at[k], sems[1].at[k], partner(k))
        for k in range(1, source.shape[0])
    ]
    copies.append(pltpu.make_async_copy(block(me), target.at[me], sems[0].at[0]))
    for copy in copies:
        copy.start()
    return copies


def norm_back(total, products, hots, router, base, gain, hot_out, gain_out):
    first, second = products
    weights = hots[0] * first + hots[1] * second - hots[2] * (first + second)
    hot_out[...] = weights.astype(BF16)
    total = total + dot_nt(hot_out[...], router[...])
    scale = lax.rsqrt(jnp.mean(base * base, axis=-1, keepdims=True) + EPSILON)
    normal = base * scale
    gain_out[...] = jnp.sum(total * normal, axis=0, keepdims=True)
    weighted = total * gain
    return scale * (weighted - normal * jnp.mean(weighted * normal, axis=-1, keepdims=True))


def three_columns(block):
    return block[:, 0:1] + block[:, 1:2] + block[:, 2:3]


def in_columns(column, lane):
    high = column.astype(BF16).astype(F32)
    mid = (column - high).astype(BF16).astype(F32)
    return jnp.where(
        lane == 0, high, jnp.where(lane == 1, mid, jnp.where(lane == 2, column - high - mid, 0.0))
    ).astype(BF16)


def hidden_kernel(
    pick, rows, x_here, gain, router, hot_0, hot_1, hit_0, hit_1, maps_hbm,
    hidden_out, mlp_in_out, gates_out, x_out, maps_out,
    parts, sent, got, z_send, z_recv, g_send, g_recv, d_send, d_recv,
):
    count = z_send.shape[0] + 1
    width = rows.shape[1]
    tokens = pick.shape[1]
    size = tokens // count
    peers = tensor_peers(count)
    greet(
        [{"dp": partner(k)} for k in range(1, d_send.shape[0])] + [{"tensor": p} for p in peers]
    )
    dealt = deal(maps_hbm, maps_out, (d_send, d_recv))

    @pl.loop(0, width // 512)
    def _(i):
        at = pl.ds(pl.multiple_of(i * 512, 512), 512)
        piece = dot_tn(pick[...], rows[:, at])
        parts[:, at] = piece
        sent[:, at] = piece.astype(BF16)

    copies = [
        send_across(sent.at[rows_of(p, size)], got.at[k], z_send.at[k], z_recv.at[k], p)
        for k, p in enumerate(peers)
    ]
    for copy in copies:
        copy.start()
    here = share_rows(size)
    hidden_out[...] = x_here[...].astype(F32) + parts[here, :]
    for k, copy in enumerate(copies):
        copy.wait_recv()
        hidden_out[...] += got[k].astype(F32)
    hidden = hidden_out[...]
    scale = lax.rsqrt(jnp.mean(hidden * hidden, axis=-1, keepdims=True) + EPSILON)
    mlp_in_out[here, :] = (hidden * scale * gain[...]).astype(BF16)
    more = [
        send_across(
            mlp_in_out.at[here], mlp_in_out.at[here], g_send.at[k], g_recv.at[k], p
        )
        for k, p in enumerate(peers)
    ]
    for copy in more:
        copy.start()
    for copy in copies:
        copy.wait_send()
    for copy in more:
        copy.wait()

    logits = dot(mlp_in_out[...], router[...])
    picked = [jnp.sum(logits * hot[...], axis=1, keepdims=True) for hot in (hot_0, hot_1)]
    highest = jnp.maximum(picked[0], picked[1])
    raised = [jnp.exp(value - highest) for value in picked]
    gates = [value / (raised[0] + raised[1]) for value in raised]
    lane = lax.broadcasted_iota(jnp.int32, (tokens, HD), 1)
    gates_out[...] = jnp.where(lane == 0, gates[0], jnp.where(lane == 1, gates[1], 0.0))
    columns = [in_columns(gate, lane) for gate in gates]
    x_out[:, width:] = (dot(hit_0[...], columns[0]) + dot(hit_1[...], columns[1])).astype(BF16)

    @pl.loop(0, width // 512)
    def _(i):
        at = pl.ds(pl.multiple_of(i * 512, 512), 512)
        x_out[:, at] = dot(hit_0[...] + hit_1[...], mlp_in_out[:, at]).astype(BF16)
    for copy in dealt:
        copy.wait()


VMEM = pl.BlockSpec(memory_space=pltpu.VMEM)
HBM = pl.BlockSpec(memory_space=pl.ANY)


def sems(*shape):
    return pltpu.SemaphoreType.DMA(shape)


def hidden_step(tensor_size, pick, rows, x_here, gain, router, hots, hits, maps):
    tokens, width = pick.shape[1], rows.shape[1]
    slots = hits[0].shape[0]
    size = tokens // tensor_size
    around = tensor_size - 1
    return pl.pallas_call(
        hidden_kernel,
        in_specs=[VMEM] * 9 + [HBM],
        out_specs=[VMEM] * 4 + [HBM],
        out_shape=[
            jax.ShapeDtypeStruct((size, width), F32),
            jax.ShapeDtypeStruct((tokens, width), BF16),
            jax.ShapeDtypeStruct((tokens, HD), F32),
            jax.ShapeDtypeStruct((slots, width + HD), BF16),
            jax.ShapeDtypeStruct(maps.shape, BF16),
        ],
        scratch_shapes=[
            pltpu.VMEM((tokens, width), F32),
            pltpu.VMEM((tokens, width), BF16),
            pltpu.VMEM((around, size, width), BF16),
            sems(around), sems(around), sems(around), sems(around),
            sems(maps.shape[0]), sems(maps.shape[0]),
        ],
        compiler_params=pltpu.CompilerParams(
            collective_id=3, has_side_effects=True, vmem_limit_bytes=48 << 20
        ),
        cost_estimate=pl.CostEstimate(
            flops=2 * pick.shape[0] * tokens * width, bytes_accessed=300 << 20, transcendentals=0
        ),
    )(pick, rows, x_here, gain, router, *hots, *hits, maps)


def back_kernel(
    back, pick, hit_0, hit_1, hidden, cot_here, gain, router, hots, gates, att_pick, gated,
    rows_hbm, gate_hbm, up_hbm,
    grad_out, pair_out, gain_out, hot_out, mixed_out, att_rows, gate_maps, up_maps, grad_output,
    parts, sent, got, z_send, z_recv, g_send, g_recv, e_send, e_recv, w_send, w_recv, u_send, u_recv,
    rows_in, columns_here, mlp_got, m_send, m_recv, own, stage, stage_sem,
):
    count = z_send.shape[0] + 1
    width = back.shape[1] - HD
    tokens = pick.shape[1]
    size = tokens // count
    peers = tensor_peers(count)
    exchange_count = e_send.shape[0]
    greet(
        [{"dp": partner(k)} for k in range(1, exchange_count)] + [{"tensor": p} for p in peers]
    )
    moves = spread(exchange_count, rows_hbm, rows_in, (e_send, e_recv))
    dealt = deal(gate_hbm, gate_maps, (w_send, w_recv))
    dealt += deal(up_hbm, up_maps, (u_send, u_recv))

    @pl.loop(0, width // 512)
    def _(i):
        at = pl.ds(pl.multiple_of(i * 512, 512), 512)
        piece = dot_tn(pick[...], back[:, at])
        parts[:, at] = piece
        sent[:, at] = piece.astype(BF16)

    for k, hit in enumerate((hit_0, hit_1)):
        at = pl.ds(width + k * HD, HD)
        piece = dot_tn(hit[...], back[:, width:])
        parts[:, at] = piece
        sent[:, at] = piece.astype(BF16)

    copies = [
        send_across(sent.at[rows_of(p, size)], got.at[k], z_send.at[k], z_recv.at[k], p)
        for k, p in enumerate(peers)
    ]
    for copy in copies:
        copy.start()
    here = share_rows(size)
    total = parts[here, :]
    for k, copy in enumerate(copies):
        copy.wait_recv()
        total = total + got[k].astype(F32)
    products = (
        three_columns(total[:, width : width + HD]), three_columns(total[:, width + HD :])
    )
    grad_out[...] = cot_here[...].astype(F32) + norm_back(
        total[:, :width], products, hots, router, hidden[...], gain[...], hot_out, gain_out
    )
    pair_out[here, :] = grad_out[...].astype(BF16)
    more = [
        send_across(pair_out.at[here], pair_out.at[here], g_send.at[k], g_recv.at[k], p)
        for k, p in enumerate(peers)
    ]
    for copy in more:
        copy.start()
    for copy in moves:
        copy.wait()
    matrix = hit_0[...].astype(F32) * gates[0:1, :] + hit_1[...].astype(F32) * gates[1:2, :]
    high = matrix.astype(BF16)
    low = (matrix - high.astype(F32)).astype(BF16)
    columns_here[...] = (dot_tn(high, rows_in[...]) + dot_tn(low, rows_in[...])).astype(BF16)
    columns = share_rows(width // count)
    turned = [
        send_across(
            columns_here.at[rows_of(p, size)], mlp_got.at[:, columns], m_send.at[k], m_recv.at[k],
            p,
        )
        for k, p in enumerate(peers)
    ]
    turned.append(
        pltpu.make_async_copy(columns_here.at[here], mlp_got.at[:, columns], own.at[0])
    )
    for copy in turned:
        copy.start()
    for copy in turned:
        copy.wait()
    mixed_out[...] = (hidden[...] + mlp_got[...].astype(F32)).astype(BF16)
    for copy in copies:
        copy.wait_send()
    for copy in more:
        copy.wait()

    @pl.loop(0, width // 512)
    def _(i):
        at = rows_of(i, 512)
        att_rows[:, at] = dot(att_pick[...], pair_out[:, at]).astype(BF16)

    experts, cap = grad_output.shape[0], gated.shape[0] // grad_output.shape[0]

    def store(e):
        slot = lax.rem(e, 2)
        return pltpu.make_async_copy(stage.at[slot], grad_output.at[e], stage_sem.at[slot])

    @pl.loop(0, experts)
    def _(e):
        @pl.when(e > 1)
        def _():
            store(e - 2).wait()

        at = rows_of(e, cap)
        stage[lax.rem(e, 2)] = dot_tn(gated[at, :], att_rows[at, :]).astype(BF16)
        store(e).start()

    for e in (experts - 2, experts - 1):
        store(e).wait()
    for copy in dealt:
        copy.wait()


def back_step(
    tensor_size, peers, back, pick, hits, hidden, cot_here, gain, router, hots, gates,
    att_pick, gated, experts, rows_send, gate_maps, up_maps,
):
    tokens, width = pick.shape[1], back.shape[1] - HD
    size = tokens // tensor_size
    around = tensor_size - 1
    wide = width + 2 * HD
    return pl.pallas_call(
        back_kernel,
        in_specs=[VMEM] * 12 + [HBM] * 3,
        out_specs=[VMEM] * 6 + [HBM] * 3,
        out_shape=[
            jax.ShapeDtypeStruct((size, width), F32),
            jax.ShapeDtypeStruct((tokens, width), BF16),
            jax.ShapeDtypeStruct((1, width), F32),
            jax.ShapeDtypeStruct((size, HD), BF16),
            jax.ShapeDtypeStruct((size, width), BF16),
            jax.ShapeDtypeStruct((att_pick.shape[0], width), BF16),
            jax.ShapeDtypeStruct(gate_maps.shape, BF16),
            jax.ShapeDtypeStruct(up_maps.shape, BF16),
            jax.ShapeDtypeStruct((experts, gated.shape[1], width), BF16),
        ],
        scratch_shapes=[
            pltpu.VMEM((tokens, wide), F32),
            pltpu.VMEM((tokens, wide), BF16),
            pltpu.VMEM((around, size, wide), BF16),
            sems(around), sems(around), sems(around), sems(around), sems(peers), sems(peers),
            sems(peers), sems(peers), sems(peers), sems(peers),
            pltpu.VMEM(rows_send.shape, BF16),
            pltpu.VMEM((tokens, width // tensor_size), BF16),
            pltpu.VMEM((size, width), BF16),
            sems(around), sems(around), sems(1),
            pltpu.VMEM((2, gated.shape[1], width), BF16),
            sems(2),
        ],
        compiler_params=pltpu.CompilerParams(
            collective_id=4, has_side_effects=True, vmem_limit_bytes=56 << 20
        ),
        cost_estimate=pl.CostEstimate(
            flops=2 * pick.shape[0] * tokens * width, bytes_accessed=300 << 20, transcendentals=0
        ),
    )(back, pick, hits[0], hits[1], hidden, cot_here, gain, router, hots, gates, att_pick, gated, rows_send, gate_maps, up_maps)


GIVE = 4
HALF_SMALL = 8


def final_kernel(
    routed_hbm, grad_q, normed, grad_kv, part_hbm,
    grad_hidden, x_here, gain, router, hots, small, maps_hbm,
    out, tokens_out, small_out, maps_out,
    give, keep, twin_in, far_in, near_in, routed, got_part, tokens_here,
    twin_send, twin_recv, far_send, far_recv, near_send, near_recv, load, own,
    p_send, p_recv, t_send, t_recv,
    hot_here, small_all, small_in, small_sum, small_got,
    s_send, s_recv, w_send, w_recv, d_send, d_recv,
):
    at = Square()
    experts = grad_q.shape[0]
    units, _, size, _ = keep.shape
    half = size // 2
    count = p_send.shape[0] + 1
    peers = tensor_peers(count)
    width = normed.shape[1]
    share = part_hbm.shape[0] // count

    def fetch(u):
        return pltpu.make_async_copy(
            routed_hbm.at[u], routed.at[lax.rem(u, 2)], load.at[lax.rem(u, 2)]
        )

    fetch(0).start()
    here = share_rows(share)
    mine = pltpu.make_async_copy(part_hbm.at[here], got_part.at[count - 1], own.at[0])
    mine.start()
    greet([{"dp": partner(k)} for k in range(1, 8)] + [{"tensor": p} for p in peers])
    part_copies = [
        send_across(part_hbm.at[rows_of(p, share)], got_part.at[k], p_send.at[k], p_recv.at[k], p)
        for k, p in enumerate(peers)
    ]
    for copy in part_copies:
        copy.start()

    def to_twin(u):
        slot = lax.rem(u, GIVE)
        return send_to(give.at[slot], twin_in.at[u], twin_send.at[slot], twin_recv.at[u], at.twin)

    def to_far(u):
        first = send_to(
            keep.at[u, at.chip_far, pl.ds(0, half)],
            far_in.at[u, 0], far_send.at[u, 0], far_recv.at[u, 0], at.near_x,
        )
        second = send_to(
            keep.at[u, at.chip_far, pl.ds(half, half)],
            far_in.at[u, 1], far_send.at[u, 1], far_recv.at[u, 1], at.near_y,
        )
        return first, second

    def to_near(u):
        first = send_to(
            keep.at[u, at.chip_x], near_in.at[u, 0], near_send.at[u, 0], near_recv.at[u, 0],
            at.near_x,
        )
        second = send_to(
            keep.at[u, at.chip_y], near_in.at[u, 1], near_send.at[u, 1], near_recv.at[u, 1],
            at.near_y,
        )
        return first, second

    def multiply(u, rows, grads):
        slot = lax.rem(u, GIVE)

        @pl.when(u >= GIVE)
        def _():
            to_twin(u - GIVE).wait_send()

        for chip in range(4):
            columns = rows_of(2 * chip + 1 - at.core, size)
            give[slot, chip] = dot_tn(rows[:, columns], grads[...]).astype(BF16)
        to_twin(u).start()
        for chip in range(4):
            columns = rows_of(2 * chip + at.core, size)
            keep[u, chip] = dot_tn(rows[:, columns], grads[...]).astype(BF16)

    def join_twin(u):
        to_twin(u).wait_recv()

        def add(chip):
            keep[u, chip] = (keep[u, chip].astype(F32) + twin_in[u, chip].astype(F32)).astype(BF16)

        add(at.chip_far)
        for copy in to_far(u):
            copy.start()
        add(at.chip_x)
        add(at.chip_y)
        add(at.chip)

    @pl.loop(0, experts)
    def _(u):
        fetch(u).wait()

        @pl.when(u < experts - 1)
        def _():
            fetch(u + 1).start()

        multiply(u, routed.at[lax.rem(u, 2)], grad_q.at[u])

        @pl.when(u > 0)
        def _():
            join_twin(u - 1)

    @pl.loop(experts, units)
    def _(u):
        multiply(u, normed, grad_kv.at[u - experts])
        join_twin(u - 1)

    join_twin(units - 1)

    mine.wait()
    total = got_part[count - 1].astype(F32)
    for k, copy in enumerate(part_copies):
        copy.wait_recv()
        total = total + got_part[k].astype(F32)
    products = (
        three_columns(total[:, width : width + HD]), three_columns(total[:, width + HD :])
    )
    tokens_here[...] = (
        grad_hidden[...]
        + norm_back(
            total[:, :width], products, hots, router, x_here[...].astype(F32), gain[...],
            hot_here, small_all.at[pl.ds(0, 1)],
        )
    ).astype(BF16)
    token_copies = [
        send_across(tokens_here, tokens_out.at[here], t_send.at[k], t_recv.at[k], p)
        for k, p in enumerate(peers)
    ]
    for copy in token_copies:
        copy.start()
    kept = pltpu.make_async_copy(tokens_here, tokens_out.at[here], own.at[1])
    kept.start()

    small_all[1:HALF_SMALL, :] = small[1:HALF_SMALL, :]
    small_all[HALF_SMALL : 2 * HALF_SMALL, :] = dot_tn(hot_here[...], normed[here, :])[:HALF_SMALL]
    small_all[2 * HALF_SMALL :, :] = small[HALF_SMALL:, :]

    def small_block(place):
        return small_all.at[:, rows_of(place, size)]

    small_copies = [
        send_to(
            small_block(partner(k)), small_in.at[k], s_send.at[k], s_recv.at[k], partner(k)
        )
        for k in range(1, 8)
    ]
    for copy in small_copies:
        copy.start()

    @pl.loop(0, units)
    def _(u):
        for copy in to_far(u):
            copy.wait_recv()
        top, bottom = pl.ds(0, half), pl.ds(half, half)
        keep[u, at.chip_y, top, :] = (
            keep[u, at.chip_y, top, :].astype(F32) + far_in[u, 0].astype(F32)
        ).astype(BF16)
        keep[u, at.chip_x, bottom, :] = (
            keep[u, at.chip_x, bottom, :].astype(F32) + far_in[u, 1].astype(F32)
        ).astype(BF16)
        for copy in to_near(u):
            copy.start()

    late = maps_out.shape[1]
    dealt = deal(maps_hbm, maps_out, (d_send, d_recv), pl.ds(maps_hbm.shape[1] - late, late))

    @pl.loop(0, units)
    def _(u):
        for copy in to_near(u):
            copy.wait_recv()
        out[u] = (
            keep[u, at.chip].astype(F32) + near_in[u, 0].astype(F32) + near_in[u, 1].astype(F32)
        ).astype(BF16)

    block = small_all[:, rows_of(2 * at.chip + at.core, size)]
    for k, copy in enumerate(small_copies):
        copy.wait_recv()
        block = block + small_in[k + 1]
    small_sum[...] = block
    last_copies = [
        send_across(small_sum, small_got.at[k], w_send.at[k], w_recv.at[k], p)
        for k, p in enumerate(peers)
    ]
    for copy in last_copies:
        copy.start()

    @pl.loop(units - GIVE, units)
    def _(u):
        to_twin(u).wait_send()

    @pl.loop(0, units)
    def _(u):
        for copy in (*to_far(u), *to_near(u)):
            copy.wait_send()

    for k, copy in enumerate(last_copies):
        copy.wait_recv()
        block = block + small_got[k]
    small_out[...] = block
    for copy in (*part_copies, *small_copies, *last_copies):
        copy.wait_send()
    for copy in (*token_copies, *dealt, kept):
        copy.wait()


def final_step(
    tensor_size, routed, grad_q, normed, grad_kv, part, grad_hidden, x_here, gain,
    router, hots, small, maps, late,
):
    experts, rows, width = routed.shape
    columns = grad_q.shape[2]
    units = experts + grad_kv.shape[0]
    size = width // 8
    tokens, wide = part.shape
    share = tokens // tensor_size
    around = tensor_size - 1
    return pl.pallas_call(
        final_kernel,
        in_specs=[HBM, VMEM, VMEM, VMEM, HBM] + [VMEM] * 6 + [HBM],
        out_specs=[VMEM, HBM, VMEM, HBM],
        out_shape=[
            jax.ShapeDtypeStruct((units, size, columns), BF16),
            jax.ShapeDtypeStruct((tokens, width), BF16),
            jax.ShapeDtypeStruct((3 * HALF_SMALL, size), F32),
            jax.ShapeDtypeStruct((maps.shape[0], late) + maps.shape[2:], BF16),
        ],
        scratch_shapes=[
            pltpu.VMEM((GIVE, 4, size, columns), BF16),
            pltpu.VMEM((units, 4, size, columns), BF16),
            pltpu.VMEM((units, 4, size, columns), BF16),
            pltpu.VMEM((units, 2, size // 2, columns), BF16),
            pltpu.VMEM((units, 2, size, columns), BF16),
            pltpu.VMEM((2, rows, width), BF16),
            pltpu.VMEM((tensor_size, share, wide), BF16),
            pltpu.VMEM((share, width), BF16),
            sems(GIVE), sems(units), sems(units, 2), sems(units, 2), sems(units, 2),
            sems(units, 2), sems(2), sems(3),
            sems(around), sems(around), sems(around), sems(around),
            pltpu.VMEM((share, HD), BF16),
            pltpu.VMEM((3 * HALF_SMALL, width), F32),
            pltpu.VMEM((8, 3 * HALF_SMALL, size), F32),
            pltpu.VMEM((3 * HALF_SMALL, size), F32),
            pltpu.VMEM((around, 3 * HALF_SMALL, size), F32),
            sems(8), sems(8), sems(around), sems(around), sems(8), sems(8),
        ],
        compiler_params=pltpu.CompilerParams(
            collective_id=1, has_side_effects=True, vmem_limit_bytes=60 << 20
        ),
        cost_estimate=pl.CostEstimate(flops=0, bytes_accessed=1 << 20, transcendentals=0),
    )(
        routed, grad_q, normed, grad_kv, part, grad_hidden, x_here, gain, router, hots, small,
        maps,
    )


def widen_kernel(first, second, third, fourth, both_out, third_out):
    both_out[:, 0] = first[...].astype(F32)
    both_out[:, 1] = second[...].astype(F32)
    early = third.shape[1]
    third_out[:, 0:early] = third[...].astype(F32)
    third_out[:, early:] = fourth[...].astype(F32)


def widen(first, second, third, fourth):
    experts, rows, columns = first.shape
    narrow = pl.BlockSpec((1, rows, columns), lambda e: (e, 0, 0))
    whole = (experts, third.shape[1] + fourth.shape[1], third.shape[2])

    def block(shape):
        return pl.BlockSpec((1,) + shape[1:], lambda e: (e, 0, 0))

    return pl.pallas_call(
        widen_kernel,
        grid=(experts,),
        in_specs=[narrow, narrow, block(third.shape), block(fourth.shape)],
        out_specs=[pl.BlockSpec((1, 2, rows, columns), lambda e: (e, 0, 0, 0)), block(whole)],
        out_shape=[
            jax.ShapeDtypeStruct((experts, 2, rows, columns), F32),
            jax.ShapeDtypeStruct(whole, F32),
        ],
        compiler_params=pltpu.CompilerParams(vmem_limit_bytes=32 << 20),
        cost_estimate=pl.CostEstimate(
            flops=0, bytes_accessed=6 * (2 * first.size + third.size + fourth.size), transcendentals=0
        ),
    )(first, second, third, fourth)


def turn_kernel(
    rows, q_ref, k_ref, v_ref, bias, gate, slot_cos, slot_sin, tok_cos, tok_sin, attended,
    hit_0, hit_1, mixed_here, output_hbm, query_hbm, keyval_hbm, maps_hbm,
    gq_out, gkv_out, part_out, maps_out, mixed_out,
    grad_gated, grad_routed, weight, product, gk_sum, gv_sum,
    load, d_send, d_recv, a_send, a_recv, own,
):
    count = a_send.shape[0] + 1
    peers = tensor_peers(count)
    experts, cap, width = rows.shape
    slots, here_width = q_ref.shape
    heads = here_width // HD
    step = 256
    greet(
        [{"dp": partner(k)} for k in range(1, d_send.shape[0])] + [{"tensor": p} for p in peers]
    )
    dealt = deal(maps_hbm, maps_out, (d_send, d_recv), pl.ds(0, maps_out.shape[1]))
    here = share_rows(mixed_here.shape[0])
    mixed_copies = [
        send_across(mixed_here, mixed_out.at[here], a_send.at[k], a_recv.at[k], p)
        for k, p in enumerate(peers)
    ]
    mixed_copies.append(pltpu.make_async_copy(mixed_here, mixed_out.at[here], own.at[0]))
    for copy in mixed_copies:
        copy.start()

    def fetch_output(e):
        slot = lax.rem(e, 2)
        return pltpu.make_async_copy(output_hbm.at[e], weight.at[slot], load.at[slot])

    def fetch_query(e, half):
        size = width // 2
        return pltpu.make_async_copy(
            query_hbm.at[e, pl.ds(half * size, size)], weight_rows(half), load.at[2 + half]
        )

    def weight_rows(half):
        return turned.at[half]

    turned = grad_routed[1]
    routed_out = grad_routed[0]

    fetch_output(0).start()

    @pl.loop(0, experts)
    def _(e):
        fetch_output(e).wait()

        @pl.when(e < experts - 1)
        def _():
            fetch_output(e + 1).start()

        at = pl.ds(pl.multiple_of(e * cap, cap), cap)
        grad_gated[at, :] = dot_nt(rows[e], weight[lax.rem(e, 2)])

    fetch_query(0, 0).start()
    fetch_query(0, 1).start()

    @pl.loop(0, heads)
    def _(h):
        lanes = rows_of(h, HD)
        gk_sum[...] = jnp.zeros_like(gk_sum)
        gv_sum[...] = jnp.zeros_like(gv_sum)

        @pl.loop(0, slots // step)
        def _(i):
            at = pl.ds(pl.multiple_of(i * step, step), step)
            q = q_ref[at, lanes]
            keys, values = k_ref[:, lanes], v_ref[:, lanes]
            probs = softmax_block(q, keys, bias[at, :].astype(F32))
            scaled = grad_gated[at, lanes] * gate[at, :]
            joined = scaled * attended[at, lanes]

            @pl.when(h == 0)
            def _():
                product[at, :] = joined

            @pl.when(h > 0)
            def _():
                product[at, :] += joined

            grad_att = scaled.astype(BF16)
            grad_probs = dot_nt(grad_att, values)
            centre = jnp.sum(probs * grad_probs, axis=-1, keepdims=True)
            grad_scores = (probs * (grad_probs - centre)).astype(BF16)
            grad_q = dot(grad_scores, keys) * HD ** (-0.5)
            gq_out[at, lanes] = rope_back(grad_q, slot_cos[at, :], slot_sin[at, :]).astype(BF16)
            gk_sum[...] += dot_tn(grad_scores, q)
            gv_sum[...] += dot_tn(probs.astype(BF16), grad_att)

        grad_k = gk_sum[...] * HD ** (-0.5)
        gkv_out[0, :, lanes] = rope_back(grad_k, tok_cos[...], tok_sin[...]).astype(BF16)
        gkv_out[1, :, lanes] = gv_sum[...].astype(BF16)

    @pl.loop(0, experts)
    def _(e):
        at = pl.ds(pl.multiple_of(e * cap, cap), cap)
        for half in range(2):
            fetch_query(e, half).wait()
            routed_out[at, pl.ds(half * (width // 2), width // 2)] = dot_nt(
                gq_out[at, :], turned[half]
            ).astype(BF16)

            @pl.when(e < experts - 1)
            def _():
                fetch_query(e + 1, half).start()

    def fetch_keyval(i):
        slot = lax.rem(i, 2)
        block = pl.ds(pl.multiple_of(i * 512, 512), 512)
        return [
            pltpu.make_async_copy(
                keyval_hbm.at[c, block], turned.at[slot, pl.ds(c * 512, 512)],
                load.at[4 + 2 * slot + c],
            )
            for c in range(2)
        ]

    for copy in fetch_keyval(0):
        copy.start()

    @pl.loop(0, width // 512)
    def _(i):
        for copy in fetch_keyval(i):
            copy.wait()

        @pl.when(i < width // 512 - 1)
        def _():
            for copy in fetch_keyval(i + 1):
                copy.start()

        at = rows_of(i, 512)
        maps = turned.at[lax.rem(i, 2)]
        part_out[:, at] = (
            dot_tn(hit_0[...] + hit_1[...], routed_out[:, at])
            + dot_nt(gkv_out[0], maps[0:512, :])
            + dot_nt(gkv_out[1], maps[512:1024, :])
        ).astype(BF16)

    columns = in_columns(
        jnp.sum(product[...], axis=1, keepdims=True),
        lax.broadcasted_iota(jnp.int32, (slots, HD), 1),
    )
    part_out[:, width : width + HD] = dot_tn(hit_0[...], columns).astype(BF16)
    part_out[:, width + HD :] = dot_tn(hit_1[...], columns).astype(BF16)
    for copy in (*mixed_copies, *dealt):
        copy.wait()


def turn_step(
    tensor_size, rows, q, k, v, bias, gate, slot_tables, tok_tables, attended, hits, mixed_here,
    output_full, query_full, keyval_full, maps, early,
):
    experts, cap, width = rows.shape
    slots, here_width = q.shape
    tok = k.shape[0]
    around = tensor_size - 1
    return pl.pallas_call(
        lambda *refs: turn_kernel(*refs[:24], (refs[24], refs[25]), *refs[26:]),
        in_specs=[VMEM] * 14 + [HBM] * 4,
        out_specs=[VMEM, VMEM, VMEM, HBM, HBM],
        out_shape=[
            jax.ShapeDtypeStruct((slots, here_width), BF16),
            jax.ShapeDtypeStruct((2, tok, here_width), BF16),
            jax.ShapeDtypeStruct((tok, width + 2 * HD), BF16),
            jax.ShapeDtypeStruct((maps.shape[0], early) + maps.shape[2:], BF16),
            jax.ShapeDtypeStruct((tok, width), BF16),
        ],
        scratch_shapes=[
            pltpu.VMEM((slots, here_width), F32),
            pltpu.VMEM((slots, width), BF16),
            pltpu.VMEM((2, width // 2, here_width), BF16),
            pltpu.VMEM((2, here_width, width), BF16),
            pltpu.VMEM((slots, HD), F32),
            pltpu.VMEM((tok, HD), F32),
            pltpu.VMEM((tok, HD), F32),
            sems(8), sems(8), sems(8), sems(around), sems(around), sems(1),
        ],
        compiler_params=pltpu.CompilerParams(
            collective_id=6, has_side_effects=True, vmem_limit_bytes=58 << 20
        ),
        cost_estimate=pl.CostEstimate(
            flops=10 * slots * tok * here_width, bytes_accessed=300 << 20, transcendentals=0
        ),
    )(
        rows, q, k, v, bias, gate, *slot_tables, *tok_tables, attended, *hits, mixed_here,
        output_full, query_full, keyval_full, maps,
    )


def partner(k):
    me = lax.axis_index("dp")
    place = me
    for bit in (1, 2, 4):
        place = place + bit * lax.rem(k // bit, 2) * (1 - 2 * lax.rem(me // bit, 2))
    return place


def expert_kernel(
    x_hbm, cot_hbm, gate_up_hbm, down_hbm, rest_hbm,
    back_out, rows_out, grad_gate_hbm, grad_up_hbm, grad_down_hbm,
    x_all, g_all, w_gate, w_up, w_down, act, grads, back, product, stage_up, stage_down,
    rows_here, rows_got, x_send, x_recv, b_send, b_recv, load, up_sem, down_sem, r_send, r_recv,
):
    peers = x_send.shape[0]
    slots, wide = x_all.shape
    width = wide - HD
    hidden = w_gate.shape[1]
    size = slots // peers
    pair = 2 * size
    step = 256
    whole_steps = hidden // step
    tail = hidden - whole_steps * step

    per = width // peers
    first = down_hbm.shape[1]
    loads = [
        pltpu.make_async_copy(cot_hbm, g_all, load.at[0]),
        pltpu.make_async_copy(down_hbm, w_down.at[:, pl.ds(0, first)], load.at[1]),
        pltpu.make_async_copy(
            rest_hbm, w_down.at[:, pl.ds(first, hidden - first)], load.at[3 + 2 * peers]
        ),
        pltpu.make_async_copy(
            x_hbm.at[pl.ds(0, size)], x_all.at[pl.ds(0, size)], load.at[2 + 2 * peers]
        ),
    ]
    for j in range(peers):
        for g, target in enumerate((w_gate, w_up)):
            loads.append(
                pltpu.make_async_copy(
                    gate_up_hbm.at[j, g], target.at[pl.ds(j * per, per)], load.at[2 + 2 * j + g]
                )
            )
    for copy in loads:
        copy.start()

    around = tensor_peers(r_send.shape[0] + 1)
    share = width // (len(around) + 1)
    greet([{"dp": partner(k)} for k in range(1, peers)] + [{"tensor": p} for p in around])

    def block(k):
        return pl.ds(pl.multiple_of(k * size, size), size)

    def send_x(k):
        return send_to(
            x_hbm.at[block(k)], x_all.at[block(k)], x_send.at[k], x_recv.at[k], partner(k)
        )

    def send_back(k):
        return send_to(
            back.at[block(k)], back_out.at[block(k)], b_send.at[k], b_recv.at[k], partner(k)
        )

    for k in (1, 2, 4, 3, 5):
        send_x(k).start()
    for copy in loads:
        copy.wait()

    def send_rows(k, group):
        rows = rows_of(group, pair)
        return send_across(
            rows_here.at[rows, rows_of(around[k], share)], rows_got.at[k, rows],
            r_send.at[k, group], r_recv.at[k, group], around[k],
        )

    @pl.loop(0, peers // 2)
    def _(group):
        rows = pl.ds(pl.multiple_of(group * pair, pair), pair)

        @pl.when(group > 0)
        def _():
            send_x(2 * group).wait_recv()

        send_x(2 * group + 1).wait_recv()
        columns = x_all[rows, width:].astype(F32)
        gate_of_row = columns[:, 0:1] + columns[:, 1:2] + columns[:, 2:3]
        g_all[rows, :] = (g_all[rows, :].astype(F32) * gate_of_row).astype(BF16)
        product[...] = jnp.zeros_like(product)

        def chunk(start, amount):
            cols = pl.ds(start, amount)
            x = x_all[rows, 0:width]
            gate = dot(x, w_gate[:, cols])
            up = dot(x, w_up[:, cols])
            grad_act = jnp.zeros((pair, amount), F32)
            for j in range(peers):
                grad_act += dot_nt(g_all[rows, j * per : (j + 1) * per], w_down[j, cols, :])
            sigmoid = 1.0 / (1.0 + jnp.exp(-gate))
            silu = gate * sigmoid
            activated = (silu * up).astype(BF16)
            act[rows, cols] = activated
            both = activated.astype(F32) * grad_act
            for part in range(amount // HD):
                product[...] += both[:, part * HD : (part + 1) * HD]
            grads[rows, cols] = (
                grad_act * up * sigmoid * (1.0 + gate * (1.0 - sigmoid))
            ).astype(BF16)
            grads[rows, pl.ds(hidden + start, amount)] = (grad_act * silu).astype(BF16)

        @pl.loop(0, whole_steps)
        def _(i):
            chunk(pl.multiple_of(i * step, step), step)

        if tail:
            chunk(whole_steps * step, tail)

        @pl.loop(0, width // step)
        def _(i):
            at = pl.ds(pl.multiple_of(i * step, step), step)
            back[rows, at] = (
                dot_nt(grads[rows, 0:hidden], w_gate[at, :])
                + dot_nt(grads[rows, hidden:], w_up[at, :])
            ).astype(BF16)

        total = jnp.sum(product[...], axis=1, keepdims=True)
        back[rows, width:] = in_columns(
            total, lax.broadcasted_iota(jnp.int32, (pair, HD), 1)
        )

        @pl.when(group == 0)
        def _():
            send_x(6).start()
            send_x(7).start()
            back_out[0:size, :] = back[0:size, :]

        @pl.when(group > 0)
        def _():
            send_back(2 * group).start()

        send_back(2 * group + 1).start()
        for j in range(peers):
            rows_here[rows, j * per : (j + 1) * per] = dot(act[rows, :], w_down[j]).astype(BF16)
        for k in range(len(around)):
            send_rows(k, group).start()

    def store_up(j, slot):
        return (
            pltpu.make_async_copy(
                stage_up.at[slot, :, pl.ds(0, hidden)], grad_gate_hbm.at[j], up_sem.at[slot, 0]
            ),
            pltpu.make_async_copy(
                stage_up.at[slot, :, pl.ds(hidden, hidden)], grad_up_hbm.at[j], up_sem.at[slot, 1]
            ),
        )

    @pl.loop(0, peers)
    def _(j):
        slot = lax.rem(j, 2)

        @pl.when(j > 1)
        def _():
            for copy in store_up(j - 2, slot):
                copy.wait()

        at = pl.ds(pl.multiple_of(j * per, per), per)
        stage_up[slot] = dot_tn(x_all[:, at], grads[...]).astype(BF16)
        for copy in store_up(j, slot):
            copy.start()

    def store_down(start, amount, slot):
        return pltpu.make_async_copy(
            stage_down.at[slot, :, pl.ds(0, amount)],
            grad_down_hbm.at[:, pl.ds(start, amount)],
            down_sem.at[slot],
        )

    def down_piece(start, amount, slot):
        piece = dot_tn(act[:, pl.ds(start, amount)], g_all[...]).astype(BF16)
        for j in range(peers):
            stage_down[slot, j, 0:amount, :] = piece[:, j * per : (j + 1) * per]
        store_down(start, amount, slot).start()

    @pl.loop(0, whole_steps)
    def _(i):
        slot = lax.rem(i, 2)

        @pl.when(i > 1)
        def _():
            store_down(pl.multiple_of((i - 2) * step, step), step, slot).wait()

        down_piece(pl.multiple_of(i * step, step), step, slot)

    last = whole_steps - 1
    store_down((last - 1) * step, step, (last - 1) % 2).wait()
    if tail:
        down_piece(whole_steps * step, tail, (last - 1) % 2)
        store_down(whole_steps * step, tail, (last - 1) % 2).wait()
    store_down(last * step, step, last % 2).wait()
    for j in (peers - 2, peers - 1):
        for copy in store_up(j, j % 2):
            copy.wait()

    @pl.loop(0, peers // 2)
    def _(group):
        rows = rows_of(group, pair)
        total = rows_here[rows, share_rows(share)].astype(F32)
        for k in range(len(around)):
            send_rows(k, group).wait()
            total = total + rows_got[k, rows, :].astype(F32)
        rows_out[rows, :] = total.astype(BF16)

    for k in range(1, peers):
        send_x(k).wait_send()
        send_back(k).wait()


def expert_step(tensor_size, x_rows, cot_rows, up_slices, down_slices, down_rest):
    slots, wide = x_rows.shape
    width = wide - HD
    peers, hidden, per = down_slices.shape
    hidden += down_rest.shape[1]
    vmem = pl.BlockSpec(memory_space=pltpu.VMEM)
    hbm = pl.BlockSpec(memory_space=pl.ANY)
    step = 256
    return pl.pallas_call(
        expert_kernel,
        in_specs=[hbm] * 5,
        out_specs=[vmem, vmem, hbm, hbm, hbm],
        out_shape=[
            jax.ShapeDtypeStruct((slots, wide), BF16),
            jax.ShapeDtypeStruct((slots, width // tensor_size), BF16),
            jax.ShapeDtypeStruct((peers, per, hidden), BF16),
            jax.ShapeDtypeStruct((peers, per, hidden), BF16),
            jax.ShapeDtypeStruct((peers, hidden, per), BF16),
        ],
        scratch_shapes=[
            pltpu.VMEM((slots, wide), BF16),
            pltpu.VMEM((slots, width), BF16),
            pltpu.VMEM((width, hidden), BF16),
            pltpu.VMEM((width, hidden), BF16),
            pltpu.VMEM((peers, hidden, per), BF16),
            pltpu.VMEM((slots, hidden), BF16),
            pltpu.VMEM((slots, 2 * hidden), BF16),
            pltpu.VMEM((slots, wide), BF16),
            pltpu.VMEM((2 * slots // peers, HD), F32),
            pltpu.VMEM((2, per, 2 * hidden), BF16),
            pltpu.VMEM((2, peers, step, per), BF16),
            pltpu.VMEM((slots, width), BF16),
            pltpu.VMEM((tensor_size - 1, slots, width // tensor_size), BF16),
            pltpu.SemaphoreType.DMA((peers,)),
            pltpu.SemaphoreType.DMA((peers,)),
            pltpu.SemaphoreType.DMA((peers,)),
            pltpu.SemaphoreType.DMA((peers,)),
            sems(4 + 2 * peers), sems(2, 2), sems(2),
            sems(tensor_size - 1, peers // 2), sems(tensor_size - 1, peers // 2),
        ],
        compiler_params=pltpu.CompilerParams(
            collective_id=2, has_side_effects=True, vmem_limit_bytes=60 << 20
        ),
        cost_estimate=pl.CostEstimate(
            flops=18 * slots * width * hidden, bytes_accessed=300 << 20, transcendentals=0
        ),
    )(x_rows, cot_rows, up_slices, down_slices, down_rest)


class Movers:
    def __init__(self, dp, experts, tensor):
        self.dp, self.experts, self.tensor = dp, experts, tensor
        self.ratio = dp // experts
        self.groups = self.pairs = None
        if self.ratio > 1:
            self.groups = [[g * experts + e for e in range(experts)] for g in range(self.ratio)]
            self.pairs = [[g * experts + e for g in range(self.ratio)] for e in range(experts)]

    def swap(self, blocks):
        return lax.all_to_all(blocks, "dp", 0, 0, axis_index_groups=self.groups, tiled=True)

    def fetch(self, shards):
        mine = self.swap(shards)
        if self.ratio > 1:
            mine = lax.all_gather(mine, "dp", axis=0, axis_index_groups=self.pairs, tiled=True)
        return mine

    def give_back(self, slices):
        if self.ratio > 1:
            slices = lax.psum_scatter(
                slices, "dp", scatter_dimension=0, axis_index_groups=self.pairs, tiled=True
            )
        return self.swap(slices)

    def exchange(self, rows):
        size = rows.shape[0] // self.experts
        blocks = [rows[:size]]
        for k in range(1, self.experts):
            pairs = [(i, i ^ k) for i in range(self.dp)]
            blocks.append(lax.ppermute(rows[k * size : (k + 1) * size], "dp", pairs))
        return jnp.concatenate(blocks, axis=0)

    def across(self, block, k):
        return lax.ppermute(block, "tensor", [(i, i ^ k) for i in range(self.tensor)])

    def reduce_rows(self, part, dtype=BF16):
        z = lax.axis_index("tensor")
        size = part.shape[0] // self.tensor
        total = lax.dynamic_slice_in_dim(part, z * size, size, axis=0)
        sent = part.astype(dtype)
        for k in range(1, self.tensor):
            block = lax.dynamic_slice_in_dim(sent, (z ^ k) * size, size, axis=0)
            total = total + self.across(block, k).astype(F32)
        return total

    def gather_rows(self, rows):
        z = lax.axis_index("tensor")
        size = rows.shape[0]
        rows = rows.astype(BF16)
        full = jnp.zeros((size * self.tensor,) + rows.shape[1:], BF16)
        for k in range(self.tensor):
            block = rows if k == 0 else self.across(rows, k)
            full = lax.dynamic_update_slice_in_dim(full, block, (z ^ k) * size, axis=0)
        return full


def expert_plain(movers, expert_in, cot_rows, up_slices, down_slices):
    dp_size, hidden_here, per_dp = down_slices.shape
    model_width = dp_size * per_dp
    gate_full, up_full = (up_slices[:, g].reshape(model_width, hidden_here) for g in range(2))
    down_full = down_slices.transpose(1, 0, 2).reshape(hidden_here, model_width)
    x_rows, gate_of_row = without_column(movers.exchange(expert_in))
    g_rows = (cot_rows.astype(F32) * gate_of_row).astype(BF16)
    gate = dot(x_rows, gate_full)
    up = dot(x_rows, up_full)
    sigmoid_gate = jax.nn.sigmoid(gate)
    silu_gate = gate * sigmoid_gate
    activated = (silu_gate * up).astype(BF16)
    grad_act = dot_nt(g_rows, down_full)
    grad_gate = (grad_act * up * sigmoid_gate * (1.0 + gate * (1.0 - sigmoid_gate))).astype(BF16)
    grad_up = (grad_act * silu_gate).astype(BF16)
    gate_times_grad = jnp.sum(activated.astype(F32) * grad_act, axis=1, keepdims=True)
    grad_expert_in = with_column(
        (dot_nt(grad_gate, gate_full) + dot_nt(grad_up, up_full)).astype(BF16), gate_times_grad
    )
    return (
        movers.exchange(grad_expert_in),
        dot(activated, down_full, BF16),
        dot_tn(x_rows, grad_gate, BF16).reshape(dp_size, per_dp, -1),
        dot_tn(x_rows, grad_up, BF16).reshape(dp_size, per_dp, -1),
        dot_tn(activated, g_rows, BF16).reshape(-1, dp_size, per_dp).transpose(1, 0, 2),
    )


def on_device(
    dp_size,
    tensor_size,
    tokens,
    cotangent,
    parents,
    attention_routes,
    expert_routes,
    slot_order,
    gain_attention,
    keyval_weight,
    query_weight,
    output_weight,
    attention_router,
    gain_feedforward,
    expert_router,
    gate_up_weight,
    down_weight,
):
    tok_count, model_width = tokens.shape
    pair_count = TOPK * tok_count
    att_experts = query_weight.shape[0]
    mlp_experts = gate_up_weight.shape[0]
    att_cap = tok_count * 5 // 16
    mlp_cap = pair_count // mlp_experts
    att_slots = att_experts * att_cap
    mlp_slots = mlp_experts * mlp_cap
    width_here = query_weight.shape[2]
    rows_here = tok_count // tensor_size
    movers = Movers(dp_size, mlp_experts, tensor_size)
    fast = dp_size == 8 and mlp_experts == 8
    tie = lax.optimization_barrier

    small = jnp.concatenate(
        [gain_attention[:, None], gain_feedforward[:, None], attention_router, expert_router], axis=1
    )
    small_full = lax.all_gather(small, "dp", axis=0, tiled=True)
    small_full, down_weight = tie((small_full, down_weight))
    gain_attn_full = small_full[:, 0].astype(F32)
    gain_mlp_full = small_full[:, 1].astype(F32)
    router_att = small_full[:, 2 : 2 + att_experts]
    router_mlp = small_full[:, 2 + att_experts :]

    inside, depth = ancestry(parents[0])
    token_index = jnp.arange(tok_count, dtype=jnp.int32)
    pair_order = jnp.arange(pair_count, dtype=jnp.int32).reshape(tok_count, TOPK)
    att_hits = slot_hits(
        slot_places(attention_routes, pair_order, att_cap, att_experts), att_slots
    )
    priority = slot_order[0][:, None] * TOPK + jnp.arange(TOPK, dtype=jnp.int32)[None, :]
    home = lax.rem(lax.axis_index("dp"), mlp_experts)
    mlp_hits = slot_hits(
        slot_places(expert_routes ^ home, priority, mlp_cap, mlp_experts), mlp_slots
    )
    att_pick = (att_hits[0] | att_hits[1]).astype(BF16)
    mlp_pick = (mlp_hits[0] | mlp_hits[1]).astype(BF16)

    def to_slots(hits, pair_values):
        return jnp.sum(
            sum(jnp.where(hits[k], pair_values[:, k][None, :], 0) for k in range(TOPK)), axis=1
        )

    def to_pairs(hits, slot_values):
        return jnp.stack(
            [jnp.sum(jnp.where(hits[k], slot_values[:, None], 0.0), axis=0) for k in range(TOPK)],
            axis=1,
        )

    def position_of(token):
        segment = token // SEG
        level = jnp.sum(
            jnp.where(segment[:, None] == jnp.arange(depth.shape[0])[None, :], depth[None, :], 0),
            axis=1,
        )
        return level * SEG + token % SEG

    pair_token = jnp.broadcast_to(token_index[:, None], (tok_count, TOPK))
    slot_token = to_slots(att_hits, pair_token)
    slot_filled = jnp.any(att_hits[0] | att_hits[1], axis=1)
    slot_tables = rope_tables(position_of(slot_token))
    tok_tables = rope_tables(position_of(token_index))
    segment_hot = (
        (slot_token // SEG)[:, None] == jnp.arange(inside.shape[0], dtype=jnp.int32)[None, :]
    ).astype(F32)
    reach = dot(segment_hot, jnp.repeat(inside.astype(F32), SEG, axis=1)) > 0.5
    allowed = reach & (token_index[None, :] <= slot_token[:, None]) & slot_filled[:, None]
    bias = jnp.where(allowed, 0.0, NEGATIVE).astype(BF16)

    early = down_weight.shape[1] // 2 if fast else down_weight.shape[1]
    down_slices = movers.fetch(down_weight[:, :early])
    cot_send = dot(mlp_pick, cotangent, BF16)

    inputs = tokens.astype(F32)
    normal_attn, scale_attn = norm_forward(inputs)
    normed = (normal_attn * gain_attn_full).astype(BF16)
    att_gates = picked_softmax(dot(normed, router_att), attention_routes)
    att_gate_slots = to_slots(att_hits, att_gates)[:, None]
    routed = dot(att_pick, normed, BF16).reshape(att_experts, att_cap, model_width)
    if fast:
        mlp_bits = tuple(hit.astype(BF16) for hit in mlp_hits)
        expert_lanes = [
            (expert_routes[:, k : k + 1] == jnp.arange(HD, dtype=jnp.int32)[None, :]).astype(F32)
            for k in range(TOPK)
        ]
        keyval_weight, query_weight, output_weight, *before = tie(
            (keyval_weight, query_weight, output_weight, routed, cot_send, bias, att_gate_slots)
            + slot_tables + tok_tables + mlp_bits + tuple(expert_lanes)
        )
        routed, cot_send, bias, att_gate_slots = before[:4]
        slot_tables, tok_tables = before[4:6], before[6:8]
        mlp_bits, expert_lanes = before[8:10], before[10:12]
        keyval_full, query_full, output_full, cot_rows = gather_maps(
            tensor_size, mlp_experts,
            (keyval_weight, query_weight, output_weight), (1, 1, 2), (2, 2, 2), cot_send,
        )
    else:
        keyval_full = lax.all_gather(keyval_weight, "dp", axis=1, tiled=True)
        query_full = lax.all_gather(query_weight, "dp", axis=1, tiled=True)
        output_full = lax.all_gather(output_weight, "dp", axis=2, tiled=True)
    query_full, keyval_full, down_slices, gate_up_weight = tie(
        (query_full, keyval_full, down_slices, gate_up_weight)
    )
    up_slices = movers.fetch(gate_up_weight)
    keyval = jnp.concatenate([dot(normed, keyval_full[0]), dot(normed, keyval_full[1])], axis=1)
    query_raw = jnp.einsum(
        "ecd,edf->ecf", routed, query_full, preferred_element_type=F32
    ).reshape(att_slots, width_here)
    queries, key_rows, values, attended, gated = attend(
        query_raw, keyval, bias, att_gate_slots, slot_tables, tok_tables
    )
    gated_slots = gated.reshape(att_experts, att_cap, width_here)
    att_rows = jnp.einsum(
        "ecf,efd->ecd", gated_slots, output_full, preferred_element_type=F32
    ).reshape(att_slots, model_width)
    att_rows = att_rows.astype(BF16)

    z = lax.axis_index("tensor")

    def share(rows):
        return lax.dynamic_slice_in_dim(rows, z * rows_here, rows_here, axis=0)

    def hots(gates, picks, experts):
        lanes = jnp.arange(HD, dtype=jnp.int32)[None, :]
        hot = [(share(picks)[:, k : k + 1] == lanes).astype(F32) for k in range(TOPK)]
        return jnp.stack(hot + [sum(hot[k] * share(gates)[:, k : k + 1] for k in range(TOPK))])

    def padded(router):
        return jnp.pad(router, ((0, 0), (0, HD - router.shape[1])))

    if fast:
        hidden, mlp_in, mlp_gates, expert_in, down_rest = hidden_step(
            tensor_size, att_pick, att_rows, share(tokens), gain_mlp_full[None],
            padded(router_mlp), expert_lanes, mlp_bits, down_weight[:, early:],
        )
        mlp_gates = mlp_gates[:, :TOPK]
    else:
        hidden = share(inputs) + movers.reduce_rows(dot_tn(att_pick, att_rows))
        mlp_in = movers.gather_rows((norm_forward(hidden)[0] * gain_mlp_full).astype(BF16))
        cot_rows = movers.exchange(cot_send)
        mlp_gates = picked_softmax(dot(mlp_in, router_mlp), expert_routes)
        expert_in = with_column(
            dot(mlp_pick, mlp_in, BF16), to_slots(mlp_hits, mlp_gates)[:, None]
        )
    expert_in, up_slices = tie((expert_in, up_slices))

    if fast:
        back = expert_step(
            tensor_size, expert_in, cot_rows, up_slices, down_slices, down_rest
        )
    else:
        back = expert_plain(movers, expert_in, cot_rows, up_slices, down_slices)
    grad_in_slots, expert_out, grad_gate_w, grad_up_w, grad_down_w = back

    if fast:
        (
            grad_hidden, _, grad_gain_mlp, grad_mlp_logits, mixed, grad_att_rows, grad_gate_w,
            grad_up_w, grad_output_w,
        ) = back_step(
            tensor_size, mlp_experts, grad_in_slots, mlp_pick,
            mlp_bits, hidden, share(cotangent),
            gain_mlp_full[None], padded(router_mlp),
            hots(mlp_gates, expert_routes, mlp_experts), mlp_gates.T, att_pick, gated, att_experts,
            expert_out, grad_gate_w, grad_up_w,
        )
        grad_gain_mlp = grad_gain_mlp[0]
        grad_mlp_logits = grad_mlp_logits[:, :mlp_experts]
    else:
        out_slots = movers.exchange(expert_out)
        grad_gate_w = movers.give_back(grad_gate_w)
        grad_up_w = movers.give_back(grad_up_w)
        grad_in_slots, gate_times_grad = without_column(grad_in_slots)
        mlp_products = movers.reduce_rows(to_pairs(mlp_hits, gate_times_grad[:, 0]), F32)
        grad_mlp_in = movers.reduce_rows(dot_tn(mlp_pick, grad_in_slots))
        grad_mlp_logits = router_backward(
            share(mlp_gates), mlp_products, share(expert_routes), mlp_experts
        )
        grad_mlp_in = grad_mlp_in + dot_nt(grad_mlp_logits, router_mlp)
        normal_mlp, scale_mlp = norm_forward(hidden)
        grad_hidden_norm, grad_gain_mlp = norm_backward(
            grad_mlp_in, normal_mlp, scale_mlp, gain_mlp_full
        )
        grad_hidden = share(cotangent).astype(F32) + grad_hidden_norm
        grad_att_pair = movers.gather_rows(grad_hidden)
        grad_att_rows = dot(att_pick, grad_att_pair, BF16)
        grad_output_w = jnp.einsum(
            "ecf,ecd->efd",
            gated_slots,
            grad_att_rows.reshape(att_experts, att_cap, model_width),
            preferred_element_type=BF16,
        )
        gate_matrix = sum(
            jnp.where(mlp_hits[k], mlp_gates[:, k][None, :], 0.0) for k in range(TOPK)
        )
        matrix_high = gate_matrix.astype(BF16)
        matrix_low = (gate_matrix - matrix_high.astype(F32)).astype(BF16)
        mlp_part = (dot_tn(matrix_high, out_slots) + dot_tn(matrix_low, out_slots)).astype(BF16)
        mixed = movers.gather_rows(hidden + movers.reduce_rows(mlp_part))
    grad_router_mlp = dot_tn(share(mlp_in), grad_mlp_logits)

    grad_att_rows = grad_att_rows.reshape(att_experts, att_cap, model_width)
    grad_output_out = lax.psum_scatter(grad_output_w, "dp", scatter_dimension=2, tiled=True)
    if fast:
        half = grad_down_w.shape[1] * 6 // 128 * 16
        grad_q, grad_kv, normed_part, grad_down_early, mixed = turn_step(
            tensor_size, grad_att_rows, queries, key_rows, values, bias, att_gate_slots,
            slot_tables, tok_tables, attended, [hit.astype(BF16) for hit in att_hits], mixed,
            output_full, query_full, keyval_full, grad_down_w, half,
        )
    else:
        grad_down_early, grad_down_late = jnp.split(movers.give_back(grad_down_w), 2, axis=1)
        grad_gated = jnp.einsum(
            "ecd,efd->ecf", grad_att_rows, output_full, preferred_element_type=F32
        ).reshape(att_slots, width_here)
        att_products = to_pairs(
            att_hits, jnp.sum(grad_gated * attended, axis=1) * att_gate_slots[:, 0]
        )
        grad_q, grad_k, grad_v = attend_back(
            queries, key_rows, values, bias, att_gate_slots, slot_tables, tok_tables, grad_gated
        )
        grad_routed = jnp.einsum(
            "ecf,edf->ecd",
            grad_q.reshape(att_experts, att_cap, width_here),
            query_full,
            preferred_element_type=F32,
        ).reshape(att_slots, model_width)
        normed_part = (
            dot_tn(att_pick, grad_routed.astype(BF16))
            + dot_nt(grad_k, keyval_full[0])
            + dot_nt(grad_v, keyval_full[1])
        )
        grad_kv = jnp.stack([grad_k, grad_v])
    grad_query_slots = grad_q.reshape(att_experts, att_cap, width_here)
    if fast:
        small = jnp.concatenate(
            [
                jnp.zeros((1, model_width), F32),
                grad_gain_mlp[None],
                jnp.zeros((HALF_SMALL - 2, model_width), F32),
                grad_router_mlp.T,
            ],
            axis=0,
        )
        map_sums, grad_tokens, small_grads, grad_down_late = final_step(
            tensor_size, routed, grad_query_slots, normed, grad_kv, normed_part,
            grad_hidden, share(tokens), gain_attn_full[None], padded(router_att),
            hots(att_gates, attention_routes, att_experts), small, grad_down_w,
            grad_down_w.shape[1] - half,
        )
        small_grads = jnp.concatenate([small_grads[:2], small_grads[HALF_SMALL:]], axis=0).T
        grad_query_out, grad_keyval_out = map_sums[:att_experts], map_sums[att_experts:]
    else:
        grad_query_w = jnp.einsum(
            "ecd,ecf->edf", routed, grad_query_slots, preferred_element_type=BF16
        )
        grad_keyval_w = jnp.stack([dot_tn(normed, grad, BF16) for grad in grad_kv])
        grad_query_out = lax.psum_scatter(grad_query_w, "dp", scatter_dimension=1, tiled=True)
        grad_keyval_out = lax.psum_scatter(grad_keyval_w, "dp", scatter_dimension=1, tiled=True)
        grad_normed = movers.reduce_rows(normed_part)
        grad_att_logits = router_backward(
            share(att_gates), movers.reduce_rows(att_products, F32), share(attention_routes),
            att_experts,
        )
        grad_normed = grad_normed + dot_nt(grad_att_logits, router_att)
        grad_input_norm, grad_gain_attn = norm_backward(
            grad_normed, share(normal_attn), share(scale_attn), gain_attn_full
        )
        grad_tokens = movers.gather_rows(grad_hidden + grad_input_norm)
        grad_router_att = dot_tn(share(normed), grad_att_logits)
        small_grads = jnp.concatenate(
            [grad_gain_attn[:, None], grad_gain_mlp[:, None], grad_router_att, grad_router_mlp],
            axis=1,
        )
        small_grads = lax.psum(
            lax.psum_scatter(small_grads, "dp", scatter_dimension=0, tiled=True), "tensor"
        )
    grad_tokens, grad_output_out = tie((grad_tokens, grad_output_out))
    grad_tokens = grad_tokens.astype(F32)
    grad_up_w, grad_down_w = widen(
        grad_gate_w, grad_up_w, grad_down_early, grad_down_late
    )
    return (
        mixed,
        grad_tokens,
        small_grads[:, 0],
        grad_keyval_out.astype(F32),
        grad_query_out.astype(F32),
        grad_output_out.astype(F32),
        small_grads[:, 2 : 2 + att_experts],
        small_grads[:, 1],
        small_grads[:, 2 + att_experts :],
        grad_up_w,
        grad_down_w,
    )


def solution(mesh):
    placed = (
        P("dp", None),
        P("dp", None),
        P("dp", None),
        P("dp", None),
        P("dp", None),
        P("dp", None),
        P("dp"),
        P(None, "dp", "tensor"),
        P(None, "dp", "tensor"),
        P(None, "tensor", "dp"),
        P("dp", None),
        P("dp"),
        P("dp", None),
        P(None, None, "dp", "tensor"),
        P(None, "tensor", "dp"),
    )
    return jax.shard_map(
        functools.partial(on_device, mesh.shape["dp"], mesh.shape["tensor"]),
        mesh=mesh,
        in_specs=placed,
        out_specs=(
            P("dp", None),
            P("dp", None),
            P("dp"),
            P(None, "dp", "tensor"),
            P(None, "dp", "tensor"),
            P(None, "tensor", "dp"),
            P("dp", None),
            P("dp"),
            P("dp", None),
            P(None, None, "dp", "tensor"),
            P(None, "tensor", "dp"),
        ),
        check_vma=False,
    )
```
